32 devices in a mesh: section: 4 (over y, core), dp: 8 (over z, x).
Axes of the slice: x: 2, y: 2, z: 4, core: 2. Of those that a mesh axis runs over, the one named last changes fastest.
Arguments:
- block_input: bfloat16 [6144, 768], P('dp', 'section'), may hold values from -6 to 6
- cotangent: bfloat16 [6144, 768], P('dp', 'section'), may hold values from -6 to 6
- grid_sizes: int32 [16, 2, 2], P('dp'), may hold values from 8 to 13
- section_weight: bfloat16 [4, 768, 4608], P('section'), may hold values from -4 to 4
- norm_gain: float32 [4, 768], P('section'), may hold values from 0.5 to 1.5
- norm_bias: float32 [4, 768], P('section'), may hold values from -1 to 1
- first_vector: float32 [4, 3072], P('section'), may hold values from -2 to 2
- second_vector: float32 [4, 768], P('section'), may hold values from -1.5 to 1.5
Outputs:
- activations: bfloat16 [4, 6144, 768], P('section', 'dp')
- input_grads: bfloat16 [4, 6144, 768], P('section', 'dp')
- section_weight_grad: float32 [4, 768, 4608], P('section')
- norm_gain_grad: float32 [4, 768], P('section')
- norm_bias_grad: float32 [4, 768], P('section')
- first_vector_grad: float32 [4, 3072], P('section')
- second_vector_grad: float32 [4, 768], P('section')
The draws below stay inside these ranges and needn't reach their ends.
Inputs may be any that keep to these rules, and one draw needn't show every extreme that they name: `grid_sizes`: each packed row holds two images laid out from slot 0; the rest of the row is padding.
All inputs are finite; a program needn't handle non-finite values.
Results may differ from the reference program's by a relative error of at most 0.015.
Values may be sent and summed in bfloat16 or wider, within the bound.
No kernel may reach another device: no remote copies, remote signals or barrier semaphores. Data moves between devices by JAX's collectives and lax.ppermute only.
A program may use at most 192 MiB of HBM per device.

```python
import math
import jax
import jax.numpy as jnp
from jax import lax

D = 768
HEADS = 12
HEAD_DIM = 64
FF = 3072
ROW_LEN = 384
SECTIONS = 4
ROWS = 16
TOKENS = 6144


def draw_section_weight(key, part):
    key = jax.random.fold_in(key, 11)
    columns = jnp.arange(6 * D)
    attention_scale = jnp.where(columns < 3 * D, D ** (-0.5), jnp.where(columns < 4 * D, (D // 64) ** (-0.5), FF ** (-0.5)))
    feed_scale = jnp.where(columns < 4 * D, D ** (-0.5), FF ** (-0.5))
    sections = jnp.arange(SECTIONS)[:, None]
    column_scale = jnp.where(sections % 2 == 0, attention_scale[None, :], feed_scale[None, :])
    base = jnp.clip(jax.random.normal(key, (SECTIONS, D, 6 * D), jnp.float32), -4.0, 4.0)
    return (base * column_scale[:, None, :]).astype(jnp.bfloat16)


def draw_first_vector(key, part):
    key = jax.random.fold_in(key, 23)
    bias_key, size_key, angle_key = jax.random.split(key, 3)
    biases = jnp.clip(0.3 * jax.random.normal(bias_key, (SECTIONS, FF), jnp.float32), -1.5, 1.5)
    magnitude = jnp.exp(jax.random.uniform(size_key, (SECTIONS, D // 2), jnp.float32, math.log(0.05), math.log(2.0)))
    direction = jax.random.uniform(angle_key, (SECTIONS, D // 2), jnp.float32, -math.pi, math.pi)
    freqs = jnp.concatenate([magnitude * jnp.cos(direction), magnitude * jnp.sin(direction)], axis=1)
    rotary_part = jnp.concatenate([jnp.zeros((SECTIONS, 3 * D), jnp.float32), freqs], axis=1)
    columns = jnp.arange(FF)[None, :]
    sections = jnp.arange(SECTIONS)[:, None]
    return jnp.where((sections % 2 == 0) & (columns >= 3 * D), rotary_part, biases)


def place_ends(drawn, stream_key, smallest, top_value):
    place = [jax.random.randint(jax.random.fold_in(stream_key, axis), (), 0, length) for axis, length in enumerate(drawn.shape)]
    widest = drawn.shape.index(max(drawn.shape))
    neighbour = place[:widest] + [(place[widest] + 1) % drawn.shape[widest]] + place[widest + 1:]
    return drawn.at[tuple(place)].set(smallest).at[tuple(neighbour)].set(top_value)


def level_of(own_key, shape, cuts, smallest, top_value):
    factor_of = 1.0
    for axis_at, blocks in cuts:
        draws = jax.random.uniform(jax.random.fold_in(jax.random.fold_in(own_key, 6), axis_at), (blocks,), jnp.float32, smallest / len(cuts), top_value / len(cuts))
        factor_of = factor_of * jnp.repeat(jnp.exp(draws), shape[axis_at] // blocks).reshape((-1,) + (1,) * (len(shape) - 1 - axis_at))
    return factor_of


def bell_draw(own_key, shape, scale, most, cuts=(), kind=jnp.bfloat16):
    values = jax.random.normal(own_key, shape, jnp.float32) * scale
    if len(cuts) > 0:
        values = level_of(own_key, shape, cuts, -0.22, 0.18) * values
    return jnp.clip(values, min=-most, max=most).astype(kind)


def setup_inputs(seed: int = 0) -> dict:
    splits = jax.random.split(jax.random.key(seed), 9)
    return {
        "block_input": bell_draw(splits[0], (TOKENS, D), 1.0, 6.0, ((0, 8), (1, 4))),
        "cotangent": bell_draw(splits[1], (TOKENS, D), 1.0, 6.0, ((0, 8), (1, 4))),
        "grid_sizes": place_ends(jax.random.randint(splits[2], (ROWS, 2, 2), 8, 14), jax.random.fold_in(splits[2], 1), 8, 13).astype(jnp.int32),
        "section_weight": draw_section_weight(jax.random.fold_in(splits[8], 71), 0),
        "norm_gain": jnp.clip(1.0 + 0.1 * jax.random.normal(splits[4], (SECTIONS, D), jnp.float32), 0.5, 1.5),
        "norm_bias": bell_draw(splits[5], (SECTIONS, D), 0.2, 1.0, ((0, 4),), jnp.float32),
        "first_vector": draw_first_vector(jax.random.fold_in(splits[8], 71), 0),
        "second_vector": bell_draw(splits[7], (SECTIONS, D), 0.3, 1.5, ((0, 4),), jnp.float32),
    }


@jax.custom_vjp
def low(v):
    return lax.optimization_barrier(v.astype(jnp.bfloat16)).astype(jnp.float32)

@jax.custom_vjp
def low_back(v):
    return v

def low_keep(v):
    return (low(v), None)

def low_pass(kept, grad):
    return (grad,)

def back_keep(v):
    return (v, None)

def back_low(kept, grad):
    return (low(grad),)
low.defvjp(low_keep, low_pass)
low_back.defvjp(back_keep, back_low)
highest = lax.Precision.HIGHEST

def layout(grid_rows, row_len):
    heights = grid_rows[:, :, 0]
    widths = grid_rows[:, :, 1]
    counts = heights * widths
    end_one = counts[:, 0:1]
    end_two = end_one + counts[:, 1:2]
    places = jnp.arange(row_len, dtype=jnp.int32)[None, :]
    segment = (places >= end_one).astype(jnp.int32) + (places >= end_two).astype(jnp.int32)
    offset = jnp.where(segment == 0, 0, end_one)
    across = jnp.where(segment == 0, widths[:, 0:1], widths[:, 1:2])
    inside = places - offset
    row_pos = jnp.where(segment < 2, inside // across, 0).astype(jnp.float32)
    col_pos = jnp.where(segment < 2, inside % across, 0).astype(jnp.float32)
    return (segment, row_pos, col_pos)

def normalize(field_in, gain_vec, shift_vec):
    center = field_in - lax.optimization_barrier(jnp.mean(field_in, axis=-1, keepdims=True))
    spread = lax.optimization_barrier(jnp.mean(center * center, axis=-1, keepdims=True))
    return center * lax.rsqrt(spread + 1e-06) * gain_vec + shift_vec

def rotate(values, cosine, sine_part):
    halfway = values.shape[-1] // 2
    leading = values[..., :halfway]
    trailing = values[..., halfway:]
    return jnp.concatenate([leading * cosine - trailing * sine_part, trailing * cosine + leading * sine_part], axis=-1)

def attention_branch(normed, weights, first_vec, second_vec, seg_rows, row_flat, col_flat):
    group_tokens = normed.shape[0]
    blocks = group_tokens // ROW_LEN
    packed = low_back(jnp.dot(low(normed), weights[:, :3 * D], precision=highest) + first_vec[:3 * D])
    freq_x = first_vec[3 * D:3 * D + D // 2].reshape(HEADS, HEAD_DIM // 2)
    freq_y = first_vec[3 * D + D // 2:].reshape(HEADS, HEAD_DIM // 2)
    angles = col_flat[:, None, None] * freq_x[None] + row_flat[:, None, None] * freq_y[None]
    cosine = jnp.cos(angles)
    sine_part = jnp.sin(angles)
    query_low = low(rotate(packed[:, :D].reshape(group_tokens, HEADS, HEAD_DIM), cosine, sine_part))
    key_low = low(rotate(packed[:, D:2 * D].reshape(group_tokens, HEADS, HEAD_DIM), cosine, sine_part))
    value_low = low(packed[:, 2 * D:].reshape(group_tokens, HEADS, HEAD_DIM))
    score_scale = HEAD_DIM ** (-0.5)

    def attend(pieces):
        query_b, key_b, value_b, seg_b = pieces
        scores = low_back(jnp.einsum('qhd,khd->hqk', query_b, key_b, precision=highest) * score_scale)
        same_image = (seg_b[:, None] == seg_b[None, :])[None]
        scores = jnp.where(same_image, scores, -1e+30)
        exponent = jnp.exp(scores - lax.optimization_barrier(jnp.max(scores, axis=-1, keepdims=True)))
        attn_probs = low(exponent / lax.optimization_barrier(jnp.sum(exponent, axis=-1, keepdims=True)))
        return jnp.einsum('hqk,khd->qhd', attn_probs, value_b, precision=highest)
    shaped = (blocks, ROW_LEN, HEADS, HEAD_DIM)
    mixed_out = lax.map(jax.checkpoint(attend), (query_low.reshape(shaped), key_low.reshape(shaped), value_low.reshape(shaped), seg_rows))
    merged = low(low_back(mixed_out.reshape(group_tokens, D)))
    return jnp.dot(merged, weights[:, 3 * D:4 * D], precision=highest) + second_vec

def feed_branch(normed, weights, borrowed, first_vec, second_vec):
    hidden = low_back(jnp.dot(low(normed), weights[:, :FF], precision=highest) + first_vec)
    active = low(jax.nn.gelu(hidden))
    down_t = jnp.concatenate([borrowed, weights[:, FF:]], axis=1)
    return jnp.dot(active, down_t.T, precision=highest) + second_vec

def stack(field_in, weights, gains, shifts, firsts, seconds, probes, seg_rows, row_flat, col_flat):
    outputs = []
    current = field_in + probes[0]
    for section_no in range(4):
        normed = normalize(current, gains[section_no], shifts[section_no])
        if section_no % 2 == 0:
            branch = attention_branch(normed, weights[section_no], firsts[section_no], seconds[section_no], seg_rows, row_flat, col_flat)
        else:
            branch = feed_branch(normed, weights[section_no], weights[section_no - 1][:, FF:], firsts[section_no], seconds[section_no])
        result = low_back(low(current + branch))
        outputs.append(result)
        if section_no < 3:
            current = result + probes[section_no + 1]
    return jnp.stack(outputs)

def reference(block_input, cotangent, grid_sizes, section_weight, norm_gain, norm_bias, first_vector, second_vector):
    rows_total = grid_sizes.shape[0]
    group_rows = math.gcd(rows_total, 8)
    step_count = rows_total // group_rows
    group_tokens = group_rows * ROW_LEN
    segment, row_pos, col_pos = layout(grid_sizes, ROW_LEN)
    fields = block_input.astype(jnp.float32).reshape(step_count, group_tokens, D)
    cotans = cotangent.astype(jnp.float32).reshape(step_count, group_tokens, D)
    segs = segment.reshape(step_count, group_rows, ROW_LEN)
    rows_at = row_pos.reshape(step_count, group_tokens)
    cols_at = col_pos.reshape(step_count, group_tokens)
    weights = section_weight.astype(jnp.float32)
    gains = norm_gain.astype(jnp.float32)
    shifts = norm_bias.astype(jnp.float32)
    firsts = first_vector.astype(jnp.float32)
    seconds = second_vector.astype(jnp.float32)

    def one_group(carry, pieces):
        field_g, cotan_g, seg_g, row_g, col_g = pieces
        probes = jnp.zeros((4, group_tokens, D), jnp.float32)

        def model(field_in, weights_in, gains_in, shifts_in, firsts_in, seconds_in, probes_in):
            return stack(field_in, weights_in, gains_in, shifts_in, firsts_in, seconds_in, probes_in, seg_g, row_g, col_g)
        outputs, pullback = jax.vjp(model, field_g, weights, gains, shifts, firsts, seconds, probes)
        seed_grad = jnp.zeros_like(outputs).at[3].set(cotan_g)
        grads = pullback(seed_grad)
        carry = tuple((running + added for running, added in zip(carry, grads[1:6])))
        return (carry, (outputs, grads[6]))
    zeros_init = (jnp.zeros_like(weights), jnp.zeros_like(gains), jnp.zeros_like(shifts), jnp.zeros_like(firsts), jnp.zeros_like(seconds))
    totals, stacked = lax.scan(one_group, zeros_init, (fields, cotans, segs, rows_at, cols_at))
    outputs, probe_grads = stacked
    activations = outputs.transpose(1, 0, 2, 3).reshape(4, rows_total * ROW_LEN, D).astype(jnp.bfloat16)
    input_grads = probe_grads.transpose(1, 0, 2, 3).reshape(4, rows_total * ROW_LEN, D).astype(jnp.bfloat16)
    return (activations, input_grads, totals[0], totals[1], totals[2], totals[3], totals[4])
```

```python
import jax
import jax.numpy as jnp
from jax import lax
from jax.experimental import pallas as pl
from jax.experimental.pallas import tpu as pltpu
from jax.sharding import PartitionSpec as P

D = 768
HEADS = 12
HEAD_DIM = 64
FF = 3072
L = 384
F32 = jnp.float32
BF = jnp.bfloat16
NT = (((1,), (1,)), ((), ()))
VM = pltpu.VMEM


def dot(a, b):
    return jnp.dot(a, b, preferred_element_type=F32)


def dot_nt(a, b):
    return lax.dot_general(a, b, NT, preferred_element_type=F32)


def norm_parts(x):
    center = x - jnp.mean(x, axis=-1, keepdims=True)
    inv = lax.rsqrt(jnp.mean(center * center, axis=-1, keepdims=True) + 1e-06)
    return center * inv, inv


def swap_halves(a):
    lane = lax.broadcasted_iota(jnp.int32, (1, 128), 1)
    first = (lane % 64) < 32
    out = []
    for i in range(a.shape[1] // 128):
        s = a[:, 128 * i : 128 * (i + 1)]
        out.append(jnp.where(first, pltpu.roll(s, 96, 1), pltpu.roll(s, 32, 1)))
    return jnp.concatenate(out, axis=1) if len(out) > 1 else out[0]


def pick(flag, want, own, oth, src, dst, sem):
    @pl.when(flag == want)
    def _():
        pltpu.make_async_copy(own.at[src], dst, sem).start()

    @pl.when(flag != want)
    def _():
        pltpu.make_async_copy(oth.at[src], dst, sem).start()


def cols(start, size):
    return (slice(None), pl.ds(start, size))


def attn_fwd_kernel(
    core, x_ref, own, oth, bias, second, gain, shift, cosf, sinf, segc, segr,
    out_ref, qkv_ref, pt_ref, ml_ref, n_ref, wbuf, vt, mlt, sems,
):
    c = core[0]
    for i in range(4):
        pick(c, 0, own, oth, cols(D * i, D), wbuf.at[i], sems.at[i])
    x = x_ref[...].astype(F32)
    xh, _ = norm_parts(x)
    n = (xh * gain[...] + shift[...]).astype(BF)
    n_ref[...] = n
    for i in range(3):
        pltpu.make_async_copy(own.at[cols(D * i, D)], wbuf.at[i], sems.at[i]).wait()
        part = dot(n, wbuf[i]) + bias[:, D * i : D * (i + 1)]
        if i < 2:
            part = part * cosf[...] + swap_halves(part) * sinf[...]
        part = part.astype(BF)
        if i == 0:
            part = part * BF(HEAD_DIM**-0.5)
        qkv_ref[:, D * i : D * (i + 1)] = part
    vt[...] = qkv_ref[:, 2 * D : 3 * D].T
    same = segc[...] == segr[...]
    lane = lax.broadcasted_iota(jnp.int32, (1, 128), 1)
    for p in range(HEADS // 2):
        qp = qkv_ref[:, 128 * p : 128 * (p + 1)]
        kp = qkv_ref[:, D + 128 * p : D + 128 * (p + 1)]
        for hh in range(2):
            h = 2 * p + hh
            km = jnp.where((lane // 64) == hh, kp, BF(0))
            st = dot_nt(km, qp)
            st = jnp.where(same, st, -1e30)
            e = jnp.exp(st - jnp.max(st, axis=0, keepdims=True))
            pt = (e * (1.0 / jnp.sum(e, axis=0, keepdims=True))).astype(BF)
            pt_ref[h] = pt
            mlt[64 * h : 64 * (h + 1), :] = dot(vt[64 * h : 64 * (h + 1), :], pt).astype(BF)
    ml = mlt[...].T
    ml_ref[...] = ml
    pltpu.make_async_copy(own.at[cols(3 * D, D)], wbuf.at[3], sems.at[3]).wait()
    out_ref[...] = (x + dot(ml, wbuf[3]) + second[...]).astype(BF)


def attn_bwd_kernel(
    core, x_ref, c_ref, own, oth, gain, shift, cosf, sinf, colp, rowp, qkv_ref, pt_ref, ml_ref,
    gx_ref, gp_ref, ggain, gshift, gbias, gfx, gfy, gsec, wbuf, kt, gm_ref, gqt, dsum, sems,
):
    c = core[0]
    for i in (3, 0, 1, 2):
        pick(c, 0, own, oth, cols(D * i, D), wbuf.at[i], sems.at[i])
    cw = c_ref[...]
    gsec[...] = jnp.sum(cw.astype(F32), axis=0, keepdims=True)
    kt[...] = qkv_ref[:, D : 2 * D].T
    pltpu.make_async_copy(own.at[cols(3 * D, D)], wbuf.at[3], sems.at[3]).wait()
    gm = dot_nt(cw, wbuf[3]).astype(BF)
    gm_ref[...] = gm
    prod = gm.astype(F32) * ml_ref[...].astype(F32)
    hi = prod.astype(BF)
    lo = (prod - hi.astype(F32)).astype(BF)
    hrow = lax.broadcasted_iota(jnp.int32, (16, D), 0)
    hcol = lax.broadcasted_iota(jnp.int32, (16, D), 1)
    sel = jnp.where(hcol // 64 == hrow, 1.0, 0.0).astype(BF)
    dsum[...] = dot_nt(sel, hi) + dot_nt(sel, lo)
    lane = lax.broadcasted_iota(jnp.int32, (1, 128), 1)
    fx = []
    fy = []
    for p in range(HEADS // 2):
        sl = slice(128 * p, 128 * (p + 1))
        qp = qkv_ref[:, sl]
        kp = qkv_ref[:, D + 128 * p : D + 128 * (p + 1)]
        vp = qkv_ref[:, 2 * D + 128 * p : 2 * D + 128 * (p + 1)]
        gmp = gm_ref[:, sl]
        gv = None
        for hh in range(2):
            h = 2 * p + hh
            here = (lane // 64) == hh
            pt = pt_ref[h]
            gpt = dot_nt(jnp.where(here, vp, BF(0)), gmp)
            gst = (pt.astype(F32) * (gpt - dsum[h : h + 1, :])).astype(BF)
            gvh = dot(pt, jnp.where(here, gmp, BF(0)))
            gkh = dot(gst, jnp.where(here, qp, BF(0)))
            gv = gvh if gv is None else gv + gvh
            gk = gkh if hh == 0 else gk + gkh
            gqt[64 * h : 64 * (h + 1), :] = dot(kt[64 * h : 64 * (h + 1), :], gst)
        gq = gqt[sl, :].T * (HEAD_DIM**-0.5)
        cs = cosf[:, sl]
        sn = sinf[:, sl]
        sq = swap_halves(gq)
        sk = swap_halves(gk)
        gqb = (gq * cs - sq * sn).astype(BF)
        gkb = (gk * cs - sk * sn).astype(BF)
        gvb = gv.astype(BF)
        gp_ref[:, sl] = gqb
        gp_ref[:, D + 128 * p : D + 128 * (p + 1)] = gkb
        gp_ref[:, 2 * D + 128 * p : 2 * D + 128 * (p + 1)] = gvb
        th = sq * (qp.astype(F32) * (HEAD_DIM**0.5)) + sk * kp.astype(F32)
        gfx[:, sl] = jnp.sum(th * colp[...], axis=0, keepdims=True)
        gfy[:, sl] = jnp.sum(th * rowp[...], axis=0, keepdims=True)
        for i, g in enumerate((gqb, gkb, gvb)):
            gbias[:, D * i + 128 * p : D * i + 128 * (p + 1)] = jnp.sum(
                g.astype(F32), axis=0, keepdims=True
            )
    gn = None
    for i in range(3):
        pltpu.make_async_copy(own.at[cols(D * i, D)], wbuf.at[i], sems.at[i]).wait()
        part = dot_nt(gp_ref[:, D * i : D * (i + 1)], wbuf[i])
        gn = part if gn is None else gn + part
    gx_ref[...] = norm_back(gn, x_ref, cw, gain, ggain, gshift)


def norm_back(gn, x_ref, cw, gain, ggain, gshift):
    xh, inv = norm_parts(x_ref[...].astype(F32))
    ggain[...] = jnp.sum(gn * xh, axis=0, keepdims=True)
    gshift[...] = jnp.sum(gn, axis=0, keepdims=True)
    u = gn * gain[...]
    gx = inv * (
        u
        - jnp.mean(u, axis=-1, keepdims=True)
        - xh * jnp.mean(u * xh, axis=-1, keepdims=True)
    )
    return (cw.astype(F32) + gx).astype(BF)


C0 = 0.7978845608028654
C1 = 0.044715


def mlp_load(c, own, oth, w1, wd, sems):
    for j in range(4):
        pick(c, 1, own, oth, cols(D * j, D), w1.at[j], sems.at[j])
        pick(c, 0 if j < 2 else 1, own, oth, cols(FF + D * (j % 2), D), wd.at[j], sems.at[4 + j])


def mlp_wait(own, w1, wd, sems, j):
    pltpu.make_async_copy(own.at[cols(D * j, D)], w1.at[j], sems.at[j]).wait()
    pltpu.make_async_copy(own.at[cols(FF + D * (j % 2), D)], wd.at[j], sems.at[4 + j]).wait()


def mlp_fwd_kernel(
    core, x_ref, own, oth, bias, second, gain, shift, out_ref, act_ref, dg_ref, n_ref, w1, wd, sems
):
    mlp_load(core[0], own, oth, w1, wd, sems)
    x = x_ref[...].astype(F32)
    xh, _ = norm_parts(x)
    n = (xh * gain[...] + shift[...]).astype(BF)
    n_ref[...] = n
    acc = x + second[...]
    for j in range(4):
        mlp_wait(own, w1, wd, sems, j)
        h = dot(n, w1[j]) + bias[:, D * j : D * (j + 1)]
        h2 = h * h
        t = jnp.tanh(C0 * (h + C1 * h * h2))
        half = 0.5 * (1.0 + t)
        act = (h * half).astype(BF)
        dg = half + (0.5 * C0) * h * (1.0 - t * t) * (1.0 + (3.0 * C1) * h2)
        act_ref[:, D * j : D * (j + 1)] = act
        dg_ref[:, D * j : D * (j + 1)] = dg.astype(BF)
        acc = acc + dot_nt(act, wd[j])
    out_ref[...] = acc.astype(BF)


def mlp_bwd_kernel(
    core, x_ref, c_ref, own, oth, gain, shift, dg_ref, gx_ref, gh_ref, ggain, gshift, gbias, gsec, w1, wd, sems
):
    mlp_load(core[0], own, oth, w1, wd, sems)
    cw = c_ref[...]
    gsec[...] = jnp.sum(cw.astype(F32), axis=0, keepdims=True)
    gn = None
    for j in range(4):
        mlp_wait(own, w1, wd, sems, j)
        ga = dot(cw, wd[j])
        gh = (ga * dg_ref[:, D * j : D * (j + 1)].astype(F32)).astype(BF)
        gh_ref[:, D * j : D * (j + 1)] = gh
        gbias[:, D * j : D * (j + 1)] = jnp.sum(gh.astype(F32), axis=0, keepdims=True)
        part = dot_nt(gh, w1[j])
        gn = part if gn is None else gn + part
    gx_ref[...] = norm_back(gn, x_ref, cw, gain, ggain, gshift)


SMEM = pl.BlockSpec(memory_space=pltpu.SMEM)
VS = pl.BlockSpec(memory_space=pltpu.VMEM)
ANY = pl.BlockSpec(memory_space=pl.ANY)
PARAMS = dict(vmem_limit_bytes=56 * 1024 * 1024)


def sds(shape, dtype=BF):
    return jax.ShapeDtypeStruct(shape, dtype)


def call(kernel, name, in_specs, outs, scratch, flops, nbytes):
    return pl.pallas_call(
        kernel,
        name=name,
        in_specs=in_specs,
        out_specs=[VS] * len(outs),
        out_shape=outs,
        scratch_shapes=scratch,
        compiler_params=pltpu.CompilerParams(**PARAMS),
        cost_estimate=pl.CostEstimate(flops=flops, bytes_accessed=nbytes, transcendentals=0),
    )


def attn_fwd(*a):
    return call(
        attn_fwd_kernel, "attn_fwd", [SMEM, VS, ANY, ANY] + [VS] * 8,
        [sds((L, D)), sds((L, 3 * D)), sds((HEADS, L, L)), sds((L, D)), sds((L, D))],
        [VM((4, D, D), BF), VM((D, L), BF), VM((D, L), BF), pltpu.SemaphoreType.DMA((4,))],
        int(4e9), int(12e6),
    )(*a)


def attn_bwd(*a):
    return call(
        attn_bwd_kernel, "attn_bwd", [SMEM, VS, VS, ANY, ANY] + [VS] * 9,
        [sds((L, D)), sds((L, 3 * D)), sds((1, D), F32), sds((1, D), F32), sds((1, 3 * D), F32),
         sds((1, D), F32), sds((1, D), F32), sds((1, D), F32)],
        [VM((4, D, D), BF), VM((D, L), BF), VM((L, D), BF), VM((D, L), F32), VM((16, L), F32),
         pltpu.SemaphoreType.DMA((4,))],
        int(6e9), int(12e6),
    )(*a)


def mlp_fwd(*a):
    return call(
        mlp_fwd_kernel, "mlp_fwd", [SMEM, VS, ANY, ANY] + [VS] * 4,
        [sds((L, D)), sds((L, FF)), sds((L, FF)), sds((L, D))],
        [VM((4, D, D), BF), VM((4, D, D), BF), pltpu.SemaphoreType.DMA((8,))],
        int(4e9), int(14e6),
    )(*a)


def mlp_bwd(*a):
    return call(
        mlp_bwd_kernel, "mlp_bwd", [SMEM, VS, VS, ANY, ANY] + [VS] * 3,
        [sds((L, D)), sds((L, FF)), sds((1, D), F32), sds((1, D), F32), sds((1, FF), F32), sds((1, D), F32)],
        [VM((4, D, D), BF), VM((4, D, D), BF), pltpu.SemaphoreType.DMA((8,))],
        int(4e9), int(14e6),
    )(*a)


def core_swap(a):
    return lax.ppermute(a, "section", [(0, 1), (1, 0), (2, 3), (3, 2)])


def layer_swap(a, pairs):
    return lax.ppermute(a, "section", pairs)


def layout(grid_rows):
    heights = grid_rows[:, 0]
    widths = grid_rows[:, 1]
    counts = heights * widths
    end_one = counts[0]
    end_two = end_one + counts[1]
    places = jnp.arange(L, dtype=jnp.int32)
    segment = (places >= end_one).astype(jnp.int32) + (places >= end_two).astype(jnp.int32)
    offset = jnp.where(segment == 0, 0, end_one)
    across = jnp.where(segment == 0, widths[0], widths[1])
    inside = places - offset
    row_pos = jnp.where(segment < 2, inside // across, 0).astype(F32)
    col_pos = jnp.where(segment < 2, inside % across, 0).astype(F32)
    return segment, row_pos, col_pos


def ring_order(n):
    return list(range(0, n, 2)) + list(range(n - 1, 0, -2))


class Ring:
    def __init__(self, array, direction, n, place):
        self.array, self.n, self.place, self.d = array, n, place, direction
        self.r = array.shape[0] // n
        order = ring_order(n)
        self.pairs = [(order[i], order[(i + direction) % n]) for i in range(n)]
        self.cur = self.own(0)
        self.shards = []

    def index(self, t):
        return (self.place - self.d * t) % self.n

    def own(self, t):
        return lax.dynamic_slice_in_dim(self.array, self.index(t) * self.r, self.r, 0)

    def step(self, t):
        got = lax.ppermute(self.cur, "dp", self.pairs)
        if t < self.n - 1:
            self.cur = got + self.own(t + 1)
            if t == self.n - 2:
                self.shards.append((self.index(-1), self.cur))
        else:
            self.cur = got
            self.shards.append((self.index(t - self.n + 1), got))

    def total(self):
        out = jnp.zeros_like(self.array)
        for index, shard in self.shards:
            out = lax.dynamic_update_slice_in_dim(out, shard, index * self.r, 0)
        return out


def all_reduce(arrays):
    n = lax.axis_size("dp")
    if n > 16:
        return [lax.psum(a, "dp") for a in arrays]
    i = lax.axis_index("dp")
    place = jnp.where(i % 2 == 0, i // 2, n - 1 - i // 2)
    rings = []
    for a in arrays:
        half = a.shape[0] // 2
        rings.append((Ring(a[:half], 1, n, place), Ring(a[half:], -1, n, place)))
    for t in range(2 * n - 2):
        for pair in rings:
            for ring in pair:
                ring.step(t)
    return [jnp.concatenate([up.total(), down.total()], axis=0) for up, down in rings]


def gram(a, b):
    return lax.dot_general(a, b, (((0,), (0,)), ((), ())), preferred_element_type=F32)


def body(
    block_input, cotangent, grid_sizes, section_weight, norm_gain, norm_bias, first_vector, second_vector
):
    section = lax.axis_index("section")
    core = section % 2
    layer = section // 2
    flag = jnp.full((1,), core, jnp.int32)
    first_core = core == 0
    first_layer = layer == 0

    own = section_weight[0]
    oth = core_swap(own)
    vec = jnp.concatenate([norm_gain[0], norm_bias[0], first_vector[0], second_vector[0]])[None]
    vec_oth = core_swap(vec)
    vec_a = jnp.where(first_core, vec, vec_oth)
    vec_m = jnp.where(first_core, vec_oth, vec)

    def split(v):
        return v[:, :D], v[:, D : 2 * D], v[:, 2 * D : 2 * D + FF], v[:, 2 * D + FF :]

    gain_a, shift_a, first_a, second_a = split(vec_a)
    gain_m, shift_m, first_m, second_m = split(vec_m)

    def half_row(block):
        rows = block.reshape(2, L, -1)
        mine = lax.dynamic_index_in_dim(rows, core, 0, keepdims=False)
        send = lax.dynamic_index_in_dim(rows, 1 - core, 0, keepdims=False)
        return mine, send

    x_mine, x_send = half_row(block_input)
    c_mine, c_send = half_row(cotangent)
    got = core_swap(jnp.concatenate([x_send, c_send], axis=1))
    quarter = x_mine.shape[1]

    def in_order(pick_first, a, b):
        return jnp.where(pick_first, jnp.concatenate([a, b], axis=1), jnp.concatenate([b, a], axis=1))

    x_half = in_order(first_core, x_mine, got[:, :quarter])
    c_half = in_order(first_core, c_mine, got[:, quarter:])
    got = layer_swap(jnp.where(first_layer, c_half, x_half), [(0, 2), (1, 3), (2, 0), (3, 1)])
    field = in_order(first_layer, jnp.where(first_layer, x_half, c_half), got)

    segment, row_pos, col_pos = layout(lax.dynamic_index_in_dim(grid_sizes, core, 0, keepdims=False))

    def lanes(freq):
        by_head = freq.reshape(HEADS, 1, HEAD_DIM // 2)
        return jnp.broadcast_to(by_head, (HEADS, 2, HEAD_DIM // 2)).reshape(1, D)

    freq_x = lanes(first_a[0, 3 * D : 3 * D + D // 2])
    freq_y = lanes(first_a[0, 3 * D + D // 2 :])
    theta = col_pos[:, None] * freq_x + row_pos[:, None] * freq_y
    sign = jnp.where(jnp.arange(D) % HEAD_DIM < HEAD_DIM // 2, -1.0, 1.0).astype(F32)
    cosf = jnp.cos(theta)
    sinf = jnp.sin(theta) * sign
    segc, segr = segment[:, None], segment[None, :]
    colp, rowp = col_pos[:, None], row_pos[:, None]

    def attn_f(x):
        return attn_fwd(
            flag, x, own, oth, first_a[:, : 3 * D], second_a, gain_a, shift_a, cosf, sinf, segc, segr
        )

    def mlp_f(x):
        return mlp_fwd(flag, x, own, oth, first_m, second_m, gain_m, shift_m)

    x_one = mlp_f(attn_f(field)[0])[0]
    arrived = layer_swap(x_one, [(0, 2), (1, 3)])
    x_in = jnp.where(first_layer, field, arrived)
    x_mid, qkv, pt, ml, n_a = attn_f(x_in)
    x_out, act, dg, n_m = mlp_f(x_mid)

    def backward(c_out):
        mlp = mlp_bwd(flag, x_mid, c_out, own, oth, gain_m, shift_m, dg)
        attn = attn_bwd(
            flag, x_in, mlp[0], own, oth, gain_a, shift_a, cosf, sinf, colp, rowp, qkv, pt, ml
        )
        return mlp, attn

    c_one = backward(field)[1][0]
    arrived = layer_swap(c_one, [(2, 0), (3, 1)])
    c_out = jnp.where(first_layer, arrived, field)
    mlp, attn = backward(c_out)
    c_mid, gh, ggain_m, gshift_m, gbias_m, gsec_m = mlp
    c_in, gp, ggain_a, gshift_a, gbias_a, gfx, gfy, gsec_a = attn

    def half(array, start, size, which):
        return lax.dynamic_slice_in_dim(array, start + which * size, size, 1)

    def pair(array, groups):
        size = array.shape[1] // groups // 2
        mine = [half(array, 2 * size * g, size, core) for g in range(groups)]
        send = [half(array, 2 * size * g, size, 1 - core) for g in range(groups)]
        mine, send = (jnp.concatenate(p, axis=1) if groups > 1 else p[0] for p in (mine, send))
        return jnp.concatenate([mine, core_swap(send)], axis=0)

    def both(array):
        return jnp.concatenate([array, core_swap(array)], axis=0)

    down_grad = gram(both(c_out), pair(act, 1)).astype(BF)
    up_grad = gram(both(n_m), pair(gh, 1)).astype(BF)
    qkv_grad = gram(both(n_a), pair(gp, 3)).astype(BF)
    out_grad = gram(both(ml), pair(c_mid, 1)).astype(BF)

    mlp_sum, attn_sum = all_reduce(
        [jnp.concatenate([down_grad, up_grad], axis=1), jnp.concatenate([qkv_grad, out_grad], axis=1)]
    )
    down_sum, up_sum = mlp_sum[:, : FF // 2], mlp_sum[:, FF // 2 :]
    other = core_swap(jnp.where(first_core, up_sum, attn_sum))
    h = D // 2

    def woven(a, b):
        return jnp.concatenate([p[:, h * g : h * (g + 1)] for g in range(4) for p in (a, b)], axis=1)

    lead = jnp.where(first_core, woven(attn_sum, other), jnp.concatenate([other, up_sum], axis=1))
    weight_grad = jnp.concatenate([lead, down_sum], axis=1).astype(F32)

    def fold(v):
        pairs = v.reshape(HEADS, 2, HEAD_DIM // 2)
        return (pairs[:, 0] - pairs[:, 1]).reshape(1, -1)

    vg_a = jnp.concatenate([ggain_a, gshift_a, gbias_a, fold(gfx), fold(gfy), gsec_a], axis=1)
    vg_m = jnp.concatenate([ggain_m, gshift_m, gbias_m, gsec_m], axis=1)
    vg = jnp.where(first_core, vg_a, vg_m) + core_swap(jnp.where(first_core, vg_m, vg_a))
    vg = lax.psum(vg, "dp")
    vgain, vshift, vfirst, vsecond = split(vg)

    def rows_of(attn_row, mlp_row):
        got = core_swap(jnp.where(first_core, mlp_row, attn_row))
        return jnp.where(
            first_core,
            jnp.concatenate([attn_row, got], axis=0),
            jnp.concatenate([got, mlp_row], axis=0),
        )[None]

    return (
        rows_of(x_mid, x_out),
        rows_of(c_in, c_mid),
        weight_grad[None],
        vgain,
        vshift,
        vfirst,
        vsecond,
    )


def solution(mesh):
    in_specs = (
        P("dp", "section"),
        P("dp", "section"),
        P("dp", None, None),
        P("section", None, None),
        P("section", None),
        P("section", None),
        P("section", None),
        P("section", None),
    )
    out_specs = (
        P("section", "dp", None),
        P("section", "dp", None),
        P("section", None, None),
        P("section", None),
        P("section", None),
        P("section", None),
        P("section", None),
    )
    return jax.shard_map(body, mesh=mesh, in_specs=in_specs, out_specs=out_specs, check_vma=False)
```

```python
import jax
import jax.numpy as jnp
from jax import lax
from jax.experimental import pallas as pl
from jax.experimental.pallas import tpu as pltpu
from jax.sharding import PartitionSpec as P

D = 768
HEADS = 12
HEAD_DIM = 64
FF = 3072
L = 384
HALF = D // 2
F32 = jnp.float32
BF = jnp.bfloat16
NT = (((1,), (1,)), ((), ()))
TN = (((0,), (0,)), ((), ()))
VM = pltpu.VMEM
MIB = 1024 * 1024


def dot(a, b):
    return jnp.dot(a, b, preferred_element_type=F32)


def dot_nt(a, b):
    return lax.dot_general(a, b, NT, preferred_element_type=F32)


def dot_tn(a, b):
    return lax.dot_general(a, b, TN, preferred_element_type=F32)


def norm_parts(x):
    center = x - jnp.mean(x, axis=-1, keepdims=True)
    inv = lax.rsqrt(jnp.mean(center * center, axis=-1, keepdims=True) + 1e-06)
    return center * inv, inv


def swap_halves(a):
    lane = lax.broadcasted_iota(jnp.int32, (1, 128), 1)
    first = (lane % HEAD_DIM) < HEAD_DIM // 2
    out = []
    for i in range(a.shape[1] // 128):
        s = a[:, 128 * i : 128 * (i + 1)]
        out.append(jnp.where(first, pltpu.roll(s, 96, 1), pltpu.roll(s, 32, 1)))
    return jnp.concatenate(out, axis=1) if len(out) > 1 else out[0]


def lanes(start, size):
    return pl.ds(pl.multiple_of(start, 128), size)


def pick(flag, want, own, oth, src, dst, sem):
    @pl.when(flag == want)
    def _():
        pltpu.make_async_copy(own.at[src], dst, sem).start()

    @pl.when(flag != want)
    def _():
        pltpu.make_async_copy(oth.at[src], dst, sem).start()


def arrived(src, dst, sem):
    pltpu.make_async_copy(src, dst, sem).wait()


def cols(start, size):
    return (slice(None), pl.ds(start, size))


def attn_fwd_kernel(
    core, x_ref, own, oth, bias, second, gain, shift, cosf, sinf, segc, segr,
    out_ref, qkv_ref, pt_ref, ml_ref, n_ref, wbuf, vt, mlt, sems,
):
    c = core[0]
    for i in range(4):
        pick(c, 0, own, oth, cols(D * i, D), wbuf.at[i], sems.at[i])
    x = x_ref[...].astype(F32)
    xh, _ = norm_parts(x)
    n = (xh * gain[...] + shift[...]).astype(BF)
    n_ref[...] = n
    for i in range(3):
        arrived(own.at[cols(D * i, D)], wbuf.at[i], sems.at[i])
        part = dot(n, wbuf[i]) + bias[:, D * i : D * (i + 1)]
        if i < 2:
            part = part * cosf[...] + swap_halves(part) * sinf[...]
        part = part.astype(BF)
        if i == 0:
            part = part * BF(HEAD_DIM**-0.5)
        qkv_ref[:, D * i : D * (i + 1)] = part
    vt[...] = qkv_ref[:, 2 * D : 3 * D].T
    same = segc[...] == segr[...]
    lane = lax.broadcasted_iota(jnp.int32, (1, 128), 1)
    for p in range(HEADS // 2):
        qp = qkv_ref[:, 128 * p : 128 * (p + 1)]
        kp = qkv_ref[:, D + 128 * p : D + 128 * (p + 1)]
        for hh in range(2):
            h = 2 * p + hh
            km = jnp.where((lane // HEAD_DIM) == hh, kp, BF(0))
            st = dot_nt(km, qp)
            st = jnp.where(same, st, -1e30)
            e = jnp.exp(st - jnp.max(st, axis=0, keepdims=True))
            pt = (e * (1.0 / jnp.sum(e, axis=0, keepdims=True))).astype(BF)
            pt_ref[h] = pt
            mlt[64 * h : 64 * (h + 1), :] = dot(vt[64 * h : 64 * (h + 1), :], pt).astype(BF)
    ml = mlt[...].T
    ml_ref[...] = ml
    arrived(own.at[cols(3 * D, D)], wbuf.at[3], sems.at[3])
    out_ref[...] = (x + dot(ml, wbuf[3]) + second[...]).astype(BF)


def norm_back(gn, x_ref, cw, gain, ggain, gshift):
    xh, inv = norm_parts(x_ref[...].astype(F32))
    ggain[...] = jnp.sum(gn * xh, axis=0, keepdims=True)
    gshift[...] = jnp.sum(gn, axis=0, keepdims=True)
    u = gn * gain[...]
    gx = inv * (
        u
        - jnp.mean(u, axis=-1, keepdims=True)
        - xh * jnp.mean(u * xh, axis=-1, keepdims=True)
    )
    return (cw.astype(F32) + gx).astype(BF)


def attn_bwd_kernel(
    core, x_ref, c_ref, own, oth, gain, cosf, sinf, colp, rowp, qkv_ref, pt_ref, ml_ref,
    gx_ref, gpm, gps, ggain, gshift, gbias, gfx, gfy, gsec, wo, wbuf, kt, gm_ref, gqt, dsum, sems,
):
    c = core[0]
    pick(c, 0, own, oth, cols(3 * D, D), wo, sems.at[0])
    for m in range(2):
        for i in range(3):
            start = pl.multiple_of(D * i + HALF * ((c + m) % 2), 128)
            pick(
                c, 0, own, oth, (slice(None), pl.ds(start, HALF)),
                wbuf.at[m, :, pl.ds(HALF * i, HALF)], sems.at[1 + 3 * m + i],
            )
    cw = c_ref[...]
    gsec[...] = jnp.sum(cw.astype(F32), axis=0, keepdims=True)
    kt[...] = qkv_ref[:, D : 2 * D].T
    arrived(own.at[cols(3 * D, D)], wo, sems.at[0])
    gm = dot_nt(cw, wo[...]).astype(BF)
    gm_ref[...] = gm
    prod = gm.astype(F32) * ml_ref[...].astype(F32)
    hi = prod.astype(BF)
    lo = (prod - hi.astype(F32)).astype(BF)
    hrow = lax.broadcasted_iota(jnp.int32, (16, D), 0)
    hcol = lax.broadcasted_iota(jnp.int32, (16, D), 1)
    sel = jnp.where(hcol // HEAD_DIM == hrow, 1.0, 0.0).astype(BF)
    dsum[...] = dot_nt(sel, hi) + dot_nt(sel, lo)
    lane = lax.broadcasted_iota(jnp.int32, (1, 128), 1)
    for p in range(HEADS // 2):
        m, pos = p // 3, p % 3
        pair = 3 * ((c + m) % 2) + pos
        sl = lanes(128 * pair, 128)
        qp = qkv_ref[:, sl]
        kp = qkv_ref[:, lanes(D + 128 * pair, 128)]
        vp = qkv_ref[:, lanes(2 * D + 128 * pair, 128)]
        gmp = gm_ref[:, sl]
        for hh in range(2):
            h = 2 * pair + hh
            here = (lane // HEAD_DIM) == hh
            pt = pt_ref[h]
            gpt = dot_nt(jnp.where(here, vp, BF(0)), gmp)
            gst = (pt.astype(F32) * (gpt - dsum[pl.ds(h, 1), :])).astype(BF)
            gvh = dot(pt, jnp.where(here, gmp, BF(0)))
            gkh = dot(gst, jnp.where(here, qp, BF(0)))
            gv = gvh if hh == 0 else gv + gvh
            gk = gkh if hh == 0 else gk + gkh
            kth = kt[pl.ds(pl.multiple_of(HEAD_DIM * h, HEAD_DIM), HEAD_DIM), :]
            gqt[HEAD_DIM * hh : HEAD_DIM * (hh + 1), :] = dot(kth, gst)
        gq = gqt[...].T * (HEAD_DIM**-0.5)
        cs = cosf[:, sl]
        sn = sinf[:, sl]
        sq = swap_halves(gq)
        sk = swap_halves(gk)
        grads = ((gq * cs - sq * sn).astype(BF), (gk * cs - sk * sn).astype(BF), gv.astype(BF))
        th = sq * (qp.astype(F32) * (HEAD_DIM**0.5)) + sk * kp.astype(F32)
        gfx[:, sl] = jnp.sum(th * colp[...], axis=0, keepdims=True)
        gfy[:, sl] = jnp.sum(th * rowp[...], axis=0, keepdims=True)
        for i, g in enumerate(grads):
            (gpm, gps)[m][:, HALF * i + 128 * pos : HALF * i + 128 * (pos + 1)] = g
            gbias[:, lanes(D * i + 128 * pair, 128)] = jnp.sum(g.astype(F32), axis=0, keepdims=True)
    for m in range(2):
        for i in range(3):
            arrived(own.at[cols(0, HALF)], wbuf.at[m, :, pl.ds(HALF * i, HALF)], sems.at[1 + 3 * m + i])
    gn = dot_nt(gpm[...], wbuf[0]) + dot_nt(gps[...], wbuf[1])
    gx_ref[...] = norm_back(gn, x_ref, cw, gain, ggain, gshift)


C0 = 0.7978845608028654
C1 = 0.044715


def hidden_start(c, j):
    return pl.multiple_of(FF // 2 * ((c + j // 2) % 2) + D * (j % 2), 128)


def mlp_load(c, own, oth, w1, wd, sems):
    for j in range(4):
        pick(c, 1, own, oth, (slice(None), pl.ds(hidden_start(c, j), D)), w1.at[j], sems.at[j])
        source = own if j < 2 else oth
        pltpu.make_async_copy(source.at[cols(FF + D * (j % 2), D)], wd.at[j], sems.at[4 + j]).start()


def mlp_wait(own, w1, wd, sems, j):
    arrived(own.at[cols(0, D)], w1.at[j], sems.at[j])
    arrived(own.at[cols(0, D)], wd.at[j], sems.at[4 + j])


def mlp_fwd_kernel(
    core, x_ref, own, oth, bias, second, gain, shift, out_ref, actm, acts, dg_ref, n_ref, w1, wd, sems
):
    c = core[0]
    mlp_load(c, own, oth, w1, wd, sems)
    x = x_ref[...].astype(F32)
    xh, _ = norm_parts(x)
    n = (xh * gain[...] + shift[...]).astype(BF)
    n_ref[...] = n
    acc = x + second[...]
    for j in range(4):
        mlp_wait(own, w1, wd, sems, j)
        h = dot(n, w1[j]) + bias[:, pl.ds(hidden_start(c, j), D)]
        h2 = h * h
        t = jnp.tanh(C0 * (h + C1 * h * h2))
        half = 0.5 * (1.0 + t)
        act = (h * half).astype(BF)
        dg = half + (0.5 * C0) * h * (1.0 - t * t) * (1.0 + (3.0 * C1) * h2)
        (actm, acts)[j // 2][:, D * (j % 2) : D * (j % 2 + 1)] = act
        dg_ref[:, D * j : D * (j + 1)] = dg.astype(BF)
        acc = acc + dot_nt(act, wd[j])
    out_ref[...] = acc.astype(BF)


def mlp_bwd_kernel(
    core, x_ref, c_ref, own, oth, gain, dg_ref,
    gx_ref, gxm, gxs, ghm, ghs, ggain, gshift, gbias, gsec, w1, wd, sems,
):
    c = core[0]
    mlp_load(c, own, oth, w1, wd, sems)
    cw = c_ref[...]
    gsec[...] = jnp.sum(cw.astype(F32), axis=0, keepdims=True)
    gn = None
    for j in range(4):
        mlp_wait(own, w1, wd, sems, j)
        ga = dot(cw, wd[j])
        gh = (ga * dg_ref[:, D * j : D * (j + 1)].astype(F32)).astype(BF)
        (ghm, ghs)[j // 2][:, D * (j % 2) : D * (j % 2 + 1)] = gh
        gbias[:, pl.ds(hidden_start(c, j), D)] = jnp.sum(gh.astype(F32), axis=0, keepdims=True)
        part = dot_nt(gh, w1[j])
        gn = part if gn is None else gn + part
    gx_ref[...] = norm_back(gn, x_ref, cw, gain, ggain, gshift)
    gxm[...] = gx_ref[:, lanes(HALF * c, HALF)]
    gxs[...] = gx_ref[:, lanes(HALF * (1 - c), HALF)]


def gram_one_kernel(c0, c1, a0, a1, n0, n1, h0, h1, out):
    out[:, : 2 * D] = (dot_tn(c0[...], a0[...]) + dot_tn(c1[...], a1[...])).astype(BF)
    out[:, 2 * D :] = (dot_tn(n0[...], h0[:, :D]) + dot_tn(n1[...], h1[:, :D])).astype(BF)


def gram_two_kernel(m0, m1, h0, h1, n0, n1, g0, g1, l0, l1, c0, c1, out):
    out[:, :D] = (dot_tn(m0[...], h0[:, D:]) + dot_tn(m1[...], h1[:, D:])).astype(BF)
    out[:, D : D + 3 * HALF] = (dot_tn(n0[...], g0[...]) + dot_tn(n1[...], g1[...])).astype(BF)
    out[:, D + 3 * HALF :] = (dot_tn(l0[...], c0[...]) + dot_tn(l1[...], c1[...])).astype(BF)


def collect_kernel(core, *refs):
    out = refs[-1]
    shards = refs[:-1]
    r = shards[0].shape[0]

    @pl.when(core[0] == 0)
    def _():
        for k in range(len(shards) // 2):
            out[r * k : r * (k + 1), :D] = shards[2 * k][:, 2 * D :]
            out[r * k : r * (k + 1), D:] = shards[2 * k + 1][:, :D]

    @pl.when(core[0] == 1)
    def _():
        for k in range(len(shards) // 2):
            out[r * k : r * (k + 1), :] = shards[2 * k + 1][:, D:]


def place_kernel(core, rows, *refs):
    out, buf, sems = refs[-3:]
    count = sems.shape[0]
    shards, got = refs[: 2 * count], refs[2 * count]
    r = shards[0].shape[0]

    @pl.when(core[0] == 0)
    def _():
        for k in range(count):
            one, two, there = shards[2 * k], shards[2 * k + 1], pl.ds(r * k, r)
            for g in range(4):
                sl = slice(HALF * g, HALF * (g + 1))
                buf[there, D * g : D * g + HALF] = two[:, D + HALF * g : D + HALF * (g + 1)].astype(F32)
                buf[there, D * g + HALF : D * (g + 1)] = got[there, sl].astype(F32)
            buf[there, 4 * D :] = one[:, : 2 * D].astype(F32)

    @pl.when(core[0] == 1)
    def _():
        for k in range(count):
            one, two, there = shards[2 * k], shards[2 * k + 1], pl.ds(r * k, r)
            buf[there, : 2 * D] = got[there, :].astype(F32)
            buf[there, 2 * D : 3 * D] = one[:, 2 * D :].astype(F32)
            buf[there, 3 * D : 4 * D] = two[:, :D].astype(F32)
            buf[there, 4 * D :] = one[:, : 2 * D].astype(F32)

    copies = []
    for k in range(count):
        start = pl.multiple_of(rows[k], 8)
        copies.append(
            pltpu.make_async_copy(buf.at[pl.ds(r * k, r), :], out.at[pl.ds(start, r), :], sems.at[k])
        )
    for copy in copies:
        copy.start()
    for copy in copies:
        copy.wait()


SMEM = pl.BlockSpec(memory_space=pltpu.SMEM)
VS = pl.BlockSpec(memory_space=pltpu.VMEM)
ANY = pl.BlockSpec(memory_space=pl.ANY)


def sds(shape, dtype=BF):
    return jax.ShapeDtypeStruct(shape, dtype)


def call(kernel, name, in_specs, outs, scratch, flops, nbytes, limit, out_specs=None, aliases=None):
    return pl.pallas_call(
        kernel,
        name=name,
        in_specs=in_specs,
        out_specs=[VS] * len(outs) if out_specs is None else out_specs,
        out_shape=outs,
        scratch_shapes=scratch,
        input_output_aliases={} if aliases is None else aliases,
        compiler_params=pltpu.CompilerParams(vmem_limit_bytes=limit * MIB),
        cost_estimate=pl.CostEstimate(flops=flops, bytes_accessed=nbytes, transcendentals=0),
    )


def attn_fwd(*a):
    return call(
        attn_fwd_kernel, "attn_fwd", [SMEM, VS, ANY, ANY] + [VS] * 8,
        [sds((L, D)), sds((L, 3 * D)), sds((HEADS, L, L)), sds((L, D)), sds((L, D))],
        [VM((4, D, D), BF), VM((D, L), BF), VM((D, L), BF), pltpu.SemaphoreType.DMA((4,))],
        int(4e9), int(12e6), 40,
    )(*a)


def attn_bwd(*a):
    return call(
        attn_bwd_kernel, "attn_bwd", [SMEM, VS, VS, ANY, ANY] + [VS] * 8,
        [sds((L, D)), sds((L, 3 * HALF)), sds((L, 3 * HALF)), sds((1, D), F32), sds((1, D), F32),
         sds((1, 3 * D), F32), sds((1, D), F32), sds((1, D), F32), sds((1, D), F32)],
        [VM((D, D), BF), VM((2, D, 3 * HALF), BF), VM((D, L), BF), VM((L, D), BF), VM((128, L), F32),
         VM((16, L), F32), pltpu.SemaphoreType.DMA((7,))],
        int(6e9), int(12e6), 40,
    )(*a)


def mlp_fwd(*a):
    return call(
        mlp_fwd_kernel, "mlp_fwd", [SMEM, VS, ANY, ANY] + [VS] * 4,
        [sds((L, D)), sds((L, FF // 2)), sds((L, FF // 2)), sds((L, FF)), sds((L, D))],
        [VM((4, D, D), BF), VM((4, D, D), BF), pltpu.SemaphoreType.DMA((8,))],
        int(4e9), int(14e6), 40,
    )(*a)


def mlp_bwd(*a):
    return call(
        mlp_bwd_kernel, "mlp_bwd", [SMEM, VS, VS, ANY, ANY] + [VS] * 2,
        [sds((L, D)), sds((L, HALF)), sds((L, HALF)), sds((L, FF // 2)), sds((L, FF // 2)),
         sds((1, D), F32), sds((1, D), F32), sds((1, FF), F32), sds((1, D), F32)],
        [VM((4, D, D), BF), VM((4, D, D), BF), pltpu.SemaphoreType.DMA((8,))],
        int(4e9), int(14e6), 40,
    )(*a)


def gram(kernel, name, *a):
    return call(
        kernel, name, [VS] * len(a), [sds((D, 3 * D))], [], int(3e9), int(8e6), 40
    )(*a)[0]


def collect(flag, shards):
    r = shards[0].shape[0]
    out = [sds((r * (len(shards) // 2), 2 * D))]
    return call(collect_kernel, "collect", [SMEM] + [VS] * len(shards), out, [], 1000, int(1e6), 16)(
        flag, *shards
    )[0]


def place(flag, rows, shards, got, total):
    r, count = shards[0].shape[0], len(shards) // 2
    into = [] if total is None else [total]
    return call(
        place_kernel, "place", [SMEM, SMEM] + [VS] * (len(shards) + 1) + [ANY] * len(into),
        [sds((D, 6 * D), F32)],
        [VM((r * count, 6 * D), F32), pltpu.SemaphoreType.DMA((count,))], 1000, int(2e6), 24,
        out_specs=[ANY], aliases={len(shards) + 3: 0} if into else {},
    )(flag, rows, *shards, got, *into)[0]


def core_swap(a):
    return lax.ppermute(a, "section", [(0, 1), (1, 0), (2, 3), (3, 2)])


def layout(grid_rows):
    heights = grid_rows[:, 0]
    widths = grid_rows[:, 1]
    counts = heights * widths
    end_one = counts[0]
    end_two = end_one + counts[1]
    places = jnp.arange(L, dtype=jnp.int32)
    segment = (places >= end_one).astype(jnp.int32) + (places >= end_two).astype(jnp.int32)
    offset = jnp.where(segment == 0, 0, end_one)
    across = jnp.where(segment == 0, widths[0], widths[1])
    inside = places - offset
    row_pos = jnp.where(segment < 2, inside // across, 0).astype(F32)
    col_pos = jnp.where(segment < 2, inside % across, 0).astype(F32)
    return segment, row_pos, col_pos


class Ring:
    def __init__(self, array, base, direction, n, place):
        self.array, self.base, self.n, self.place, self.d = array, base, n, place, direction
        self.r = array.shape[0] // (2 * n)
        order = list(range(0, n, 2)) + list(range(n - 1, 0, -2))
        self.pairs = [(order[i], order[(i + direction) % n]) for i in range(n)]
        self.cur = self.own(0)
        self.shards = []

    def start(self, t):
        return self.base + ((self.place - self.d * t) % self.n) * self.r

    def own(self, t):
        return lax.dynamic_slice_in_dim(self.array, self.start(t), self.r, 0)

    def step(self, t):
        got = lax.ppermute(self.cur, "dp", self.pairs)
        if t < self.n - 1:
            self.cur = got + self.own(t + 1)
            if t == self.n - 2:
                self.shards.append((self.start(-1), self.cur))
        else:
            self.cur = got
            self.shards.append((self.start(t - self.n + 1), got))


def summed_weight_grad(flag, one, two):
    n = lax.axis_size("dp")
    if n > 16:
        one, two = lax.psum((one, two), "dp")
        got = core_swap(collect(flag, [one, two]))
        return place(flag, jnp.zeros((1,), jnp.int32), [one, two], got, None)
    i = lax.axis_index("dp")
    where = jnp.where(i % 2 == 0, i // 2, n - 1 - i // 2)
    rings = [Ring(a, base, d, n, where) for a in (one, two) for base, d in ((0, 1), (D // 2, -1))]
    total = None
    done = 0
    groups = (3, 3, 1, 1)
    marks = [sum(groups[: k + 1]) for k in range(len(groups))]
    for t in range(2 * n - 2):
        for ring in rings:
            ring.step(t)
        have = len(rings[0].shards)
        if have in marks:
            up, down, up_two, down_two = (ring.shards[done:have] for ring in rings)
            shards, rows = [], []
            for a, b in list(zip(up, up_two)) + list(zip(down, down_two)):
                shards += [a[1], b[1]]
                rows.append(a[0])
            got = core_swap(collect(flag, shards))
            total = place(flag, jnp.stack(rows).astype(jnp.int32), shards, got, total)
            done = have
    return total


def summed_vector(v):
    n = lax.axis_size("dp")
    if n & (n - 1):
        return lax.psum(v, "dp")
    hop = 1
    while hop < n:
        v = v + lax.ppermute(v, "dp", [(i, i ^ hop) for i in range(n)])
        hop *= 2
    return v


def body(
    block_input, cotangent, grid_sizes, section_weight, norm_gain, norm_bias, first_vector, second_vector
):
    section = lax.axis_index("section")
    core = section % 2
    flag = jnp.full((1,), core, jnp.int32)
    first_core = core == 0
    first_layer = section < 2

    quarter = block_input.shape[1]
    mine = jnp.where(first_layer, block_input, cotangent)
    away = jnp.where(first_layer, cotangent, block_input)
    got = lax.ppermute(away, "section", [(0, 2), (1, 3), (2, 0), (3, 1)])
    parts = jnp.where(
        first_layer, jnp.concatenate([mine, got], axis=1), jnp.concatenate([got, mine], axis=1)
    ).reshape(2, L, 2 * quarter)
    keep = lax.dynamic_index_in_dim(parts, core, 0, keepdims=False)
    got = core_swap(lax.dynamic_index_in_dim(parts, 1 - core, 0, keepdims=False))
    left, right = jnp.where(first_core, keep, got), jnp.where(first_core, got, keep)
    field = jnp.concatenate(
        [left[:, :quarter], right[:, :quarter], left[:, quarter:], right[:, quarter:]], axis=1
    )

    own = section_weight[0]
    oth = core_swap(own)
    vec = jnp.concatenate([norm_gain[0], norm_bias[0], first_vector[0], second_vector[0]])[None]
    vec_oth = core_swap(vec)
    vec_a = jnp.where(first_core, vec, vec_oth)
    vec_m = jnp.where(first_core, vec_oth, vec)

    def split(v):
        return v[:, :D], v[:, D : 2 * D], v[:, 2 * D : 2 * D + FF], v[:, 2 * D + FF :]

    gain_a, shift_a, first_a, second_a = split(vec_a)
    gain_m, shift_m, first_m, second_m = split(vec_m)

    segment, row_pos, col_pos = layout(lax.dynamic_index_in_dim(grid_sizes, core, 0, keepdims=False))

    def by_lane(freq):
        by_head = freq.reshape(HEADS, 1, HEAD_DIM // 2)
        return jnp.broadcast_to(by_head, (HEADS, 2, HEAD_DIM // 2)).reshape(1, D)

    freq_x = by_lane(first_a[0, 3 * D : 3 * D + D // 2])
    freq_y = by_lane(first_a[0, 3 * D + D // 2 :])
    theta = col_pos[:, None] * freq_x + row_pos[:, None] * freq_y
    sign = jnp.where(jnp.arange(D) % HEAD_DIM < HEAD_DIM // 2, -1.0, 1.0).astype(F32)
    cosf = jnp.cos(theta)
    sinf = jnp.sin(theta) * sign
    segc, segr = segment[:, None], segment[None, :]
    colp, rowp = col_pos[:, None], row_pos[:, None]

    def attn_f(x):
        return attn_fwd(
            flag, x, own, oth, first_a[:, : 3 * D], second_a, gain_a, shift_a, cosf, sinf, segc, segr
        )

    def mlp_f(x):
        return mlp_fwd(flag, x, own, oth, first_m, second_m, gain_m, shift_m)

    x_two = mlp_f(attn_f(field)[0])[0]
    x_in = jnp.where(first_layer, field, lax.ppermute(x_two, "section", [(0, 2), (1, 3)]))
    x_mid, qkv, pt, ml, n_a = attn_f(x_in)
    x_out, act_mine, act_send, dg, n_m = mlp_f(x_mid)

    def mlp_b(c_out):
        return mlp_bwd(flag, x_mid, c_out, own, oth, gain_m, dg)

    def attn_b(c_mid):
        return attn_bwd(
            flag, x_in, c_mid, own, oth, gain_a, cosf, sinf, colp, rowp, qkv, pt, ml
        )

    c_two = attn_b(mlp_b(field)[0])[0]
    c_out = jnp.where(first_layer, lax.ppermute(c_two, "section", [(2, 0), (3, 1)]), field)
    c_mid, c_mid_mine, c_mid_send, gh_mine, gh_send, ggain_m, gshift_m, gbias_m, gsec_m = mlp_b(c_out)
    c_in, gp_mine, gp_send, ggain_a, gshift_a, gbias_a, gfx, gfy, gsec_a = attn_b(c_mid)

    n_m_oth = core_swap(n_m)
    gh_oth = core_swap(gh_send)
    one = gram(
        gram_one_kernel, "gram_one", c_out, core_swap(c_out), act_mine, core_swap(act_send),
        n_m, n_m_oth, gh_mine, gh_oth,
    )
    two = gram(
        gram_two_kernel, "gram_two", n_m, n_m_oth, gh_mine, gh_oth, n_a, core_swap(n_a),
        gp_mine, core_swap(gp_send), ml, core_swap(ml), c_mid_mine, core_swap(c_mid_send),
    )
    weight_grad = summed_weight_grad(flag, one, two)

    def fold(v):
        pairs = v.reshape(HEADS, 2, HEAD_DIM // 2)
        return (pairs[:, 0] - pairs[:, 1]).reshape(1, -1)

    vg_a = jnp.concatenate([ggain_a, gshift_a, gbias_a, fold(gfx), fold(gfy), gsec_a], axis=1)
    vg_m = jnp.concatenate([ggain_m, gshift_m, gbias_m, gsec_m], axis=1)
    vg = jnp.where(first_core, vg_a, vg_m) + core_swap(jnp.where(first_core, vg_m, vg_a))
    vgain, vshift, vfirst, vsecond = split(summed_vector(vg))

    def rows_of(attn_row, mlp_row):
        got = core_swap(jnp.where(first_core, mlp_row, attn_row))
        kept = jnp.where(first_core, attn_row, mlp_row)
        above, below = jnp.where(first_core, kept, got), jnp.where(first_core, got, kept)
        return jnp.concatenate([above, below], axis=0)[None]

    return (
        rows_of(x_mid, x_out),
        rows_of(c_in, c_mid),
        weight_grad[None],
        vgain,
        vshift,
        vfirst,
        vsecond,
    )


def solution(mesh):
    in_specs = (
        P("dp", "section"),
        P("dp", "section"),
        P("dp", None, None),
        P("section", None, None),
        P("section", None),
        P("section", None),
        P("section", None),
        P("section", None),
    )
    out_specs = (
        P("section", "dp", None),
        P("section", "dp", None),
        P("section", None, None),
        P("section", None),
        P("section", None),
        P("section", None),
        P("section", None),
    )
    return jax.shard_map(body, mesh=mesh, in_specs=in_specs, out_specs=out_specs, check_vma=False)
```

```python
import jax
import jax.numpy as jnp
from jax import lax
from jax.experimental import pallas as pl
from jax.experimental.pallas import tpu as pltpu
from jax.sharding import PartitionSpec as P

D = 768
HEADS = 12
HEAD_DIM = 64
FF = 3072
L = 384
HALF = D // 2
F32 = jnp.float32
BF = jnp.bfloat16
I32 = jnp.int32
NT = (((1,), (1,)), ((), ()))
TN = (((0,), (0,)), ((), ()))
VM = pltpu.VMEM
DMA = pltpu.SemaphoreType.DMA
MIB = 1024 * 1024
LN2 = 0.6931471805599453
GAIN, SHIFT = slice(0, D), slice(D, 2 * D)
FIRST, SECOND = 2 * D, 2 * D + FF
VECTOR = 3 * D + FF


def dot(a, b):
    return jnp.dot(a, b, preferred_element_type=F32)


def dot_nt(a, b):
    return lax.dot_general(a, b, NT, preferred_element_type=F32)


def dot_tn(a, b):
    return lax.dot_general(a, b, TN, preferred_element_type=F32)


def norm_parts(x):
    center = x - jnp.mean(x, axis=-1, keepdims=True)
    inv = lax.rsqrt(jnp.mean(center * center, axis=-1, keepdims=True) + 1e-06)
    return center * inv, inv


def swap_halves(a):
    lane = lax.broadcasted_iota(I32, (1, 128), 1)
    first = (lane % HEAD_DIM) < HEAD_DIM // 2
    out = []
    for i in range(a.shape[1] // 128):
        s = a[:, 128 * i : 128 * (i + 1)]
        out.append(jnp.where(first, pltpu.roll(s, 96, 1), pltpu.roll(s, 32, 1)))
    return jnp.concatenate(out, axis=1) if len(out) > 1 else out[0]


def lanes(start, size):
    if isinstance(start, int):
        return slice(start, start + size)
    return pl.ds(pl.multiple_of(start, 128), size)


def rows_at(start, size):
    if isinstance(start, int):
        return slice(start, start + size)
    return pl.ds(pl.multiple_of(start, size), size)


def cols(start, size):
    return (slice(None), pl.ds(start, size))


def pick(flag, want, own, oth, src, dst, sem):
    @pl.when(flag == want)
    def _():
        pltpu.make_async_copy(own.at[src], dst, sem).start()

    @pl.when(flag != want)
    def _():
        pltpu.make_async_copy(oth.at[src], dst, sem).start()


def load(src, dst, sem):
    pltpu.make_async_copy(src, dst, sem).start()


def arrived(src, dst, sem):
    pltpu.make_async_copy(src, dst, sem).wait()


def load_attn(core, own, oth, wa, sems):
    for i in range(4):
        pick(core, 0, own, oth, cols(D * i, D), wa.at[i], sems.at[i])


def wait_attn(own, wa, sems, i):
    arrived(own.at[cols(D * i, D)], wa.at[i], sems.at[i])


def hidden_start(core, j):
    return pl.multiple_of(FF // 2 * ((core + j // 2) % 2) + D * (j % 2), 128)


def load_mlp(core, own, oth, w1, wd, sems):
    for j in range(4):
        pick(core, 1, own, oth, (slice(None), pl.ds(hidden_start(core, j), D)), w1.at[j], sems.at[j])
        load((own if j < 2 else oth).at[cols(FF + D * (j % 2), D)], wd.at[j], sems.at[4 + j])


def wait_mlp(own, w1, wd, sems, j):
    if w1 is not None:
        arrived(own.at[cols(0, D)], w1.at[j], sems.at[j])
    arrived(own.at[cols(0, D)], wd.at[j], sems.at[4 + j])


def vectors(core, own, oth):
    a, b = own[...], oth[...]
    return jnp.where(core == 0, a, b), jnp.where(core == 0, b, a)


def attention(x, vec, wa, wait, cosf, sinf, segc, segr, qkv, pt, rec, ml, mlt, vt, n_ref):
    xh, inv = norm_parts(x)
    n = (xh * vec[:, GAIN] + vec[:, SHIFT]).astype(BF)
    n_ref[...] = n
    for i in range(3):
        wait(i)
        part = dot(n, wa[i]) + vec[:, FIRST + D * i : FIRST + D * (i + 1)]
        if i < 2:
            part = part * cosf[...] + swap_halves(part) * sinf[...]
        if i == 0:
            part = part * (HEAD_DIM**-0.5 / LN2)
        qkv[:, D * i : D * (i + 1)] = part.astype(BF)
    vt[...] = qkv[:, 2 * D : 3 * D].T
    same = segc == segr
    lane = lax.broadcasted_iota(I32, (1, 128), 1)

    def score(h):
        p = 128 * (h // 2)
        keys = jnp.where((lane // HEAD_DIM) == h % 2, qkv[:, D + p : D + p + 128], BF(0))
        return dot_nt(keys, qkv[:, p : p + 128])

    ahead = score(0)
    for h in range(HEADS):
        st = ahead
        if h + 1 < HEADS:
            ahead = score(h + 1)
        st = jnp.where(same, st, -1e30)
        e = jnp.exp2(st - jnp.max(st, axis=0, keepdims=True))
        r = 1.0 / jnp.sum(e, axis=0, keepdims=True)
        rec[h : h + 1, :] = r
        e = e.astype(BF)
        pt[h] = e
        here = slice(HEAD_DIM * h, HEAD_DIM * (h + 1))
        mlt[here, :] = (dot(vt[here, :], e) * r).astype(BF)
    ml[...] = mlt[...].T
    wait(3)
    out = x + dot(ml[...], wa[3]) + vec[:, SECOND : SECOND + D]
    return out.astype(BF), xh, inv


C0 = 0.7978845608028654
C1 = 0.044715


def gelu(h):
    h2 = h * h
    t = jnp.tanh(C0 * (h + C1 * h * h2))
    half = 0.5 * (1.0 + t)
    return h * half, half + (0.5 * C0) * h * (1.0 - t * t) * (1.0 + (3.0 * C1) * h2)


def norm_back(gn, xh, inv, gain, c):
    u = gn * gain
    gx = inv * (
        u - jnp.mean(u, axis=-1, keepdims=True) - xh * jnp.mean(u * xh, axis=-1, keepdims=True)
    )
    return (c.astype(F32) + gx).astype(BF)


def head_select():
    head = lax.broadcasted_iota(I32, (16, D), 0)
    lane = lax.broadcasted_iota(I32, (16, D), 1)
    return jnp.where(lane // HEAD_DIM == head, 1.0, 0.0).astype(BF)


def split_two(a):
    hi = a.astype(BF)
    return hi, (a - hi.astype(F32)).astype(BF)


def attention_back(c, wo, cosf, sinf, qkv, pt, rec, ml, kt, gm, gqt, dsum, pair_of, emit):
    kt[...] = qkv[:, D : 2 * D].T
    gm_wide = dot_nt(c, wo[...])
    sel = head_select()
    hi, lo = split_two(gm_wide * ml[...].astype(F32))
    row = lax.broadcasted_iota(I32, (16, L), 0)
    recs = jnp.where(row < HEADS, rec[...], 0.0)
    dsum[...] = (dot_nt(sel, hi) + dot_nt(sel, lo)) * recs
    hi, lo = split_two(recs)
    gm[...] = (gm_wide * (dot_tn(hi, sel) + dot_tn(lo, sel))).astype(BF)
    lane = lax.broadcasted_iota(I32, (1, 128), 1)

    def spot(h):
        return lanes(128 * pair_of(h // 2), 128), (lane // HEAD_DIM) == h % 2

    def from_values(h):
        sl, here = spot(h)
        values = qkv[:, lanes(2 * D + 128 * pair_of(h // 2), 128)]
        return dot_nt(jnp.where(here, values, BF(0)), gm[:, sl])

    ahead = from_values(0)
    for h in range(HEADS):
        gpt = ahead
        if h + 1 < HEADS:
            ahead = from_values(h + 1)
        sl, here = spot(h)
        head = 2 * pair_of(h // 2) + h % 2
        e = pt[head]
        gvh = dot(e, jnp.where(here, gm[:, sl], BF(0)))
        gst = (e.astype(F32) * (gpt - dsum[rows_at(head, 1), :])).astype(BF)
        gkh = dot(gst, jnp.where(here, qkv[:, sl], BF(0)))
        kth = kt[rows_at(HEAD_DIM * head, HEAD_DIM), :]
        gqt[h // 2 % 2, HEAD_DIM * (h % 2) : HEAD_DIM * (h % 2 + 1), :] = dot(kth, gst)
        gv = gvh if h % 2 == 0 else gv + gvh
        gk = gkh if h % 2 == 0 else gk + gkh
        if h % 2 == 1:
            gq = gqt[h // 2 % 2].T * (HEAD_DIM**-0.5)
            gk = gk * LN2
            cs, sn = cosf[:, sl], sinf[:, sl]
            sq, sk = swap_halves(gq), swap_halves(gk)
            emit(
                h // 2, sl, sq, sk,
                ((gq * cs - sq * sn).astype(BF), (gk * cs - sk * sn).astype(BF), gv.astype(BF)),
            )


def positions_kernel(flags, grid, vown, voth, cosf, sinf, pos, segr):
    core = flags[0]
    vec = vectors(core, vown, voth)[0]
    h0, w0, h1, w1 = (grid[core, k // 2, k % 2] for k in range(4))
    e1 = h0 * w0
    e2 = e1 + h1 * w1

    def place(t):
        segment = (t >= e1).astype(I32) + (t >= e2).astype(I32)
        width = jnp.where(segment == 0, w0, w1).astype(F32)
        inside = (t - jnp.where(segment == 0, 0, e1)).astype(F32)
        row = jnp.floor((inside + 0.5) / width)
        column = inside - row * width
        return segment, jnp.where(segment < 2, row, 0.0), jnp.where(segment < 2, column, 0.0)

    segment, row, column = place(lax.broadcasted_iota(I32, (L, 128), 0))
    lane = lax.broadcasted_iota(I32, (L, 128), 1)
    pos[...] = jnp.where(lane == 0, column, jnp.where(lane == 1, row, segment.astype(F32)))
    t = lax.broadcasted_iota(I32, (8, L), 1)
    segr[...] = (t >= e1).astype(F32) + (t >= e2).astype(F32)

    def by_lane(start):
        parts = []
        for h in range(HEADS):
            f = vec[:, start + 32 * h : start + 32 * (h + 1)]
            parts += [f, f]
        return jnp.concatenate(parts, axis=1)

    number = lax.broadcasted_iota(I32, (16, D), 0).astype(F32)

    def look_up(which, table):
        hi, rest = split_two(table)
        mid, low = split_two(table - hi.astype(F32))
        tables = jnp.concatenate([hi, mid, low], axis=0)
        hit = (lax.broadcasted_iota(I32, (L, 48), 1) % 16).astype(F32) == which[:, :48]
        return dot(jnp.where(hit, 1.0, 0.0).astype(BF), tables)

    ax = number * by_lane(FIRST + 3 * D)
    ay = number * by_lane(FIRST + 3 * D + HALF)
    cx, sx = look_up(column, jnp.cos(ax)), look_up(column, jnp.sin(ax))
    cy, sy = look_up(row, jnp.cos(ay)), look_up(row, jnp.sin(ay))
    cosf[...] = cx * cy - sx * sy
    lane = lax.broadcasted_iota(I32, (1, D), 1)
    sign = jnp.where(lane % HEAD_DIM < HEAD_DIM // 2, -1.0, 1.0)
    sinf[...] = (sx * cy + cx * sy) * sign


def split_kernel(flags, x, cot, got, keep, send):
    core, layer = flags[0], flags[1]
    mine = jnp.where(layer == 0, x[...].astype(F32), cot[...].astype(F32)).astype(BF)
    other = got[...]
    w = mine.shape[1]
    for k in range(2):
        rows = slice(L * k, L * (k + 1))

        for at in range(2):
            first, second = (mine, other) if at == 0 else (other, mine)

            @pl.when((core == k) & (layer == at))
            def _(first=first, second=second, rows=rows):
                keep[:, :w] = first[rows]
                keep[:, w:] = second[rows]

            @pl.when((core != k) & (layer == at))
            def _(first=first, second=second, rows=rows):
                send[:, :w] = first[rows]
                send[:, w:] = second[rows]


def first_kernel(
    flags, keep, got, vown, voth, cos_in, sin_in, pos, segr, own, oth,
    field, out, wa, w1, wd, cosf, sinf, qkv, pt, rec, ml, mlt, vt, n_ref, sems,
):
    core = flags[0]
    load_attn(core, own, oth, wa, sems)
    load(cos_in, cosf, sems.at[12])
    load(sin_in, sinf, sems.at[13])
    load_mlp(core, own, oth, w1, wd, sems.at[pl.ds(4, 8)])
    w = keep.shape[1] // 2
    for k in range(2):

        @pl.when(core == k)
        def _(k=k):
            parts = (keep, got) if k == 0 else (got, keep)
            for s in range(4):
                field[:, w * s : w * (s + 1)] = parts[s % 2][:, w * (s // 2) : w * (s // 2 + 1)]

    va, vm = vectors(core, vown, voth)

    def wait(i):
        wait_attn(own, wa, sems, i)
        if i == 0:
            arrived(cos_in, cosf, sems.at[12])
            arrived(sin_in, sinf, sems.at[13])

    x_mid, _, _ = attention(
        field[...].astype(F32), va, wa, wait, cosf, sinf, pos[:, 2:3], segr[0:1, :],
        qkv, pt, rec, ml, mlt, vt, n_ref,
    )
    x = x_mid.astype(F32)
    xh, _ = norm_parts(x)
    n = (xh * vm[:, GAIN] + vm[:, SHIFT]).astype(BF)
    for j in range(4):
        wait_mlp(own, w1, wd, sems.at[pl.ds(4, 8)], j)
    acc = x + vm[:, SECOND : SECOND + D]
    first = jnp.where(core == 0, vm[:, FIRST:SECOND], jnp.concatenate(
        [vm[:, FIRST + FF // 2 : SECOND], vm[:, FIRST : FIRST + FF // 2]], axis=1))
    ahead = dot(n, w1[0])
    for j in range(4):
        h = ahead + first[:, D * j : D * (j + 1)]
        if j < 3:
            ahead = dot(n, w1[j + 1])
        acc = acc + dot_nt(gelu(h)[0].astype(BF), wd[j])
    out[...] = acc.astype(BF)


def second_kernel(
    flags, field, got, vown, voth, cos_in, sin_in, pos, segr, own, oth,
    cx, xm_out, qkv_out, pt_out, rec_out, ml_out, mlt_out, na_out, nm_out, actm_out, acts_out, dg_out,
    wa, w1, wd, cosf, sinf, qkv, pt, rec, ml, mlt, vt, na, nm, xm, actm, acts, dg, xha, xhm,
    kt, gm, gqt, dsum, gp, sems, outs,
):
    core, layer = flags[0], flags[1]
    load_attn(core, own, oth, wa, sems)
    load(cos_in, cosf, sems.at[12])
    load(sin_in, sinf, sems.at[13])
    mlp_sems = sems.at[pl.ds(4, 8)]
    load_mlp(core, own, oth, w1, wd, mlp_sems)
    va, vm = vectors(core, vown, voth)
    sent = []

    def send(src, dst):
        copy = pltpu.make_async_copy(src, dst, outs.at[len(sent)])
        copy.start()
        sent.append(copy)

    def wait(i):
        wait_attn(own, wa, sems, i)
        if i == 0:
            arrived(cos_in, cosf, sems.at[12])
            arrived(sin_in, sinf, sems.at[13])

    x = jnp.where(layer == 0, field[...].astype(F32), got[...].astype(F32))
    x_mid, xh, inv_a = attention(
        x, va, wa, wait, cosf, sinf, pos[:, 2:3], segr[0:1, :], qkv, pt, rec, ml, mlt, vt, na
    )
    xha[...] = xh
    xm[...] = x_mid
    send(qkv, qkv_out)
    send(pt, pt_out)
    send(rec, rec_out)
    send(ml, ml_out)
    send(mlt, mlt_out)
    send(na, na_out)
    send(xm, xm_out)
    xh, inv_m = norm_parts(x_mid.astype(F32))
    xhm[...] = xh
    n = (xh * vm[:, GAIN] + vm[:, SHIFT]).astype(BF)
    nm[...] = n
    send(nm, nm_out)
    for j in range(4):
        wait_mlp(own, w1, wd, mlp_sems, j)
    first = jnp.where(core == 0, vm[:, FIRST:SECOND], jnp.concatenate(
        [vm[:, FIRST + FF // 2 : SECOND], vm[:, FIRST : FIRST + FF // 2]], axis=1))
    c = field[...]
    ahead = dot(n, w1[0]), dot(c, wd[0])
    gn = None
    for j in range(4):
        h, ga = ahead
        h = h + first[:, D * j : D * (j + 1)]
        if j < 3:
            ahead = dot(n, w1[j + 1]), dot(c, wd[j + 1])
        act, slope = gelu(h)
        (actm, acts)[j // 2][:, D * (j % 2) : D * (j % 2 + 1)] = act.astype(BF)
        slope = slope.astype(BF)
        dg[:, D * j : D * (j + 1)] = slope
        part = dot_nt((ga * slope.astype(F32)).astype(BF), w1[j])
        gn = part if gn is None else gn + part
    send(actm, actm_out)
    send(acts, acts_out)
    send(dg, dg_out)
    c = norm_back(gn, xhm[...], inv_m, vm[:, GAIN], c)

    def emit(p, sl, sq, sk, grads):
        for i in range(3):
            gp[:, D * i + 128 * p : D * i + 128 * (p + 1)] = grads[i]

    attention_back(
        c, wa.at[3], cosf, sinf, qkv, pt, rec, ml, kt, gm, gqt, dsum, lambda p: p, emit
    )
    gn = None
    for i in range(3):
        part = dot_nt(gp[:, D * i : D * (i + 1)], wa[i])
        gn = part if gn is None else gn + part
    cx[...] = norm_back(gn, xha[...], inv_a, va[:, GAIN], c)
    for copy in sent:
        copy.wait()


def late_kernel(flags, xm, nm, na, actm, acts, vown, voth, own, oth, out, nmt, nat, wd, sems):
    for j in range(4):
        load((own if j < 2 else oth).at[cols(FF + D * (j % 2), D)], wd.at[j], sems.at[4 + j])
    vm = vectors(flags[0], vown, voth)[1]
    nmt[...] = nm[...].T
    nat[...] = na[...].T
    acc = xm[...].astype(F32) + vm[:, SECOND : SECOND + D]
    for j in range(4):
        wait_mlp(own, None, wd, sems, j)
        acc = acc + dot_nt((actm, acts)[j // 2][:, D * (j % 2) : D * (j % 2 + 1)], wd[j])
    out[...] = acc.astype(BF)


def norm_stats(gn, x, ggain, gshift):
    xh, inv = norm_parts(x)
    ggain[...] = jnp.sum(gn * xh, axis=0, keepdims=True)
    gshift[...] = jnp.sum(gn, axis=0, keepdims=True)
    return xh, inv


def mlp_back_kernel(
    flags, field, got, xm, vown, voth, dg_in, own, oth,
    cm, cmm, cms, ghm, ghs, ggain, gshift, gbias, gsec, w1, wd, dg, sems,
):
    core, layer = flags[0], flags[1]
    for j in range(4):
        load(dg_in.at[cols(D * j, D)], dg.at[j], sems.at[8 + j])
        pick(core, 1, own, oth, (slice(None), pl.ds(hidden_start(core, j), D)), w1.at[j], sems.at[j])
        load((own if j < 2 else oth).at[cols(FF + D * (j % 2), D)], wd.at[j], sems.at[4 + j])
    vm = vectors(core, vown, voth)[1]
    wide = jnp.where(layer == 0, got[...].astype(F32), field[...].astype(F32))
    c = wide.astype(BF)
    gsec[...] = jnp.sum(wide, axis=0, keepdims=True)

    def back(j):
        wait_mlp(own, w1, wd, sems, j)
        arrived(dg_in.at[cols(0, D)], dg.at[j], sems.at[8 + j])
        return dot(c, wd[j])

    ahead = back(0)
    gn = None
    for j in range(4):
        ga = ahead
        if j < 3:
            ahead = back(j + 1)
        gh = (ga * dg[j].astype(F32)).astype(BF)
        (ghm, ghs)[j // 2][:, D * (j % 2) : D * (j % 2 + 1)] = gh
        gbias[:, pl.ds(hidden_start(core, j), D)] = jnp.sum(gh.astype(F32), axis=0, keepdims=True)
        part = dot_nt(gh, w1[j])
        gn = part if gn is None else gn + part
    xh, inv = norm_stats(gn, xm[...].astype(F32), ggain, gshift)
    cm[...] = norm_back(gn, xh, inv, vm[:, GAIN], c)
    cmm[...] = cm[:, lanes(HALF * core, HALF)]
    cms[...] = cm[:, lanes(HALF * (1 - core), HALF)]


def attn_back_kernel(
    flags, field, got, c_ref, vown, voth, pos, rec, cos_in, sin_in, qkv_in, pt_in, ml_in, own, oth,
    cx, gpm, gps, ggain, gshift, gbias, gfx, gfy, gsec,
    wo, wbuf, cosf, sinf, qkv, pt, ml, kt, gm, gqt, dsum, sems,
):
    core, layer = flags[0], flags[1]
    pick(core, 0, own, oth, cols(3 * D, D), wo, sems.at[0])
    loads = [(qkv_in, qkv), (ml_in, ml), (pt_in, pt), (cos_in, cosf), (sin_in, sinf)]
    for k, (src, dst) in enumerate(loads):
        load(src, dst, sems.at[7 + k])
    for m in range(2):
        for i in range(3):
            start = pl.multiple_of(D * i + HALF * ((core + m) % 2), 128)
            pick(
                core, 0, own, oth, (slice(None), pl.ds(start, HALF)),
                wbuf.at[m, :, pl.ds(HALF * i, HALF)], sems.at[1 + 3 * m + i],
            )
    va = vectors(core, vown, voth)[0]
    c = c_ref[...]
    gsec[...] = jnp.sum(c.astype(F32), axis=0, keepdims=True)
    colp, rowp = pos[:, 0:1], pos[:, 1:2]
    arrived(own.at[cols(3 * D, D)], wo, sems.at[0])
    for k, (src, dst) in enumerate(loads):
        arrived(src, dst, sems.at[7 + k])

    def pair_of(p):
        return 3 * ((core + p // 3) % 2) + p % 3

    def emit(p, sl, sq, sk, grads):
        pair = pair_of(p)
        qr = qkv[:, sl].astype(F32) * (LN2 * HEAD_DIM**0.5)
        th = sq * qr + sk * qkv[:, lanes(D + 128 * pair, 128)].astype(F32)
        gfx[:, sl] = jnp.sum(th * colp, axis=0, keepdims=True)
        gfy[:, sl] = jnp.sum(th * rowp, axis=0, keepdims=True)
        at = p % 3
        for i, g in enumerate(grads):
            (gpm, gps)[p // 3][:, HALF * i + 128 * at : HALF * i + 128 * (at + 1)] = g
            gbias[:, lanes(D * i + 128 * pair, 128)] = jnp.sum(g.astype(F32), axis=0, keepdims=True)

    attention_back(c, wo, cosf, sinf, qkv, pt, rec, ml, kt, gm, gqt, dsum, pair_of, emit)
    for m in range(2):
        for i in range(3):
            arrived(own.at[cols(0, HALF)], wbuf.at[m, :, pl.ds(HALF * i, HALF)], sems.at[1 + 3 * m + i])
    gn = dot_nt(gpm[...], wbuf[0]) + dot_nt(gps[...], wbuf[1])
    x = jnp.where(layer == 0, field[...].astype(F32), got[...].astype(F32))
    xh, inv = norm_stats(gn, x, ggain, gshift)
    cx[...] = norm_back(gn, xh, inv, va[:, GAIN], c)


def gram_down_kernel(flags, f0, f1, g0, g1, a0, a1, out):
    first = flags[1] == 0
    c0 = jnp.where(first, g0[...].astype(F32), f0[...].astype(F32)).astype(BF)
    c1 = jnp.where(first, g1[...].astype(F32), f1[...].astype(F32)).astype(BF)
    out[...] = (dot_tn(c0, a0[...]) + dot_tn(c1, a1[...])).astype(BF)


def gram_up_kernel(n0, n1, h0, h1, out):
    out[...] = (dot(n0[...], h0[...]) + dot(n1[...], h1[...])).astype(BF)


def gram_attn_kernel(n0, n1, g0, g1, l0, l1, c0, c1, out):
    out[:, : 3 * HALF] = (dot(n0[...], g0[...]) + dot(n1[...], g1[...])).astype(BF)
    out[:, 3 * HALF :] = (dot(l0[...], c0[...]) + dot(l1[...], c1[...])).astype(BF)


def collect_kernel(flags, *refs):
    out = refs[-1]
    shards = refs[:-1]
    r = shards[0].shape[0]

    @pl.when(flags[0] == 0)
    def _():
        for k in range(len(shards) // 2):
            out[r * k : r * (k + 1), :D] = shards[2 * k][:, 2 * D :]
            out[r * k : r * (k + 1), D:] = shards[2 * k + 1][:, :D]

    @pl.when(flags[0] == 1)
    def _():
        for k in range(len(shards) // 2):
            out[r * k : r * (k + 1), :] = shards[2 * k + 1][:, D:]


def place_kernel(flags, rows, *refs):
    out, buf, sems = refs[-3:]
    count = sems.shape[0]
    shards, got = refs[: 2 * count], refs[2 * count]
    r = shards[0].shape[0]

    @pl.when(flags[0] == 0)
    def _():
        for k in range(count):
            one, two, there = shards[2 * k], shards[2 * k + 1], pl.ds(r * k, r)
            for g in range(4):
                sl = slice(HALF * g, HALF * (g + 1))
                buf[there, D * g : D * g + HALF] = two[:, D + HALF * g : D + HALF * (g + 1)].astype(F32)
                buf[there, D * g + HALF : D * (g + 1)] = got[there, sl].astype(F32)
            buf[there, 4 * D :] = one[:, : 2 * D].astype(F32)

    @pl.when(flags[0] == 1)
    def _():
        for k in range(count):
            one, two, there = shards[2 * k], shards[2 * k + 1], pl.ds(r * k, r)
            buf[there, : 2 * D] = got[there, :].astype(F32)
            buf[there, 2 * D : 3 * D] = one[:, 2 * D :].astype(F32)
            buf[there, 3 * D : 4 * D] = two[:, :D].astype(F32)
            buf[there, 4 * D :] = one[:, : 2 * D].astype(F32)

    copies = []
    for k in range(count):
        start = pl.multiple_of(rows[k], 8)
        copies.append(
            pltpu.make_async_copy(buf.at[pl.ds(r * k, r), :], out.at[pl.ds(start, r), :], sems.at[k])
        )
    for copy in copies:
        copy.start()
    for copy in copies:
        copy.wait()


SMEM = pl.BlockSpec(memory_space=pltpu.SMEM)
VS = pl.BlockSpec(memory_space=pltpu.VMEM)
HBM = pl.BlockSpec(memory_space=pltpu.HBM)


def sds(shape, dtype=BF):
    return jax.ShapeDtypeStruct(shape, dtype)


def call(kernel, name, in_specs, outs, scratch, flops, nbytes, limit=58, out_specs=None, aliases=None):
    return pl.pallas_call(
        kernel,
        name=name,
        in_specs=in_specs,
        out_specs=[VS] * len(outs) if out_specs is None else out_specs,
        out_shape=outs,
        scratch_shapes=scratch,
        input_output_aliases={} if aliases is None else aliases,
        compiler_params=pltpu.CompilerParams(vmem_limit_bytes=limit * MIB),
        cost_estimate=pl.CostEstimate(flops=flops, bytes_accessed=nbytes, transcendentals=0),
    )


ATTN_W = [VM((4, D, D), BF)]
MLP_W = [VM((4, D, D), BF), VM((4, D, D), BF)]
ANGLES = [VM((L, D), F32), VM((L, D), F32)]
ATTN_S = [
    VM((L, 3 * D), BF), VM((HEADS, L, L), BF), VM((16, L), F32), VM((L, D), BF), VM((D, L), BF),
    VM((D, L), BF),
]
BACK_S = [VM((D, L), BF), VM((L, D), BF), VM((2, 128, L), F32), VM((16, L), F32)]


def positions(flags, grid, vown, voth):
    return call(
        positions_kernel, "positions", [SMEM, SMEM, VS, VS],
        [sds((L, D), F32), sds((L, D), F32), sds((L, 128), F32), sds((8, L), F32)],
        [], int(1e8), int(3e6), 30,
    )(flags, grid, vown, voth)


def split_rows(flags, x, cot, got):
    out = sds((L, 2 * x.shape[1]))
    return call(split_kernel, "split", [SMEM, VS, VS, VS], [out, out], [], 1000, int(1e6), 20)(
        flags, x, cot, got
    )


def first_pass(*a):
    return call(
        first_kernel, "first_pass", [SMEM] + [VS] * 4 + [HBM] * 2 + [VS] * 2 + [HBM] * 2,
        [sds((L, D)), sds((L, D))],
        ATTN_W + MLP_W + ANGLES + ATTN_S + [VM((L, D), BF), DMA((14,))],
        int(8e9), int(20e6),
    )(*a)


def second_pass(*a):
    saved = [
        sds((L, D)), sds((L, 3 * D)), sds((HEADS, L, L)), sds((16, L), F32), sds((L, D)), sds((D, L)),
        sds((L, D)), sds((L, D)), sds((L, FF // 2)), sds((L, FF // 2)), sds((L, FF)),
    ]
    return call(
        second_kernel, "second_pass", [SMEM] + [VS] * 4 + [HBM] * 2 + [VS] * 2 + [HBM] * 2,
        [sds((L, D))] + saved,
        ATTN_W + MLP_W + ANGLES + ATTN_S
        + [VM((L, D), BF), VM((L, D), BF), VM((L, D), BF), VM((L, FF // 2), BF), VM((L, FF // 2), BF),
           VM((L, FF), BF), VM((L, D), F32), VM((L, D), F32)]
        + BACK_S + [VM((L, 3 * D), BF), DMA((14,)), DMA((11,))],
        int(18e9), int(35e6), out_specs=[VS] + [HBM] * len(saved),
    )(*a)


def late_pass(*a):
    return call(
        late_kernel, "late_pass", [SMEM] + [VS] * 7 + [HBM] * 2,
        [sds((L, D)), sds((D, L)), sds((D, L))], [VM((4, D, D), BF), DMA((8,))], int(2e9), int(10e6),
    )(*a)


def mlp_back(*a):
    return call(
        mlp_back_kernel, "mlp_back", [SMEM] + [VS] * 5 + [HBM] * 3,
        [sds((L, D)), sds((L, HALF)), sds((L, HALF)), sds((L, FF // 2)), sds((L, FF // 2)),
         sds((1, D), F32), sds((1, D), F32), sds((1, FF), F32), sds((1, D), F32)],
        MLP_W + [VM((4, L, D), BF), DMA((12,))], int(4e9), int(14e6),
    )(*a)


def attn_back(*a):
    return call(
        attn_back_kernel, "attn_back", [SMEM] + [VS] * 7 + [HBM] * 7,
        [sds((L, D)), sds((L, 3 * HALF)), sds((L, 3 * HALF)), sds((1, D), F32), sds((1, D), F32),
         sds((1, 3 * D), F32), sds((1, D), F32), sds((1, D), F32), sds((1, D), F32)],
        [VM((D, D), BF), VM((2, D, 3 * HALF), BF)] + ANGLES
        + [VM((L, 3 * D), BF), VM((HEADS, L, L), BF), VM((L, D), BF)] + BACK_S + [DMA((12,))],
        int(6e9), int(14e6),
    )(*a)


def gram(kernel, name, specs, *a):
    return call(kernel, name, specs, [sds((D, 2 * D))], [], int(2e9), int(6e6))(*a)[0]


def collect(flags, shards):
    r = shards[0].shape[0]
    out = [sds((r * (len(shards) // 2), 2 * D))]
    return call(collect_kernel, "collect", [SMEM] + [VS] * len(shards), out, [], 1000, int(1e6))(
        flags, *shards
    )[0]


def place(flags, rows, shards, got, total):
    r, count = shards[0].shape[0], len(shards) // 2
    into = [] if total is None else [total]
    return call(
        place_kernel, "place", [SMEM, SMEM] + [VS] * (len(shards) + 1) + [HBM] * len(into),
        [sds((D, 6 * D), F32)],
        [VM((r * count, 6 * D), F32), DMA((count,))], 1000, int(2e6),
        out_specs=[HBM], aliases={len(shards) + 3: 0} if into else {},
    )(flags, rows, *shards, got, *into)[0]


def core_swap(a):
    return lax.ppermute(a, "section", [(0, 1), (1, 0), (2, 3), (3, 2)])


class Ring:
    def __init__(self, parts, base, direction, n, where):
        self.parts, self.base, self.n, self.where, self.d = parts, base, n, where, direction
        self.r = D // (2 * n)
        order = list(range(0, n, 2)) + list(range(n - 1, 0, -2))
        self.pairs = [(order[i], order[(i + direction) % n]) for i in range(n)]
        self.cur = self.own(0)
        self.shards = []

    def start(self, t):
        return self.base + ((self.where - self.d * t) % self.n) * self.r

    def own(self, t):
        at = self.start(t)
        return jnp.concatenate(
            [lax.dynamic_slice(a, (at, first), (self.r, size)) for a, first, size in self.parts], axis=1
        )

    def step(self, t):
        got = lax.ppermute(self.cur, "dp", self.pairs)
        if t < self.n - 1:
            self.cur = got + self.own(t + 1)
            if t == self.n - 2:
                self.shards.append((self.start(-1), self.cur))
        else:
            self.cur = got
            self.shards.append((self.start(t - self.n + 1), got))


def summed_weight_grad(flags, one, two):
    n = lax.axis_size("dp")
    if n > 16:
        one, two = lax.psum(
            tuple(
                jnp.concatenate([a[:, first : first + size] for a, first, size in parts], axis=1)
                for parts in (one, two)
            ),
            "dp",
        )
        got = core_swap(collect(flags, [one, two]))
        return place(flags, jnp.zeros((1,), I32), [one, two], got, None)
    i = lax.axis_index("dp")
    where = jnp.where(i % 2 == 0, i // 2, n - 1 - i // 2)
    rings = [Ring(parts, base, d, n, where) for parts in (one, two) for base, d in ((0, 1), (HALF, -1))]
    total = None
    done = 0
    groups = (3, 3, 1, 1)
    marks = [sum(groups[: k + 1]) for k in range(len(groups))]
    for t in range(2 * n - 2):
        for ring in rings:
            ring.step(t)
        have = len(rings[0].shards)
        if have in marks:
            up, down, up_two, down_two = (ring.shards[done:have] for ring in rings)
            shards, rows = [], []
            for a, b in list(zip(up, up_two)) + list(zip(down, down_two)):
                shards += [a[1], b[1]]
                rows.append(a[0])
            got = core_swap(collect(flags, shards))
            total = place(flags, jnp.stack(rows).astype(I32), shards, got, total)
            done = have
    return total


def summed_vector(v):
    n = lax.axis_size("dp")
    if n & (n - 1):
        return lax.psum(v, "dp")
    hop = 1
    while hop < n:
        v = v + lax.ppermute(v, "dp", [(i, i ^ hop) for i in range(n)])
        hop *= 2
    return v


def after(value, first):
    return lax.optimization_barrier((value, first))[0]


def body(
    block_input, cotangent, grid_sizes, section_weight, norm_gain, norm_bias, first_vector, second_vector
):
    section = lax.axis_index("section")
    core = section % 2
    flags = jnp.stack([core, section // 2]).astype(I32)
    first_core = core == 0
    first_layer = section < 2

    away = jnp.where(first_layer, cotangent, block_input)
    got = lax.ppermute(away, "section", [(0, 2), (1, 3), (2, 0), (3, 1)])
    own = section_weight[0]
    oth = core_swap(own)
    vown = jnp.concatenate([norm_gain[0], norm_bias[0], first_vector[0], second_vector[0]])[None]
    voth = core_swap(vown)
    keep, send = split_rows(flags, block_input, cotangent, got)
    angles = positions(flags, grid_sizes, vown, voth)
    cosf, sinf, pos, segr = angles

    field, x_two = first_pass(
        flags, keep, core_swap(send), vown, voth, cosf, sinf, pos, segr, own, oth
    )
    x_got = lax.ppermute(x_two, "section", [(0, 2), (1, 3)])
    c_two, x_mid, qkv, pt, rec, ml, mlt, n_a, n_m, act_mine, act_send, dg = second_pass(
        flags, field, x_got, vown, voth, cosf, sinf, pos, segr, own, oth
    )
    c_got = lax.ppermute(c_two, "section", [(2, 0), (3, 1)])
    x_four, nt_m, nt_a = late_pass(flags, x_mid, n_m, n_a, act_mine, act_send, vown, voth, own, oth)
    x_out = jnp.where(first_layer, x_two, x_four)

    c_mid, c_mid_mine, c_mid_send, gh_mine, gh_send, ggain_m, gshift_m, gbias_m, gsec_m = mlp_back(
        flags, field, c_got, x_mid, vown, voth, dg, own, oth
    )
    gh_oth = core_swap(gh_send)
    down = gram(
        gram_down_kernel, "gram_down", [SMEM] + [VS] * 6, flags, field, core_swap(field), c_got,
        core_swap(c_got), act_mine, core_swap(act_send),
    )
    up = gram(gram_up_kernel, "gram_up", [VS] * 4, nt_m, core_swap(nt_m), gh_mine, gh_oth)
    c_in, gp_mine, gp_send, ggain_a, gshift_a, gbias_a, gfx, gfy, gsec_a = attn_back(
        flags, field, x_got, after(c_mid, up), vown, voth, pos, rec, cosf, sinf, qkv, pt, ml, own, oth
    )
    attn = gram(
        gram_attn_kernel, "gram_attn", [VS] * 8, nt_a, core_swap(nt_a), gp_mine, core_swap(gp_send),
        mlt, core_swap(mlt), c_mid_mine, core_swap(c_mid_send),
    )
    weight_grad = summed_weight_grad(
        flags, [(down, 0, 2 * D), (up, 0, D)], [(up, D, D), (attn, 0, 2 * D)]
    )

    def fold(v):
        pairs = v.reshape(HEADS, 2, HEAD_DIM // 2)
        return (pairs[:, 0] - pairs[:, 1]).reshape(1, -1)

    vg_a = jnp.concatenate([ggain_a, gshift_a, gbias_a, fold(gfx), fold(gfy), gsec_a], axis=1)
    vg_m = jnp.concatenate([ggain_m, gshift_m, gbias_m, gsec_m], axis=1)
    vg = jnp.where(first_core, vg_a, vg_m) + core_swap(jnp.where(first_core, vg_m, vg_a))
    vg = summed_vector(vg)

    def rows_of(attn_row, mlp_row):
        got = core_swap(jnp.where(first_core, mlp_row, attn_row))
        kept = jnp.where(first_core, attn_row, mlp_row)
        above, below = jnp.where(first_core, kept, got), jnp.where(first_core, got, kept)
        return jnp.concatenate([above, below], axis=0)[None]

    return (
        rows_of(x_mid, x_out),
        rows_of(c_in, c_mid),
        weight_grad[None],
        vg[:, GAIN],
        vg[:, SHIFT],
        vg[:, FIRST:SECOND],
        vg[:, SECOND:],
    )


def solution(mesh):
    in_specs = (
        P("dp", "section"),
        P("dp", "section"),
        P("dp", None, None),
        P("section", None, None),
        P("section", None),
        P("section", None),
        P("section", None),
        P("section", None),
    )
    out_specs = (
        P("section", "dp", None),
        P("section", "dp", None),
        P("section", None, None),
        P("section", None),
        P("section", None),
        P("section", None),
        P("section", None),
    )
    return jax.shard_map(body, mesh=mesh, in_specs=in_specs, out_specs=out_specs, check_vma=False)
```

```python
import jax
import jax.numpy as jnp
from jax import lax
from jax.experimental import pallas as pl
from jax.experimental.pallas import tpu as pltpu
from jax.sharding import PartitionSpec as P

D = 768
HEADS = 12
HEAD_DIM = 64
FF = 3072
L = 384
HALF = D // 2
F32 = jnp.float32
BF = jnp.bfloat16
I32 = jnp.int32
NT = (((1,), (1,)), ((), ()))
TN = (((0,), (0,)), ((), ()))
VM = pltpu.VMEM
DMA = pltpu.SemaphoreType.DMA
MIB = 1024 * 1024
LN2 = 0.6931471805599453
GAIN, SHIFT = slice(0, D), slice(D, 2 * D)
FIRST, SECOND = 2 * D, 2 * D + FF
VECTOR = 3 * D + FF


def dot(a, b):
    return jnp.dot(a, b, preferred_element_type=F32)


def dot_nt(a, b):
    return lax.dot_general(a, b, NT, preferred_element_type=F32)


def dot_tn(a, b):
    return lax.dot_general(a, b, TN, preferred_element_type=F32)


def norm_parts(x):
    center = x - jnp.mean(x, axis=-1, keepdims=True)
    inv = lax.rsqrt(jnp.mean(center * center, axis=-1, keepdims=True) + 1e-06)
    return center * inv, inv


def swap_halves(a):
    lane = lax.broadcasted_iota(I32, (1, 128), 1)
    first = (lane % HEAD_DIM) < HEAD_DIM // 2
    out = []
    for i in range(a.shape[1] // 128):
        s = a[:, 128 * i : 128 * (i + 1)]
        out.append(jnp.where(first, pltpu.roll(s, 96, 1), pltpu.roll(s, 32, 1)))
    return jnp.concatenate(out, axis=1) if len(out) > 1 else out[0]


def lanes(start, size):
    if isinstance(start, int):
        return slice(start, start + size)
    return pl.ds(pl.multiple_of(start, 128), size)


def rows_at(start, size):
    if isinstance(start, int):
        return slice(start, start + size)
    return pl.ds(pl.multiple_of(start, size), size)


def cols(start, size):
    return (slice(None), pl.ds(start, size))


def pick(flag, want, own, oth, src, dst, sem):
    @pl.when(flag == want)
    def _():
        pltpu.make_async_copy(own.at[src], dst, sem).start()

    @pl.when(flag != want)
    def _():
        pltpu.make_async_copy(oth.at[src], dst, sem).start()


def load(src, dst, sem):
    pltpu.make_async_copy(src, dst, sem).start()


def arrived(src, dst, sem):
    pltpu.make_async_copy(src, dst, sem).wait()


def load_attn(core, own, oth, wa, sems, i):
    pick(core, 0, own, oth, cols(D * i, D), wa.at[i], sems.at[i])


def wait_attn(own, wa, sems, i):
    arrived(own.at[cols(D * i, D)], wa.at[i], sems.at[i])


def hidden_start(core, j):
    return pl.multiple_of(FF // 2 * ((core + j // 2) % 2) + D * (j % 2), 128)


def load_mlp(core, own, oth, w1, wd, sems, j):
    pick(core, 1, own, oth, (slice(None), pl.ds(hidden_start(core, j), D)), w1.at[j], sems.at[j])
    load((own if j < 2 else oth).at[cols(FF + D * (j % 2), D)], wd.at[j], sems.at[4 + j])


class Forward:
    def __init__(self, core, own, oth, wa, w1, wd, cos_in, sin_in, cosf, sinf, sems, angle_sems):
        self.attn = core, own, oth, wa, sems
        self.mlp = core, own, oth, w1, wd, sems.at[pl.ds(4, 8)]
        self.angles = cos_in, sin_in, cosf, sinf, angle_sems
        self.own, self.wa, self.sems = own, wa, sems
        load_attn(*self.attn, 0)
        load_angles(*self.angles)
        load_attn(*self.attn, 1)

    def wait(self, what):
        if what == "angles":
            wait_angles(*self.angles)
            return
        wait_attn(self.own, self.wa, self.sems, what)
        if what < 2:
            load_attn(*self.attn, what + 2)
        elif what == 2:
            for j in range(4):
                load_mlp(*self.mlp, j)

    def wait_mlp(self):
        core, own, oth, w1, wd, sems = self.mlp
        for j in range(4):
            wait_mlp(own, w1, wd, sems, j)


def wait_mlp(own, w1, wd, sems, j):
    if w1 is not None:
        arrived(own.at[cols(0, D)], w1.at[j], sems.at[j])
    arrived(own.at[cols(0, D)], wd.at[j], sems.at[4 + j])


def vectors(core, own, oth):
    a, b = own[...], oth[...]
    return jnp.where(core == 0, a, b), jnp.where(core == 0, b, a)


def attention(x, vec, wa, wait, cosf, sinf, segc, segr, qkv, pt, rec, ml, mlt, vt, n_ref):
    xh, inv = norm_parts(x)
    n = (xh * vec[:, GAIN] + vec[:, SHIFT]).astype(BF)
    n_ref[...] = n
    for i in range(3):
        wait(i)
        part = dot(n, wa[i]) + vec[:, FIRST + D * i : FIRST + D * (i + 1)]
        if i == 0:
            wait("angles")
        if i < 2:
            part = part * cosf[...] + swap_halves(part) * sinf[...]
        if i == 0:
            part = part * (HEAD_DIM**-0.5 / LN2)
        qkv[:, D * i : D * (i + 1)] = part.astype(BF)
    vt[...] = qkv[:, 2 * D : 3 * D].T
    same = segc == segr
    lane = lax.broadcasted_iota(I32, (1, 128), 1)

    def score(h):
        p = 128 * (h // 2)
        keys = jnp.where((lane // HEAD_DIM) == h % 2, qkv[:, D + p : D + p + 128], BF(0))
        return dot_nt(keys, qkv[:, p : p + 128])

    ahead = score(0)
    for h in range(HEADS):
        st = ahead
        if h + 1 < HEADS:
            ahead = score(h + 1)
        st = jnp.where(same, st, -1e30)
        e = jnp.exp2(st - jnp.max(st, axis=0, keepdims=True))
        r = 1.0 / jnp.sum(e, axis=0, keepdims=True)
        rec[h : h + 1, :] = r
        e = e.astype(BF)
        pt[h] = e
        here = slice(HEAD_DIM * h, HEAD_DIM * (h + 1))
        mlt[here, :] = (dot(vt[here, :], e) * r).astype(BF)
    ml[...] = mlt[...].T
    wait(3)
    out = x + dot(ml[...], wa[3]) + vec[:, SECOND : SECOND + D]
    return out.astype(BF), xh, inv


C0 = 0.7978845608028654
C1 = 0.044715


def gelu(h):
    h2 = h * h
    t = jnp.tanh(C0 * (h + C1 * h * h2))
    half = 0.5 * (1.0 + t)
    return h * half, half + (0.5 * C0) * h * (1.0 - t * t) * (1.0 + (3.0 * C1) * h2)


def norm_back(gn, xh, inv, gain, c):
    u = gn * gain
    gx = inv * (
        u - jnp.mean(u, axis=-1, keepdims=True) - xh * jnp.mean(u * xh, axis=-1, keepdims=True)
    )
    return (c.astype(F32) + gx).astype(BF)


def head_select():
    head = lax.broadcasted_iota(I32, (16, D), 0)
    lane = lax.broadcasted_iota(I32, (16, D), 1)
    return jnp.where(lane // HEAD_DIM == head, 1.0, 0.0).astype(BF)


def split_two(a):
    hi = a.astype(BF)
    return hi, (a - hi.astype(F32)).astype(BF)


def attention_back(c, wo, cosf, sinf, qkv, pt, rec, ml, kt, gm, gqt, dsum, pair_of, emit):
    kt[...] = qkv[:, D : 2 * D].T
    gm_wide = dot_nt(c, wo[...])
    sel = head_select()
    hi, lo = split_two(gm_wide * ml[...].astype(F32))
    row = lax.broadcasted_iota(I32, (16, L), 0)
    recs = jnp.where(row < HEADS, rec[...], 0.0)
    dsum[...] = (dot_nt(sel, hi) + dot_nt(sel, lo)) * recs
    hi, lo = split_two(recs)
    gm[...] = (gm_wide * (dot_tn(hi, sel) + dot_tn(lo, sel))).astype(BF)
    lane = lax.broadcasted_iota(I32, (1, 128), 1)

    def spot(h):
        return lanes(128 * pair_of(h // 2), 128), (lane // HEAD_DIM) == h % 2

    def from_values(h):
        sl, here = spot(h)
        values = qkv[:, lanes(2 * D + 128 * pair_of(h // 2), 128)]
        return dot_nt(jnp.where(here, values, BF(0)), gm[:, sl])

    ahead = from_values(0)
    for h in range(HEADS):
        gpt = ahead
        if h + 1 < HEADS:
            ahead = from_values(h + 1)
        sl, here = spot(h)
        head = 2 * pair_of(h // 2) + h % 2
        e = pt[head]
        gvh = dot(e, jnp.where(here, gm[:, sl], BF(0)))
        gst = (e.astype(F32) * (gpt - dsum[rows_at(head, 1), :])).astype(BF)
        gkh = dot(gst, jnp.where(here, qkv[:, sl], BF(0)))
        kth = kt[rows_at(HEAD_DIM * head, HEAD_DIM), :]
        gqt[h // 2 % 2, HEAD_DIM * (h % 2) : HEAD_DIM * (h % 2 + 1), :] = dot(kth, gst)
        gv = gvh if h % 2 == 0 else gv + gvh
        gk = gkh if h % 2 == 0 else gk + gkh
        if h % 2 == 1:
            gq = gqt[h // 2 % 2].T * (HEAD_DIM**-0.5)
            gk = gk * LN2
            cs, sn = cosf[:, sl], sinf[:, sl]
            sq, sk = swap_halves(gq), swap_halves(gk)
            emit(
                h // 2, sl, sq, sk,
                ((gq * cs - sq * sn).astype(BF), (gk * cs - sk * sn).astype(BF), gv.astype(BF)),
            )


def positions_kernel(flags, grid, vown, voth, cosf, sinf, pos, segr):
    core = flags[0]
    vec = vectors(core, vown, voth)[0]
    h0, w0, h1, w1 = (grid[core, k // 2, k % 2] for k in range(4))
    e1 = h0 * w0
    e2 = e1 + h1 * w1

    def place(t):
        segment = (t >= e1).astype(I32) + (t >= e2).astype(I32)
        width = jnp.where(segment == 0, w0, w1).astype(F32)
        inside = (t - jnp.where(segment == 0, 0, e1)).astype(F32)
        row = jnp.floor((inside + 0.5) / width)
        column = inside - row * width
        return segment, jnp.where(segment < 2, row, 0.0), jnp.where(segment < 2, column, 0.0)

    segment, row, column = place(lax.broadcasted_iota(I32, (L, 128), 0))
    lane = lax.broadcasted_iota(I32, (L, 128), 1)
    pos[...] = jnp.where(lane == 0, column, jnp.where(lane == 1, row, segment.astype(F32)))
    t = lax.broadcasted_iota(I32, (8, L), 1)
    segr[...] = (t >= e1).astype(F32) + (t >= e2).astype(F32)

    def by_lane(start):
        parts = []
        for h in range(HEADS):
            f = vec[:, start + 32 * h : start + 32 * (h + 1)]
            parts += [f, f]
        return jnp.concatenate(parts, axis=1)

    number = lax.broadcasted_iota(I32, (16, D), 0).astype(F32)

    def look_up(which, table):
        hi, rest = split_two(table)
        mid, low = split_two(table - hi.astype(F32))
        tables = jnp.concatenate([hi, mid, low], axis=0)
        hit = (lax.broadcasted_iota(I32, (L, 48), 1) % 16).astype(F32) == which[:, :48]
        return dot(jnp.where(hit, 1.0, 0.0).astype(BF), tables)

    ax = number * by_lane(FIRST + 3 * D)
    ay = number * by_lane(FIRST + 3 * D + HALF)
    cx, sx = look_up(column, jnp.cos(ax)), look_up(column, jnp.sin(ax))
    cy, sy = look_up(row, jnp.cos(ay)), look_up(row, jnp.sin(ay))
    cosf[...] = cx * cy - sx * sy
    lane = lax.broadcasted_iota(I32, (1, D), 1)
    sign = jnp.where(lane % HEAD_DIM < HEAD_DIM // 2, -1.0, 1.0)
    sinf[...] = (sx * cy + cx * sy) * sign


def prepare_kernel(
    flags, x, cot, gain, shift, first, second, keep, send, away, across, vec
):
    core, layer = flags[0], flags[1]
    for at, (mine, other) in enumerate(((x, cot), (cot, x))):

        @pl.when(layer == at)
        def _(mine=mine, other=other):
            keep[...] = mine[:, lanes(L * core, L)]
            send[...] = mine[:, lanes(L * (1 - core), L)]
            away[...] = other[:, lanes(L * core, L)]
            across[...] = other[:, lanes(L * (1 - core), L)]

    vec[:, GAIN] = gain[...]
    vec[:, SHIFT] = shift[...]
    vec[:, FIRST:SECOND] = first[...]
    vec[:, SECOND:] = second[...]


def load_angles(cos_in, sin_in, cosf, sinf, sems):
    load(cos_in, cosf, sems.at[0])
    load(sin_in, sinf, sems.at[1])


def wait_angles(cos_in, sin_in, cosf, sinf, sems):
    arrived(cos_in, cosf, sems.at[0])
    arrived(sin_in, sinf, sems.at[1])


def first_kernel(
    flags, keep, got, away, across, vown, voth, pos, segr, cos_in, sin_in, own, oth,
    out, field_out, wa, w1, wd, cosf, sinf, field, turned, qkv, pt, rec, ml, mlt, vt, n_ref, sems, angle_sems,
):
    core, layer = flags[0], flags[1]
    w = keep.shape[0]
    for k in range(2):
        for at in range(2):

            @pl.when((core == k) & (layer == at))
            def _(k=k, at=at):
                parts = {(at, k): keep, (at, 1 - k): got, (1 - at, k): away, (1 - at, 1 - k): across}
                for s in range(4):
                    turned[w * s : w * (s + 1), :] = parts[s // 2, s % 2][...]

    field[...] = turned[...].T
    keeping = pltpu.make_async_copy(field, field_out, sems.at[12])
    keeping.start()
    @pl.when(layer == 0)
    def _():
        loads = Forward(core, own, oth, wa, w1, wd, cos_in, sin_in, cosf, sinf, sems, angle_sems)
        va, vm = vectors(core, vown, voth)
        x_mid, _, _ = attention(
            field[...].astype(F32), va, wa, loads.wait, cosf, sinf, pos[:, 2:3], segr[0:1, :],
            qkv, pt, rec, ml, mlt, vt, n_ref,
        )
        x = x_mid.astype(F32)
        xh, _ = norm_parts(x)
        n = (xh * vm[:, GAIN] + vm[:, SHIFT]).astype(BF)
        loads.wait_mlp()
        acc = x + vm[:, SECOND : SECOND + D]
        first = hidden_bias(core, vm)
        ahead = dot(n, w1[0])
        for j in range(4):
            h = ahead + first[:, D * j : D * (j + 1)]
            if j < 3:
                ahead = dot(n, w1[j + 1])
            acc = acc + dot_nt(gelu(h)[0].astype(BF), wd[j])
        out[...] = acc.astype(BF)

    keeping.wait()


def hidden_bias(core, vm):
    a, b = vm[:, FIRST : FIRST + FF // 2], vm[:, FIRST + FF // 2 : SECOND]
    return jnp.concatenate([jnp.where(core == 0, a, b), jnp.where(core == 0, b, a)], axis=1)


def second_kernel(
    flags, field, got, vown, voth, pos, segr, cos_in, sin_in, own, oth,
    cx, xi_out, xm_out, qkv_out, pt_out, rec_out, ml_out, actm_out, acts_out, dg_out,
    main_out, tail_out, main_send, tail_send,
    wa, w1, wd, cosf, sinf, xi, xm, qkv, pt, rec, ml, na, nm, actm, acts, dg,
    mlt, vt, xha, xhm, kt, gm, gqt, dsum, gp, sems, angle_sems, outs,
):
    core, layer = flags[0], flags[1]
    loads = Forward(core, own, oth, wa, w1, wd, cos_in, sin_in, cosf, sinf, sems, angle_sems)
    va, vm = vectors(core, vown, voth)
    sent = []

    def send(src, dst):
        copy = pltpu.make_async_copy(src, dst, outs.at[len(sent)])
        copy.start()
        sent.append(copy)

    x = jnp.where(layer == 0, field[...].astype(F32), got[...].astype(F32))
    xi[...] = x.astype(BF)
    send(xi, xi_out)
    x_mid, xh, inv_a = attention(
        x, va, wa, loads.wait, cosf, sinf, pos[:, 2:3], segr[0:1, :], qkv, pt, rec, ml, mlt, vt, na
    )
    xha[...] = xh
    xm[...] = x_mid
    for src, dst in ((xm, xm_out), (qkv, qkv_out), (pt, pt_out), (rec, rec_out), (ml, ml_out)):
        send(src, dst)
    xh, inv_m = norm_parts(x_mid.astype(F32))
    xhm[...] = xh
    n = (xh * vm[:, GAIN] + vm[:, SHIFT]).astype(BF)
    nm[...] = n
    for when, sources in ((core == 0, (na, ml, nm, nm)), (core != 0, (nm, nm, na, ml))):

        @pl.when(when)
        def _(sources=sources):
            for k, (src, dst) in enumerate(zip(sources, (main_out, tail_out, main_send, tail_send))):
                load(src, dst, outs.at[9 + k])

    loads.wait_mlp()
    first = hidden_bias(core, vm)
    c = field[...]

    def forward(j):
        return dot(n, w1[j])

    def chunk(j, h):
        act, slope = gelu(h + first[:, D * j : D * (j + 1)])
        (actm, acts)[j // 2][:, D * (j % 2) : D * (j % 2 + 1)] = act.astype(BF)
        slope = slope.astype(BF)
        dg[:, D * j : D * (j + 1)] = slope
        return slope

    def leave():
        for k, (src, dst) in enumerate(((actm, actm_out), (acts, acts_out), (dg, dg_out))):
            load(src, dst, outs.at[6 + k])

    @pl.when(layer == 0)
    def _():
        ahead = forward(0)
        for j in range(4):
            h = ahead
            if j < 3:
                ahead = forward(j + 1)
            chunk(j, h)
        leave()

    @pl.when(layer != 0)
    def _():
        ahead = forward(0), dot(c, wd[0])
        gn = None
        for j in range(4):
            h, ga = ahead
            if j < 3:
                ahead = forward(j + 1), dot(c, wd[j + 1])
            slope = chunk(j, h)
            part = dot_nt((ga * slope.astype(F32)).astype(BF), w1[j])
            gn = part if gn is None else gn + part
        leave()
        c_mid = norm_back(gn, xhm[...], inv_m, vm[:, GAIN], c)

        def emit(p, sl, sq, sk, grads):
            for i in range(3):
                gp[:, D * i + 128 * p : D * i + 128 * (p + 1)] = grads[i]

        attention_back(
            c_mid, wa.at[3], cosf, sinf, qkv, pt, rec, ml, kt, gm, gqt, dsum, lambda p: p, emit
        )
        gn = None
        for i in range(3):
            part = dot_nt(gp[:, D * i : D * (i + 1)], wa[i])
            gn = part if gn is None else gn + part
        cx[...] = norm_back(gn, xha[...], inv_a, va[:, GAIN], c_mid)

    for copy in sent:
        copy.wait()
    for k, (src, dst) in enumerate(
        ((actm, actm_out), (acts, acts_out), (dg, dg_out), (nm, main_out), (nm, tail_out), (nm, main_send),
         (nm, tail_send))
    ):
        arrived(src, dst, outs.at[6 + k])


def late_kernel(flags, xm, x_two, actm, acts, vown, voth, own, oth, keep, send, wd, sems):
    core, layer = flags[0], flags[1]
    for j in range(4):
        load((own if j < 2 else oth).at[cols(FF + D * (j % 2), D)], wd.at[j], sems.at[4 + j])
    vm = vectors(core, vown, voth)[1]
    mid = xm[...].astype(F32)
    acc = mid + vm[:, SECOND : SECOND + D]
    for j in range(4):
        wait_mlp(own, None, wd, sems, j)
        acc = acc + dot_nt((actm, acts)[j // 2][:, D * (j % 2) : D * (j % 2 + 1)], wd[j])
    acc = jnp.where(layer == 0, x_two[...].astype(F32), acc)
    keep[...] = jnp.where(core == 0, mid, acc).astype(BF)
    send[...] = jnp.where(core == 0, acc, mid).astype(BF)


def both_rows_kernel(flags, keep, got, out):
    core = flags[0]
    out[rows_at(L * core, L), :] = keep[...]
    out[rows_at(L * (1 - core), L), :] = got[...]


def norm_stats(gn, x, vec):
    xh, inv = norm_parts(x)
    vec[:, GAIN] = jnp.sum(gn * xh, axis=0, keepdims=True)
    vec[:, SHIFT] = jnp.sum(gn, axis=0, keepdims=True)
    return xh, inv


def back_kernel(
    flags, field, got, vown, voth, pos, xi_in, xm_in, dg_in, qkv_in, pt_in, rec_in, ml_in, cos_in, sin_in,
    own, oth,
    row_keep, row_send, va_grad, vm_grad, c_out, keep_out, send_out,
    wa, w1, wd, cosf, sinf, xi, xm, dg, qkv, pt, rec, ml, gh, gp, c_kept, kt, gm, gqt, dsum,
    sems, angle_sems, ins, outs,
):
    core, layer = flags[0], flags[1]
    mlp_sems = sems.at[pl.ds(4, 8)]
    held = ((xm_in, xm), (ml_in, ml), (rec_in, rec), (qkv_in, qkv), (pt_in, pt), (xi_in, xi))

    def slopes(j):
        sl = (slice(None), pl.ds(D * j, D))
        return dg_in.at[sl], dg.at[sl], ins.at[6 + j]

    def start_chunk(j):
        load_mlp(core, own, oth, w1, wd, mlp_sems, j)
        load(*slopes(j))

    start_chunk(0)
    start_chunk(1)
    va, vm = vectors(core, vown, voth)
    wide = jnp.where(layer == 0, got[...].astype(F32), field[...].astype(F32))
    c = wide.astype(BF)
    c_kept[...] = c
    leaving = [pltpu.make_async_copy(c_kept, c_out, outs.at[0])]
    leaving[0].start()
    vm_grad[:, SECOND:] = jnp.sum(wide, axis=0, keepdims=True)

    def from_output(j):
        wait_mlp(own, w1, wd, mlp_sems, j)
        arrived(*slopes(j))
        if j < 2:
            start_chunk(j + 2)
        elif j == 2:
            load_attn(core, own, oth, wa, sems, 3)
            for k in range(4):
                load(*held[k], ins.at[k])
        else:
            for k in range(4, len(held)):
                load(*held[k], ins.at[k])
            load_angles(cos_in, sin_in, cosf, sinf, angle_sems)
            for i in range(3):
                load_attn(core, own, oth, wa, sems, i)
        return dot(c, wd[j])

    ahead = from_output(0)
    gn = None
    for j in range(4):
        ga = ahead
        if j < 3:
            ahead = from_output(j + 1)
        part = (ga * dg[:, D * j : D * (j + 1)].astype(F32)).astype(BF)
        start = hidden_start(core, j)
        gh[:, pl.ds(start, D)] = part
        vm_grad[:, pl.ds(pl.multiple_of(FIRST + start, 128), D)] = jnp.sum(
            part.astype(F32), axis=0, keepdims=True
        )
        part = dot_nt(part, w1[j])
        gn = part if gn is None else gn + part
    for when, dst in ((core == 0, send_out), (core != 0, keep_out)):

        @pl.when(when)
        def _(dst=dst):
            load(gh, dst, outs.at[1])

    arrived(xm_in, xm, ins.at[0])
    xh, inv = norm_stats(gn, xm[...].astype(F32), vm_grad)
    c = norm_back(gn, xh, inv, vm[:, GAIN], c)
    gp[:, 3 * D :] = c
    va_grad[:, FIRST + 5 * D :] = jnp.sum(c.astype(F32), axis=0, keepdims=True)
    colp, rowp = pos[:, 0:1], pos[:, 1:2]

    def emit(p, sl, sq, sk, grads):
        qr = qkv[:, sl].astype(F32) * (LN2 * HEAD_DIM**0.5)
        th = sq * qr + sk * qkv[:, D + 128 * p : D + 128 * (p + 1)].astype(F32)
        at = FIRST + 3 * D + 128 * p
        va_grad[:, at : at + 128] = jnp.sum(th * colp, axis=0, keepdims=True)
        va_grad[:, at + D : at + D + 128] = jnp.sum(th * rowp, axis=0, keepdims=True)
        for i, g in enumerate(grads):
            gp[:, D * i + 128 * p : D * i + 128 * (p + 1)] = g
            va_grad[:, FIRST + D * i + 128 * p : FIRST + D * i + 128 * (p + 1)] = jnp.sum(
                g.astype(F32), axis=0, keepdims=True
            )

    for k in range(1, len(held)):
        arrived(*held[k], ins.at[k])
    for i in range(4):
        wait_attn(own, wa, sems, i)
    wait_angles(cos_in, sin_in, cosf, sinf, angle_sems)
    attention_back(
        c, wa.at[3], cosf, sinf, qkv, pt, rec, ml, kt, gm, gqt, dsum, lambda p: p, emit
    )
    for when, dst in ((core == 0, keep_out), (core != 0, send_out)):

        @pl.when(when)
        def _(dst=dst):
            load(gp, dst, outs.at[2])

    gn = None
    for i in range(3):
        part = dot_nt(gp[:, D * i : D * (i + 1)], wa[i])
        gn = part if gn is None else gn + part
    xh, inv = norm_stats(gn, xi[...].astype(F32), va_grad)
    cx = norm_back(gn, xh, inv, va[:, GAIN], c).astype(F32)
    wide = c.astype(F32)
    row_keep[...] = jnp.where(core == 0, cx, wide).astype(BF)
    row_send[...] = jnp.where(core == 0, wide, cx).astype(BF)
    leaving[0].wait()
    arrived(gh, send_out, outs.at[1])
    arrived(gp, keep_out, outs.at[2])


def put(stage, value, out, first, sem):
    stage[...] = value.astype(BF)
    copy = pltpu.make_async_copy(stage, out.at[:, pl.ds(first, stage.shape[1])], sem)
    copy.start()
    return copy


def gram_down_kernel(flags, c, c_oth, field_oth, a0, a1, out, c0, c1, left, right, stages, sems):
    load(c, c0, sems.at[0])
    for at, src in enumerate((c_oth, field_oth)):

        @pl.when(flags[1] == at)
        def _(src=src):
            load(src, c1, sems.at[1])

    load(a0, right.at[pl.ds(0, L), :], sems.at[2])
    load(a1, right.at[pl.ds(L, L), :], sems.at[3])
    arrived(c, c0, sems.at[0])
    arrived(c, c1, sems.at[1])
    left[:, :L] = c0[...].T
    left[:, L:] = c1[...].T
    arrived(a0, right.at[pl.ds(0, L), :], sems.at[2])
    arrived(a1, right.at[pl.ds(L, L), :], sems.at[3])
    copies = [
        put(stages.at[k], dot(left[...], right[:, D * k : D * (k + 1)]), out, D * (k + 1), sems.at[4 + k])
        for k in range(2)
    ]
    for copy in copies:
        copy.wait()


def gram_main_kernel(
    flags, main0, main1, tail0, tail1, b0, b1, tail_in, main_out, tail_out,
    m0, m1, t0, t1, left, right, stages, sems,
):
    sides = ((tail0, t0), (tail1, t1), (main0, m0), (main1, m1))

    def chunk(k, row):
        sl = pl.ds(D * k, D)
        return (b0, b1)[row].at[:, sl], right.at[k, pl.ds(L * row, L), :], sems.at[4 + 2 * k + row]

    order = (3, 0, 1, 2)
    for k in range(2):
        load(*sides[k], sems.at[k])
        load(*chunk(3, k))
    for k in range(2, 4):
        load(*sides[k], sems.at[k])
        load(*chunk(0, k - 2))
    copies = []
    for at, k in enumerate(order):
        if at < 2:
            for row in range(2):
                arrived(*sides[2 * at + row], sems.at[2 * at + row])
                load(*chunk(order[at + 2], row))
                left[at, :, L * row : L * (row + 1)] = (t0, t1, m0, m1)[2 * at + row][...].T
        for row in range(2):
            arrived(*chunk(k, row))
        out, first = (tail_out, 0) if k == 3 else (main_out, D * k)
        copies.append(put(stages.at[at], dot(left[min(at, 1)], right[k]), out, first, sems.at[12 + at]))
    for copy in copies:
        copy.wait()


def vector_grads_kernel(flags, va, vm, mine, send):
    def fold(start):
        v = va[:, start : start + D]
        w = HEAD_DIM // 2
        return jnp.concatenate(
            [v[:, 2 * w * h : 2 * w * h + w] - v[:, 2 * w * h + w : 2 * w * (h + 1)] for h in range(HEADS)],
            axis=1,
        )

    def attn(out):
        at = FIRST + 3 * D
        out[:, :at] = va[:, :at]
        out[:, at : at + HALF] = fold(at)
        out[:, at + HALF : SECOND] = fold(at + D)
        out[:, SECOND:] = va[:, at + 2 * D :]

    @pl.when(flags[0] == 0)
    def _():
        attn(mine)
        send[...] = vm[...]

    @pl.when(flags[0] != 0)
    def _():
        mine[...] = vm[...]
        attn(send)


def place_kernel(flags, rows, *refs):
    out, buf, sems = refs[-3:]
    count = sems.shape[0]
    shards = refs[: 2 * count]
    r = shards[0].shape[0]
    copies = []
    for k in range(count):
        there = pl.ds(r * k, r)
        buf[there, : 3 * D] = shards[2 * k][...].astype(F32)
        buf[there, 3 * D :] = shards[2 * k + 1][...].astype(F32)
        copy = pltpu.make_async_copy(
            buf.at[there, :], out.at[pl.ds(pl.multiple_of(rows[k], 8), r), :], sems.at[k]
        )
        copy.start()
        copies.append(copy)
    for copy in copies:
        copy.wait()


SMEM = pl.BlockSpec(memory_space=pltpu.SMEM)
VS = pl.BlockSpec(memory_space=pltpu.VMEM)
HBM = pl.BlockSpec(memory_space=pltpu.HBM)


def sds(shape, dtype=BF):
    return jax.ShapeDtypeStruct(shape, dtype)


def call(kernel, name, in_specs, outs, scratch, flops, nbytes, limit=58, out_specs=None, aliases=None):
    return pl.pallas_call(
        kernel,
        name=name,
        in_specs=in_specs,
        out_specs=[VS] * len(outs) if out_specs is None else out_specs,
        out_shape=outs,
        scratch_shapes=scratch,
        input_output_aliases={} if aliases is None else aliases,
        compiler_params=pltpu.CompilerParams(vmem_limit_bytes=limit * MIB),
        cost_estimate=pl.CostEstimate(flops=flops, bytes_accessed=nbytes, transcendentals=0),
    )


ATTN_W = [VM((4, D, D), BF)]
ANGLES = [VM((L, D), F32), VM((L, D), F32)]
MLP_W = [VM((4, D, D), BF), VM((4, D, D), BF)]
BACK_S = [VM((D, L), BF), VM((L, D), BF), VM((2, 128, L), F32), VM((16, L), F32)]


def in_hbm(a):
    return pltpu.with_memory_space_constraint(a, pltpu.HBM)


def row(width=D):
    return VM((L, width), BF)


def row_out(width=D):
    return pltpu.HBM((L, width), BF)


def prepare(flags, x, cot, *vecs):
    out = VM((x.shape[0], L), BF)
    return call(
        prepare_kernel, "prepare", [SMEM] + [VS] * 6, [out] * 4 + [VM((1, VECTOR), F32)], [], 1000,
        int(1e6), 8,
    )(flags, *(in_hbm(a) for a in (x, cot) + vecs))


def positions(flags, grid, own, oth):
    hbm = pltpu.HBM
    return call(
        positions_kernel, "positions", [SMEM, SMEM, VS, VS],
        [hbm((L, D), F32), hbm((L, D), F32), hbm((L, 128), F32), hbm((8, L), F32)],
        [], int(1e8), int(3e6), 58,
    )(flags, grid, own, oth)


def first_pass(*a):
    return call(
        first_kernel, "first_pass", [SMEM] + [VS] * 8 + [HBM] * 4, [row(), row_out()],
        ATTN_W + MLP_W + ANGLES
        + [row(), VM((D, L), BF), row(3 * D), VM((HEADS, L, L), BF), VM((16, L), F32), row(), VM((D, L), BF),
           VM((D, L), BF), row(), DMA((13,)), DMA((2,))],
        int(8e9), int(20e6), 40, out_specs=[VS, HBM],
    )(*a)


def second_pass(*a):
    saved = [
        row_out(), row_out(), row_out(3 * D), pltpu.HBM((HEADS, L, L), BF), pltpu.HBM((16, L), F32), row_out(),
        row_out(FF // 2), row_out(FF // 2), row_out(FF), row_out(), row_out(), row_out(), row_out(),
    ]
    return call(
        second_kernel, "second_pass", [SMEM] + [VS] * 6 + [HBM] * 4, [row()] + saved,
        ATTN_W + MLP_W + ANGLES
        + [row(), row(), row(3 * D), VM((HEADS, L, L), BF), VM((16, L), F32), row(), row(), row(),
           row(FF // 2), row(FF // 2), row(FF), VM((D, L), BF), VM((D, L), BF), VM((L, D), F32),
           VM((L, D), F32)]
        + BACK_S + [row(3 * D), DMA((12,)), DMA((2,)), DMA((13,))],
        int(18e9), int(35e6), 48, out_specs=[VS] + [HBM] * len(saved),
    )(*a)


def late_pass(*a):
    return call(
        late_kernel, "late_pass", [SMEM] + [VS] * 6 + [HBM] * 2, [sds((L, D))] * 2,
        [VM((4, D, D), BF), DMA((8,))], int(2e9), int(10e6), 16,
    )(*a)


def back_pass(*a):
    return call(
        back_kernel, "back_pass", [SMEM] + [VS] * 5 + [HBM] * 11,
        [sds((L, D)), sds((L, D)), VM((1, FIRST + 6 * D), F32), VM((1, VECTOR), F32), row_out(),
         row_out(FF), row_out(FF)],
        ATTN_W + MLP_W + ANGLES
        + [row(), row(), row(FF), row(3 * D), VM((HEADS, L, L), BF), VM((16, L), F32), row(), row(FF),
           row(FF), row()]
        + BACK_S + [DMA((12,)), DMA((2,)), DMA((10,)), DMA((3,))],
        int(10e9), int(30e6), 52, out_specs=[VS] * 4 + [HBM] * 3,
    )(*a)


def gram_down(flags, *a):
    return call(
        gram_down_kernel, "gram_down", [SMEM] + [HBM] * 5, [pltpu.HBM((D, 3 * D), BF)],
        [row(), row(), VM((D, 2 * L), BF), VM((2 * L, 2 * D), BF), VM((2, D, D), BF), DMA((6,))],
        int(2e9), int(8e6), 24, out_specs=[HBM],
    )(flags, *(in_hbm(x) for x in a))[0]


def gram_main(flags, *a):
    return call(
        gram_main_kernel, "gram_main", [SMEM] + [HBM] * 7, [pltpu.HBM((D, 3 * D), BF)] * 2,
        [row()] * 4 + [VM((2, D, 2 * L), BF), VM((4, 2 * L, D), BF), VM((4, D, D), BF), DMA((16,))],
        int(4e9), int(12e6), 32, out_specs=[HBM, HBM], aliases={7: 1},
    )(flags, *(in_hbm(x) for x in a))


def both_rows(flags, keep, got):
    return call(
        both_rows_kernel, "both_rows", [SMEM, VS, VS], [sds((2 * L, D))], [], 1000, int(2e6), 6
    )(flags, keep, got)[0]


def mlp_back(flags, *a):
    return call(
        mlp_back_kernel, "mlp_back", [SMEM] + [VS] * 6 + [HBM] * 2,
        [row(), row(FF), row(), row(), VM((1, VECTOR), F32)],
        MLP_W + [DMA((8,))], int(4e9), int(14e6), 22,
    )(*resident(flags, 6, a))


def attn_back(flags, *a):
    return call(
        attn_back_kernel, "attn_back", [SMEM] + [VS] * 13 + [HBM] * 2,
        [row(), row(), row(3 * D), row(3 * D), VM((1, FIRST + 6 * D), F32)],
        ATTN_W + BACK_S + [row(3 * D), DMA((4,))],
        int(6e9), int(14e6), 20,
    )(*resident(flags, 13, a))


def vector_grads(flags, va, vm):
    out = VM((1, VECTOR), F32)
    return call(vector_grads_kernel, "vector_grads", [SMEM, VS, VS], [out, out], [], 1000, 100000, 4)(
        flags, va, vm
    )


def place(flags, rows, shards, total):
    r, count = shards[0].shape[0], len(shards) // 2
    into = [] if total is None else [total]
    return call(
        place_kernel, "place", [SMEM, SMEM] + [VS] * len(shards) + [HBM] * len(into),
        [pltpu.HBM((D, 6 * D), F32)],
        [VM((r * count, 6 * D), F32), DMA((count,))], 1000, int(2e6), 24,
        out_specs=[HBM], aliases={len(shards) + 2: 0} if into else {},
    )(flags, rows, *shards, *into)[0]


def core_swap(a):
    return lax.ppermute(a, "section", [(0, 1), (1, 0), (2, 3), (3, 2)])


def after(value, first):
    return lax.optimization_barrier((value, first))[0]


class Chain:
    def __init__(self, array):
        self.array = array
        self.n = n = lax.axis_size("dp")
        self.r = array.shape[0] // (2 * n)
        i = lax.axis_index("dp")
        self.where = jnp.where(i % 2 == 0, i // 2, n - 1 - i // 2)
        order = list(range(0, n, 2)) + list(range(n - 1, 0, -2))
        self.pairs = [[(order[k], order[(k + d) % n]) for k in range(n)] for d in (1, -1)]
        self.t = 0
        self.shards = []
        self.cur = self.own(0)

    def rows(self, t):
        return [
            base + ((self.where - d * t) % self.n) * self.r
            for base, d in ((0, 1), (self.array.shape[0] // 2, -1))
        ]

    def own(self, t):
        return [lax.dynamic_slice_in_dim(self.array, at, self.r, 0) for at in self.rows(t)]

    def step(self, token):
        got = [lax.ppermute(c, "dp", p) for c, p in zip(self.cur, self.pairs)]
        got = after(got, token)
        if self.t < self.n - 1:
            self.cur = [g + o for g, o in zip(got, self.own(self.t + 1))]
            if self.t == self.n - 2:
                self.shards.append((self.rows(-1), self.cur))
        else:
            self.cur = got
            self.shards.append((self.rows(self.t - self.n + 1), got))
        self.t += 1
        return self.cur


def small_ring():
    return lax.axis_size("dp") <= 16


def summed_weight_grad(flags, main, tail, token, beside):
    if not small_ring():
        for f in beside:
            token = f(token)
        return place(flags, jnp.zeros((1,), I32), lax.psum([main, tail], "dp"), None)
    n = main.n
    total = None
    beside = list(beside)
    while main.t < 2 * n - 2:
        token = tail.step(token)
        if total is not None:
            token = (token, total)
        token = main.step(token)
        if main.shards:
            (rows, a), (_, b) = main.shards[-1], tail.shards[len(main.shards) - 1]
            total = place(flags, jnp.stack(rows).astype(I32), [a[0], b[0], a[1], b[1]], total)
            if beside and len(main.shards) > 1:
                token = (token, beside.pop(0)(token))
    for f in beside:
        token = f(token)
    return total


class VectorSum:
    def __init__(self, mine, send):
        self.value, self.coming = mine, core_swap(send)
        n = lax.axis_size("dp")
        self.hops = [1 << k for k in range(n.bit_length() - 1)]
        self.whole = n & (n - 1) == 0

    def step(self, token):
        self.value = self.value + after(self.coming, token)
        if self.whole and self.hops:
            hop = self.hops.pop(0)
            self.coming = lax.ppermute(
                self.value, "dp", [(i, i ^ hop) for i in range(lax.axis_size("dp"))]
            )
        else:
            self.coming = None
        return self.value

    def steps(self):
        return [self.step] * (len(self.hops) + 1 if self.whole else 1)

    def total(self):
        return self.value if self.whole else lax.psum(self.value, "dp")


def body(
    block_input, cotangent, grid_sizes, section_weight, norm_gain, norm_bias, first_vector, second_vector
):
    section = lax.axis_index("section")
    core = section % 2
    flags = jnp.stack([core, section // 2]).astype(I32)
    first_layer = section < 2

    keep, send, away, across, vown = prepare(
        flags, block_input.T, cotangent.T, norm_gain, norm_bias, first_vector, second_vector
    )
    got, voth = core_swap(send), core_swap(vown)
    away = lax.ppermute(away, "section", [(0, 2), (1, 3), (2, 0), (3, 1)])
    across = lax.ppermute(across, "section", [(0, 3), (1, 2), (2, 1), (3, 0)])
    own = in_hbm(section_weight[0])
    oth = in_hbm(core_swap(after(section_weight[0], (got, voth))))
    cosf, sinf, pos, segr = (in_hbm(a) for a in positions(flags, grid_sizes, vown, voth))

    x_two, field = first_pass(
        flags, keep, got, away, across, vown, voth, pos, segr, cosf, sinf, own, oth
    )
    field = in_hbm(field)
    x_got = lax.ppermute(x_two, "section", [(0, 2), (1, 3)])
    (
        c_two, x_in, x_mid, qkv, pt, rec, ml, act_mine, act_send, dg, main_left, tail_left, main_send,
        tail_send,
    ) = (in_hbm(a) if k else a for k, a in enumerate(
        second_pass(flags, field, x_got, vown, voth, pos, segr, cosf, sinf, own, oth)
    ))
    c_got = lax.ppermute(c_two, "section", [(2, 0), (3, 1)])
    act_oth, main_oth, tail_oth, field_oth = (
        core_swap(a) for a in (act_send, main_send, tail_send, field)
    )
    x_keep, x_send = late_pass(
        flags, after(x_mid, (act_oth, main_oth, tail_oth, field_oth)), x_two, act_mine, act_send, vown, voth,
        own, oth,
    )
    c_got = after(c_got, x_keep)
    activations = both_rows(flags, x_keep, core_swap(x_send))

    c_keep, c_send, va, vm, c_out, right, right_send = back_pass(
        flags, field, c_got, vown, voth, pos, x_in, x_mid, dg, qkv, pt, rec, ml, cosf, sinf, own, oth
    )
    tail = gram_down(
        flags, c_out, core_swap(c_got), field_oth, act_mine, act_oth
    )
    main, tail = gram_main(
        flags, main_left, main_oth, tail_left, tail_oth, right, core_swap(right_send), tail
    )
    token = main
    if small_ring():
        main, tail = Chain(main), Chain(tail)
        token = main.cur
    vector = VectorSum(*vector_grads(flags, va, vm))
    rows = {}

    def send_rows(token):
        rows["got"] = core_swap(after(c_send, token))
        return c_send

    def join_rows(token):
        rows["out"] = both_rows(flags, c_keep, after(rows["got"], token))
        return rows["out"]

    weight_grad = summed_weight_grad(flags, main, tail, token, vector.steps() + [send_rows, join_rows])
    vg = vector.total()
    input_grads = rows["out"]
    return (
        activations[None],
        input_grads[None],
        weight_grad[None],
        vg[:, GAIN],
        vg[:, SHIFT],
        vg[:, FIRST:SECOND],
        vg[:, SECOND:],
    )


def solution(mesh):
    in_specs = (
        P("dp", "section"),
        P("dp", "section"),
        P("dp", None, None),
        P("section", None, None),
        P("section", None),
        P("section", None),
        P("section", None),
        P("section", None),
    )
    out_specs = (
        P("section", "dp", None),
        P("section", "dp", None),
        P("section", None, None),
        P("section", None),
        P("section", None),
        P("section", None),
        P("section", None),
    )
    return jax.shard_map(body, mesh=mesh, in_specs=in_specs, out_specs=out_specs, check_vma=False)
```

```python
import jax
import jax.numpy as jnp
from jax import lax
from jax.experimental import pallas as pl
from jax.experimental.pallas import tpu as pltpu
from jax.sharding import PartitionSpec as P

D = 768
HEADS = 12
HEAD_DIM = 64
FF = 3072
L = 384
HALF = D // 2
F32 = jnp.float32
BF = jnp.bfloat16
I32 = jnp.int32
NT = (((1,), (1,)), ((), ()))
TN = (((0,), (0,)), ((), ()))
VM = pltpu.VMEM
DMA = pltpu.SemaphoreType.DMA
MIB = 1024 * 1024
LN2 = 0.6931471805599453
GAIN, SHIFT = slice(0, D), slice(D, 2 * D)
FIRST, SECOND = 2 * D, 2 * D + FF
VECTOR = 3 * D + FF
PACKED = (48, 128)


def dot(a, b):
    return jnp.dot(a, b, preferred_element_type=F32)


def dot_nt(a, b):
    return lax.dot_general(a, b, NT, preferred_element_type=F32)


def dot_tn(a, b):
    return lax.dot_general(a, b, TN, preferred_element_type=F32)


def norm_parts(x):
    center = x - jnp.mean(x, axis=-1, keepdims=True)
    inv = lax.rsqrt(jnp.mean(center * center, axis=-1, keepdims=True) + 1e-06)
    return center * inv, inv


def swap_halves(a):
    lane = lax.broadcasted_iota(I32, (1, 128), 1)
    first = (lane % HEAD_DIM) < HEAD_DIM // 2
    out = []
    for i in range(a.shape[1] // 128):
        s = a[:, 128 * i : 128 * (i + 1)]
        out.append(jnp.where(first, pltpu.roll(s, 96, 1), pltpu.roll(s, 32, 1)))
    return jnp.concatenate(out, axis=1) if len(out) > 1 else out[0]


def lanes(start, size):
    if isinstance(start, int):
        return slice(start, start + size)
    return pl.ds(pl.multiple_of(start, 128), size)


def rows_at(start, size):
    if isinstance(start, int):
        return slice(start, start + size)
    return pl.ds(pl.multiple_of(start, size), size)


def cols(start, size):
    return (slice(None), pl.ds(start, size))


def pick(flag, want, own, oth, src, dst, sem):
    @pl.when(flag == want)
    def _():
        pltpu.make_async_copy(own.at[src], dst, sem).start()

    @pl.when(flag != want)
    def _():
        pltpu.make_async_copy(oth.at[src], dst, sem).start()


def load(src, dst, sem):
    pltpu.make_async_copy(src, dst, sem).start()


def arrived(src, dst, sem):
    pltpu.make_async_copy(src, dst, sem).wait()


def load_attn(core, own, oth, wa, sems, i):
    pick(core, 0, own, oth, cols(D * i, D), wa.at[i], sems.at[i])


def wait_attn(own, wa, sems, i):
    arrived(own.at[cols(D * i, D)], wa.at[i], sems.at[i])


def hidden_start(core, j):
    return pl.multiple_of(FF // 2 * ((core + j // 2) % 2) + D * (j % 2), 128)


def load_mlp(core, own, oth, w1, wd, sems, j):
    pick(core, 1, own, oth, (slice(None), pl.ds(hidden_start(core, j), D)), w1.at[j], sems.at[j])
    load((own if j < 2 else oth).at[cols(FF + D * (j % 2), D)], wd.at[j], sems.at[4 + j])


class Forward:
    def __init__(self, core, own, oth, wa, w1, wd, cos_in, sin_in, cosf, sinf, sems, angle_sems):
        self.attn = core, own, oth, wa, sems
        self.mlp = core, own, oth, w1, wd, sems.at[pl.ds(4, 8)]
        self.angles = cos_in, sin_in, cosf, sinf, angle_sems
        self.own, self.wa, self.sems = own, wa, sems
        load_attn(*self.attn, 0)
        load_angles(*self.angles)
        load_attn(*self.attn, 1)

    def wait(self, what):
        if what == "angles":
            wait_angles(*self.angles)
            return
        wait_attn(self.own, self.wa, self.sems, what)
        if what < 2:
            load_attn(*self.attn, what + 2)
        elif what == 2:
            for j in range(4):
                load_mlp(*self.mlp, j)

    def wait_mlp(self):
        core, own, oth, w1, wd, sems = self.mlp
        for j in range(4):
            wait_mlp(own, w1, wd, sems, j)


def wait_mlp(own, w1, wd, sems, j):
    if w1 is not None:
        arrived(own.at[cols(0, D)], w1.at[j], sems.at[j])
    arrived(own.at[cols(0, D)], wd.at[j], sems.at[4 + j])


def vectors(core, own, oth):
    a, b = own[...], oth[...]
    return jnp.where(core == 0, a, b), jnp.where(core == 0, b, a)


def attention(x, vec, wa, wait, cosf, sinf, segc, segr, qkv, pt, rec, ml, mlt, vt, n_ref):
    xh, inv = norm_parts(x)
    n = (xh * vec[:, GAIN] + vec[:, SHIFT]).astype(BF)
    n_ref[...] = n
    for i in range(3):
        wait(i)
        part = dot(n, wa[i]) + vec[:, FIRST + D * i : FIRST + D * (i + 1)]
        if i == 0:
            wait("angles")
        if i < 2:
            part = part * cosf[...] + swap_halves(part) * sinf[...]
        if i == 0:
            part = part * (HEAD_DIM**-0.5 / LN2)
        qkv[:, D * i : D * (i + 1)] = part.astype(BF)
    vt[...] = qkv[:, 2 * D : 3 * D].T
    same = segc == segr
    lane = lax.broadcasted_iota(I32, (1, 128), 1)

    def score(h):
        p = 128 * (h // 2)
        keys = jnp.where((lane // HEAD_DIM) == h % 2, qkv[:, D + p : D + p + 128], BF(0))
        return dot_nt(keys, qkv[:, p : p + 128])

    ahead = score(0)
    for h in range(HEADS):
        st = ahead
        if h + 1 < HEADS:
            ahead = score(h + 1)
        st = jnp.where(same, st, -1e30)
        e = jnp.exp2(st - jnp.max(st, axis=0, keepdims=True))
        r = 1.0 / jnp.sum(e, axis=0, keepdims=True)
        rec[h : h + 1, :] = r
        e = e.astype(BF)
        pt[h] = e
        here = slice(HEAD_DIM * h, HEAD_DIM * (h + 1))
        mlt[here, :] = (dot(vt[here, :], e) * r).astype(BF)
    ml[...] = mlt[...].T
    wait(3)
    out = x + dot(ml[...], wa[3]) + vec[:, SECOND : SECOND + D]
    return out.astype(BF), xh, inv


C0 = 0.7978845608028654
C1 = 0.044715


def gelu(h):
    h2 = h * h
    t = jnp.tanh(C0 * (h + C1 * h * h2))
    half = 0.5 * (1.0 + t)
    return h * half, half + (0.5 * C0) * h * (1.0 - t * t) * (1.0 + (3.0 * C1) * h2)


def norm_back(gn, xh, inv, gain, c):
    u = gn * gain
    gx = inv * (
        u - jnp.mean(u, axis=-1, keepdims=True) - xh * jnp.mean(u * xh, axis=-1, keepdims=True)
    )
    return (c.astype(F32) + gx).astype(BF)


def head_select():
    head = lax.broadcasted_iota(I32, (16, D), 0)
    lane = lax.broadcasted_iota(I32, (16, D), 1)
    return jnp.where(lane // HEAD_DIM == head, 1.0, 0.0).astype(BF)


def split_two(a):
    hi = a.astype(BF)
    return hi, (a - hi.astype(F32)).astype(BF)


def attention_back(c, wo, cosf, sinf, qkv, pt, rec, ml, kt, gm, gqt, dsum, pair_of, emit):
    kt[...] = qkv[:, D : 2 * D].T
    gm_wide = dot_nt(c, wo[...])
    sel = head_select()
    hi, lo = split_two(gm_wide * ml[...].astype(F32))
    row = lax.broadcasted_iota(I32, (16, L), 0)
    recs = jnp.where(row < HEADS, rec[...], 0.0)
    dsum[...] = (dot_nt(sel, hi) + dot_nt(sel, lo)) * recs
    hi, lo = split_two(recs)
    gm[...] = (gm_wide * (dot_tn(hi, sel) + dot_tn(lo, sel))).astype(BF)
    lane = lax.broadcasted_iota(I32, (1, 128), 1)

    def spot(h):
        return lanes(128 * pair_of(h // 2), 128), (lane // HEAD_DIM) == h % 2

    def from_values(h):
        sl, here = spot(h)
        values = qkv[:, lanes(2 * D + 128 * pair_of(h // 2), 128)]
        return dot_nt(jnp.where(here, values, BF(0)), gm[:, sl])

    ahead = from_values(0)
    for h in range(HEADS):
        gpt = ahead
        if h + 1 < HEADS:
            ahead = from_values(h + 1)
        sl, here = spot(h)
        head = 2 * pair_of(h // 2) + h % 2
        e = pt[head]
        gvh = dot(e, jnp.where(here, gm[:, sl], BF(0)))
        gst = (e.astype(F32) * (gpt - dsum[rows_at(head, 1), :])).astype(BF)
        gkh = dot(gst, jnp.where(here, qkv[:, sl], BF(0)))
        kth = kt[rows_at(HEAD_DIM * head, HEAD_DIM), :]
        gqt[h // 2 % 2, HEAD_DIM * (h % 2) : HEAD_DIM * (h % 2 + 1), :] = dot(kth, gst)
        gv = gvh if h % 2 == 0 else gv + gvh
        gk = gkh if h % 2 == 0 else gk + gkh
        if h % 2 == 1:
            gq = gqt[h // 2 % 2].T * (HEAD_DIM**-0.5)
            gk = gk * LN2
            cs, sn = cosf[:, sl], sinf[:, sl]
            sq, sk = swap_halves(gq), swap_halves(gk)
            emit(
                h // 2, sl, sq, sk,
                ((gq * cs - sq * sn).astype(BF), (gk * cs - sk * sn).astype(BF), gv.astype(BF)),
            )


def positions_kernel(flags, grid, vown, voth, cosf, sinf, pos, segr):
    core = flags[0]
    vec = vectors(core, vown, voth)[0]
    h0, w0, h1, w1 = (grid[core, k // 2, k % 2] for k in range(4))
    e1 = h0 * w0
    e2 = e1 + h1 * w1

    def place(t):
        segment = (t >= e1).astype(I32) + (t >= e2).astype(I32)
        width = jnp.where(segment == 0, w0, w1).astype(F32)
        inside = (t - jnp.where(segment == 0, 0, e1)).astype(F32)
        row = jnp.floor((inside + 0.5) / width)
        column = inside - row * width
        return segment, jnp.where(segment < 2, row, 0.0), jnp.where(segment < 2, column, 0.0)

    segment, row, column = place(lax.broadcasted_iota(I32, (L, 128), 0))
    lane = lax.broadcasted_iota(I32, (L, 128), 1)
    pos[...] = jnp.where(lane == 0, column, jnp.where(lane == 1, row, segment.astype(F32)))
    t = lax.broadcasted_iota(I32, (8, L), 1)
    segr[...] = (t >= e1).astype(F32) + (t >= e2).astype(F32)

    def by_lane(start):
        parts = []
        for h in range(HEADS):
            f = vec[:, start + 32 * h : start + 32 * (h + 1)]
            parts += [f, f]
        return jnp.concatenate(parts, axis=1)

    number = lax.broadcasted_iota(I32, (16, D), 0).astype(F32)

    def look_up(which, table):
        hi, rest = split_two(table)
        mid, low = split_two(table - hi.astype(F32))
        tables = jnp.concatenate([hi, mid, low], axis=0)
        hit = (lax.broadcasted_iota(I32, (L, 48), 1) % 16).astype(F32) == which[:, :48]
        return dot(jnp.where(hit, 1.0, 0.0).astype(BF), tables)

    ax = number * by_lane(FIRST + 3 * D)
    ay = number * by_lane(FIRST + 3 * D + HALF)
    cx, sx = look_up(column, jnp.cos(ax)), look_up(column, jnp.sin(ax))
    cy, sy = look_up(row, jnp.cos(ay)), look_up(row, jnp.sin(ay))
    cosf[...] = cx * cy - sx * sy
    lane = lax.broadcasted_iota(I32, (1, D), 1)
    sign = jnp.where(lane % HEAD_DIM < HEAD_DIM // 2, -1.0, 1.0)
    sinf[...] = (sx * cy + cx * sy) * sign


def prepare_kernel(
    flags, x, cot, gain, shift, first, second, keep, send, away, across, vec
):
    core, layer = flags[0], flags[1]
    for at, (mine, other) in enumerate(((x, cot), (cot, x))):

        @pl.when(layer == at)
        def _(mine=mine, other=other):
            keep[...] = mine[:, lanes(L * core, L)]
            send[...] = mine[:, lanes(L * (1 - core), L)]
            away[...] = other[:, lanes(L * core, L)]
            across[...] = other[:, lanes(L * (1 - core), L)]

    vec[:, GAIN] = gain[...]
    vec[:, SHIFT] = shift[...]
    vec[:, FIRST:SECOND] = first[...]
    vec[:, SECOND:] = second[...]


def load_angles(cos_in, sin_in, cosf, sinf, sems):
    load(cos_in, cosf, sems.at[0])
    load(sin_in, sinf, sems.at[1])


def wait_angles(cos_in, sin_in, cosf, sinf, sems):
    arrived(cos_in, cosf, sems.at[0])
    arrived(sin_in, sinf, sems.at[1])


def first_kernel(
    flags, keep, got, away, across, vown, voth, pos, segr, cos_in, sin_in, own, oth,
    out, field_out, wa, w1, wd, cosf, sinf, field, turned, qkv, pt, rec, ml, mlt, vt, n_ref, sems, angle_sems,
):
    core, layer = flags[0], flags[1]
    w = keep.shape[0]
    for k in range(2):
        for at in range(2):

            @pl.when((core == k) & (layer == at))
            def _(k=k, at=at):
                parts = {(at, k): keep, (at, 1 - k): got, (1 - at, k): away, (1 - at, 1 - k): across}
                for s in range(4):
                    turned[w * s : w * (s + 1), :] = parts[s // 2, s % 2][...]

    field[...] = turned[...].T
    keeping = pltpu.make_async_copy(field, field_out, sems.at[12])
    keeping.start()
    @pl.when(layer == 0)
    def _():
        loads = Forward(core, own, oth, wa, w1, wd, cos_in, sin_in, cosf, sinf, sems, angle_sems)
        va, vm = vectors(core, vown, voth)
        x_mid, _, _ = attention(
            field[...].astype(F32), va, wa, loads.wait, cosf, sinf, pos[:, 2:3], segr[0:1, :],
            qkv, pt, rec, ml, mlt, vt, n_ref,
        )
        x = x_mid.astype(F32)
        xh, _ = norm_parts(x)
        n = (xh * vm[:, GAIN] + vm[:, SHIFT]).astype(BF)
        loads.wait_mlp()
        acc = x + vm[:, SECOND : SECOND + D]
        first = hidden_bias(core, vm)
        ahead = dot(n, w1[0])
        for j in range(4):
            h = ahead + first[:, D * j : D * (j + 1)]
            if j < 3:
                ahead = dot(n, w1[j + 1])
            acc = acc + dot_nt(gelu(h)[0].astype(BF), wd[j])
        out[...] = acc.astype(BF)

    keeping.wait()


def hidden_bias(core, vm):
    a, b = vm[:, FIRST : FIRST + FF // 2], vm[:, FIRST + FF // 2 : SECOND]
    return jnp.concatenate([jnp.where(core == 0, a, b), jnp.where(core == 0, b, a)], axis=1)


def fetch_kernel(flags, cos_in, sin_in, own, oth, cosf, sinf, wa, w1, wd, sems):
    core = flags[0]
    for i in range(4):
        load_attn(core, own, oth, wa, sems, i)
        load_mlp(core, own, oth, w1, wd, sems.at[pl.ds(4, 8)], i)
    load_angles(cos_in, sin_in, cosf, sinf, sems.at[pl.ds(12, 2)])
    for i in range(4):
        wait_attn(own, wa, sems, i)
        wait_mlp(own, w1, wd, sems.at[pl.ds(4, 8)], i)
    wait_angles(cos_in, sin_in, cosf, sinf, sems.at[pl.ds(12, 2)])


def second_kernel(
    flags, field, got, vown, voth, pos, segr, cosf, sinf, wa, w1, wd,
    cx, xi_out, xm_out, qkv_out, pt_out, rec_out, ml_out, actm_out, acts_out, dg_out, main_out, tail_out, bundle,
    xi, xm, qkv, pt, rec, ml, na, nm, actm, acts, dg, mlt, vt, xha, xhm, kt, gm, gqt, dsum, gp, outs,
):
    core, layer = flags[0], flags[1]
    va, vm = vectors(core, vown, voth)
    sent = []

    def send(src, dst):
        copy = pltpu.make_async_copy(src, dst, outs.at[len(sent)])
        copy.start()
        sent.append(copy)

    x = jnp.where(layer == 0, field[...].astype(F32), got[...].astype(F32))
    xi[...] = x.astype(BF)
    send(xi, xi_out)
    x_mid, xh, inv_a = attention(
        x, va, wa, lambda what: None, cosf, sinf, pos[:, 2:3], segr[0:1, :], qkv, pt, rec, ml, mlt, vt, na
    )
    xha[...] = xh
    xm[...] = x_mid
    for src, dst in ((xm, xm_out), (qkv, qkv_out), (pt, pt_out), (rec, rec_out), (ml, ml_out)):
        send(src, dst)
    xh, inv_m = norm_parts(x_mid.astype(F32))
    xhm[...] = xh
    n = (xh * vm[:, GAIN] + vm[:, SHIFT]).astype(BF)
    nm[...] = n
    sides = (
        main_out, tail_out, bundle.at[:, pl.ds(2 * D, D)], bundle.at[:, pl.ds(3 * D, D)],
    )
    load(field, bundle.at[:, pl.ds(4 * D, D)], outs.at[13])
    for when, sources in ((core == 0, (na, ml, nm, nm)), (core != 0, (nm, nm, na, ml))):

        @pl.when(when)
        def _(sources=sources):
            for k, (src, dst) in enumerate(zip(sources, sides)):
                load(src, dst, outs.at[9 + k])

    first = hidden_bias(core, vm)
    c = field[...]

    def forward(j):
        return dot(n, w1[j])

    def chunk(j, h):
        act, slope = gelu(h + first[:, D * j : D * (j + 1)])
        (actm, acts)[j // 2][:, D * (j % 2) : D * (j % 2 + 1)] = act.astype(BF)
        slope = slope.astype(BF)
        dg[:, D * j : D * (j + 1)] = slope
        return slope

    def leave():
        load(acts, bundle.at[:, pl.ds(0, 2 * D)], outs.at[14])
        for k, (src, dst) in enumerate(((actm, actm_out), (acts, acts_out), (dg, dg_out))):
            load(src, dst, outs.at[6 + k])

    @pl.when(layer == 0)
    def _():
        ahead = forward(0)
        for j in range(4):
            h = ahead
            if j < 3:
                ahead = forward(j + 1)
            chunk(j, h)
        leave()

    @pl.when(layer != 0)
    def _():
        ahead = forward(0), dot(c, wd[0])
        gn = None
        for j in range(4):
            h, ga = ahead
            if j < 3:
                ahead = forward(j + 1), dot(c, wd[j + 1])
            slope = chunk(j, h)
            part = dot_nt((ga * slope.astype(F32)).astype(BF), w1[j])
            gn = part if gn is None else gn + part
        leave()
        c_mid = norm_back(gn, xhm[...], inv_m, vm[:, GAIN], c)

        def emit(p, sl, sq, sk, grads):
            for i in range(3):
                gp[:, D * i + 128 * p : D * i + 128 * (p + 1)] = grads[i]

        attention_back(
            c_mid, wa.at[3], cosf, sinf, qkv, pt, rec, ml, kt, gm, gqt, dsum, lambda p: p, emit
        )
        gn = None
        for i in range(3):
            part = dot_nt(gp[:, D * i : D * (i + 1)], wa[i])
            gn = part if gn is None else gn + part
        cx[...] = norm_back(gn, xha[...], inv_a, va[:, GAIN], c_mid)

    for copy in sent:
        copy.wait()
    for k, (src, dst) in enumerate(
        ((actm, actm_out), (acts, acts_out), (dg, dg_out)) + tuple((nm, side) for side in sides)
        + ((field, sides[2]), (acts, bundle.at[:, pl.ds(0, 2 * D)]))
    ):
        arrived(src, dst, outs.at[6 + k])


def late_kernel(
    flags, x_two, vown, voth, xm_in, dg_in, actm_in, acts_in, own, oth,
    keep, send, xm, dg, wa, w1, wd, actm, acts, sems, ins,
):
    core, layer = flags[0], flags[1]
    held = ((xm_in, xm), (actm_in, actm), (acts_in, acts), (dg_in, dg))
    for j in range(4):
        load((own if j < 2 else oth).at[cols(FF + D * (j % 2), D)], wd.at[j], sems.at[8 + j])
    for k, (src, dst) in enumerate(held):
        load(src, dst, ins.at[k])
    for j in range(4):
        pick(core, 1, own, oth, (slice(None), pl.ds(hidden_start(core, j), D)), w1.at[j], sems.at[4 + j])
        load_attn(core, own, oth, wa, sems, j)
    vm = vectors(core, vown, voth)[1]
    for k, (src, dst) in enumerate(held):
        arrived(src, dst, ins.at[k])
    mid = xm[...].astype(F32)
    acc = mid + vm[:, SECOND : SECOND + D]
    for j in range(4):
        arrived(own.at[cols(0, D)], wd.at[j], sems.at[8 + j])
        acc = acc + dot_nt((actm, acts)[j // 2][:, D * (j % 2) : D * (j % 2 + 1)], wd[j])
    acc = jnp.where(layer == 0, x_two[...].astype(F32), acc)
    keep[...] = jnp.where(core == 0, mid, acc).astype(BF)
    send[...] = jnp.where(core == 0, acc, mid).astype(BF)
    for j in range(4):
        arrived(own.at[cols(0, D)], w1.at[j], sems.at[4 + j])
        wait_attn(own, wa, sems, j)


def both_rows_kernel(flags, keep, got, out):
    core = flags[0]
    out[rows_at(L * core, L), :] = keep[...]
    out[rows_at(L * (1 - core), L), :] = got[...]


def norm_stats(gn, x, vec):
    xh, inv = norm_parts(x)
    vec[:, GAIN] = jnp.sum(gn * xh, axis=0, keepdims=True)
    vec[:, SHIFT] = jnp.sum(gn, axis=0, keepdims=True)
    return xh, inv


def back_kernel(
    flags, field, got, vown, voth, pos, xm, dg, wa, w1, wd, xi_in, qkv_in, pt_in, rec_in, ml_in, cos_in, sin_in,
    row_keep, row_send, c_out, vec_keep, keep_out, send_out,
    cosf, sinf, xi, qkv, pt, rec, ml, gh, gp, va_grad, vm_grad, folded, vec_send, kt, gm, gqt, dsum,
    angle_sems, ins, outs,
):
    core, layer = flags[0], flags[1]
    held = ((ml_in, ml), (rec_in, rec), (qkv_in, qkv), (pt_in, pt), (xi_in, xi))
    for k, (src, dst) in enumerate(held):
        load(src, dst, ins.at[k])
    load_angles(cos_in, sin_in, cosf, sinf, angle_sems)
    va, vm = vectors(core, vown, voth)
    wide = jnp.where(layer == 0, got[...].astype(F32), field[...].astype(F32))
    c = wide.astype(BF)
    c_out[...] = c
    vm_grad[:, SECOND:] = jnp.sum(wide, axis=0, keepdims=True)

    def from_output(j):
        return dot(c, wd[j])

    ahead = from_output(0)
    gn = None
    for j in range(4):
        ga = ahead
        if j < 3:
            ahead = from_output(j + 1)
        part = (ga * dg[:, D * j : D * (j + 1)].astype(F32)).astype(BF)
        start = hidden_start(core, j)
        gh[:, pl.ds(start, D)] = part
        vm_grad[:, pl.ds(pl.multiple_of(FIRST + start, 128), D)] = jnp.sum(
            part.astype(F32), axis=0, keepdims=True
        )
        part = dot_nt(part, w1[j])
        gn = part if gn is None else gn + part
    for when, dst in ((core == 0, send_out.at[pl.ds(0, L), :]), (core != 0, keep_out)):

        @pl.when(when)
        def _(dst=dst):
            load(gh, dst, outs.at[1])

    xh, inv = norm_stats(gn, xm[...].astype(F32), vm_grad)
    c = norm_back(gn, xh, inv, vm[:, GAIN], c)
    gp[:, 3 * D :] = c
    va_grad[:, FIRST + 5 * D :] = jnp.sum(c.astype(F32), axis=0, keepdims=True)
    colp, rowp = pos[:, 0:1], pos[:, 1:2]

    def emit(p, sl, sq, sk, grads):
        qr = qkv[:, sl].astype(F32) * (LN2 * HEAD_DIM**0.5)
        th = sq * qr + sk * qkv[:, D + 128 * p : D + 128 * (p + 1)].astype(F32)
        at = FIRST + 3 * D + 128 * p
        va_grad[:, at : at + 128] = jnp.sum(th * colp, axis=0, keepdims=True)
        va_grad[:, at + D : at + D + 128] = jnp.sum(th * rowp, axis=0, keepdims=True)
        for i, g in enumerate(grads):
            gp[:, D * i + 128 * p : D * i + 128 * (p + 1)] = g
            va_grad[:, FIRST + D * i + 128 * p : FIRST + D * i + 128 * (p + 1)] = jnp.sum(
                g.astype(F32), axis=0, keepdims=True
            )

    for k, (src, dst) in enumerate(held):
        arrived(src, dst, ins.at[k])
    wait_angles(cos_in, sin_in, cosf, sinf, angle_sems)
    attention_back(
        c, wa.at[3], cosf, sinf, qkv, pt, rec, ml, kt, gm, gqt, dsum, lambda p: p, emit
    )
    for when, dst in ((core == 0, keep_out), (core != 0, send_out.at[pl.ds(0, L), :])):

        @pl.when(when)
        def _(dst=dst):
            load(gp, dst, outs.at[2])

    gn = None
    for i in range(3):
        part = dot_nt(gp[:, D * i : D * (i + 1)], wa[i])
        gn = part if gn is None else gn + part
    xh, inv = norm_stats(gn, xi[...].astype(F32), va_grad)
    cx = norm_back(gn, xh, inv, va[:, GAIN], c).astype(F32)
    wide = c.astype(F32)
    row_keep[...] = jnp.where(core == 0, cx, wide).astype(BF)
    row_send[...] = jnp.where(core == 0, wide, cx).astype(BF)
    fold_vector(va_grad, folded)
    a, m = packed_vector(folded), packed_vector(vm_grad)
    vec_keep[...] = jnp.where(core == 0, a, m)
    for k, part in enumerate(split_two(jnp.where(core == 0, m, a))):
        for b in range(3):
            vec_send[:, 128 * (3 * k + b) : 128 * (3 * k + b + 1)] = part[16 * b : 16 * (b + 1), :]
    vec_out = send_out.at[pl.ds(L, 16), pl.ds(0, D)]
    load(vec_send, vec_out, outs.at[0])
    main_rows = pl.ds(0, L)
    arrived(gh, send_out.at[main_rows, :], outs.at[1])
    arrived(gp, keep_out, outs.at[2])
    arrived(vec_send, vec_out, outs.at[0])


def put(stage, value, out, first, sem):
    stage[...] = value.astype(BF)
    copy = pltpu.make_async_copy(stage, out.at[:, pl.ds(first, stage.shape[1])], sem)
    copy.start()
    return copy


def gram_down_kernel(
    flags, c, c_oth, act, bundle, main0, tail0, right0, down, left_main, left_tail, right_out,
    c1, sides, left, right, sems,
):
    loads = (
        (bundle.at[:, pl.ds(4 * D, D)], c1), (act, right.at[pl.ds(0, L), :]),
        (bundle.at[:, pl.ds(0, 2 * D)], right.at[pl.ds(L, L), :]),
        (tail0, sides.at[0]), (bundle.at[:, pl.ds(3 * D, D)], sides.at[1]),
        (main0, sides.at[2]), (bundle.at[:, pl.ds(2 * D, D)], sides.at[3]),
        (right0, right_out.at[pl.ds(0, L), :]),
    )
    for k, (src, dst) in enumerate(loads):
        load(src, dst, sems.at[k])
    left[:, :L] = c[...].T
    arrived(*loads[0], sems.at[0])

    @pl.when(flags[1] == 0)
    def _():
        left[:, L:] = c_oth[...].T

    @pl.when(flags[1] != 0)
    def _():
        left[:, L:] = c1[...].T

    for k in range(1, 3):
        arrived(*loads[k], sems.at[k])
    down[...] = dot(left[...], right[...]).astype(BF)
    for k in range(4):
        arrived(*loads[3 + k], sems.at[3 + k])
        (left_tail, left_main)[k // 2][:, L * (k % 2) : L * (k % 2 + 1)] = sides[k].T
    arrived(*loads[7], sems.at[7])


def gram_main_kernel(
    rows, right1, down, left_main, left_tail, vec, right_in,
    right, main, head, main_up, main_down, tail_up, tail_down, vec_out,
):
    right[L:, :] = right1[:L, :]
    head[...] = dot(left_tail[...], right[:, 3 * D :]).astype(BF)
    main[...] = dot(left_main[...], right[:, : 3 * D]).astype(BF)
    other = [
        jnp.concatenate(
            [right1[L : L + 16, 128 * (3 * k + b) : 128 * (3 * k + b + 1)].astype(F32) for b in range(3)], axis=0
        )
        for k in range(2)
    ]
    total = vec[...] + (other[0] + other[1])
    hi, lo = split_two(total)
    vec_out[...] = hi.astype(F32) + lo.astype(F32)
    r = main_up.shape[0]
    for k, (m, t) in enumerate(((main_up, tail_up), (main_down, tail_down))):
        here = own_rows(rows, 0, k, r)
        m[:, : 3 * D] = main[here, :]
        m[:, 3 * D :] = hi
        t[:, :D] = head[here, :]
        t[:, D : 3 * D] = down[here, :]
        t[:, 3 * D :] = lo


def own_rows(rows, t, way, r):
    return pl.ds(pl.multiple_of(rows[t, way], 16), r)


def add_kernel(t, rows, up, down, *refs, count, vector):
    parts, outs, vectors = refs[:count], refs[count : count + 2], refs[count + 2 :]
    for k, (got, out) in enumerate(zip((up, down), outs)):
        here = own_rows(rows, t, k, got.shape[0])
        at = 0
        for part in parts:
            sl = slice(at, at + part.shape[1])
            out[:, sl] = (got[:, sl].astype(F32) + part[here, :].astype(F32)).astype(BF)
            at += part.shape[1]
        if out.shape[1] > at:
            out[:, at:] = got[:, at:]
        if k < vector:
            vectors[k][...] = got[:, at : at + 128].astype(F32)


def fold_vector(va, out):
    def fold(start):
        v = va[:, start : start + D]
        w = HEAD_DIM // 2
        return jnp.concatenate(
            [v[:, 2 * w * h : 2 * w * h + w] - v[:, 2 * w * h + w : 2 * w * (h + 1)] for h in range(HEADS)],
            axis=1,
        )

    at = FIRST + 3 * D
    out[:, :at] = va[:, :at]
    out[:, at : at + HALF] = fold(at)
    out[:, at + HALF : SECOND] = fold(at + D)
    out[:, SECOND:] = va[:, at + 2 * D :]


def packed_vector(ref):
    rows = [ref[:, 128 * k : 128 * (k + 1)] for k in range(VECTOR // 128)]
    rows += [jnp.zeros((1, 128), F32)] * (PACKED[0] - len(rows))
    return jnp.concatenate(rows, axis=0)


def vector_sum_kernel(table, *refs):
    out, slots = refs[-2:]
    own, pieces = refs[0], refs[1:-2]
    n = len(pieces) // 2 + 1
    slots[table[0, 2]] = own[...]
    for k in range(1, n):
        t, way = (k + 1) // 2, (k + 1) % 2
        slots[table[t, 2 + way]] = pieces[k - 1][...] + pieces[n + k - 2][...]
    total = slots[0]
    for k in range(1, n):
        total = total + slots[k]
    out[...] = total


def place_kernel(t, rows, *refs):
    out, buf, sems = refs[-3:]
    count = sems.shape[0]
    shards = refs[: 2 * count]
    r = shards[0].shape[0]
    copies = []
    for k in range(count):
        there = pl.ds(r * k, r)
        buf[there, : 3 * D] = shards[2 * k][...].astype(F32)
        buf[there, 3 * D :] = shards[2 * k + 1][...].astype(F32)
        copy = pltpu.make_async_copy(
            buf.at[there, :], out.at[own_rows(rows, t, k, r), :], sems.at[k]
        )
        copy.start()
        copies.append(copy)
    for copy in copies:
        copy.wait()


SMEM = pl.BlockSpec(memory_space=pltpu.SMEM)
VS = pl.BlockSpec(memory_space=pltpu.VMEM)
HBM = pl.BlockSpec(memory_space=pltpu.HBM)


def sds(shape, dtype=BF):
    return jax.ShapeDtypeStruct(shape, dtype)


def call(kernel, name, in_specs, outs, scratch, flops, nbytes, limit=58, out_specs=None, aliases=None):
    return pl.pallas_call(
        kernel,
        name=name,
        in_specs=in_specs,
        out_specs=[VS] * len(outs) if out_specs is None else out_specs,
        out_shape=outs,
        scratch_shapes=scratch,
        input_output_aliases={} if aliases is None else aliases,
        compiler_params=pltpu.CompilerParams(vmem_limit_bytes=limit * MIB),
        cost_estimate=pl.CostEstimate(flops=flops, bytes_accessed=nbytes, transcendentals=0),
    )


ATTN_W = [VM((4, D, D), BF)]
ANGLES = [VM((L, D), F32), VM((L, D), F32)]
MLP_W = [VM((4, D, D), BF), VM((4, D, D), BF)]
BACK_S = [VM((D, L), BF), VM((L, D), BF), VM((2, 128, L), F32), VM((16, L), F32)]


def in_vmem(a):
    return pltpu.with_memory_space_constraint(a, pltpu.VMEM)


def in_hbm(a):
    return pltpu.with_memory_space_constraint(a, pltpu.HBM)


def row(width=D):
    return VM((L, width), BF)


def row_out(width=D):
    return pltpu.HBM((L, width), BF)


def prepare(flags, x, cot, *vecs):
    out = VM((x.shape[0], L), BF)
    return call(
        prepare_kernel, "prepare", [SMEM] + [VS] * 6, [out] * 4 + [pltpu.HBM((1, VECTOR), F32)], [], 1000,
        int(1e6), 8,
    )(flags, *(in_hbm(a) for a in (x, cot) + vecs))


def positions(flags, grid, own, oth):
    hbm = pltpu.HBM
    return call(
        positions_kernel, "positions", [SMEM, SMEM, VS, VS],
        [hbm((L, D), F32), hbm((L, D), F32), hbm((L, 128), F32), hbm((8, L), F32)],
        [], int(1e8), int(3e6), 56,
    )(flags, grid, own, oth)


def first_pass(*a):
    return call(
        first_kernel, "first_pass", [SMEM] + [VS] * 8 + [HBM] * 4, [row(), row_out()],
        ATTN_W + MLP_W + ANGLES
        + [row(), VM((D, L), BF), row(3 * D), VM((HEADS, L, L), BF), VM((16, L), F32), row(), VM((D, L), BF),
           VM((D, L), BF), row(), DMA((13,)), DMA((2,))],
        int(8e9), int(20e6), 40, out_specs=[VS, HBM],
    )(*a)


def fetch(*a):
    return call(
        fetch_kernel, "fetch", [SMEM] + [HBM] * 4, ANGLES + ATTN_W + MLP_W, [DMA((14,))], int(1e8), int(17e6), 8
    )(*a)


def second_pass(*a):
    saved = [
        row_out(), row_out(), row_out(3 * D), pltpu.HBM((HEADS, L, L), BF), pltpu.HBM((16, L), F32), row_out(),
        row_out(FF // 2), row_out(FF // 2), row_out(FF), row_out(), row_out(), row_out(5 * D),
    ]
    return call(
        second_kernel, "second_pass", [SMEM] + [VS] * 11, [row()] + saved,
        [row(), row(), row(3 * D), VM((HEADS, L, L), BF), VM((16, L), F32), row(), row(), row(),
         row(FF // 2), row(FF // 2), row(FF), VM((D, L), BF), VM((D, L), BF), VM((L, D), F32),
         VM((L, D), F32)]
        + BACK_S + [row(3 * D), DMA((15,))],
        int(18e9), int(20e6), 32, out_specs=[VS] + [HBM] * len(saved),
    )(*a)


def late_pass(*a):
    return call(
        late_kernel, "late_pass", [SMEM] + [VS] * 3 + [HBM] * 6,
        [sds((L, D))] * 2 + [row(), row(FF)] + ATTN_W + MLP_W,
        [row(FF // 2), row(FF // 2), DMA((12,)), DMA((4,))], int(2e9), int(20e6), 14,
    )(*a)


def back_pass(*a):
    return call(
        back_kernel, "back_pass", [SMEM] + [VS] * 10 + [HBM] * 7,
        [sds((L, D)), sds((L, D)), row(), VM(PACKED, F32), row_out(FF), pltpu.HBM((L + 16, FF), BF)],
        ANGLES
        + [row(), row(3 * D), VM((HEADS, L, L), BF), VM((16, L), F32), row(), row(FF), row(FF),
           VM((1, FIRST + 6 * D), F32), VM((1, VECTOR), F32), VM((1, VECTOR), F32), VM((16, D), BF)]
        + BACK_S + [DMA((2,)), DMA((5,)), DMA((3,))],
        int(10e9), int(15e6), 30, out_specs=[VS] * 4 + [HBM] * 2,
    )(*a)


def gram_down(*a):
    square = VM((D, 2 * L), BF)
    return call(
        gram_down_kernel, "gram_down", [SMEM] + [VS] * 2 + [HBM] * 5,
        [VM((D, 2 * D), BF), square, square, VM((2 * L, FF), BF)],
        [row(), VM((4, L, D), BF), square, VM((2 * L, 2 * D), BF), DMA((8,))], int(2e9), int(8e6), 18,
    )(*a)


def gram_main(rows, r, *a):
    wide = VM((r, 3 * D + 128), BF)
    return call(
        gram_main_kernel, "gram_main", [SMEM] + [VS] * 6,
        [VM((2 * L, FF), BF), VM((D, 3 * D), BF), VM((D, D), BF)] + [wide] * 4 + [VM(PACKED, F32)],
        [], int(4e9), int(12e6), 20, aliases={6: 0},
    )(rows, *a)


def add(t, rows, up, down, parts, vector, wide):
    count = len(parts)

    def kernel(*refs):
        add_kernel(t, *refs, count=count, vector=vector)

    width = sum(p.shape[1] for p in parts)
    out = VM((up.shape[0], width + (128 if wide else 0)), BF)
    results = call(
        kernel, "add", [SMEM] + [VS] * (2 + count), [out, out] + [pltpu.HBM(PACKED, F32)] * vector, [], 1000,
        int(1e6), 4,
    )(rows, in_vmem(up), in_vmem(down), *(in_vmem(p) for p in parts))
    return results[:2], results[2:]


def both_rows(flags, keep, got):
    return call(
        both_rows_kernel, "both_rows", [SMEM, VS, VS], [sds((2 * L, D))], [], 1000, int(2e6), 6
    )(flags, keep, got)[0]


def mlp_back(flags, *a):
    return call(
        mlp_back_kernel, "mlp_back", [SMEM] + [VS] * 6 + [HBM] * 2,
        [row(), row(FF), row(), row(), VM((1, VECTOR), F32)],
        MLP_W + [DMA((8,))], int(4e9), int(14e6), 22,
    )(*resident(flags, 6, a))


def attn_back(flags, *a):
    return call(
        attn_back_kernel, "attn_back", [SMEM] + [VS] * 13 + [HBM] * 2,
        [row(), row(), row(3 * D), row(3 * D), VM((1, FIRST + 6 * D), F32)],
        ATTN_W + BACK_S + [row(3 * D), DMA((4,))],
        int(6e9), int(14e6), 20,
    )(*resident(flags, 13, a))


def vector_sum(table, own, pieces):
    n = len(pieces) // 2 + 1
    return call(
        vector_sum_kernel, "vector_sum", [SMEM] + [VS] * (2 * n - 1), [sds(PACKED, F32)],
        [VM((n,) + PACKED, F32)], 1000, 100000, 4,
    )(table, own, *pieces)[0]


def place(t, rows, shards, total):
    def kernel(*refs):
        place_kernel(t, *refs)

    r, count = shards[0].shape[0], len(shards) // 2
    into = [] if total is None else [total]
    return call(
        kernel, "place", [SMEM] + [VS] * len(shards) + [HBM] * len(into),
        [pltpu.HBM((D, 6 * D), F32)],
        [VM((r * count, 6 * D), F32), DMA((count,))], 1000, int(2e6), 24,
        out_specs=[HBM], aliases={len(shards) + 1: 0} if into else {},
    )(rows, *shards, *into)[0]


def core_swap(a):
    return lax.ppermute(a, "section", [(0, 1), (1, 0), (2, 3), (3, 2)])


def after(value, first):
    return lax.optimization_barrier((value, first))[0]


class Cycle:
    def __init__(self):
        self.n = n = lax.axis_size("dp")
        self.r = D // (2 * n)
        i = lax.axis_index("dp")
        where = jnp.where(i % 2 == 0, i // 2, n - 1 - i // 2)
        order = list(range(0, n, 2)) + list(range(n - 1, 0, -2))
        self.pairs = [[(order[k], order[(k + d) % n]) for k in range(n)] for d in (1, -1)]
        t = jnp.arange(2 * n, dtype=I32)[:, None]
        way = jnp.array([[1, -1]], I32)
        step = jnp.where(t < n, t, t - n)
        at = (where - way * step) % n
        whose = jnp.where(2 * at < n, 2 * at, 2 * (n - at) - 1)
        self.rows = in_hbm(jnp.concatenate([at * self.r + jnp.array([[0, HALF]], I32), whose], axis=1))

    def placed(self, k):
        return 2 * self.n - 1 if k == 0 else self.n + k - 1


class Chain:
    def __init__(self, cycle, parts, cur):
        self.cycle, self.parts, self.cur = cycle, parts, cur
        self.t = 0
        self.shards = []
        self.vectors = []

    def step(self, token):
        c = self.cycle
        got = [lax.ppermute(a, "dp", p) for a, p in zip(self.cur, c.pairs)]
        got = after(got, token)
        self.t += 1
        if self.t < c.n:
            t = self.t
            ways = int(t <= c.n // 2) + int(t <= (c.n - 1) // 2)
            self.cur, came = add(t, c.rows, *got, self.parts, ways, t < c.n // 2)
            self.vectors += came
        else:
            self.cur = got
        if self.t >= c.n - 1:
            self.shards.append(self.cur)
        return self.cur


def small_ring():
    return lax.axis_size("dp") <= 16


def summed_weight_grad(main, tail, token, beside):
    if not small_ring():
        for f in beside:
            token = f(token)
        return place(0, jnp.zeros((1, 1), I32), lax.psum([main, tail], "dp"), None)
    cycle = main.cycle
    n = cycle.n
    total = None
    beside = list(beside)
    while main.t < 2 * n - 2:
        token = tail.step(token)
        if total is not None:
            token = (token, total)
        token = main.step(token)
        if main.shards:
            k = len(main.shards) - 1
            a, b = main.shards[k], tail.shards[k]
            total = place(cycle.placed(k), cycle.rows, [a[0], b[0], a[1], b[1]], total)
        if beside and main.t >= n:
            token = (token, beside.pop(0)(token))
    for f in beside:
        token = f(token)
    return total


def body(
    block_input, cotangent, grid_sizes, section_weight, norm_gain, norm_bias, first_vector, second_vector
):
    section = lax.axis_index("section")
    core = section % 2
    flags = in_hbm(jnp.stack([core, section // 2]).astype(I32))
    first_layer = section < 2

    keep, send, away, across, vown = prepare(
        flags, block_input.T, cotangent.T, norm_gain, norm_bias, first_vector, second_vector
    )
    n = lax.axis_size("dp")
    if n % 2 == 0:
        voth = lax.ppermute(
            vown, ("section", "dp"), [(n * s + d, n * (s ^ 1) + (d ^ 1)) for s in range(4) for d in range(n)]
        )
    else:
        voth = core_swap(vown)
    vown, voth = in_hbm(vown), in_hbm(voth)
    got = core_swap(send)
    away = lax.ppermute(away, "section", [(0, 2), (1, 3), (2, 0), (3, 1)])
    across = lax.ppermute(across, "section", [(0, 3), (1, 2), (2, 1), (3, 0)])
    own = in_hbm(section_weight[0])
    oth = in_hbm(core_swap(section_weight[0]))
    cosf, sinf, pos, segr = (in_hbm(a) for a in positions(flags, grid_sizes, vown, voth))

    x_two, field = first_pass(
        flags, keep, got, away, across, vown, voth, pos, segr, cosf, sinf, own, oth
    )
    field = in_hbm(field)
    fetched = fetch(flags, cosf, sinf, own, after(oth, x_two))
    x_got = after(lax.ppermute(x_two, "section", [(0, 2), (1, 3)]), fetched)
    (
        c_two, x_in, x_mid, qkv, pt, rec, ml, act_mine, act_send, dg, main_left, tail_left, bundle,
    ) = second_pass(flags, field, x_got, vown, voth, pos, segr, *(in_vmem(a) for a in fetched))
    x_in, qkv, pt, rec, ml = (in_hbm(a) for a in (x_in, qkv, pt, rec, ml))
    act_mine, main_left, tail_left = (in_hbm(a) for a in (act_mine, main_left, tail_left))
    c_got = lax.ppermute(c_two, "section", [(2, 0), (3, 1)])
    bundle = in_hbm(core_swap(bundle))
    x_keep, x_send, *held = late_pass(
        flags, x_two, vown, voth, in_hbm(after(x_mid, bundle)), in_hbm(dg), act_mine, in_hbm(act_send), own, oth
    )
    c_got = after(c_got, x_keep)

    c_keep, c_send, c_out, vec, right, right_send = back_pass(
        flags, field, c_got, vown, voth, pos,
        *(in_vmem(a) for a in held), x_in, qkv, pt, rec, ml, cosf, sinf,
    )
    c_oth = core_swap(c_got)
    right_oth = core_swap(after(right_send, c_oth))
    down, left_main, left_tail, right = gram_down(
        flags, c_out, c_oth, act_mine, bundle, main_left, tail_left, in_hbm(right)
    )
    if small_ring():
        cycle = Cycle()
        rows, r = cycle.rows, cycle.r
    else:
        rows, r = jnp.zeros((1, 2), I32), PACKED[0]
    right, main, head, *first, vec = gram_main(
        rows, r, right_oth, down, left_main, left_tail, vec, right
    )
    token = main
    if small_ring():
        main, tail = Chain(cycle, [main], first[:2]), Chain(cycle, [head, down], first[2:])
    else:
        tail = jnp.concatenate([head, down], axis=1)
    swapped = {}

    def send_rows(token):
        swapped["x"], swapped["c"] = core_swap(after(x_send, token)), core_swap(after(c_send, token))
        return x_keep

    def join(name, keep):
        def f(token):
            swapped[name] = both_rows(flags, keep, after(swapped[name], token))
            return swapped[name]

        return f

    weight_grad = summed_weight_grad(
        main, tail, token, [send_rows, join("x", x_keep), join("c", c_keep)]
    )
    if small_ring():
        vec = vector_sum(cycle.rows, vec, main.vectors + tail.vectors)
    else:
        vec = lax.psum(vec, "dp")
    vg = vec.reshape(1, -1)[:, :VECTOR]
    activations, input_grads = swapped["x"], swapped["c"]
    return (
        activations[None],
        input_grads[None],
        weight_grad[None],
        vg[:, GAIN],
        vg[:, SHIFT],
        vg[:, FIRST:SECOND],
        vg[:, SECOND:],
    )


def solution(mesh):
    in_specs = (
        P("dp", "section"),
        P("dp", "section"),
        P("dp", None, None),
        P("section", None, None),
        P("section", None),
        P("section", None),
        P("section", None),
        P("section", None),
    )
    out_specs = (
        P("section", "dp", None),
        P("section", "dp", None),
        P("section", None, None),
        P("section", None),
        P("section", None),
        P("section", None),
        P("section", None),
    )
    return jax.shard_map(body, mesh=mesh, in_specs=in_specs, out_specs=out_specs, check_vma=False)
```

```python
import jax
import jax.numpy as jnp
from jax import lax
from jax.experimental import pallas as pl
from jax.experimental.pallas import tpu as pltpu
from jax.sharding import PartitionSpec as P

D = 768
HEADS = 12
HEAD_DIM = 64
FF = 3072
L = 384
HALF = D // 2
F32 = jnp.float32
BF = jnp.bfloat16
I32 = jnp.int32
NT = (((1,), (1,)), ((), ()))
TN = (((0,), (0,)), ((), ()))
VM = pltpu.VMEM
DMA = pltpu.SemaphoreType.DMA
MIB = 1024 * 1024
LN2 = 0.6931471805599453
GAIN, SHIFT = slice(0, D), slice(D, 2 * D)
FIRST, SECOND = 2 * D, 2 * D + FF
VECTOR = 3 * D + FF
PACKED = (48, 128)


def dot(a, b):
    return jnp.dot(a, b, preferred_element_type=F32)


def dot_nt(a, b):
    return lax.dot_general(a, b, NT, preferred_element_type=F32)


def dot_tn(a, b):
    return lax.dot_general(a, b, TN, preferred_element_type=F32)


def norm_parts(x):
    center = x - jnp.mean(x, axis=-1, keepdims=True)
    inv = lax.rsqrt(jnp.mean(center * center, axis=-1, keepdims=True) + 1e-06)
    return center * inv, inv


def swap_halves(a):
    lane = lax.broadcasted_iota(I32, (1, 128), 1)
    first = (lane % HEAD_DIM) < HEAD_DIM // 2
    out = []
    for i in range(a.shape[1] // 128):
        s = a[:, 128 * i : 128 * (i + 1)]
        out.append(jnp.where(first, pltpu.roll(s, 96, 1), pltpu.roll(s, 32, 1)))
    return jnp.concatenate(out, axis=1) if len(out) > 1 else out[0]


def lanes(start, size):
    if isinstance(start, int):
        return slice(start, start + size)
    return pl.ds(pl.multiple_of(start, 128), size)


def rows_at(start, size):
    if isinstance(start, int):
        return slice(start, start + size)
    return pl.ds(pl.multiple_of(start, size), size)


def cols(start, size):
    return (slice(None), pl.ds(start, size))


def pick(flag, want, own, oth, src, dst, sem):
    @pl.when(flag == want)
    def _():
        pltpu.make_async_copy(own.at[src], dst, sem).start()

    @pl.when(flag != want)
    def _():
        pltpu.make_async_copy(oth.at[src], dst, sem).start()


def load(src, dst, sem):
    pltpu.make_async_copy(src, dst, sem).start()


def arrived(src, dst, sem):
    pltpu.make_async_copy(src, dst, sem).wait()


def load_attn(core, own, oth, wa, sems, i):
    pick(core, 0, own, oth, cols(D * i, D), wa.at[i], sems.at[i])


def wait_attn(own, wa, sems, i):
    arrived(own.at[cols(D * i, D)], wa.at[i], sems.at[i])


def hidden_start(core, j):
    return pl.multiple_of(FF // 2 * ((core + j // 2) % 2) + D * (j % 2), 128)


def load_mlp(core, own, oth, w1, wd, sems, j):
    pick(core, 1, own, oth, (slice(None), pl.ds(hidden_start(core, j), D)), w1.at[j], sems.at[j])
    load((own if j < 2 else oth).at[cols(FF + D * (j % 2), D)], wd.at[j], sems.at[4 + j])


class Forward:
    def __init__(self, when, core, own, oth, wa, w1, wd, cos_in, sin_in, cosf, sinf, sems):
        self.attn = core, own, oth, wa, sems
        self.mlp = core, own, oth, w1, wd, sems.at[pl.ds(4, 8)]
        self.angles = cos_in, sin_in, cosf, sinf, sems.at[pl.ds(12, 2)]
        self.own, self.wa, self.sems, self.when = own, wa, sems, when

        @pl.when(when)
        def _():
            load_attn(*self.attn, 0)
            load_angles(*self.angles)
            load_attn(*self.attn, 1)

    def wait(self, what):
        @pl.when(self.when)
        def _():
            if what == "angles":
                wait_angles(*self.angles)
                return
            wait_attn(self.own, self.wa, self.sems, what)
            if what < 2:
                load_attn(*self.attn, what + 2)
            elif what == 2:
                for j in range(4):
                    load_mlp(*self.mlp, j)

    def wait_mlp(self):
        core, own, oth, w1, wd, sems = self.mlp

        @pl.when(self.when)
        def _():
            for j in range(4):
                wait_mlp(own, w1, wd, sems, j)


def wait_mlp(own, w1, wd, sems, j):
    if w1 is not None:
        arrived(own.at[cols(0, D)], w1.at[j], sems.at[j])
    arrived(own.at[cols(0, D)], wd.at[j], sems.at[4 + j])


def vectors(core, own, oth):
    a, b = own[...], oth[...]
    return jnp.where(core == 0, a, b), jnp.where(core == 0, b, a)


def attention(x, vec, wa, wait, cosf, sinf, segc, segr, qkv, pt, rec, ml, mlt, vt, n_ref):
    xh, inv = norm_parts(x)
    n = (xh * vec[:, GAIN] + vec[:, SHIFT]).astype(BF)
    n_ref[...] = n
    for i in range(3):
        wait(i)
        part = dot(n, wa[i]) + vec[:, FIRST + D * i : FIRST + D * (i + 1)]
        if i == 0:
            wait("angles")
        if i < 2:
            part = part * cosf[...] + swap_halves(part) * sinf[...]
        if i == 0:
            part = part * (HEAD_DIM**-0.5 / LN2)
        qkv[:, D * i : D * (i + 1)] = part.astype(BF)
    vt[...] = qkv[:, 2 * D : 3 * D].T
    same = segc == segr
    lane = lax.broadcasted_iota(I32, (1, 128), 1)

    def score(h):
        p = 128 * (h // 2)
        keys = jnp.where((lane // HEAD_DIM) == h % 2, qkv[:, D + p : D + p + 128], BF(0))
        return dot_nt(keys, qkv[:, p : p + 128])

    ahead = score(0)
    for h in range(HEADS):
        st = ahead
        if h + 1 < HEADS:
            ahead = score(h + 1)
        st = jnp.where(same, st, -1e30)
        e = jnp.exp2(st - jnp.max(st, axis=0, keepdims=True))
        r = 1.0 / jnp.sum(e, axis=0, keepdims=True)
        rec[h : h + 1, :] = r
        e = e.astype(BF)
        pt[h] = e
        here = slice(HEAD_DIM * h, HEAD_DIM * (h + 1))
        mlt[here, :] = (dot(vt[here, :], e) * r).astype(BF)
    ml[...] = mlt[...].T
    wait(3)
    out = x + dot(ml[...], wa[3]) + vec[:, SECOND : SECOND + D]
    return out.astype(BF), xh, inv


C0 = 0.7978845608028654
C1 = 0.044715


def gelu(h):
    h2 = h * h
    t = jnp.tanh(C0 * (h + C1 * h * h2))
    half = 0.5 * (1.0 + t)
    return h * half, half + (0.5 * C0) * h * (1.0 - t * t) * (1.0 + (3.0 * C1) * h2)


def norm_back(gn, xh, inv, gain, c):
    u = gn * gain
    gx = inv * (
        u - jnp.mean(u, axis=-1, keepdims=True) - xh * jnp.mean(u * xh, axis=-1, keepdims=True)
    )
    return (c.astype(F32) + gx).astype(BF)


def head_select():
    head = lax.broadcasted_iota(I32, (16, D), 0)
    lane = lax.broadcasted_iota(I32, (16, D), 1)
    return jnp.where(lane // HEAD_DIM == head, 1.0, 0.0).astype(BF)


def split_two(a):
    hi = a.astype(BF)
    return hi, (a - hi.astype(F32)).astype(BF)


def attention_back(c, wo, cosf, sinf, qkv, pt, rec, ml, kt, gm, gqt, dsum, pair_of, emit):
    kt[...] = qkv[:, D : 2 * D].T
    gm_wide = dot_nt(c, wo[...])
    sel = head_select()
    hi, lo = split_two(gm_wide * ml[...].astype(F32))
    row = lax.broadcasted_iota(I32, (16, L), 0)
    recs = jnp.where(row < HEADS, rec[...], 0.0)
    dsum[...] = (dot_nt(sel, hi) + dot_nt(sel, lo)) * recs
    hi, lo = split_two(recs)
    gm[...] = (gm_wide * (dot_tn(hi, sel) + dot_tn(lo, sel))).astype(BF)
    lane = lax.broadcasted_iota(I32, (1, 128), 1)

    def spot(h):
        return lanes(128 * pair_of(h // 2), 128), (lane // HEAD_DIM) == h % 2

    def from_values(h):
        sl, here = spot(h)
        values = qkv[:, lanes(2 * D + 128 * pair_of(h // 2), 128)]
        return dot_nt(jnp.where(here, values, BF(0)), gm[:, sl])

    ahead = from_values(0)
    for h in range(HEADS):
        gpt = ahead
        if h + 1 < HEADS:
            ahead = from_values(h + 1)
        sl, here = spot(h)
        head = 2 * pair_of(h // 2) + h % 2
        e = pt[head]
        gvh = dot(e, jnp.where(here, gm[:, sl], BF(0)))
        gst = (e.astype(F32) * (gpt - dsum[rows_at(head, 1), :])).astype(BF)
        gkh = dot(gst, jnp.where(here, qkv[:, sl], BF(0)))
        kth = kt[rows_at(HEAD_DIM * head, HEAD_DIM), :]
        gqt[h // 2 % 2, HEAD_DIM * (h % 2) : HEAD_DIM * (h % 2 + 1), :] = dot(kth, gst)
        gv = gvh if h % 2 == 0 else gv + gvh
        gk = gkh if h % 2 == 0 else gk + gkh
        if h % 2 == 1:
            gq = gqt[h // 2 % 2].T * (HEAD_DIM**-0.5)
            gk = gk * LN2
            cs, sn = cosf[:, sl], sinf[:, sl]
            sq, sk = swap_halves(gq), swap_halves(gk)
            emit(
                h // 2, sl, sq, sk,
                ((gq * cs - sq * sn).astype(BF), (gk * cs - sk * sn).astype(BF), gv.astype(BF)),
            )


def positions_kernel(flags, grid, vown, voth, cosf, sinf, pos, segr):
    core = flags[0]
    vec = vectors(core, vown, voth)[0]
    h0, w0, h1, w1 = (grid[core, k // 2, k % 2] for k in range(4))
    e1 = h0 * w0
    e2 = e1 + h1 * w1

    def place(t):
        segment = (t >= e1).astype(I32) + (t >= e2).astype(I32)
        width = jnp.where(segment == 0, w0, w1).astype(F32)
        inside = (t - jnp.where(segment == 0, 0, e1)).astype(F32)
        row = jnp.floor((inside + 0.5) / width)
        column = inside - row * width
        return segment, jnp.where(segment < 2, row, 0.0), jnp.where(segment < 2, column, 0.0)

    segment, row, column = place(lax.broadcasted_iota(I32, (L, 128), 0))
    lane = lax.broadcasted_iota(I32, (L, 128), 1)
    pos[...] = jnp.where(lane == 0, column, jnp.where(lane == 1, row, segment.astype(F32)))
    t = lax.broadcasted_iota(I32, (8, L), 1)
    segr[...] = (t >= e1).astype(F32) + (t >= e2).astype(F32)

    def by_lane(start):
        parts = []
        for h in range(HEADS):
            f = vec[:, start + 32 * h : start + 32 * (h + 1)]
            parts += [f, f]
        return jnp.concatenate(parts, axis=1)

    number = lax.broadcasted_iota(I32, (16, D), 0).astype(F32)

    def look_up(which, table):
        hi, rest = split_two(table)
        mid, low = split_two(table - hi.astype(F32))
        tables = jnp.concatenate([hi, mid, low], axis=0)
        hit = (lax.broadcasted_iota(I32, (L, 48), 1) % 16).astype(F32) == which[:, :48]
        return dot(jnp.where(hit, 1.0, 0.0).astype(BF), tables)

    ax = number * by_lane(FIRST + 3 * D)
    ay = number * by_lane(FIRST + 3 * D + HALF)
    cx, sx = look_up(column, jnp.cos(ax)), look_up(column, jnp.sin(ax))
    cy, sy = look_up(row, jnp.cos(ay)), look_up(row, jnp.sin(ay))
    cosf[...] = cx * cy - sx * sy
    lane = lax.broadcasted_iota(I32, (1, D), 1)
    sign = jnp.where(lane % HEAD_DIM < HEAD_DIM // 2, -1.0, 1.0)
    sinf[...] = (sx * cy + cx * sy) * sign


def prepare_kernel(
    flags, x, cot, gain, shift, first, second, keep, send, away, across, vec
):
    core, layer = flags[0], flags[1]
    for at, (mine, other) in enumerate(((x, cot), (cot, x))):

        @pl.when(layer == at)
        def _(mine=mine, other=other):
            keep[...] = mine[:, lanes(L * core, L)]
            send[...] = mine[:, lanes(L * (1 - core), L)]
            away[...] = other[:, lanes(L * core, L)]
            across[...] = other[:, lanes(L * (1 - core), L)]

    vec[:, GAIN] = gain[...]
    vec[:, SHIFT] = shift[...]
    vec[:, FIRST:SECOND] = first[...]
    vec[:, SECOND:] = second[...]


def load_angles(cos_in, sin_in, cosf, sinf, sems):
    load(cos_in, cosf, sems.at[0])
    load(sin_in, sinf, sems.at[1])


def wait_angles(cos_in, sin_in, cosf, sinf, sems):
    arrived(cos_in, cosf, sems.at[0])
    arrived(sin_in, sinf, sems.at[1])


HELD = 5


def first_kernel(
    flags, keep, got, away, across, vown, voth, pos, segr, cos_in, sin_in, own, oth, *refs,
):
    out, field_out, cosf, sinf, wa, w1, wd, field, turned, qkv, pt, rec, ml, mlt, vt, n_ref, sems = refs[HELD:]
    core, layer = flags[0], flags[1]
    w = keep.shape[0]
    for k in range(2):
        for at in range(2):

            @pl.when((core == k) & (layer == at))
            def _(k=k, at=at):
                parts = {(at, k): keep, (at, 1 - k): got, (1 - at, k): away, (1 - at, 1 - k): across}
                for s in range(4):
                    turned[w * s : w * (s + 1), :] = parts[s // 2, s % 2][...]

    field[...] = turned[...].T
    keeping = pltpu.make_async_copy(field, field_out, sems.at[14])
    keeping.start()
    @pl.when(layer == 0)
    def _():
        loads = Forward(core == 0, core, own, oth, wa, w1, wd, cos_in, sin_in, cosf, sinf, sems)
        va, vm = vectors(core, vown, voth)
        x_mid, _, _ = attention(
            field[...].astype(F32), va, wa, loads.wait, cosf, sinf, pos[:, 2:3], segr[0:1, :],
            qkv, pt, rec, ml, mlt, vt, n_ref,
        )
        x = x_mid.astype(F32)
        xh, _ = norm_parts(x)
        n = (xh * vm[:, GAIN] + vm[:, SHIFT]).astype(BF)
        loads.wait_mlp()
        acc = x + vm[:, SECOND : SECOND + D]
        first = hidden_bias(core, vm)
        ahead = dot(n, w1[0])
        for j in range(4):
            h = ahead + first[:, D * j : D * (j + 1)]
            if j < 3:
                ahead = dot(n, w1[j + 1])
            acc = acc + dot_nt(gelu(h)[0].astype(BF), wd[j])
        out[...] = acc.astype(BF)

    keeping.wait()


def hidden_bias(core, vm):
    a, b = vm[:, FIRST : FIRST + FF // 2], vm[:, FIRST + FF // 2 : SECOND]
    return jnp.concatenate([jnp.where(core == 0, a, b), jnp.where(core == 0, b, a)], axis=1)


def fetch_kernel(flags, cos_in, sin_in, own, oth, cosf, sinf, wa, w1, wd, sems):
    core = flags[0]

    @pl.when((core != 0) | (flags[1] != 0))
    def _():
        for i in range(4):
            load_attn(core, own, oth, wa, sems, i)
            load_mlp(core, own, oth, w1, wd, sems.at[pl.ds(4, 8)], i)
        load_angles(cos_in, sin_in, cosf, sinf, sems.at[pl.ds(12, 2)])
        for i in range(4):
            wait_attn(own, wa, sems, i)
            wait_mlp(own, w1, wd, sems.at[pl.ds(4, 8)], i)
        wait_angles(cos_in, sin_in, cosf, sinf, sems.at[pl.ds(12, 2)])


def second_kernel(
    flags, field, got, got_late, vown, voth, pos, segr, *refs,
):
    (
        cosf, sinf, wa, w1, wd, xi, xm, rec, ml, dg, actm, acts, cx, act_out, main_out, tail_out, bundle,
        qkv_out, pt_out, qkv, pt, na, nm, mlt, vt, xha, xhm, kt, gm, gqt, dsum, gp, outs,
    ) = refs[HELD:]
    core, layer = flags[0], flags[1]
    va, vm = vectors(core, vown, voth)
    x = jnp.where(core == 0, got[...].astype(F32), got_late[...].astype(F32))
    x = jnp.where(layer == 0, field[...].astype(F32), x)
    xi[...] = x.astype(BF)
    x_mid, xh, inv_a = attention(
        x, va, wa, lambda what: None, cosf, sinf, pos[:, 2:3], segr[0:1, :], qkv, pt, rec, ml, mlt, vt, na
    )
    xha[...] = xh
    xm[...] = x_mid
    load(qkv, qkv_out, outs.at[7])
    load(pt, pt_out, outs.at[8])
    xh, inv_m = norm_parts(x_mid.astype(F32))
    xhm[...] = xh
    n = (xh * vm[:, GAIN] + vm[:, SHIFT]).astype(BF)
    nm[...] = n
    sides = (
        main_out, tail_out, bundle.at[:, pl.ds(2 * D, D)], bundle.at[:, pl.ds(3 * D, D)],
    )
    load(field, bundle.at[:, pl.ds(4 * D, D)], outs.at[4])
    for when, sources in ((core == 0, (na, ml, nm, nm)), (core != 0, (nm, nm, na, ml))):

        @pl.when(when)
        def _(sources=sources):
            for k, (src, dst) in enumerate(zip(sources, sides)):
                load(src, dst, outs.at[k])

    first = hidden_bias(core, vm)
    c = field[...]

    def forward(j):
        return dot(n, w1[j])

    def chunk(j, h):
        act, slope = gelu(h + first[:, D * j : D * (j + 1)])
        (actm, acts)[j // 2][:, D * (j % 2) : D * (j % 2 + 1)] = act.astype(BF)
        slope = slope.astype(BF)
        dg[:, D * j : D * (j + 1)] = slope
        return slope

    def leave():
        load(acts, bundle.at[:, pl.ds(0, 2 * D)], outs.at[5])
        load(actm, act_out, outs.at[6])

    @pl.when(layer >= 0)
    def _():
        ahead = forward(0), dot(c, wd[0])
        gn = None
        for j in range(4):
            h, ga = ahead
            if j < 3:
                ahead = forward(j + 1), dot(c, wd[j + 1])
            slope = chunk(j, h)
            part = dot_nt((ga * slope.astype(F32)).astype(BF), w1[j])
            gn = part if gn is None else gn + part
        leave()
        c_mid = norm_back(gn, xhm[...], inv_m, vm[:, GAIN], c)

        def emit(p, sl, sq, sk, grads):
            for i in range(3):
                gp[:, D * i + 128 * p : D * i + 128 * (p + 1)] = grads[i]

        attention_back(
            c_mid, wa.at[3], cosf, sinf, qkv, pt, rec, ml, kt, gm, gqt, dsum, lambda p: p, emit
        )
        gn = None
        for i in range(3):
            part = dot_nt(gp[:, D * i : D * (i + 1)], wa[i])
            gn = part if gn is None else gn + part
        cx[...] = norm_back(gn, xha[...], inv_a, va[:, GAIN], c_mid)

    for k, (src, dst) in enumerate(
        tuple((nm, side) for side in sides)
        + ((field, sides[2]), (acts, bundle.at[:, pl.ds(0, 2 * D)]), (actm, act_out), (qkv, qkv_out), (pt, pt_out))
    ):
        arrived(src, dst, outs.at[k])


def late_kernel(flags, x_two, vown, voth, actm, acts, *refs):
    xm, wd = refs[HELD + 1], refs[HELD - 1]
    keep, send = refs[-2:]
    core, layer = flags[0], flags[1]
    vm = vectors(core, vown, voth)[1]
    mid = xm[...].astype(F32)
    acc = mid + vm[:, SECOND : SECOND + D]
    for j in range(4):
        acc = acc + dot_nt((actm, acts)[j // 2][:, D * (j % 2) : D * (j % 2 + 1)], wd[j])
    acc = jnp.where(layer == 0, x_two[...].astype(F32), acc)
    keep[...] = jnp.where(core == 0, mid, acc).astype(BF)
    send[...] = jnp.where(core == 0, acc, mid).astype(BF)


def both_rows(core, keep, got, out, sems):
    return [
        pltpu.make_async_copy(src, out.at[rows_at(L * at, L), :], sems.at[k])
        for k, (src, at) in enumerate(((keep, core), (got, 1 - core)))
    ]


def norm_stats(gn, x, vec):
    xh, inv = norm_parts(x)
    vec[:, GAIN] = jnp.sum(gn * xh, axis=0, keepdims=True)
    vec[:, SHIFT] = jnp.sum(gn, axis=0, keepdims=True)
    return xh, inv


def back_kernel(
    flags, field, got, vown, voth, pos, qkv_in, pt_in, cosf, sinf, wa, w1, wd, xi, xm, rec, ml, dg,
    row_keep, row_send, c_out, vec_keep, keep_out, send_out,
    qkv, pt, gh, gp, va_grad, vm_grad, folded, vec_send, kt, gm, gqt, dsum, outs,
):
    core, layer = flags[0], flags[1]
    load(qkv_in, qkv, outs.at[3])
    load(pt_in, pt, outs.at[4])
    va, vm = vectors(core, vown, voth)
    wide = jnp.where(layer == 0, got[...].astype(F32), field[...].astype(F32))
    c = wide.astype(BF)
    c_out[...] = c
    vm_grad[:, SECOND:] = jnp.sum(wide, axis=0, keepdims=True)

    def from_output(j):
        return dot(c, wd[j])

    ahead = from_output(0)
    gn = None
    for j in range(4):
        ga = ahead
        if j < 3:
            ahead = from_output(j + 1)
        part = (ga * dg[:, D * j : D * (j + 1)].astype(F32)).astype(BF)
        start = hidden_start(core, j)
        gh[:, pl.ds(start, D)] = part
        vm_grad[:, pl.ds(pl.multiple_of(FIRST + start, 128), D)] = jnp.sum(
            part.astype(F32), axis=0, keepdims=True
        )
        part = dot_nt(part, w1[j])
        gn = part if gn is None else gn + part
    for when, dst in ((core == 0, send_out.at[pl.ds(0, L), :]), (core != 0, keep_out)):

        @pl.when(when)
        def _(dst=dst):
            load(gh, dst, outs.at[1])

    xh, inv = norm_stats(gn, xm[...].astype(F32), vm_grad)
    c = norm_back(gn, xh, inv, vm[:, GAIN], c)
    gp[:, 3 * D :] = c
    va_grad[:, FIRST + 5 * D :] = jnp.sum(c.astype(F32), axis=0, keepdims=True)
    colp, rowp = pos[:, 0:1], pos[:, 1:2]

    def emit(p, sl, sq, sk, grads):
        qr = qkv[:, sl].astype(F32) * (LN2 * HEAD_DIM**0.5)
        th = sq * qr + sk * qkv[:, D + 128 * p : D + 128 * (p + 1)].astype(F32)
        at = FIRST + 3 * D + 128 * p
        va_grad[:, at : at + 128] = jnp.sum(th * colp, axis=0, keepdims=True)
        va_grad[:, at + D : at + D + 128] = jnp.sum(th * rowp, axis=0, keepdims=True)
        for i, g in enumerate(grads):
            gp[:, D * i + 128 * p : D * i + 128 * (p + 1)] = g
            va_grad[:, FIRST + D * i + 128 * p : FIRST + D * i + 128 * (p + 1)] = jnp.sum(
                g.astype(F32), axis=0, keepdims=True
            )

    arrived(qkv_in, qkv, outs.at[3])
    arrived(pt_in, pt, outs.at[4])
    attention_back(
        c, wa.at[3], cosf, sinf, qkv, pt, rec, ml, kt, gm, gqt, dsum, lambda p: p, emit
    )
    for when, dst in ((core == 0, keep_out), (core != 0, send_out.at[pl.ds(0, L), :])):

        @pl.when(when)
        def _(dst=dst):
            load(gp, dst, outs.at[2])

    gn = None
    for i in range(3):
        part = dot_nt(gp[:, D * i : D * (i + 1)], wa[i])
        gn = part if gn is None else gn + part
    xh, inv = norm_stats(gn, xi[...].astype(F32), va_grad)
    cx = norm_back(gn, xh, inv, va[:, GAIN], c).astype(F32)
    wide = c.astype(F32)
    row_keep[...] = jnp.where(core == 0, cx, wide).astype(BF)
    row_send[...] = jnp.where(core == 0, wide, cx).astype(BF)
    fold_vector(va_grad, folded)
    a, m = packed_vector(folded), packed_vector(vm_grad)
    vec_keep[...] = jnp.where(core == 0, a, m)
    for k, part in enumerate(split_two(jnp.where(core == 0, m, a))):
        for b in range(3):
            vec_send[:, 128 * (3 * k + b) : 128 * (3 * k + b + 1)] = part[16 * b : 16 * (b + 1), :]
    vec_out = send_out.at[pl.ds(L, 16), pl.ds(0, D)]
    load(vec_send, vec_out, outs.at[0])
    main_rows = pl.ds(0, L)
    arrived(gh, send_out.at[main_rows, :], outs.at[1])
    arrived(gp, keep_out, outs.at[2])
    arrived(vec_send, vec_out, outs.at[0])


def put(stage, value, out, first, sem):
    stage[...] = value.astype(BF)
    copy = pltpu.make_async_copy(stage, out.at[:, pl.ds(first, stage.shape[1])], sem)
    copy.start()
    return copy


def gram_down_kernel(
    flags, c, c_oth, x_keep, x_oth, act, bundle, main0, tail0, right0,
    down, left_main, left_tail, right_out, activations,
    c1, sides, left, right, sems, row_sems,
):
    leaving = both_rows(flags[0], x_keep, x_oth, activations, row_sems)
    for copy in leaving:
        copy.start()
    loads = (
        (bundle.at[:, pl.ds(4 * D, D)], c1), (act, right.at[pl.ds(0, L), :]),
        (bundle.at[:, pl.ds(0, 2 * D)], right.at[pl.ds(L, L), :]),
        (tail0, sides.at[0]), (bundle.at[:, pl.ds(3 * D, D)], sides.at[1]),
        (main0, sides.at[2]), (bundle.at[:, pl.ds(2 * D, D)], sides.at[3]),
        (right0, right_out.at[pl.ds(0, L), :]),
    )
    for k, (src, dst) in enumerate(loads):
        load(src, dst, sems.at[k])
    left[:, :L] = c[...].T
    arrived(*loads[0], sems.at[0])

    @pl.when(flags[1] == 0)
    def _():
        left[:, L:] = c_oth[...].T

    @pl.when(flags[1] != 0)
    def _():
        left[:, L:] = c1[...].T

    for k in range(1, 3):
        arrived(*loads[k], sems.at[k])
    down[...] = dot(left[...], right[...]).astype(BF)
    for k in range(4):
        arrived(*loads[3 + k], sems.at[3 + k])
        (left_tail, left_main)[k // 2][:, L * (k % 2) : L * (k % 2 + 1)] = sides[k].T
    arrived(*loads[7], sems.at[7])
    for copy in leaving:
        copy.wait()


def gram_main_kernel(
    rows, right1, down, left_main, left_tail, vec, right_in,
    right, main, head, main_up, main_down, tail_up, tail_down, vec_out,
):
    right[L:, :] = right1[:L, :]
    head[...] = dot(left_tail[...], right[:, 3 * D :]).astype(BF)
    main[...] = dot(left_main[...], right[:, : 3 * D]).astype(BF)
    other = [
        jnp.concatenate(
            [right1[L : L + 16, 128 * (3 * k + b) : 128 * (3 * k + b + 1)].astype(F32) for b in range(3)], axis=0
        )
        for k in range(2)
    ]
    total = vec[...] + (other[0] + other[1])
    total = total.astype(BF)
    vec_out[...] = total.astype(F32)
    r = main_up.shape[0]
    for k, (m, t) in enumerate(((main_up, tail_up), (main_down, tail_down))):
        here = own_rows(rows, 0, k, r)
        m[:, : 3 * D] = main[here, :]
        m[:, 3 * D :] = total
        t[:, :D] = head[here, :]
        t[:, D : 3 * D] = down[here, :]
        t[:, 3 * D :] = total


def own_rows(rows, t, way, r):
    return pl.ds(pl.multiple_of(rows[t, way], 16), r)


def add_kernel(t, rows, up, down, *refs, count, vector):
    parts, outs, vectors = refs[:count], refs[count : count + 2], refs[count + 2 :]
    for k, (got, out) in enumerate(zip((up, down), outs)):
        here = own_rows(rows, t, k, got.shape[0])
        at = 0
        for part in parts:
            sl = slice(at, at + part.shape[1])
            out[:, sl] = (got[:, sl].astype(F32) + part[here, :].astype(F32)).astype(BF)
            at += part.shape[1]
        if out.shape[1] > at:
            out[:, at:] = got[:, at:]
        if k < vector:
            vectors[k][...] = got[:, at : at + 128].astype(F32)


def fold_vector(va, out):
    def fold(start):
        v = va[:, start : start + D]
        w = HEAD_DIM // 2
        return jnp.concatenate(
            [v[:, 2 * w * h : 2 * w * h + w] - v[:, 2 * w * h + w : 2 * w * (h + 1)] for h in range(HEADS)],
            axis=1,
        )

    at = FIRST + 3 * D
    out[:, :at] = va[:, :at]
    out[:, at : at + HALF] = fold(at)
    out[:, at + HALF : SECOND] = fold(at + D)
    out[:, SECOND:] = va[:, at + 2 * D :]


def packed_vector(ref):
    rows = [ref[:, 128 * k : 128 * (k + 1)] for k in range(VECTOR // 128)]
    rows += [jnp.zeros((1, 128), F32)] * (PACKED[0] - len(rows))
    return jnp.concatenate(rows, axis=0)


def sum_vectors(table, vectors, slots, outs):
    n = len(vectors)
    if table is None:
        total = vectors[0][...]
    else:
        slots[table[0, 2]] = vectors[0][...]
        for k in range(1, n):
            t, way = (k + 1) // 2, (k + 1) % 2
            slots[table[t, 2 + way]] = vectors[k][...]
        total = slots[0]
        for k in range(1, n):
            total = total + slots[k]
    at = 0
    for out in outs:
        for k in range(out.shape[1] // 128):
            out[:, 128 * k : 128 * (k + 1)] = total[at + k : at + k + 1, :]
        at += out.shape[1] // 128


def place_kernel(spots, whole, flags, rows, *refs):
    count, pair, vectors, into = whole
    ins, refs = refs[: 2 * count + pair + vectors], refs[2 * count + pair + vectors + into :]
    out, buf, sems = refs[0], refs[-3], refs[-2]
    copies = []
    if pair:
        copies += both_rows(flags[0], ins[2 * count], ins[2 * count + 1], refs[1], refs[-1])
        copies[0].start()
        copies[1].start()
    r = ins[0].shape[0]
    for k in range(count):
        there = pl.ds(r * k, r)
        buf[there, : 3 * D] = ins[2 * k][...].astype(F32)
        buf[there, 3 * D :] = ins[2 * k + 1][...].astype(F32)
        copy = pltpu.make_async_copy(
            buf.at[there, :], out.at[own_rows(rows, *spots[k], r), :], sems.at[k]
        )
        copy.start()
        copies.append(copy)
    if vectors:
        outs = refs[1 + pair // 2 : 5 + pair // 2]
        sum_vectors(rows if vectors > 1 else None, ins[2 * count + pair :], refs[-4], outs)
    for copy in copies:
        copy.wait()


SMEM = pl.BlockSpec(memory_space=pltpu.SMEM)
VS = pl.BlockSpec(memory_space=pltpu.VMEM)
HBM = pl.BlockSpec(memory_space=pltpu.HBM)


def sds(shape, dtype=BF):
    return jax.ShapeDtypeStruct(shape, dtype)


def call(kernel, name, in_specs, outs, scratch, flops, nbytes, limit=58, out_specs=None, aliases=None):
    return pl.pallas_call(
        kernel,
        name=name,
        in_specs=in_specs,
        out_specs=[VS] * len(outs) if out_specs is None else out_specs,
        out_shape=outs,
        scratch_shapes=scratch,
        input_output_aliases={} if aliases is None else aliases,
        compiler_params=pltpu.CompilerParams(vmem_limit_bytes=limit * MIB),
        cost_estimate=pl.CostEstimate(flops=flops, bytes_accessed=nbytes, transcendentals=0),
    )


ATTN_W = [VM((4, D, D), BF)]
ANGLES = [VM((L, D), F32), VM((L, D), F32)]
MLP_W = [VM((4, D, D), BF), VM((4, D, D), BF)]
BACK_S = [VM((D, L), BF), VM((L, D), BF), VM((2, 128, L), F32), VM((16, L), F32)]


def in_vmem(a):
    return pltpu.with_memory_space_constraint(a, pltpu.VMEM)


def in_hbm(a):
    return pltpu.with_memory_space_constraint(a, pltpu.HBM)


def row(width=D):
    return VM((L, width), BF)


def row_out(width=D):
    return pltpu.HBM((L, width), BF)


def prepare(flags, x, cot, *vecs):
    out = VM((x.shape[0], L), BF)
    return call(
        prepare_kernel, "prepare", [SMEM] + [VS] * 6, [out] * 4 + [pltpu.HBM((1, VECTOR), F32)], [], 1000,
        int(1e6), 8,
    )(flags, *(in_hbm(a) for a in (x, cot) + vecs))


def positions(flags, grid, own, oth):
    hbm = pltpu.HBM
    return call(
        positions_kernel, "positions", [SMEM, SMEM, VS, VS],
        [hbm((L, D), F32), hbm((L, D), F32), hbm((L, 128), F32), hbm((8, L), F32)],
        [], int(1e8), int(3e6), 56,
    )(flags, grid, own, oth)


def fetch(flags, *sources):
    return call(
        fetch_kernel, "fetch", [SMEM] + [HBM] * 4, ANGLES + ATTN_W + MLP_W, [DMA((14,))], int(1e8), int(17e6), 28
    )(flags, *sources)


def first_pass(held, *a):
    results = call(
        first_kernel, "first_pass", [SMEM] + [VS] * 8 + [HBM] * 4 + [VS] * HELD,
        [row(), row_out()] + ANGLES + ATTN_W + MLP_W,
        [row(), VM((D, L), BF), row(3 * D), VM((HEADS, L, L), BF), VM((16, L), F32), row(), VM((D, L), BF),
         VM((D, L), BF), row(), DMA((15,))],
        int(8e9), int(20e6), 28, out_specs=[VS, HBM] + [VS] * HELD,
        aliases={len(a) + k: 2 + k for k in range(HELD)},
    )(*a, *(in_vmem(x) for x in held))
    return results[0], results[1], results[2:]


SAVED = [VM((L, D), BF), VM((L, D), BF), VM((16, L), F32), VM((L, D), BF), VM((L, FF), BF)]
HEAD_S = [VM((L, 3 * D), BF), VM((HEADS, L, L), BF)]


def second_pass(held, *a):
    outs = [
        row_out(FF // 2), row_out(), row_out(), row_out(5 * D), row_out(3 * D), pltpu.HBM((HEADS, L, L), BF)
    ]
    resident = ANGLES + ATTN_W + MLP_W + SAVED
    results = call(
        second_kernel, "second_pass", [SMEM] + [VS] * (7 + HELD),
        resident + [row(FF // 2), row(FF // 2), row()] + outs,
        HEAD_S + [row(), row(), VM((D, L), BF), VM((D, L), BF), VM((L, D), F32), VM((L, D), F32)]
        + BACK_S + [row(3 * D), DMA((9,))],
        int(18e9), int(20e6), 28, out_specs=[VS] * (len(resident) + 3) + [HBM] * len(outs),
        aliases={len(a) + k: k for k in range(HELD)},
    )(*a, *(in_vmem(x) for x in held))
    n = len(resident)
    return results[:n], results[n : n + 2], results[n + 2], results[n + 3 :]


def late_pass(held, *a):
    results = call(
        late_kernel, "late_pass", [SMEM] + [VS] * (len(a) - 1 + len(held)),
        ANGLES + ATTN_W + MLP_W + SAVED + [sds((L, D))] * 2, [], int(2e9), int(5e6), 28,
        aliases={len(a) + k: k for k in range(len(held))},
    )(*a, *(in_vmem(x) for x in held))
    return results[: len(held)], results[len(held) :]


def back_pass(held, *a):
    return call(
        back_kernel, "back_pass", [SMEM] + [VS] * 5 + [HBM] * 2 + [VS] * len(held),
        [sds((L, D)), sds((L, D)), row(), VM(PACKED, F32), row_out(FF), pltpu.HBM((L + 16, FF), BF)],
        HEAD_S
        + [row(FF), row(FF), VM((1, FIRST + 6 * D), F32), VM((1, VECTOR), F32), VM((1, VECTOR), F32),
           VM((16, D), BF)]
        + BACK_S + [DMA((5,))],
        int(10e9), int(15e6), 28, out_specs=[VS] * 4 + [HBM] * 2,
    )(*a, *(in_vmem(x) for x in held))


def gram_down(*a):
    square = VM((D, 2 * L), BF)
    return call(
        gram_down_kernel, "gram_down", [SMEM] + [VS] * 4 + [HBM] * 5,
        [VM((D, 2 * D), BF), square, square, VM((2 * L, FF), BF), pltpu.HBM((2 * L, D), BF)],
        [row(), VM((4, L, D), BF), square, VM((2 * L, 2 * D), BF), DMA((8,)), DMA((2,))], int(2e9), int(8e6), 20,
        out_specs=[VS] * 4 + [HBM],
    )(*a)


def gram_main(rows, r, *a):
    wide = VM((r, 3 * D + 128), BF)
    return call(
        gram_main_kernel, "gram_main", [SMEM] + [VS] * 6,
        [VM((2 * L, FF), BF), VM((D, 3 * D), BF), VM((D, D), BF)] + [wide] * 4 + [VM(PACKED, F32)],
        [], int(4e9), int(12e6), 20, aliases={6: 0},
    )(rows, *a)


def add(t, rows, up, down, parts, vector, wide):
    count = len(parts)

    def kernel(*refs):
        add_kernel(t, *refs, count=count, vector=vector)

    width = sum(p.shape[1] for p in parts)
    out = VM((up.shape[0], width + (128 if wide else 0)), BF)
    results = call(
        kernel, "add", [SMEM] + [VS] * (2 + count), [out, out] + [pltpu.HBM(PACKED, F32)] * vector, [], 1000,
        int(1e6), 4,
    )(rows, in_vmem(up), in_vmem(down), *(in_vmem(p) for p in parts))
    return results[:2], results[2:]


def place(flags, spots, rows, shards, total, pair=(), vectors=()):
    r, count = shards[0].shape[0], len(shards) // 2
    into = [] if total is None else [total]
    whole = count, len(pair), len(vectors), len(into)

    def kernel(*refs):
        place_kernel(spots, whole, *refs)

    outs = [pltpu.HBM((D, 6 * D), F32)]
    outs += [pltpu.HBM((2 * L, D), BF)] if pair else []
    outs += [sds((1, w), F32) for w in (D, D, FF, D)] if vectors else []
    given = len(shards) + len(pair) + len(vectors)
    return call(
        kernel, "place", [SMEM, SMEM] + [VS] * given + [HBM] * len(into), outs,
        [VM((max(len(vectors), 1),) + PACKED, F32), VM((r * count, 6 * D), F32), DMA((count,)), DMA((2,))], 1000,
        int(2e7), 24, out_specs=[HBM] * (2 if pair else 1) + ([VS] * 4 if vectors else []),
        aliases={given + 2: 0} if into else {},
    )(flags, rows, *shards, *pair, *vectors, *into)


def core_swap(a):
    return lax.ppermute(a, "section", [(0, 1), (1, 0), (2, 3), (3, 2)])


def after(value, first):
    return lax.optimization_barrier((value, first))[0]


class Cycle:
    def __init__(self):
        self.n = n = lax.axis_size("dp")
        self.r = D // (2 * n)
        i = lax.axis_index("dp")
        where = jnp.where(i % 2 == 0, i // 2, n - 1 - i // 2)
        order = list(range(0, n, 2)) + list(range(n - 1, 0, -2))
        self.pairs = [[(order[k], order[(k + d) % n]) for k in range(n)] for d in (1, -1)]
        t = jnp.arange(2 * n, dtype=I32)[:, None]
        way = jnp.array([[1, -1]], I32)
        step = jnp.where(t < n, t, t - n)
        at = (where - way * step) % n
        whose = jnp.where(2 * at < n, 2 * at, 2 * (n - at) - 1)
        self.rows = in_hbm(jnp.concatenate([at * self.r + jnp.array([[0, HALF]], I32), whose], axis=1))

    def placed(self, k):
        return 2 * self.n - 1 if k == 0 else self.n + k - 1


class Chain:
    def __init__(self, cycle, parts, cur, carries=False):
        self.cycle, self.parts, self.cur, self.carries = cycle, parts, cur, carries
        self.t = 0
        self.shards = []
        self.vectors = []

    def step(self, token):
        c = self.cycle
        got = [lax.ppermute(a, "dp", p) for a, p in zip(self.cur, c.pairs)]
        got = after(got, token)
        self.t += 1
        if self.t < c.n:
            t = self.t
            ways = int(t <= c.n // 2) + int(t <= (c.n - 1) // 2) if self.carries else 0
            self.cur, came = add(t, c.rows, *got, self.parts, ways, t < c.n // 2)
            self.vectors += came
        else:
            self.cur = got
        if self.t >= c.n - 1:
            self.shards.append(self.cur)
        return self.cur


def small_ring():
    return lax.axis_size("dp") <= 16


def summed(flags, main, tail, token, pair, vector):
    if not small_ring():
        chains, vector = lax.psum([main, tail], "dp"), lax.psum(vector, "dp")
        return place(flags, [(0, 0)], jnp.zeros((1, 1), I32), chains, None, pair, [vector])
    cycle = main.cycle
    n = cycle.n
    total, placed = None, 0
    results = {}
    while main.t < 2 * n - 2:
        token = tail.step(token)
        if total is not None:
            token = (token, total)
        token = main.step(token)
        whole = len(main.shards)
        if whole > placed and (whole % 2 == 0 or whole == n - 1):
            spots, shards = [], []
            for k in range(placed, whole):
                for way in range(2):
                    spots.append((cycle.placed(k), way))
                    shards += [main.shards[k][way], tail.shards[k][way]]
            now, then = placed == 0, "vectors" not in results and whole >= min(4, n)
            total, *more = place(
                flags, spots, cycle.rows, shards, total, pair if now else (), [vector] + main.vectors if then else ()
            )
            if now:
                results["rows"] = more[0]
            if then:
                results["vectors"] = more
            placed = whole
    return total, results["rows"], *results["vectors"]


def body(
    block_input, cotangent, grid_sizes, section_weight, norm_gain, norm_bias, first_vector, second_vector
):
    section = lax.axis_index("section")
    core = section % 2
    flags = in_hbm(jnp.stack([core, section // 2]).astype(I32))
    first_layer = section < 2

    keep, send, away, across, vown = prepare(
        flags, block_input.T, cotangent.T, norm_gain, norm_bias, first_vector, second_vector
    )
    n = lax.axis_size("dp")
    if n % 2 == 0:
        voth = lax.ppermute(
            vown, ("section", "dp"), [(n * s + d, n * (s ^ 1) + (d ^ 1)) for s in range(4) for d in range(n)]
        )
    else:
        voth = core_swap(vown)
    if small_ring():
        cycle = Cycle()
        rows, r = cycle.rows, cycle.r
    else:
        rows, r = jnp.zeros((1, 2), I32), PACKED[0]
    vown, voth = in_hbm(vown), in_hbm(after(voth, rows))
    got = core_swap(send)
    away = lax.ppermute(away, "section", [(0, 2), (1, 3), (2, 0), (3, 1)])
    across = lax.ppermute(across, "section", [(0, 3), (1, 2), (2, 1), (3, 0)])
    own = in_hbm(section_weight[0])
    oth = in_hbm(core_swap(section_weight[0]))
    cosf, sinf, pos, segr = (in_hbm(a) for a in positions(flags, grid_sizes, vown, voth))

    held = fetch(flags, cosf, sinf, own, oth)
    x_two, field, held = first_pass(
        held, flags, keep, got, away, across, vown, voth, pos, segr, cosf, sinf, own, oth
    )
    field = in_hbm(field)
    x_got, x_late = (lax.ppermute(x_two, "section", [pair]) for pair in ((0, 2), (1, 3)))
    held, active, c_two, (act_mine, main_left, tail_left, bundle, qkv, pt) = second_pass(
        held, flags, field, x_got, x_late, vown, voth, pos, segr
    )
    act_mine, main_left, tail_left = (in_hbm(a) for a in (act_mine, main_left, tail_left))
    c_got = lax.ppermute(c_two, "section", [(2, 0), (3, 1)])
    held, (x_keep, x_send) = late_pass(held, flags, x_two, vown, voth, *(in_vmem(a) for a in active))
    c_got = after(c_got, x_keep)
    bundle = in_hbm(core_swap(after(bundle, c_got)))
    x_oth = core_swap(after(x_send, c_got))

    c_keep, c_send, c_out, vec, right, right_send = back_pass(
        held, flags, field, c_got, vown, voth, pos, in_hbm(qkv), in_hbm(pt)
    )
    c_oth = core_swap(c_got)
    right_oth = core_swap(after(right_send, (c_oth, bundle, x_oth)))
    down, left_main, left_tail, right, activations = gram_down(
        flags, c_out, c_oth, x_keep, x_oth, act_mine, bundle, main_left, tail_left, in_hbm(right)
    )
    right, main, head, *first, vec = gram_main(
        rows, r, right_oth, down, left_main, left_tail, vec, right
    )
    token = main
    if small_ring():
        main, tail = Chain(cycle, [main], first[:2], True), Chain(cycle, [head, down], first[2:])
    else:
        tail = jnp.concatenate([head, down], axis=1)
    weight_grad, input_grads, *vectors = summed(
        flags, main, tail, token, (c_keep, core_swap(after(c_send, token))), vec
    )
    return (
        activations[None],
        input_grads[None],
        weight_grad[None],
        *vectors,
    )


def solution(mesh):
    in_specs = (
        P("dp", "section"),
        P("dp", "section"),
        P("dp", None, None),
        P("section", None, None),
        P("section", None),
        P("section", None),
        P("section", None),
        P("section", None),
    )
    out_specs = (
        P("section", "dp", None),
        P("section", "dp", None),
        P("section", None, None),
        P("section", None),
        P("section", None),
        P("section", None),
        P("section", None),
    )
    return jax.shard_map(body, mesh=mesh, in_specs=in_specs, out_specs=out_specs, check_vma=False)
```

```python
import jax
import jax.numpy as jnp
from jax import lax
from jax.experimental import pallas as pl
from jax.experimental.pallas import tpu as pltpu
from jax.sharding import PartitionSpec as P

D = 768
HEADS = 12
HEAD_DIM = 64
FF = 3072
L = 384
HALF = D // 2
F32 = jnp.float32
BF = jnp.bfloat16
I32 = jnp.int32
NT = (((1,), (1,)), ((), ()))
TN = (((0,), (0,)), ((), ()))
VM = pltpu.VMEM
DMA = pltpu.SemaphoreType.DMA
MIB = 1024 * 1024
LN2 = 0.6931471805599453
GAIN, SHIFT = slice(0, D), slice(D, 2 * D)
FIRST, SECOND = 2 * D, 2 * D + FF
VECTOR = 3 * D + FF
PACKED = (48, 128)


def dot(a, b):
    return jnp.dot(a, b, preferred_element_type=F32)


def dot_nt(a, b):
    return lax.dot_general(a, b, NT, preferred_element_type=F32)


def dot_tn(a, b):
    return lax.dot_general(a, b, TN, preferred_element_type=F32)


def norm_parts(x):
    center = x - jnp.mean(x, axis=-1, keepdims=True)
    inv = lax.rsqrt(jnp.mean(center * center, axis=-1, keepdims=True) + 1e-06)
    return center * inv, inv


def swap_halves(a):
    lane = lax.broadcasted_iota(I32, (1, 128), 1)
    first = (lane % HEAD_DIM) < HEAD_DIM // 2
    out = []
    for i in range(a.shape[1] // 128):
        s = a[:, 128 * i : 128 * (i + 1)]
        out.append(jnp.where(first, pltpu.roll(s, 96, 1), pltpu.roll(s, 32, 1)))
    return jnp.concatenate(out, axis=1) if len(out) > 1 else out[0]


def lanes(start, size):
    if isinstance(start, int):
        return slice(start, start + size)
    return pl.ds(pl.multiple_of(start, 128), size)


def rows_at(start, size):
    if isinstance(start, int):
        return slice(start, start + size)
    return pl.ds(pl.multiple_of(start, size), size)


def cols(start, size):
    return (slice(None), pl.ds(start, size))


def pick(flag, want, own, oth, src, dst, sem):
    @pl.when(flag == want)
    def _():
        pltpu.make_async_copy(own.at[src], dst, sem).start()

    @pl.when(flag != want)
    def _():
        pltpu.make_async_copy(oth.at[src], dst, sem).start()


def load(src, dst, sem):
    pltpu.make_async_copy(src, dst, sem).start()


def arrived(src, dst, sem):
    pltpu.make_async_copy(src, dst, sem).wait()


def load_attn(core, own, oth, wa, sems, i):
    pick(core, 0, own, oth, cols(D * i, D), wa.at[i], sems.at[i])


def wait_attn(own, wa, sems, i):
    arrived(own.at[cols(D * i, D)], wa.at[i], sems.at[i])


def hidden_start(core, j):
    return pl.multiple_of(FF // 2 * ((core + j // 2) % 2) + D * (j % 2), 128)


def load_mlp(core, own, oth, w1, wd, sems, j):
    pick(core, 1, own, oth, (slice(None), pl.ds(hidden_start(core, j), D)), w1.at[j], sems.at[j])
    load((own if j < 2 else oth).at[cols(FF + D * (j % 2), D)], wd.at[j], sems.at[4 + j])


class Forward:
    def __init__(self, when, core, own, oth, wa, w1, wd, cos_in, sin_in, cosf, sinf, sems):
        self.attn = core, own, oth, wa, sems
        self.mlp = core, own, oth, w1, wd, sems.at[pl.ds(4, 8)]
        self.angles = cos_in, sin_in, cosf, sinf, sems.at[pl.ds(12, 2)]
        self.own, self.wa, self.sems, self.when = own, wa, sems, when

        @pl.when(when)
        def _():
            load_attn(*self.attn, 0)
            load_angles(*self.angles)
            load_attn(*self.attn, 1)

    def wait(self, what):
        @pl.when(self.when)
        def _():
            if what == "angles":
                wait_angles(*self.angles)
                return
            wait_attn(self.own, self.wa, self.sems, what)
            if what < 2:
                load_attn(*self.attn, what + 2)
            elif what == 2:
                for j in range(4):
                    load_mlp(*self.mlp, j)

    def wait_mlp(self):
        core, own, oth, w1, wd, sems = self.mlp

        @pl.when(self.when)
        def _():
            for j in range(4):
                wait_mlp(own, w1, wd, sems, j)


def wait_mlp(own, w1, wd, sems, j):
    if w1 is not None:
        arrived(own.at[cols(0, D)], w1.at[j], sems.at[j])
    arrived(own.at[cols(0, D)], wd.at[j], sems.at[4 + j])


def vectors(core, own, oth):
    a, b = own[...], oth[...]
    return jnp.where(core == 0, a, b), jnp.where(core == 0, b, a)


def attention(x, vec, wa, wait, cosf, sinf, segc, segr, qkv, pt, rec, ml, mlt, vt, n_ref):
    xh, inv = norm_parts(x)
    n = (xh * vec[:, GAIN] + vec[:, SHIFT]).astype(BF)
    n_ref[...] = n
    for i in range(3):
        wait(i)
        part = dot(n, wa[i]) + vec[:, FIRST + D * i : FIRST + D * (i + 1)]
        if i == 0:
            wait("angles")
        if i < 2:
            part = part * cosf[...] + swap_halves(part) * sinf[...]
        if i == 0:
            part = part * (HEAD_DIM**-0.5 / LN2)
        qkv[:, D * i : D * (i + 1)] = part.astype(BF)
    vt[...] = qkv[:, 2 * D : 3 * D].T
    same = segc == segr
    lane = lax.broadcasted_iota(I32, (1, 128), 1)

    def score(h):
        p = 128 * (h // 2)
        keys = jnp.where((lane // HEAD_DIM) == h % 2, qkv[:, D + p : D + p + 128], BF(0))
        return dot_nt(keys, qkv[:, p : p + 128])

    ahead = score(0)
    for h in range(HEADS):
        st = ahead
        if h + 1 < HEADS:
            ahead = score(h + 1)
        st = jnp.where(same, st, -1e30)
        e = jnp.exp2(st - jnp.max(st, axis=0, keepdims=True))
        r = 1.0 / jnp.sum(e, axis=0, keepdims=True)
        rec[h : h + 1, :] = r
        e = e.astype(BF)
        pt[h] = e
        here = slice(HEAD_DIM * h, HEAD_DIM * (h + 1))
        mlt[here, :] = (dot(vt[here, :], e) * r).astype(BF)
    ml[...] = mlt[...].T
    wait(3)
    out = x + dot(ml[...], wa[3]) + vec[:, SECOND : SECOND + D]
    return out.astype(BF), xh, inv


C0 = 0.7978845608028654
C1 = 0.044715


def gelu(h):
    h2 = h * h
    t = jnp.tanh(C0 * (h + C1 * h * h2))
    half = 0.5 * (1.0 + t)
    return h * half, half + (0.5 * C0) * h * (1.0 - t * t) * (1.0 + (3.0 * C1) * h2)


def norm_back(gn, xh, inv, gain, c):
    u = gn * gain
    gx = inv * (
        u - jnp.mean(u, axis=-1, keepdims=True) - xh * jnp.mean(u * xh, axis=-1, keepdims=True)
    )
    return (c.astype(F32) + gx).astype(BF)


def head_select():
    head = lax.broadcasted_iota(I32, (16, D), 0)
    lane = lax.broadcasted_iota(I32, (16, D), 1)
    return jnp.where(lane // HEAD_DIM == head, 1.0, 0.0).astype(BF)


def split_two(a):
    hi = a.astype(BF)
    return hi, (a - hi.astype(F32)).astype(BF)


def attention_back(c, wo, cosf, sinf, qkv, pt, rec, ml, kt, gm, gqt, dsum, pair_of, emit):
    kt[...] = qkv[:, D : 2 * D].T
    gm_wide = dot_nt(c, wo[...])
    sel = head_select()
    hi, lo = split_two(gm_wide * ml[...].astype(F32))
    row = lax.broadcasted_iota(I32, (16, L), 0)
    recs = jnp.where(row < HEADS, rec[...], 0.0)
    dsum[...] = (dot_nt(sel, hi) + dot_nt(sel, lo)) * recs
    hi, lo = split_two(recs)
    gm[...] = (gm_wide * (dot_tn(hi, sel) + dot_tn(lo, sel))).astype(BF)
    lane = lax.broadcasted_iota(I32, (1, 128), 1)

    def spot(h):
        return lanes(128 * pair_of(h // 2), 128), (lane // HEAD_DIM) == h % 2

    def from_values(h):
        sl, here = spot(h)
        values = qkv[:, lanes(2 * D + 128 * pair_of(h // 2), 128)]
        return dot_nt(jnp.where(here, values, BF(0)), gm[:, sl])

    ahead = from_values(0)
    for h in range(HEADS):
        gpt = ahead
        if h + 1 < HEADS:
            ahead = from_values(h + 1)
        sl, here = spot(h)
        head = 2 * pair_of(h // 2) + h % 2
        e = pt[head]
        gvh = dot(e, jnp.where(here, gm[:, sl], BF(0)))
        gst = (e.astype(F32) * (gpt - dsum[rows_at(head, 1), :])).astype(BF)
        gkh = dot(gst, jnp.where(here, qkv[:, sl], BF(0)))
        kth = kt[rows_at(HEAD_DIM * head, HEAD_DIM), :]
        gqt[h // 2 % 2, HEAD_DIM * (h % 2) : HEAD_DIM * (h % 2 + 1), :] = dot(kth, gst)
        gv = gvh if h % 2 == 0 else gv + gvh
        gk = gkh if h % 2 == 0 else gk + gkh
        if h % 2 == 1:
            gq = gqt[h // 2 % 2].T * (HEAD_DIM**-0.5)
            gk = gk * LN2
            cs, sn = cosf[:, sl], sinf[:, sl]
            sq, sk = swap_halves(gq), swap_halves(gk)
            emit(
                h // 2, sl, sq, sk,
                ((gq * cs - sq * sn).astype(BF), (gk * cs - sk * sn).astype(BF), gv.astype(BF)),
            )


def positions_kernel(flags, grid, vown, voth, cosf, sinf, pos, segr):
    core = flags[0]
    vec = vectors(core, vown, voth)[0]
    h0, w0, h1, w1 = (grid[core, k // 2, k % 2] for k in range(4))
    e1 = h0 * w0
    e2 = e1 + h1 * w1

    def place(t):
        segment = (t >= e1).astype(I32) + (t >= e2).astype(I32)
        width = jnp.where(segment == 0, w0, w1).astype(F32)
        inside = (t - jnp.where(segment == 0, 0, e1)).astype(F32)
        row = jnp.floor((inside + 0.5) / width)
        column = inside - row * width
        return segment, jnp.where(segment < 2, row, 0.0), jnp.where(segment < 2, column, 0.0)

    segment, row, column = place(lax.broadcasted_iota(I32, (L, 128), 0))
    lane = lax.broadcasted_iota(I32, (L, 128), 1)
    pos[...] = jnp.where(lane == 0, column, jnp.where(lane == 1, row, segment.astype(F32)))
    t = lax.broadcasted_iota(I32, (8, L), 1)
    segr[...] = (t >= e1).astype(F32) + (t >= e2).astype(F32)

    def by_lane(start):
        parts = []
        for h in range(HEADS):
            f = vec[:, start + 32 * h : start + 32 * (h + 1)]
            parts += [f, f]
        return jnp.concatenate(parts, axis=1)

    number = lax.broadcasted_iota(I32, (16, D), 0).astype(F32)

    def look_up(which, table):
        hi, rest = split_two(table)
        mid, low = split_two(table - hi.astype(F32))
        tables = jnp.concatenate([hi, mid, low], axis=0)
        hit = (lax.broadcasted_iota(I32, (L, 48), 1) % 16).astype(F32) == which[:, :48]
        return dot(jnp.where(hit, 1.0, 0.0).astype(BF), tables)

    ax = number * by_lane(FIRST + 3 * D)
    ay = number * by_lane(FIRST + 3 * D + HALF)
    cx, sx = look_up(column, jnp.cos(ax)), look_up(column, jnp.sin(ax))
    cy, sy = look_up(row, jnp.cos(ay)), look_up(row, jnp.sin(ay))
    cosf[...] = cx * cy - sx * sy
    lane = lax.broadcasted_iota(I32, (1, D), 1)
    sign = jnp.where(lane % HEAD_DIM < HEAD_DIM // 2, -1.0, 1.0)
    sinf[...] = (sx * cy + cx * sy) * sign


def prepare_kernel(
    flags, x, cot, gain, shift, first, second, keep, send, away, across, vec, table, n
):
    core, layer, where = flags[0], flags[1], flags[2]
    for t in range(table.shape[0]):
        for way, d in ((0, 1), (1, -1)):
            at = lax.rem(where - d * (t % n) + 2 * n, n)
            table[t, way] = at * (D // (2 * n)) + way * HALF
            table[t, 2 + way] = jnp.where(2 * at < n, 2 * at, 2 * (n - at) - 1)
    for at, (mine, other) in enumerate(((x, cot), (cot, x))):

        @pl.when(layer == at)
        def _(mine=mine, other=other):
            keep[...] = mine[:, lanes(L * core, L)]
            send[...] = mine[:, lanes(L * (1 - core), L)]
            away[...] = other[:, lanes(L * core, L)]
            across[...] = other[:, lanes(L * (1 - core), L)]

    vec[:, GAIN] = gain[...]
    vec[:, SHIFT] = shift[...]
    vec[:, FIRST:SECOND] = first[...]
    vec[:, SECOND:] = second[...]


def load_angles(cos_in, sin_in, cosf, sinf, sems):
    load(cos_in, cosf, sems.at[0])
    load(sin_in, sinf, sems.at[1])


def wait_angles(cos_in, sin_in, cosf, sinf, sems):
    arrived(cos_in, cosf, sems.at[0])
    arrived(sin_in, sinf, sems.at[1])


HELD = 5


def first_kernel(
    flags, keep, got, away, across, vown, voth, pos, segr, cos_in, sin_in, own, oth, *refs,
):
    out, field_out, cosf, sinf, wa, w1, wd, field, turned, qkv, pt, rec, ml, mlt, vt, n_ref, sems = refs[HELD:]
    core, layer = flags[0], flags[1]
    w = keep.shape[0]
    for k in range(2):
        for at in range(2):

            @pl.when((core == k) & (layer == at))
            def _(k=k, at=at):
                parts = {(at, k): keep, (at, 1 - k): got, (1 - at, k): away, (1 - at, 1 - k): across}
                for s in range(4):
                    turned[w * s : w * (s + 1), :] = parts[s // 2, s % 2][...]

    field[...] = turned[...].T
    keeping = pltpu.make_async_copy(field, field_out, sems.at[14])
    keeping.start()
    @pl.when(layer == 0)
    def _():
        loads = Forward(core == 0, core, own, oth, wa, w1, wd, cos_in, sin_in, cosf, sinf, sems)
        va, vm = vectors(core, vown, voth)
        x_mid, _, _ = attention(
            field[...].astype(F32), va, wa, loads.wait, cosf, sinf, pos[:, 2:3], segr[0:1, :],
            qkv, pt, rec, ml, mlt, vt, n_ref,
        )
        x = x_mid.astype(F32)
        xh, _ = norm_parts(x)
        n = (xh * vm[:, GAIN] + vm[:, SHIFT]).astype(BF)
        loads.wait_mlp()
        acc = x + vm[:, SECOND : SECOND + D]
        first = hidden_bias(core, vm)
        ahead = dot(n, w1[0])
        for j in range(4):
            h = ahead + first[:, D * j : D * (j + 1)]
            if j < 3:
                ahead = dot(n, w1[j + 1])
            acc = acc + dot_nt(gelu(h)[0].astype(BF), wd[j])
        out[...] = acc.astype(BF)

    keeping.wait()


def hidden_bias(core, vm):
    a, b = vm[:, FIRST : FIRST + FF // 2], vm[:, FIRST + FF // 2 : SECOND]
    return jnp.concatenate([jnp.where(core == 0, a, b), jnp.where(core == 0, b, a)], axis=1)


def fetch_kernel(flags, cos_in, sin_in, own, oth, cosf, sinf, wa, w1, wd, sems):
    core = flags[0]

    @pl.when((core != 0) | (flags[1] != 0))
    def _():
        for j in range(2):
            for i in range(2 * j, 2 * j + 2):
                load_attn(core, own, oth, wa, sems, i)
                load_mlp(core, own, oth, w1, wd, sems.at[pl.ds(4, 8)], i)
            for i in range(2 * j, 2 * j + 2):
                wait_attn(own, wa, sems, i)
                wait_mlp(own, w1, wd, sems.at[pl.ds(4, 8)], i)
        load_angles(cos_in, sin_in, cosf, sinf, sems.at[pl.ds(12, 2)])
        wait_angles(cos_in, sin_in, cosf, sinf, sems.at[pl.ds(12, 2)])


def second_kernel(
    flags, field, got, got_late, vown, voth, pos, segr, *refs,
):
    (
        cosf, sinf, wa, w1, wd, xi, xm, rec, ml, dg, actm, acts, cx, act_out, main_out, tail_out, bundle,
        qkv_out, pt_out, qkv, pt, na, nm, mlt, vt, xha, xhm, kt, gm, gqt, dsum, gp, outs,
    ) = refs[HELD:]
    core, layer = flags[0], flags[1]
    va, vm = vectors(core, vown, voth)
    x = jnp.where(core == 0, got[...].astype(F32), got_late[...].astype(F32))
    x = jnp.where(layer == 0, field[...].astype(F32), x)
    xi[...] = x.astype(BF)
    x_mid, xh, inv_a = attention(
        x, va, wa, lambda what: None, cosf, sinf, pos[:, 2:3], segr[0:1, :], qkv, pt, rec, ml, mlt, vt, na
    )
    xha[...] = xh
    xm[...] = x_mid
    load(qkv, qkv_out, outs.at[7])
    load(pt, pt_out, outs.at[8])
    xh, inv_m = norm_parts(x_mid.astype(F32))
    xhm[...] = xh
    n = (xh * vm[:, GAIN] + vm[:, SHIFT]).astype(BF)
    nm[...] = n
    sides = (
        main_out, tail_out, bundle.at[:, pl.ds(2 * D, D)], bundle.at[:, pl.ds(3 * D, D)],
    )
    load(field, bundle.at[:, pl.ds(4 * D, D)], outs.at[4])
    for when, sources in ((core == 0, (na, ml, nm, nm)), (core != 0, (nm, nm, na, ml))):

        @pl.when(when)
        def _(sources=sources):
            for k, (src, dst) in enumerate(zip(sources, sides)):
                load(src, dst, outs.at[k])

    first = hidden_bias(core, vm)
    c = field[...]

    def forward(j):
        return dot(n, w1[j])

    def chunk(j, h):
        act, slope = gelu(h + first[:, D * j : D * (j + 1)])
        (actm, acts)[j // 2][:, D * (j % 2) : D * (j % 2 + 1)] = act.astype(BF)
        slope = slope.astype(BF)
        dg[:, D * j : D * (j + 1)] = slope
        return slope

    def leave():
        load(acts, bundle.at[:, pl.ds(0, 2 * D)], outs.at[5])
        load(actm, act_out, outs.at[6])

    @pl.when(layer >= 0)
    def _():
        ahead = forward(0), dot(c, wd[0])
        gn = None
        for j in range(4):
            h, ga = ahead
            if j < 3:
                ahead = forward(j + 1), dot(c, wd[j + 1])
            slope = chunk(j, h)
            part = dot_nt((ga * slope.astype(F32)).astype(BF), w1[j])
            gn = part if gn is None else gn + part
        leave()
        c_mid = norm_back(gn, xhm[...], inv_m, vm[:, GAIN], c)

        def emit(p, sl, sq, sk, grads):
            for i in range(3):
                gp[:, D * i + 128 * p : D * i + 128 * (p + 1)] = grads[i]

        attention_back(
            c_mid, wa.at[3], cosf, sinf, qkv, pt, rec, ml, kt, gm, gqt, dsum, lambda p: p, emit
        )
        gn = None
        for i in range(3):
            part = dot_nt(gp[:, D * i : D * (i + 1)], wa[i])
            gn = part if gn is None else gn + part
        cx[...] = norm_back(gn, xha[...], inv_a, va[:, GAIN], c_mid)

    for k, (src, dst) in enumerate(
        tuple((nm, side) for side in sides)
        + ((field, sides[2]), (acts, bundle.at[:, pl.ds(0, 2 * D)]), (actm, act_out), (qkv, qkv_out), (pt, pt_out))
    ):
        arrived(src, dst, outs.at[k])


def late_kernel(flags, x_two, vown, voth, actm, acts, *refs):
    xm, wd = refs[HELD + 1], refs[HELD - 1]
    keep, send = refs[-2:]
    core, layer = flags[0], flags[1]
    vm = vectors(core, vown, voth)[1]
    mid = xm[...].astype(F32)
    acc = mid + vm[:, SECOND : SECOND + D]
    for j in range(4):
        acc = acc + dot_nt((actm, acts)[j // 2][:, D * (j % 2) : D * (j % 2 + 1)], wd[j])
    acc = jnp.where(layer == 0, x_two[...].astype(F32), acc)
    keep[...] = jnp.where(core == 0, mid, acc).astype(BF)
    send[...] = jnp.where(core == 0, acc, mid).astype(BF)


def both_rows(core, keep, got, out, sems):
    return [
        pltpu.make_async_copy(src, out.at[rows_at(L * at, L), :], sems.at[k])
        for k, (src, at) in enumerate(((keep, core), (got, 1 - core)))
    ]


def norm_stats(gn, x, vec):
    xh, inv = norm_parts(x)
    vec[:, GAIN] = jnp.sum(gn * xh, axis=0, keepdims=True)
    vec[:, SHIFT] = jnp.sum(gn, axis=0, keepdims=True)
    return xh, inv


def back_kernel(
    flags, field, got, vown, voth, pos, qkv_in, pt_in, cosf, sinf, wa, w1, wd, xi, xm, rec, ml, dg,
    row_keep, row_send, c_out, vec_keep, keep_out, send_out,
    qkv, pt, gh, gp, va_grad, vm_grad, folded, vec_send, kt, gm, gqt, dsum, outs,
):
    core, layer = flags[0], flags[1]
    load(qkv_in, qkv, outs.at[3])
    load(pt_in, pt, outs.at[4])
    va, vm = vectors(core, vown, voth)
    wide = jnp.where(layer == 0, got[...].astype(F32), field[...].astype(F32))
    c = wide.astype(BF)
    c_out[...] = c
    vm_grad[:, SECOND:] = jnp.sum(wide, axis=0, keepdims=True)

    def from_output(j):
        return dot(c, wd[j])

    ahead = from_output(0)
    gn = None
    for j in range(4):
        ga = ahead
        if j < 3:
            ahead = from_output(j + 1)
        part = (ga * dg[:, D * j : D * (j + 1)].astype(F32)).astype(BF)
        start = hidden_start(core, j)
        gh[:, pl.ds(start, D)] = part
        vm_grad[:, pl.ds(pl.multiple_of(FIRST + start, 128), D)] = jnp.sum(
            part.astype(F32), axis=0, keepdims=True
        )
        part = dot_nt(part, w1[j])
        gn = part if gn is None else gn + part
    for when, dst in ((core == 0, send_out.at[pl.ds(0, L), :]), (core != 0, keep_out)):

        @pl.when(when)
        def _(dst=dst):
            load(gh, dst, outs.at[1])

    xh, inv = norm_stats(gn, xm[...].astype(F32), vm_grad)
    c = norm_back(gn, xh, inv, vm[:, GAIN], c)
    gp[:, 3 * D :] = c
    va_grad[:, FIRST + 5 * D :] = jnp.sum(c.astype(F32), axis=0, keepdims=True)
    colp, rowp = pos[:, 0:1], pos[:, 1:2]

    def emit(p, sl, sq, sk, grads):
        qr = qkv[:, sl].astype(F32) * (LN2 * HEAD_DIM**0.5)
        th = sq * qr + sk * qkv[:, D + 128 * p : D + 128 * (p + 1)].astype(F32)
        at = FIRST + 3 * D + 128 * p
        va_grad[:, at : at + 128] = jnp.sum(th * colp, axis=0, keepdims=True)
        va_grad[:, at + D : at + D + 128] = jnp.sum(th * rowp, axis=0, keepdims=True)
        for i, g in enumerate(grads):
            gp[:, D * i + 128 * p : D * i + 128 * (p + 1)] = g
            va_grad[:, FIRST + D * i + 128 * p : FIRST + D * i + 128 * (p + 1)] = jnp.sum(
                g.astype(F32), axis=0, keepdims=True
            )

    arrived(qkv_in, qkv, outs.at[3])
    arrived(pt_in, pt, outs.at[4])
    attention_back(
        c, wa.at[3], cosf, sinf, qkv, pt, rec, ml, kt, gm, gqt, dsum, lambda p: p, emit
    )
    for when, dst in ((core == 0, keep_out), (core != 0, send_out.at[pl.ds(0, L), :])):

        @pl.when(when)
        def _(dst=dst):
            load(gp, dst, outs.at[2])

    gn = None
    for i in range(3):
        part = dot_nt(gp[:, D * i : D * (i + 1)], wa[i])
        gn = part if gn is None else gn + part
    xh, inv = norm_stats(gn, xi[...].astype(F32), va_grad)
    cx = norm_back(gn, xh, inv, va[:, GAIN], c).astype(F32)
    wide = c.astype(F32)
    row_keep[...] = jnp.where(core == 0, cx, wide).astype(BF)
    row_send[...] = jnp.where(core == 0, wide, cx).astype(BF)
    fold_vector(va_grad, folded)
    a, m = packed_vector(folded), packed_vector(vm_grad)
    vec_keep[...] = jnp.where(core == 0, a, m)
    for k, part in enumerate(split_two(jnp.where(core == 0, m, a))):
        for b in range(3):
            vec_send[:, 128 * (3 * k + b) : 128 * (3 * k + b + 1)] = part[16 * b : 16 * (b + 1), :]
    vec_out = send_out.at[pl.ds(L, 16), pl.ds(0, D)]
    load(vec_send, vec_out, outs.at[0])
    main_rows = pl.ds(0, L)
    arrived(gh, send_out.at[main_rows, :], outs.at[1])
    arrived(gp, keep_out, outs.at[2])
    arrived(vec_send, vec_out, outs.at[0])


def put(stage, value, out, first, sem):
    stage[...] = value.astype(BF)
    copy = pltpu.make_async_copy(stage, out.at[:, pl.ds(first, stage.shape[1])], sem)
    copy.start()
    return copy


def gram_down_kernel(
    flags, c, c_oth, x_keep, x_oth, c_keep, c_send, act, bundle, main0, tail0, right0,
    down, left_main, left_tail, right_out, activations, c_kept, c_sent,
    c1, sides, left, right, sems, row_sems,
):
    leaving = both_rows(flags[0], x_keep, x_oth, activations, row_sems) + [
        pltpu.make_async_copy(src, dst, row_sems.at[2 + k])
        for k, (src, dst) in enumerate(((c_keep, c_kept), (c_send, c_sent)))
    ]
    for copy in leaving:
        copy.start()
    loads = (
        (bundle.at[:, pl.ds(4 * D, D)], c1), (act, right.at[pl.ds(0, L), :]),
        (bundle.at[:, pl.ds(0, 2 * D)], right.at[pl.ds(L, L), :]),
        (tail0, sides.at[0]), (bundle.at[:, pl.ds(3 * D, D)], sides.at[1]),
        (main0, sides.at[2]), (bundle.at[:, pl.ds(2 * D, D)], sides.at[3]),
        (right0, right_out.at[pl.ds(0, L), :]),
    )
    for k, (src, dst) in enumerate(loads):
        load(src, dst, sems.at[k])
    left[:, :L] = c[...].T
    arrived(*loads[0], sems.at[0])

    @pl.when(flags[1] == 0)
    def _():
        left[:, L:] = c_oth[...].T

    @pl.when(flags[1] != 0)
    def _():
        left[:, L:] = c1[...].T

    for k in range(1, 3):
        arrived(*loads[k], sems.at[k])
    down[...] = dot(left[...], right[...]).astype(BF)
    for k in range(4):
        arrived(*loads[3 + k], sems.at[3 + k])
        (left_tail, left_main)[k // 2][:, L * (k % 2) : L * (k % 2 + 1)] = sides[k].T
    arrived(*loads[7], sems.at[7])
    for copy in leaving:
        copy.wait()


def gram_head_kernel(rows, right1, down, left, vec, right0, head, tail_up, tail_down, vec_out, right):
    right[:L, :] = right0[:L, 3 * D :]
    right[L:, :] = right1[:L, 3 * D :]
    head[...] = dot(left[...], right[...]).astype(BF)
    other = [
        jnp.concatenate(
            [right1[L : L + 16, 128 * (3 * k + b) : 128 * (3 * k + b + 1)].astype(F32) for b in range(3)], axis=0
        )
        for k in range(2)
    ]
    total = (vec[...] + (other[0] + other[1])).astype(BF)
    vec_out[...] = total.astype(F32)
    for k, t in enumerate((tail_up, tail_down)):
        here = own_rows(rows, 0, k, t.shape[0])
        t[:, :D] = head[here, :]
        t[:, D : 3 * D] = down[here, :]
        t[:, 3 * D :] = total


def gram_main_kernel(rows, right1, left, vec, right_in, right, main, main_up, main_down):
    right[L:, :] = right1[:L, :]
    main[...] = dot(left[...], right[:, : 3 * D]).astype(BF)
    for k, m in enumerate((main_up, main_down)):
        m[:, : 3 * D] = main[own_rows(rows, 0, k, m.shape[0]), :]
        m[:, 3 * D :] = vec[...].astype(BF)


def own_rows(rows, t, way, r):
    return pl.ds(pl.multiple_of(rows[t, way], 16), r)


def add_kernel(t, rows, up, down, *refs, count, vector):
    parts, outs, vectors = refs[:count], refs[count : count + 2], refs[count + 2 :]
    for k, (got, out) in enumerate(zip((up, down), outs)):
        here = own_rows(rows, t, k, got.shape[0])
        at = 0
        for part in parts:
            sl = slice(at, at + part.shape[1])
            out[:, sl] = (got[:, sl].astype(F32) + part[here, :].astype(F32)).astype(BF)
            at += part.shape[1]
        if out.shape[1] > at:
            out[:, at:] = got[:, at:]
        if k < vector:
            vectors[k][...] = got[:, at : at + 128].astype(F32)


def fold_vector(va, out):
    def fold(start):
        v = va[:, start : start + D]
        w = HEAD_DIM // 2
        return jnp.concatenate(
            [v[:, 2 * w * h : 2 * w * h + w] - v[:, 2 * w * h + w : 2 * w * (h + 1)] for h in range(HEADS)],
            axis=1,
        )

    at = FIRST + 3 * D
    out[:, :at] = va[:, :at]
    out[:, at : at + HALF] = fold(at)
    out[:, at + HALF : SECOND] = fold(at + D)
    out[:, SECOND:] = va[:, at + 2 * D :]


def packed_vector(ref):
    rows = [ref[:, 128 * k : 128 * (k + 1)] for k in range(VECTOR // 128)]
    rows += [jnp.zeros((1, 128), F32)] * (PACKED[0] - len(rows))
    return jnp.concatenate(rows, axis=0)


def sum_vectors(table, vectors, slots, outs):
    n = len(vectors)
    if table is None:
        total = vectors[0][...]
    else:
        slots[table[0, 2]] = vectors[0][...]
        for k in range(1, n):
            t, way = (k + 1) // 2, (k + 1) % 2
            slots[table[t, 2 + way]] = vectors[k][...]
        total = slots[0]
        for k in range(1, n):
            total = total + slots[k]
    at = 0
    for out in outs:
        for k in range(out.shape[1] // 128):
            out[:, 128 * k : 128 * (k + 1)] = total[at + k : at + k + 1, :]
        at += out.shape[1] // 128


def place_kernel(spots, whole, flags, rows, *refs):
    count, pair, vectors, into = whole
    ins, refs = refs[: 2 * count + pair + vectors], refs[2 * count + pair + vectors + into :]
    out, buf, sems = refs[0], refs[-3], refs[-2]
    copies = []
    if pair:
        copies += both_rows(flags[0], ins[2 * count], ins[2 * count + 1], refs[1], refs[-1])
        copies[0].start()
        copies[1].start()
    r = ins[0].shape[0]
    for k in range(count):
        there = pl.ds(r * k, r)
        buf[there, : 3 * D] = ins[2 * k][...].astype(F32)
        buf[there, 3 * D :] = ins[2 * k + 1][...].astype(F32)
        copy = pltpu.make_async_copy(
            buf.at[there, :], out.at[own_rows(rows, *spots[k], r), :], sems.at[k]
        )
        copy.start()
        copies.append(copy)
    if vectors:
        outs = refs[1 + pair // 2 : 5 + pair // 2]
        sum_vectors(rows if vectors > 1 else None, ins[2 * count + pair :], refs[-4], outs)
    for copy in copies:
        copy.wait()


SMEM = pl.BlockSpec(memory_space=pltpu.SMEM)
VS = pl.BlockSpec(memory_space=pltpu.VMEM)
HBM = pl.BlockSpec(memory_space=pltpu.HBM)
ANY = pl.BlockSpec(memory_space=pl.ANY)


def sds(shape, dtype=BF):
    return jax.ShapeDtypeStruct(shape, dtype)


def call(kernel, name, in_specs, outs, scratch, flops, nbytes, limit=58, out_specs=None, aliases=None):
    return pl.pallas_call(
        kernel,
        name=name,
        in_specs=in_specs,
        out_specs=[VS] * len(outs) if out_specs is None else out_specs,
        out_shape=outs,
        scratch_shapes=scratch,
        input_output_aliases={} if aliases is None else aliases,
        compiler_params=pltpu.CompilerParams(vmem_limit_bytes=limit * MIB),
        cost_estimate=pl.CostEstimate(flops=flops, bytes_accessed=nbytes, transcendentals=0),
    )


ATTN_W = [VM((4, D, D), BF)]
ANGLES = [VM((L, D), F32), VM((L, D), F32)]
MLP_W = [VM((4, D, D), BF), VM((4, D, D), BF)]
BACK_S = [VM((D, L), BF), VM((L, D), BF), VM((2, 128, L), F32), VM((16, L), F32)]


def in_vmem(a):
    return pltpu.with_memory_space_constraint(a, pltpu.VMEM)


def in_hbm(a):
    return pltpu.with_memory_space_constraint(a, pltpu.HBM)


def row(width=D):
    return VM((L, width), BF)


def row_out(width=D):
    return pltpu.HBM((L, width), BF)


def prepare(flags, n, x, cot, *vecs):
    out = VM((x.shape[0], L), BF)

    def kernel(*refs):
        prepare_kernel(*refs, n)

    table = pltpu.HBM((2 * n if n <= 16 else 1, 4), I32)
    return call(
        kernel, "prepare", [SMEM] + [VS] * 6, [out] * 4 + [pltpu.HBM((1, VECTOR), F32), table], [], 1000,
        int(1e6), 8, out_specs=[VS] * 5 + [SMEM],
    )(flags, *(in_hbm(a) for a in (x, cot) + vecs))


def positions(flags, grid, own, oth):
    hbm = pltpu.HBM
    return call(
        positions_kernel, "positions", [SMEM, SMEM, VS, VS],
        [hbm((L, D), F32), hbm((L, D), F32), hbm((L, 128), F32), hbm((8, L), F32)],
        [], int(1e8), int(3e6), 56,
    )(flags, grid, own, oth)


def fetch(flags, *sources):
    return call(
        fetch_kernel, "fetch", [SMEM] + [HBM] * 4, ANGLES + ATTN_W + MLP_W, [DMA((14,))], int(1e8), int(17e6), 28
    )(flags, *sources)


def first_pass(held, *a):
    results = call(
        first_kernel, "first_pass", [SMEM] + [VS] * 8 + [HBM] * 4 + [VS] * HELD,
        [row(), row_out()] + ANGLES + ATTN_W + MLP_W,
        [row(), VM((D, L), BF), row(3 * D), VM((HEADS, L, L), BF), VM((16, L), F32), row(), VM((D, L), BF),
         VM((D, L), BF), row(), DMA((15,))],
        int(8e9), int(20e6), 28, out_specs=[VS, HBM] + [VS] * HELD,
        aliases={len(a) + k: 2 + k for k in range(HELD)},
    )(*a, *(in_vmem(x) for x in held))
    return results[0], results[1], results[2:]


SAVED = [VM((L, D), BF), VM((L, D), BF), VM((16, L), F32), VM((L, D), BF), VM((L, FF), BF)]
HEAD_S = [VM((L, 3 * D), BF), VM((HEADS, L, L), BF)]


def second_pass(held, *a):
    outs = [
        row_out(FF // 2), row_out(), row_out(), row_out(5 * D), row_out(3 * D), pltpu.HBM((HEADS, L, L), BF)
    ]
    resident = ANGLES + ATTN_W + MLP_W + SAVED
    results = call(
        second_kernel, "second_pass", [SMEM] + [VS] * (7 + HELD),
        resident + [row(FF // 2), row(FF // 2), row()] + outs,
        HEAD_S + [row(), row(), VM((D, L), BF), VM((D, L), BF), VM((L, D), F32), VM((L, D), F32)]
        + BACK_S + [row(3 * D), DMA((9,))],
        int(18e9), int(20e6), 28, out_specs=[VS] * (len(resident) + 3) + [HBM] * len(outs),
        aliases={len(a) + k: k for k in range(HELD)},
    )(*a, *(in_vmem(x) for x in held))
    n = len(resident)
    return results[:n], results[n : n + 2], results[n + 2], results[n + 3 :]


def late_pass(held, *a):
    results = call(
        late_kernel, "late_pass", [SMEM] + [VS] * (len(a) - 1 + len(held)),
        ANGLES + ATTN_W + MLP_W + SAVED + [sds((L, D))] * 2, [], int(2e9), int(5e6), 28,
        aliases={len(a) + k: k for k in range(len(held))},
    )(*a, *(in_vmem(x) for x in held))
    return results[: len(held)], results[len(held) :]


def back_pass(held, *a):
    return call(
        back_kernel, "back_pass", [SMEM] + [VS] * 5 + [HBM] * 2 + [VS] * len(held),
        [row(), row(), row(), VM(PACKED, F32), row_out(FF), pltpu.HBM((L + 16, FF), BF)],
        HEAD_S
        + [row(FF), row(FF), VM((1, FIRST + 6 * D), F32), VM((1, VECTOR), F32), VM((1, VECTOR), F32),
           VM((16, D), BF)]
        + BACK_S + [DMA((5,))],
        int(10e9), int(15e6), 28, out_specs=[VS] * 4 + [HBM] * 2,
    )(*a, *(in_vmem(x) for x in held))


def gram_down(*a):
    square = VM((D, 2 * L), BF)
    return call(
        gram_down_kernel, "gram_down", [SMEM] + [VS] * 6 + [HBM, ANY] + [HBM] * 3,
        [VM((D, 2 * D), BF), square, square, VM((2 * L, FF), BF), pltpu.HBM((2 * L, D), BF), row_out(), row_out()],
        [row(), VM((4, L, D), BF), square, VM((2 * L, 2 * D), BF), DMA((8,)), DMA((4,))], int(2e9), int(8e6), 20,
        out_specs=[VS] * 4 + [HBM] * 3,
    )(*a)


def gram_head(rows, r, *a):
    wide = VM((r, 3 * D + 128), BF)
    return call(
        gram_head_kernel, "gram_head", [SMEM] + [VS] * 5, [VM((D, D), BF), wide, wide, VM(PACKED, F32)],
        [VM((2 * L, D), BF)], int(1e9), int(5e6), 12,
    )(rows, *a)


def gram_main(rows, r, *a):
    wide = VM((r, 3 * D + 128), BF)
    return call(
        gram_main_kernel, "gram_main", [SMEM] + [VS] * 4,
        [VM((2 * L, FF), BF), VM((D, 3 * D), BF), wide, wide], [], int(6e9), int(12e6), 20, aliases={4: 0},
    )(rows, *a)[1:]


def add(t, rows, up, down, parts, vector, wide):
    count = len(parts)

    def kernel(*refs):
        add_kernel(t, *refs, count=count, vector=vector)

    width = sum(p.shape[1] for p in parts)
    out = VM((up.shape[0], width + (128 if wide else 0)), BF)
    results = call(
        kernel, "add", [SMEM] + [VS] * (2 + count), [out, out] + [VM(PACKED, F32)] * vector, [], 1000,
        int(1e6), 4,
    )(rows, in_vmem(up), in_vmem(down), *(in_vmem(p) for p in parts))
    return results[:2], results[2:]


def place(flags, spots, rows, shards, total, pair=(), vectors=()):
    r, count = shards[0].shape[0], len(shards) // 2
    into = [] if total is None else [total]
    whole = count, len(pair), len(vectors), len(into)

    def kernel(*refs):
        place_kernel(spots, whole, *refs)

    outs = [pltpu.HBM((D, 6 * D), F32)]
    outs += [pltpu.HBM((2 * L, D), BF)] if pair else []
    outs += [sds((1, w), F32) for w in (D, D, FF, D)] if vectors else []
    given = len(shards) + len(pair) + len(vectors)
    return call(
        kernel, "place", [SMEM, SMEM] + [VS] * given + [HBM] * len(into), outs,
        [VM((max(len(vectors), 1),) + PACKED, F32), VM((r * count, 6 * D), F32), DMA((count,)), DMA((2,))], 1000,
        int(2e7), 24, out_specs=[HBM] * (2 if pair else 1) + ([VS] * 4 if vectors else []),
        aliases={given + 2: 0} if into else {},
    )(flags, rows, *shards, *pair, *vectors, *into)


def core_swap(a):
    return lax.ppermute(a, "section", [(0, 1), (1, 0), (2, 3), (3, 2)])


def after(value, first):
    return lax.optimization_barrier((value, first))[0]


class Cycle:
    def __init__(self, rows):
        self.n = n = lax.axis_size("dp")
        self.r = D // (2 * n)
        order = list(range(0, n, 2)) + list(range(n - 1, 0, -2))
        self.pairs = [[(order[k], order[(k + d) % n]) for k in range(n)] for d in (1, -1)]
        self.rows = rows

    def placed(self, k):
        return 2 * self.n - 1 if k == 0 else self.n + k - 1


class Chain:
    def __init__(self, cycle, parts, cur, carries=False):
        self.cycle, self.parts, self.cur, self.carries = cycle, parts, cur, carries
        self.t = 0
        self.shards = []
        self.vectors = []

    def step(self, token):
        c = self.cycle
        got = [lax.ppermute(a, "dp", p) for a, p in zip(self.cur, c.pairs)]
        got = after(got, token)
        self.t += 1
        if self.t < c.n:
            t = self.t
            ways = int(t <= c.n // 2) + int(t <= (c.n - 1) // 2) if self.carries else 0
            self.cur, came = add(t, c.rows, *got, self.parts, ways, t < c.n // 2)
            self.vectors += came
        else:
            self.cur = got
        if self.t >= c.n - 1:
            self.shards.append(self.cur)
        return self.cur


def small_ring():
    return lax.axis_size("dp") <= 16


def summed(flags, rows, main, tail, token, pair, vector):
    if not small_ring():
        chains, vector = lax.psum([main, tail], "dp"), lax.psum(vector, "dp")
        return place(flags, [(0, 0)], rows, chains, None, pair, [vector])
    cycle = main.cycle
    n = cycle.n
    total, placed = None, 0
    results = {}
    while main.t < 2 * n - 2:
        token = tail.step(token)
        if total is not None:
            token = (token, total)
        token = main.step(token)
        whole = len(main.shards)
        if whole > placed and (whole % 2 == 0 or whole == n - 1):
            spots, shards = [], []
            for k in range(placed, whole):
                for way in range(2):
                    spots.append((cycle.placed(k), way))
                    shards += [main.shards[k][way], tail.shards[k][way]]
            now, then = placed == 0, "vectors" not in results and whole >= min(4, n)
            total, *more = place(
                flags, spots, cycle.rows, shards, total, pair if now else (), [vector] + main.vectors if then else ()
            )
            if now:
                results["rows"] = more[0]
            if then:
                results["vectors"] = more
            placed = whole
    return total, results["rows"], *results["vectors"]


def body(
    block_input, cotangent, grid_sizes, section_weight, norm_gain, norm_bias, first_vector, second_vector
):
    section = lax.axis_index("section")
    core = section % 2
    n = lax.axis_size("dp")
    i = lax.axis_index("dp")
    where = jnp.where(i % 2 == 0, i // 2, n - 1 - i // 2)
    flags = in_hbm(jnp.stack([core, section // 2, where]).astype(I32))
    first_layer = section < 2

    keep, send, away, across, vown, rows = prepare(
        flags, n, block_input.T, cotangent.T, norm_gain, norm_bias, first_vector, second_vector
    )
    if n % 2 == 0:
        voth = lax.ppermute(
            vown, ("section", "dp"), [(n * s + d, n * (s ^ 1) + (d ^ 1)) for s in range(4) for d in range(n)]
        )
    else:
        voth = core_swap(vown)
    r = D // (2 * n) if small_ring() else PACKED[0]
    vown, voth, rows = in_hbm(vown), in_hbm(voth), in_hbm(rows)
    got = core_swap(send)
    away = lax.ppermute(away, "section", [(0, 2), (1, 3), (2, 0), (3, 1)])
    across = lax.ppermute(across, "section", [(0, 3), (1, 2), (2, 1), (3, 0)])
    own = in_hbm(section_weight[0])
    oth = in_hbm(core_swap(section_weight[0]))
    cosf, sinf, pos, segr = (in_hbm(a) for a in positions(flags, grid_sizes, vown, voth))

    held = fetch(flags, cosf, sinf, own, oth)
    x_two, field, held = first_pass(
        held, flags, keep, got, away, across, vown, voth, pos, segr, cosf, sinf, own, oth
    )
    field = in_hbm(field)
    x_got, x_late = (lax.ppermute(x_two, "section", [pair]) for pair in ((0, 2), (1, 3)))
    held, active, c_two, (act_mine, main_left, tail_left, bundle, qkv, pt) = second_pass(
        held, flags, field, x_got, x_late, vown, voth, pos, segr
    )
    act_mine, main_left, tail_left = (in_hbm(a) for a in (act_mine, main_left, tail_left))
    c_got = lax.ppermute(c_two, "section", [(2, 0), (3, 1)])
    held, (x_keep, x_send) = late_pass(held, flags, x_two, vown, voth, *(in_vmem(a) for a in active))
    c_got = after(c_got, x_keep)
    bundle = core_swap(after(bundle, c_got))
    x_oth = core_swap(after(x_send, c_got))

    c_keep, c_send, c_out, vec, right, right_send = back_pass(
        held, flags, field, c_got, vown, voth, pos, in_hbm(qkv), in_hbm(pt)
    )
    c_oth = core_swap(c_got)
    right_oth = core_swap(after(right_send, (c_oth, bundle, x_oth)))
    down, left_main, left_tail, right, activations, c_keep, c_send = gram_down(
        flags, c_out, c_oth, x_keep, x_oth, in_vmem(c_keep), in_vmem(c_send), act_mine, bundle, main_left, tail_left, in_hbm(right)
    )
    head, *tail_first, vec = gram_head(rows, r, right_oth, down, left_tail, vec, right)
    if small_ring():
        cycle = Cycle(rows)
        tail = Chain(cycle, [head, down], tail_first)
    else:
        tail = jnp.concatenate([head, down], axis=1)
    main, *main_first = gram_main(rows, r, right_oth, left_main, vec, right)
    if small_ring():
        main = Chain(cycle, [main], main_first, True)
        token = main.cur
    else:
        token = main
    weight_grad, input_grads, *vectors = summed(
        flags, rows, main, tail, token, (c_keep, core_swap(after(c_send, token))), vec
    )
    return (
        activations[None],
        input_grads[None],
        weight_grad[None],
        *vectors,
    )


def solution(mesh):
    in_specs = (
        P("dp", "section"),
        P("dp", "section"),
        P("dp", None, None),
        P("section", None, None),
        P("section", None),
        P("section", None),
        P("section", None),
        P("section", None),
    )
    out_specs = (
        P("section", "dp", None),
        P("section", "dp", None),
        P("section", None, None),
        P("section", None),
        P("section", None),
        P("section", None),
        P("section", None),
    )
    return jax.shard_map(body, mesh=mesh, in_specs=in_specs, out_specs=out_specs, check_vma=False)
```

```python
import jax
import jax.numpy as jnp
from jax import lax
from jax.experimental import pallas as pl
from jax.experimental.pallas import tpu as pltpu
from jax.sharding import PartitionSpec as P

D = 768
HEADS = 12
HEAD_DIM = 64
FF = 3072
L = 384
HALF = D // 2
F32 = jnp.float32
BF = jnp.bfloat16
I32 = jnp.int32
NT = (((1,), (1,)), ((), ()))
TN = (((0,), (0,)), ((), ()))
VM = pltpu.VMEM
DMA = pltpu.SemaphoreType.DMA
MIB = 1024 * 1024
LN2 = 0.6931471805599453
GAIN, SHIFT = slice(0, D), slice(D, 2 * D)
FIRST, SECOND = 2 * D, 2 * D + FF
VECTOR = 3 * D + FF
PACKED = (48, 128)


def dot(a, b):
    return jnp.dot(a, b, preferred_element_type=F32)


def dot_nt(a, b):
    return lax.dot_general(a, b, NT, preferred_element_type=F32)


def dot_tn(a, b):
    return lax.dot_general(a, b, TN, preferred_element_type=F32)


def norm_parts(x):
    center = x - jnp.mean(x, axis=-1, keepdims=True)
    inv = lax.rsqrt(jnp.mean(center * center, axis=-1, keepdims=True) + 1e-06)
    return center * inv, inv


def swap_halves(a):
    lane = lax.broadcasted_iota(I32, (1, 128), 1)
    first = (lane % HEAD_DIM) < HEAD_DIM // 2
    out = []
    for i in range(a.shape[1] // 128):
        s = a[:, 128 * i : 128 * (i + 1)]
        out.append(jnp.where(first, pltpu.roll(s, 96, 1), pltpu.roll(s, 32, 1)))
    return jnp.concatenate(out, axis=1) if len(out) > 1 else out[0]


def lanes(start, size):
    if isinstance(start, int):
        return slice(start, start + size)
    return pl.ds(pl.multiple_of(start, 128), size)


def rows_at(start, size):
    if isinstance(start, int):
        return slice(start, start + size)
    return pl.ds(pl.multiple_of(start, size), size)


def cols(start, size):
    return (slice(None), pl.ds(start, size))


def pick(flag, want, own, oth, src, dst, sem):
    @pl.when(flag == want)
    def _():
        pltpu.make_async_copy(own.at[src], dst, sem).start()

    @pl.when(flag != want)
    def _():
        pltpu.make_async_copy(oth.at[src], dst, sem).start()


def load(src, dst, sem):
    pltpu.make_async_copy(src, dst, sem).start()


def arrived(src, dst, sem):
    pltpu.make_async_copy(src, dst, sem).wait()


def load_attn(core, own, oth, wa, sems, i):
    pick(core, 0, own, oth, cols(D * i, D), wa.at[i], sems.at[i])


def wait_attn(own, wa, sems, i):
    arrived(own.at[cols(D * i, D)], wa.at[i], sems.at[i])


def hidden_start(core, j):
    return pl.multiple_of(FF // 2 * ((core + j // 2) % 2) + D * (j % 2), 128)


def load_mlp(core, own, oth, w1, wd, sems, j):
    pick(core, 1, own, oth, (slice(None), pl.ds(hidden_start(core, j), D)), w1.at[j], sems.at[j])
    load((own if j < 2 else oth).at[cols(FF + D * (j % 2), D)], wd.at[j], sems.at[4 + j])


class Forward:
    def __init__(self, on_the_way, core, own, oth, wa, w1, wd, sems):
        self.attn = core, own, oth, wa, sems
        self.mlp = core, own, oth, w1, wd, sems.at[pl.ds(4, 8)]
        self.own, self.wa, self.sems, self.on_the_way = own, wa, sems, on_the_way

        @pl.when(on_the_way)
        def _():
            load_attn(*self.attn, 0)
            load_attn(*self.attn, 1)

        @pl.when(jnp.logical_not(on_the_way))
        def _():
            for i in range(4):
                load_attn(*self.attn, i)
                load_mlp(*self.mlp, i)
                wait_attn(own, wa, sems, i)
                wait_mlp(own, w1, wd, self.mlp[-1], i)

    def wait(self, i):
        @pl.when(self.on_the_way)
        def _():
            wait_attn(self.own, self.wa, self.sems, i)
            if i < 2:
                load_attn(*self.attn, i + 2)
            elif i == 2:
                for j in range(4):
                    load_mlp(*self.mlp, j)

    def wait_mlp(self):
        core, own, oth, w1, wd, sems = self.mlp

        @pl.when(self.on_the_way)
        def _():
            for j in range(4):
                wait_mlp(own, w1, wd, sems, j)


def wait_mlp(own, w1, wd, sems, j):
    if w1 is not None:
        arrived(own.at[cols(0, D)], w1.at[j], sems.at[j])
    arrived(own.at[cols(0, D)], wd.at[j], sems.at[4 + j])


def vectors(core, own, oth):
    a, b = own[...], oth[...]
    return jnp.where(core == 0, a, b), jnp.where(core == 0, b, a)


def attention(x, vec, wa, wait, cosf, sinf, segc, segr, qkv, pt, rec, ml, mlt, vt, n_ref):
    xh, inv = norm_parts(x)
    n = (xh * vec[:, GAIN] + vec[:, SHIFT]).astype(BF)
    n_ref[...] = n
    for i in range(3):
        wait(i)
        part = dot(n, wa[i]) + vec[:, FIRST + D * i : FIRST + D * (i + 1)]
        if i < 2:
            part = part * cosf[...] + swap_halves(part) * sinf[...]
        if i == 0:
            part = part * (HEAD_DIM**-0.5 / LN2)
        qkv[:, D * i : D * (i + 1)] = part.astype(BF)
    vt[...] = qkv[:, 2 * D : 3 * D].T
    same = segc == segr
    lane = lax.broadcasted_iota(I32, (1, 128), 1)

    def score(h):
        p = 128 * (h // 2)
        keys = jnp.where((lane // HEAD_DIM) == h % 2, qkv[:, D + p : D + p + 128], BF(0))
        return dot_nt(keys, qkv[:, p : p + 128])

    ahead = score(0)
    for h in range(HEADS):
        st = ahead
        if h + 1 < HEADS:
            ahead = score(h + 1)
        st = jnp.where(same, st, -1e30)
        e = jnp.exp2(st - jnp.max(st, axis=0, keepdims=True))
        r = 1.0 / jnp.sum(e, axis=0, keepdims=True)
        rec[h : h + 1, :] = r
        e = e.astype(BF)
        pt[h] = e
        here = slice(HEAD_DIM * h, HEAD_DIM * (h + 1))
        mlt[here, :] = (dot(vt[here, :], e) * r).astype(BF)
    ml[...] = mlt[...].T
    wait(3)
    out = x + dot(ml[...], wa[3]) + vec[:, SECOND : SECOND + D]
    return out.astype(BF), xh, inv


C0 = 0.7978845608028654
C1 = 0.044715


def gelu(h):
    h2 = h * h
    t = jnp.tanh(C0 * (h + C1 * h * h2))
    half = 0.5 * (1.0 + t)
    return h * half, half + (0.5 * C0) * h * (1.0 - t * t) * (1.0 + (3.0 * C1) * h2)


def norm_back(gn, xh, inv, gain, c):
    u = gn * gain
    gx = inv * (
        u - jnp.mean(u, axis=-1, keepdims=True) - xh * jnp.mean(u * xh, axis=-1, keepdims=True)
    )
    return (c.astype(F32) + gx).astype(BF)


def head_select():
    head = lax.broadcasted_iota(I32, (16, D), 0)
    lane = lax.broadcasted_iota(I32, (16, D), 1)
    return jnp.where(lane // HEAD_DIM == head, 1.0, 0.0).astype(BF)


def split_two(a):
    hi = a.astype(BF)
    return hi, (a - hi.astype(F32)).astype(BF)


def attention_back(c, wo, cosf, sinf, qkv, pt, rec, ml, kt, gm, gqt, dsum, pair_of, emit):
    kt[...] = qkv[:, D : 2 * D].T
    gm_wide = dot_nt(c, wo[...])
    sel = head_select()
    hi, lo = split_two(gm_wide * ml[...].astype(F32))
    row = lax.broadcasted_iota(I32, (16, L), 0)
    recs = jnp.where(row < HEADS, rec[...], 0.0)
    dsum[...] = (dot_nt(sel, hi) + dot_nt(sel, lo)) * recs
    hi, lo = split_two(recs)
    gm[...] = (gm_wide * (dot_tn(hi, sel) + dot_tn(lo, sel))).astype(BF)
    lane = lax.broadcasted_iota(I32, (1, 128), 1)

    def spot(h):
        return lanes(128 * pair_of(h // 2), 128), (lane // HEAD_DIM) == h % 2

    def from_values(h):
        sl, here = spot(h)
        values = qkv[:, lanes(2 * D + 128 * pair_of(h // 2), 128)]
        return dot_nt(jnp.where(here, values, BF(0)), gm[:, sl])

    ahead = from_values(0)
    for h in range(HEADS):
        gpt = ahead
        if h + 1 < HEADS:
            ahead = from_values(h + 1)
        sl, here = spot(h)
        head = 2 * pair_of(h // 2) + h % 2
        e = pt[head]
        gvh = dot(e, jnp.where(here, gm[:, sl], BF(0)))
        gst = (e.astype(F32) * (gpt - dsum[rows_at(head, 1), :])).astype(BF)
        gkh = dot(gst, jnp.where(here, qkv[:, sl], BF(0)))
        kth = kt[rows_at(HEAD_DIM * head, HEAD_DIM), :]
        gqt[h // 2 % 2, HEAD_DIM * (h % 2) : HEAD_DIM * (h % 2 + 1), :] = dot(kth, gst)
        gv = gvh if h % 2 == 0 else gv + gvh
        gk = gkh if h % 2 == 0 else gk + gkh
        if h % 2 == 1:
            gq = gqt[h // 2 % 2].T * (HEAD_DIM**-0.5)
            gk = gk * LN2
            cs, sn = cosf[:, sl], sinf[:, sl]
            sq, sk = swap_halves(gq), swap_halves(gk)
            emit(
                h // 2, sl, sq, sk,
                ((gq * cs - sq * sn).astype(BF), (gk * cs - sk * sn).astype(BF), gv.astype(BF)),
            )


def positions_kernel(flags, grid, vown, voth, cosf, sinf, pos, segr):
    core = flags[0]
    vec = vectors(core, vown, voth)[0]
    h0, w0, h1, w1 = (grid[core, k // 2, k % 2] for k in range(4))
    e1 = h0 * w0
    e2 = e1 + h1 * w1

    def place(t):
        segment = (t >= e1).astype(I32) + (t >= e2).astype(I32)
        width = jnp.where(segment == 0, w0, w1).astype(F32)
        inside = (t - jnp.where(segment == 0, 0, e1)).astype(F32)
        row = jnp.floor((inside + 0.5) / width)
        column = inside - row * width
        return segment, jnp.where(segment < 2, row, 0.0), jnp.where(segment < 2, column, 0.0)

    segment, row, column = place(lax.broadcasted_iota(I32, (L, 128), 0))
    lane = lax.broadcasted_iota(I32, (L, 128), 1)
    pos[...] = jnp.where(lane == 0, column, jnp.where(lane == 1, row, segment.astype(F32)))
    t = lax.broadcasted_iota(I32, (8, L), 1)
    segr[...] = (t >= e1).astype(F32) + (t >= e2).astype(F32)

    def by_lane(start):
        parts = []
        for h in range(HEADS):
            f = vec[:, start + 32 * h : start + 32 * (h + 1)]
            parts += [f, f]
        return jnp.concatenate(parts, axis=1)

    number = lax.broadcasted_iota(I32, (16, D), 0).astype(F32)

    def look_up(which, table):
        hi, rest = split_two(table)
        mid, low = split_two(table - hi.astype(F32))
        tables = jnp.concatenate([hi, mid, low], axis=0)
        hit = (lax.broadcasted_iota(I32, (L, 48), 1) % 16).astype(F32) == which[:, :48]
        return dot(jnp.where(hit, 1.0, 0.0).astype(BF), tables)

    ax = number * by_lane(FIRST + 3 * D)
    ay = number * by_lane(FIRST + 3 * D + HALF)
    cx, sx = look_up(column, jnp.cos(ax)), look_up(column, jnp.sin(ax))
    cy, sy = look_up(row, jnp.cos(ay)), look_up(row, jnp.sin(ay))
    cosf[...] = cx * cy - sx * sy
    lane = lax.broadcasted_iota(I32, (1, D), 1)
    sign = jnp.where(lane % HEAD_DIM < HEAD_DIM // 2, -1.0, 1.0)
    sinf[...] = (sx * cy + cx * sy) * sign


def prepare_kernel(
    flags, x, cot, gain, shift, first, second, keep, send, away, across, vec, table, n
):
    core, layer, where = flags[0], flags[1], flags[2]
    for t in range(table.shape[0]):
        for way, d in ((0, 1), (1, -1)):
            at = lax.rem(where - d * (t % n) + 2 * n, n)
            table[t, way] = at * (D // (2 * n)) + way * HALF
            table[t, 2 + way] = jnp.where(2 * at < n, 2 * at, 2 * (n - at) - 1)
    for at, (mine, other) in enumerate(((x, cot), (cot, x))):

        @pl.when(layer == at)
        def _(mine=mine, other=other):
            keep[...] = mine[:, lanes(L * core, L)]
            send[...] = mine[:, lanes(L * (1 - core), L)]
            away[...] = other[:, lanes(L * core, L)]
            across[...] = other[:, lanes(L * (1 - core), L)]

    vec[:, GAIN] = gain[...]
    vec[:, SHIFT] = shift[...]
    vec[:, FIRST:SECOND] = first[...]
    vec[:, SECOND:] = second[...]


HELD = 5


def first_kernel(
    flags, keep, got, away, across, vown, voth, pos, segr, own, oth, cos_in, sin_in,
    out, field_out, cosf, sinf, wa, w1, wd, field, turned, qkv, pt, rec, ml, mlt, vt, n_ref, sems,
):
    core, layer = flags[0], flags[1]
    loads = Forward((core == 0) & (layer == 0), core, own, oth, wa, w1, wd, sems)
    w = keep.shape[0]
    for k in range(2):
        for at in range(2):

            @pl.when((core == k) & (layer == at))
            def _(k=k, at=at):
                parts = {(at, k): keep, (at, 1 - k): got, (1 - at, k): away, (1 - at, 1 - k): across}
                for s in range(4):
                    turned[w * s : w * (s + 1), :] = parts[s // 2, s % 2][...]

    field[...] = turned[...].T
    keeping = pltpu.make_async_copy(field, field_out, sems.at[12])
    keeping.start()
    @pl.when(layer == 0)
    def _():
        va, vm = vectors(core, vown, voth)
        x_mid, _, _ = attention(
            field[...].astype(F32), va, wa, loads.wait, cosf, sinf, pos[:, 2:3], segr[0:1, :],
            qkv, pt, rec, ml, mlt, vt, n_ref,
        )
        x = x_mid.astype(F32)
        xh, _ = norm_parts(x)
        n = (xh * vm[:, GAIN] + vm[:, SHIFT]).astype(BF)
        loads.wait_mlp()
        acc = x + vm[:, SECOND : SECOND + D]
        first = hidden_bias(core, vm)
        ahead = dot(n, w1[0])
        for j in range(4):
            h = ahead + first[:, D * j : D * (j + 1)]
            if j < 3:
                ahead = dot(n, w1[j + 1])
            acc = acc + dot_nt(gelu(h)[0].astype(BF), wd[j])
        out[...] = acc.astype(BF)

    keeping.wait()


def hidden_bias(core, vm):
    a, b = vm[:, FIRST : FIRST + FF // 2], vm[:, FIRST + FF // 2 : SECOND]
    return jnp.concatenate([jnp.where(core == 0, a, b), jnp.where(core == 0, b, a)], axis=1)


def second_kernel(
    flags, field, got, got_late, vown, voth, pos, segr, *refs,
):
    (
        cosf, sinf, wa, w1, wd, xi, xm, rec, ml, dg, actm, acts, cx, act_out, main_out, tail_out, bundle,
        qkv_out, pt_out, qkv, pt, na, nm, mlt, vt, xha, xhm, kt, gm, gqt, dsum, gp, outs,
    ) = refs[HELD:]
    core, layer = flags[0], flags[1]
    va, vm = vectors(core, vown, voth)
    x = jnp.where(core == 0, got[...].astype(F32), got_late[...].astype(F32))
    x = jnp.where(layer == 0, field[...].astype(F32), x)
    xi[...] = x.astype(BF)
    x_mid, xh, inv_a = attention(
        x, va, wa, lambda what: None, cosf, sinf, pos[:, 2:3], segr[0:1, :], qkv, pt, rec, ml, mlt, vt, na
    )
    xha[...] = xh
    xm[...] = x_mid
    load(qkv, qkv_out, outs.at[7])
    load(pt, pt_out, outs.at[8])
    xh, inv_m = norm_parts(x_mid.astype(F32))
    xhm[...] = xh
    n = (xh * vm[:, GAIN] + vm[:, SHIFT]).astype(BF)
    nm[...] = n
    sides = (
        main_out, tail_out, bundle.at[:, pl.ds(2 * D, D)], bundle.at[:, pl.ds(3 * D, D)],
    )
    load(field, bundle.at[:, pl.ds(4 * D, D)], outs.at[4])
    for when, sources in ((core == 0, (na, ml, nm, nm)), (core != 0, (nm, nm, na, ml))):

        @pl.when(when)
        def _(sources=sources):
            for k, (src, dst) in enumerate(zip(sources, sides)):
                load(src, dst, outs.at[k])

    first = hidden_bias(core, vm)
    c = field[...]

    def forward(j):
        return dot(n, w1[j])

    def chunk(j, h):
        act, slope = gelu(h + first[:, D * j : D * (j + 1)])
        (actm, acts)[j // 2][:, D * (j % 2) : D * (j % 2 + 1)] = act.astype(BF)
        slope = slope.astype(BF)
        dg[:, D * j : D * (j + 1)] = slope
        return slope

    def leave():
        load(acts, bundle.at[:, pl.ds(0, 2 * D)], outs.at[5])
        load(actm, act_out, outs.at[6])

    @pl.when(layer >= 0)
    def _():
        ahead = forward(0), dot(c, wd[0])
        gn = None
        for j in range(4):
            h, ga = ahead
            if j < 3:
                ahead = forward(j + 1), dot(c, wd[j + 1])
            slope = chunk(j, h)
            part = dot_nt((ga * slope.astype(F32)).astype(BF), w1[j])
            gn = part if gn is None else gn + part
        leave()
        c_mid = norm_back(gn, xhm[...], inv_m, vm[:, GAIN], c)

        def emit(p, sl, sq, sk, grads):
            for i in range(3):
                gp[:, D * i + 128 * p : D * i + 128 * (p + 1)] = grads[i]

        attention_back(
            c_mid, wa.at[3], cosf, sinf, qkv, pt, rec, ml, kt, gm, gqt, dsum, lambda p: p, emit
        )
        gn = None
        for i in range(3):
            part = dot_nt(gp[:, D * i : D * (i + 1)], wa[i])
            gn = part if gn is None else gn + part
        cx[...] = norm_back(gn, xha[...], inv_a, va[:, GAIN], c_mid)

    for k, (src, dst) in enumerate(
        tuple((nm, side) for side in sides)
        + ((field, sides[2]), (acts, bundle.at[:, pl.ds(0, 2 * D)]), (actm, act_out), (qkv, qkv_out), (pt, pt_out))
    ):
        arrived(src, dst, outs.at[k])


def late_kernel(flags, x_two, vown, voth, actm, acts, *refs):
    xm, wd = refs[HELD + 1], refs[HELD - 1]
    keep, send = refs[-2:]
    core, layer = flags[0], flags[1]
    vm = vectors(core, vown, voth)[1]
    mid = xm[...].astype(F32)
    acc = mid + vm[:, SECOND : SECOND + D]
    for j in range(4):
        acc = acc + dot_nt((actm, acts)[j // 2][:, D * (j % 2) : D * (j % 2 + 1)], wd[j])
    acc = jnp.where(layer == 0, x_two[...].astype(F32), acc)
    keep[...] = jnp.where(core == 0, mid, acc).astype(BF)
    send[...] = jnp.where(core == 0, acc, mid).astype(BF)


def both_rows(core, keep, got, out, sems):
    return [
        pltpu.make_async_copy(src, out.at[rows_at(L * at, L), :], sems.at[k])
        for k, (src, at) in enumerate(((keep, core), (got, 1 - core)))
    ]


def norm_stats(gn, x, vec):
    xh, inv = norm_parts(x)
    vec[:, GAIN] = jnp.sum(gn * xh, axis=0, keepdims=True)
    vec[:, SHIFT] = jnp.sum(gn, axis=0, keepdims=True)
    return xh, inv


def back_kernel(
    flags, field, got, vown, voth, pos, qkv_in, pt_in, cosf, sinf, wa, w1, wd, xi, xm, rec, ml, dg,
    row_keep, row_send, c_out, vec_keep, keep_out, send_out,
    qkv, pt, gh, gp, va_grad, vm_grad, folded, vec_send, kt, gm, gqt, dsum, outs,
):
    core, layer = flags[0], flags[1]
    load(qkv_in, qkv, outs.at[3])
    load(pt_in, pt, outs.at[4])
    va, vm = vectors(core, vown, voth)
    wide = jnp.where(layer == 0, got[...].astype(F32), field[...].astype(F32))
    c = wide.astype(BF)
    c_out[...] = c
    vm_grad[:, SECOND:] = jnp.sum(wide, axis=0, keepdims=True)

    def from_output(j):
        return dot(c, wd[j])

    ahead = from_output(0)
    gn = None
    for j in range(4):
        ga = ahead
        if j < 3:
            ahead = from_output(j + 1)
        part = (ga * dg[:, D * j : D * (j + 1)].astype(F32)).astype(BF)
        start = hidden_start(core, j)
        gh[:, pl.ds(start, D)] = part
        vm_grad[:, pl.ds(pl.multiple_of(FIRST + start, 128), D)] = jnp.sum(
            part.astype(F32), axis=0, keepdims=True
        )
        part = dot_nt(part, w1[j])
        gn = part if gn is None else gn + part
    for when, dst in ((core == 0, send_out.at[pl.ds(0, L), :]), (core != 0, keep_out)):

        @pl.when(when)
        def _(dst=dst):
            load(gh, dst, outs.at[1])

    xh, inv = norm_stats(gn, xm[...].astype(F32), vm_grad)
    c = norm_back(gn, xh, inv, vm[:, GAIN], c)
    gp[:, 3 * D :] = c
    va_grad[:, FIRST + 5 * D :] = jnp.sum(c.astype(F32), axis=0, keepdims=True)
    colp, rowp = pos[:, 0:1], pos[:, 1:2]

    def emit(p, sl, sq, sk, grads):
        qr = qkv[:, sl].astype(F32) * (LN2 * HEAD_DIM**0.5)
        th = sq * qr + sk * qkv[:, D + 128 * p : D + 128 * (p + 1)].astype(F32)
        at = FIRST + 3 * D + 128 * p
        va_grad[:, at : at + 128] = jnp.sum(th * colp, axis=0, keepdims=True)
        va_grad[:, at + D : at + D + 128] = jnp.sum(th * rowp, axis=0, keepdims=True)
        for i, g in enumerate(grads):
            gp[:, D * i + 128 * p : D * i + 128 * (p + 1)] = g
            va_grad[:, FIRST + D * i + 128 * p : FIRST + D * i + 128 * (p + 1)] = jnp.sum(
                g.astype(F32), axis=0, keepdims=True
            )

    arrived(qkv_in, qkv, outs.at[3])
    arrived(pt_in, pt, outs.at[4])
    attention_back(
        c, wa.at[3], cosf, sinf, qkv, pt, rec, ml, kt, gm, gqt, dsum, lambda p: p, emit
    )
    for when, dst in ((core == 0, keep_out), (core != 0, send_out.at[pl.ds(0, L), :])):

        @pl.when(when)
        def _(dst=dst):
            load(gp, dst, outs.at[2])

    gn = None
    for i in range(3):
        part = dot_nt(gp[:, D * i : D * (i + 1)], wa[i])
        gn = part if gn is None else gn + part
    xh, inv = norm_stats(gn, xi[...].astype(F32), va_grad)
    cx = norm_back(gn, xh, inv, va[:, GAIN], c).astype(F32)
    wide = c.astype(F32)
    row_keep[...] = jnp.where(core == 0, cx, wide).astype(BF)
    row_send[...] = jnp.where(core == 0, wide, cx).astype(BF)
    fold_vector(va_grad, folded)
    a, m = packed_vector(folded), packed_vector(vm_grad)
    vec_keep[...] = jnp.where(core == 0, a, m)
    for k, part in enumerate(split_two(jnp.where(core == 0, m, a))):
        for b in range(3):
            vec_send[:, 128 * (3 * k + b) : 128 * (3 * k + b + 1)] = part[16 * b : 16 * (b + 1), :]
    vec_out = send_out.at[pl.ds(L, 16), pl.ds(0, D)]
    load(vec_send, vec_out, outs.at[0])
    main_rows = pl.ds(0, L)
    arrived(gh, send_out.at[main_rows, :], outs.at[1])
    arrived(gp, keep_out, outs.at[2])
    arrived(vec_send, vec_out, outs.at[0])


def put(stage, value, out, first, sem):
    stage[...] = value.astype(BF)
    copy = pltpu.make_async_copy(stage, out.at[:, pl.ds(first, stage.shape[1])], sem)
    copy.start()
    return copy


def gram_down_kernel(
    flags, c, c_oth, x_keep, x_oth, c_keep, c_send, act, bundle, main0, tail0, right0,
    down, left_main, left_tail, right_out, activations, c_kept, c_sent,
    c1, sides, left, right, sems, row_sems,
):
    leaving = both_rows(flags[0], x_keep, x_oth, activations, row_sems) + [
        pltpu.make_async_copy(src, dst, row_sems.at[2 + k])
        for k, (src, dst) in enumerate(((c_keep, c_kept), (c_send, c_sent)))
    ]
    for copy in leaving:
        copy.start()
    loads = (
        (bundle.at[:, pl.ds(4 * D, D)], c1), (act, right.at[pl.ds(0, L), :]),
        (bundle.at[:, pl.ds(0, 2 * D)], right.at[pl.ds(L, L), :]),
        (tail0, sides.at[0]), (bundle.at[:, pl.ds(3 * D, D)], sides.at[1]),
        (main0, sides.at[2]), (bundle.at[:, pl.ds(2 * D, D)], sides.at[3]),
        (right0, right_out.at[pl.ds(0, L), :]),
    )
    for k, (src, dst) in enumerate(loads):
        load(src, dst, sems.at[k])
    left[:, :L] = c[...].T
    arrived(*loads[0], sems.at[0])

    @pl.when(flags[1] == 0)
    def _():
        left[:, L:] = c_oth[...].T

    @pl.when(flags[1] != 0)
    def _():
        left[:, L:] = c1[...].T

    for k in range(1, 3):
        arrived(*loads[k], sems.at[k])
    down[...] = dot(left[...], right[...]).astype(BF)
    for k in range(4):
        arrived(*loads[3 + k], sems.at[3 + k])
        (left_tail, left_main)[k // 2][:, L * (k % 2) : L * (k % 2 + 1)] = sides[k].T
    arrived(*loads[7], sems.at[7])
    for copy in leaving:
        copy.wait()


def gram_head_kernel(rows, right1, down, left, vec, right0, head, tail_up, tail_down, vec_out, right):
    right[:L, :] = right0[:L, 3 * D :]
    right[L:, :] = right1[:L, 3 * D :]
    head[...] = dot(left[...], right[...]).astype(BF)
    other = [
        jnp.concatenate(
            [right1[L : L + 16, 128 * (3 * k + b) : 128 * (3 * k + b + 1)].astype(F32) for b in range(3)], axis=0
        )
        for k in range(2)
    ]
    total = (vec[...] + (other[0] + other[1])).astype(BF)
    vec_out[...] = total.astype(F32)
    for k, t in enumerate((tail_up, tail_down)):
        here = own_rows(rows, 0, k, t.shape[0])
        t[:, :D] = head[here, :]
        t[:, D : 3 * D] = down[here, :]
        t[:, 3 * D :] = total


def gram_main_kernel(rows, right1, left, right_in, right, main, main_up, main_down):
    right[L:, :] = right1[:L, :]
    main[...] = dot(left[...], right[:, : 3 * D]).astype(BF)
    for k, m in enumerate((main_up, main_down)):
        m[...] = main[own_rows(rows, 0, k, m.shape[0]), :]


def own_rows(rows, t, way, r):
    return pl.ds(pl.multiple_of(rows[t, way], 16), r)


def add_kernel(t, rows, up, down, *refs, count, vector):
    parts, outs, vectors = refs[:count], refs[count : count + 2], refs[count + 2 :]
    for k, (got, out) in enumerate(zip((up, down), outs)):
        here = own_rows(rows, t, k, got.shape[0])
        at = 0
        for part in parts:
            sl = slice(at, at + part.shape[1])
            out[:, sl] = (got[:, sl].astype(F32) + part[here, :].astype(F32)).astype(BF)
            at += part.shape[1]
        if out.shape[1] > at:
            out[:, at:] = got[:, at:]
        if k < vector:
            vectors[k][...] = got[:, at : at + 128].astype(F32)


def fold_vector(va, out):
    def fold(start):
        v = va[:, start : start + D]
        w = HEAD_DIM // 2
        return jnp.concatenate(
            [v[:, 2 * w * h : 2 * w * h + w] - v[:, 2 * w * h + w : 2 * w * (h + 1)] for h in range(HEADS)],
            axis=1,
        )

    at = FIRST + 3 * D
    out[:, :at] = va[:, :at]
    out[:, at : at + HALF] = fold(at)
    out[:, at + HALF : SECOND] = fold(at + D)
    out[:, SECOND:] = va[:, at + 2 * D :]


def packed_vector(ref):
    rows = [ref[:, 128 * k : 128 * (k + 1)] for k in range(VECTOR // 128)]
    rows += [jnp.zeros((1, 128), F32)] * (PACKED[0] - len(rows))
    return jnp.concatenate(rows, axis=0)


def sum_vectors(table, vectors, slots, outs):
    n = len(vectors)
    if table is None:
        total = vectors[0][...]
    else:
        slots[table[0, 2]] = vectors[0][...]
        for k in range(1, n):
            t, way = (k + 1) // 2, (k + 1) % 2
            slots[table[t, 2 + way]] = vectors[k][...]
        total = slots[0]
        for k in range(1, n):
            total = total + slots[k]
    at = 0
    for out in outs:
        for k in range(out.shape[1] // 128):
            out[:, 128 * k : 128 * (k + 1)] = total[at + k : at + k + 1, :]
        at += out.shape[1] // 128


def place_kernel(spots, whole, flags, rows, *refs):
    count, pair, vectors, into = whole
    ins, refs = refs[: 2 * count + pair + vectors], refs[2 * count + pair + vectors + into :]
    out, buf, sems = refs[0], refs[-3], refs[-2]
    copies = []
    if pair:
        copies += both_rows(flags[0], ins[2 * count], ins[2 * count + 1], refs[1], refs[-1])
        copies[0].start()
        copies[1].start()
    r = ins[0].shape[0]
    for k in range(count):
        there = pl.ds(r * k, r)
        buf[there, : 3 * D] = ins[2 * k][...].astype(F32)
        buf[there, 3 * D :] = ins[2 * k + 1][...].astype(F32)
        copy = pltpu.make_async_copy(
            buf.at[there, :], out.at[own_rows(rows, *spots[k], r), :], sems.at[k]
        )
        copy.start()
        copies.append(copy)
    if vectors:
        outs = refs[1 + pair // 2 : 5 + pair // 2]
        sum_vectors(rows if vectors > 1 else None, ins[2 * count + pair :], refs[-4], outs)
    for copy in copies:
        copy.wait()


SMEM = pl.BlockSpec(memory_space=pltpu.SMEM)
VS = pl.BlockSpec(memory_space=pltpu.VMEM)
HBM = pl.BlockSpec(memory_space=pltpu.HBM)
ANY = pl.BlockSpec(memory_space=pl.ANY)


def sds(shape, dtype=BF):
    return jax.ShapeDtypeStruct(shape, dtype)


def call(kernel, name, in_specs, outs, scratch, flops, nbytes, limit=58, out_specs=None, aliases=None):
    return pl.pallas_call(
        kernel,
        name=name,
        in_specs=in_specs,
        out_specs=[VS] * len(outs) if out_specs is None else out_specs,
        out_shape=outs,
        scratch_shapes=scratch,
        input_output_aliases={} if aliases is None else aliases,
        compiler_params=pltpu.CompilerParams(vmem_limit_bytes=limit * MIB),
        cost_estimate=pl.CostEstimate(flops=flops, bytes_accessed=nbytes, transcendentals=0),
    )


ATTN_W = [VM((4, D, D), BF)]
ANGLES = [VM((L, D), F32), VM((L, D), F32)]
MLP_W = [VM((4, D, D), BF), VM((4, D, D), BF)]
BACK_S = [VM((D, L), BF), VM((L, D), BF), VM((2, 128, L), F32), VM((16, L), F32)]


def in_vmem(a):
    return pltpu.with_memory_space_constraint(a, pltpu.VMEM)


def in_hbm(a):
    return pltpu.with_memory_space_constraint(a, pltpu.HBM)


def row(width=D):
    return VM((L, width), BF)


def row_out(width=D):
    return pltpu.HBM((L, width), BF)


def prepare(flags, n, x, cot, *vecs):
    out = VM((x.shape[0], L), BF)

    def kernel(*refs):
        prepare_kernel(*refs, n)

    table = pltpu.HBM((2 * n if n <= 16 else 1, 4), I32)
    return call(
        kernel, "prepare", [SMEM] + [VS] * 6, [out] * 4 + [pltpu.HBM((1, VECTOR), F32), table], [], 1000,
        int(1e6), 8, out_specs=[VS] * 5 + [SMEM],
    )(flags, *(in_hbm(a) for a in (x, cot) + vecs))


def positions(flags, grid, own, oth):
    hbm = pltpu.HBM
    return call(
        positions_kernel, "positions", [SMEM, SMEM, VS, VS],
        [VM((L, D), F32), VM((L, D), F32), hbm((L, 128), F32), hbm((8, L), F32)],
        [], int(1e8), int(3e6), 56,
    )(flags, grid, own, oth)


def first_pass(*a):
    results = call(
        first_kernel, "first_pass", [SMEM] + [VS] * 8 + [HBM] * 2 + [VS] * 2,
        [row(), row_out()] + ANGLES + ATTN_W + MLP_W,
        [row(), VM((D, L), BF), row(3 * D), VM((HEADS, L, L), BF), VM((16, L), F32), row(), VM((D, L), BF),
         VM((D, L), BF), row(), DMA((13,))],
        int(8e9), int(20e6), 26, out_specs=[VS, HBM] + [VS] * HELD,
        aliases={len(a) - 2: 2, len(a) - 1: 3},
    )(*a)
    return results[0], results[1], results[2:]


SAVED = [VM((L, D), BF), VM((L, D), BF), VM((16, L), F32), VM((L, D), BF), VM((L, FF), BF)]
HEAD_S = [VM((L, 3 * D), BF), VM((HEADS, L, L), BF)]


def second_pass(held, *a):
    outs = [
        row_out(FF // 2), row_out(), row_out(), row_out(5 * D), row_out(3 * D), pltpu.HBM((HEADS, L, L), BF)
    ]
    resident = ANGLES + ATTN_W + MLP_W + SAVED
    results = call(
        second_kernel, "second_pass", [SMEM] + [VS] * (7 + HELD),
        resident + [row(FF // 2), row(FF // 2), row()] + outs,
        HEAD_S + [row(), row(), VM((D, L), BF), VM((D, L), BF), VM((L, D), F32), VM((L, D), F32)]
        + BACK_S + [row(3 * D), DMA((9,))],
        int(18e9), int(20e6), 26, out_specs=[VS] * (len(resident) + 3) + [HBM] * len(outs),
        aliases={len(a) + k: k for k in range(HELD)},
    )(*a, *(in_vmem(x) for x in held))
    n = len(resident)
    return results[:n], results[n : n + 2], results[n + 2], results[n + 3 :]


def late_pass(held, *a):
    results = call(
        late_kernel, "late_pass", [SMEM] + [VS] * (len(a) - 1 + len(held)),
        ANGLES + ATTN_W + MLP_W + SAVED + [sds((L, D))] * 2, [], int(2e9), int(5e6), 26,
        aliases={len(a) + k: k for k in range(len(held))},
    )(*a, *(in_vmem(x) for x in held))
    return results[: len(held)], results[len(held) :]


def back_pass(held, *a):
    return call(
        back_kernel, "back_pass", [SMEM] + [VS] * 5 + [HBM] * 2 + [VS] * len(held),
        [row(), row(), row(), VM(PACKED, F32), row_out(FF), pltpu.HBM((L + 16, FF), BF)],
        HEAD_S
        + [row(FF), row(FF), VM((1, FIRST + 6 * D), F32), VM((1, VECTOR), F32), VM((1, VECTOR), F32),
           VM((16, D), BF)]
        + BACK_S + [DMA((5,))],
        int(10e9), int(15e6), 26, out_specs=[VS] * 4 + [HBM] * 2,
    )(*a, *(in_vmem(x) for x in held))


def gram_down(*a):
    square = VM((D, 2 * L), BF)
    return call(
        gram_down_kernel, "gram_down", [SMEM] + [VS] * 6 + [HBM, ANY] + [HBM] * 3,
        [VM((D, 2 * D), BF), square, square, VM((2 * L, FF), BF), pltpu.HBM((2 * L, D), BF), row_out(), row_out()],
        [row(), VM((4, L, D), BF), square, VM((2 * L, 2 * D), BF), DMA((8,)), DMA((4,))], int(2e9), int(8e6), 20,
        out_specs=[VS] * 4 + [HBM] * 3,
    )(*a)


def gram_head(rows, r, *a):
    wide = VM((r, 3 * D + 128), BF)
    return call(
        gram_head_kernel, "gram_head", [SMEM] + [VS] * 5, [VM((D, D), BF), wide, wide, VM(PACKED, F32)],
        [VM((2 * L, D), BF)], int(1e9), int(5e6), 12,
    )(rows, *a)


def gram_main(rows, r, *a):
    shard = VM((r, 3 * D), BF)
    return call(
        gram_main_kernel, "gram_main", [SMEM] + [VS] * 3,
        [VM((2 * L, FF), BF), VM((D, 3 * D), BF), shard, shard], [], int(6e9), int(12e6), 20, aliases={3: 0},
    )(rows, *a)[1:]


def add(t, rows, up, down, parts, vector, wide):
    count = len(parts)

    def kernel(*refs):
        add_kernel(t, *refs, count=count, vector=vector)

    width = sum(p.shape[1] for p in parts)
    out = VM((up.shape[0], width + (128 if wide else 0)), BF)
    results = call(
        kernel, "add", [SMEM] + [VS] * (2 + count), [out, out] + [VM(PACKED, F32)] * vector, [], 1000,
        int(1e6), 4,
    )(rows, in_vmem(up), in_vmem(down), *(in_vmem(p) for p in parts))
    return results[:2], results[2:]


def place(flags, spots, rows, shards, total, pair=(), vectors=()):
    r, count = shards[0].shape[0], len(shards) // 2
    into = [] if total is None else [total]
    whole = count, len(pair), len(vectors), len(into)

    def kernel(*refs):
        place_kernel(spots, whole, *refs)

    outs = [pltpu.HBM((D, 6 * D), F32)]
    outs += [pltpu.HBM((2 * L, D), BF)] if pair else []
    outs += [sds((1, w), F32) for w in (D, D, FF, D)] if vectors else []
    given = len(shards) + len(pair) + len(vectors)
    return call(
        kernel, "place", [SMEM, SMEM] + [VS] * given + [HBM] * len(into), outs,
        [VM((max(len(vectors), 1),) + PACKED, F32), VM((r * count, 6 * D), F32), DMA((count,)), DMA((2,))], 1000,
        int(2e7), 24, out_specs=[HBM] * (2 if pair else 1) + ([VS] * 4 if vectors else []),
        aliases={given + 2: 0} if into else {},
    )(flags, rows, *shards, *pair, *vectors, *into)


def core_swap(a):
    return lax.ppermute(a, "section", [(0, 1), (1, 0), (2, 3), (3, 2)])


def after(value, first):
    return lax.optimization_barrier((value, first))[0]


class Cycle:
    def __init__(self, rows):
        self.n = n = lax.axis_size("dp")
        self.r = D // (2 * n)
        order = list(range(0, n, 2)) + list(range(n - 1, 0, -2))
        self.pairs = [[(order[k], order[(k + d) % n]) for k in range(n)] for d in (1, -1)]
        self.rows = rows

    def placed(self, k):
        return 2 * self.n - 1 if k == 0 else self.n + k - 1


class Chain:
    def __init__(self, cycle, parts, cur, carries=False):
        self.cycle, self.parts, self.cur, self.carries = cycle, parts, cur, carries
        self.t = 0
        self.shards = []
        self.vectors = []

    def step(self, token):
        c = self.cycle
        got = [lax.ppermute(a, "dp", p) for a, p in zip(self.cur, c.pairs)]
        got = after(got, token)
        self.t += 1
        if self.t < c.n:
            t = self.t
            ways = int(t <= c.n // 2) + int(t <= (c.n - 1) // 2) if self.carries else 0
            self.cur, came = add(t, c.rows, *got, self.parts, ways, self.carries and t < c.n // 2)
            self.vectors += came
        else:
            self.cur = got
        if self.t >= c.n - 1:
            self.shards.append(self.cur)
        return self.cur


def small_ring():
    return lax.axis_size("dp") <= 16


def summed(flags, rows, main, tail, token, pair, vector):
    if not small_ring():
        chains, vector = lax.psum([main, tail], "dp"), lax.psum(vector, "dp")
        return place(flags, [(0, 0)], rows, chains, None, pair, [vector])
    cycle = main.cycle
    n = cycle.n
    total, placed = None, 0
    results = {}
    while main.t < 2 * n - 2:
        token = tail.step(token)
        if total is not None:
            token = (token, total)
        token = main.step(token)
        whole = len(main.shards)
        if whole > placed and (whole % 2 == 0 or whole == n - 1):
            spots, shards = [], []
            for k in range(placed, whole):
                for way in range(2):
                    spots.append((cycle.placed(k), way))
                    shards += [main.shards[k][way], tail.shards[k][way]]
            now, then = placed == 0, "vectors" not in results and whole >= min(4, n)
            total, *more = place(
                flags, spots, cycle.rows, shards, total, pair if now else (), [vector] + tail.vectors if then else ()
            )
            if now:
                results["rows"] = more[0]
            if then:
                results["vectors"] = more
            placed = whole
    return total, results["rows"], *results["vectors"]


def body(
    block_input, cotangent, grid_sizes, section_weight, norm_gain, norm_bias, first_vector, second_vector
):
    section = lax.axis_index("section")
    core = section % 2
    n = lax.axis_size("dp")
    i = lax.axis_index("dp")
    where = jnp.where(i % 2 == 0, i // 2, n - 1 - i // 2)
    flags = in_hbm(jnp.stack([core, section // 2, where]).astype(I32))
    first_layer = section < 2

    keep, send, away, across, vown, rows = prepare(
        flags, n, block_input.T, cotangent.T, norm_gain, norm_bias, first_vector, second_vector
    )
    if n % 2 == 0:
        voth = lax.ppermute(
            vown, ("section", "dp"), [(n * s + d, n * (s ^ 1) + (d ^ 1)) for s in range(4) for d in range(n)]
        )
    else:
        voth = core_swap(vown)
    r = D // (2 * n) if small_ring() else PACKED[0]
    cosf, sinf, pos, segr = positions(flags, grid_sizes, in_hbm(vown), voth)
    vown, voth, rows, pos, segr = (in_hbm(a) for a in (vown, voth, rows, pos, segr))
    got = core_swap(send)
    away = lax.ppermute(away, "section", [(0, 2), (1, 3), (2, 0), (3, 1)])
    across = lax.ppermute(across, "section", [(0, 3), (1, 2), (2, 1), (3, 0)])
    own = in_hbm(section_weight[0])
    oth = in_hbm(core_swap(section_weight[0]))

    x_two, field, held = first_pass(
        flags, keep, got, away, across, vown, voth, pos, segr, own, oth, in_vmem(cosf), in_vmem(sinf)
    )
    field = in_hbm(field)
    x_got, x_late = (lax.ppermute(x_two, "section", [pair]) for pair in ((0, 2), (1, 3)))
    held, active, c_two, (act_mine, main_left, tail_left, bundle, qkv, pt) = second_pass(
        held, flags, field, x_got, x_late, vown, voth, pos, segr
    )
    act_mine, main_left, tail_left = (in_hbm(a) for a in (act_mine, main_left, tail_left))
    c_got = lax.ppermute(c_two, "section", [(2, 0), (3, 1)])
    held, (x_keep, x_send) = late_pass(held, flags, x_two, vown, voth, *(in_vmem(a) for a in active))
    c_got = after(c_got, x_keep)
    bundle = core_swap(after(bundle, c_got))
    x_oth = core_swap(after(x_send, c_got))

    c_keep, c_send, c_out, vec, right, right_send = back_pass(
        held, flags, field, c_got, vown, voth, pos, in_hbm(qkv), in_hbm(pt)
    )
    c_oth = core_swap(c_got)
    right_oth = core_swap(after(right_send, (c_oth, bundle, x_oth)))
    down, left_main, left_tail, right, activations, c_keep, c_send = gram_down(
        flags, c_out, c_oth, x_keep, x_oth, in_vmem(c_keep), in_vmem(c_send), act_mine, bundle, main_left, tail_left, in_hbm(right)
    )
    head, *tail_first, vec = gram_head(rows, r, right_oth, down, left_tail, vec, right)
    if small_ring():
        cycle = Cycle(rows)
        tail = Chain(cycle, [head, down], tail_first, True)
    else:
        tail = jnp.concatenate([head, down], axis=1)
    main, *main_first = gram_main(rows, r, right_oth, left_main, right)
    if small_ring():
        main = Chain(cycle, [main], main_first)
        token = main.cur
    else:
        token = main
    weight_grad, input_grads, *vectors = summed(
        flags, rows, main, tail, token, (c_keep, core_swap(after(c_send, token))), vec
    )
    return (
        activations[None],
        input_grads[None],
        weight_grad[None],
        *vectors,
    )


def solution(mesh):
    in_specs = (
        P("dp", "section"),
        P("dp", "section"),
        P("dp", None, None),
        P("section", None, None),
        P("section", None),
        P("section", None),
        P("section", None),
        P("section", None),
    )
    out_specs = (
        P("section", "dp", None),
        P("section", "dp", None),
        P("section", None, None),
        P("section", None),
        P("section", None),
        P("section", None),
        P("section", None),
    )
    return jax.shard_map(body, mesh=mesh, in_specs=in_specs, out_specs=out_specs, check_vma=False)
```

```python
import jax
import jax.numpy as jnp
from jax import lax
from jax.experimental import pallas as pl
from jax.experimental.pallas import tpu as pltpu
from jax.sharding import PartitionSpec as P

D = 768
HEADS = 12
HEAD_DIM = 64
FF = 3072
L = 384
HALF = D // 2
F32 = jnp.float32
BF = jnp.bfloat16
I32 = jnp.int32
NT = (((1,), (1,)), ((), ()))
TN = (((0,), (0,)), ((), ()))
VM = pltpu.VMEM
DMA = pltpu.SemaphoreType.DMA
MIB = 1024 * 1024
LN2 = 0.6931471805599453
GAIN, SHIFT = slice(0, D), slice(D, 2 * D)
FIRST, SECOND = 2 * D, 2 * D + FF
VECTOR = 3 * D + FF
PACKED = (48, 128)


def dot(a, b):
    return jnp.dot(a, b, preferred_element_type=F32)


def dot_nt(a, b):
    return lax.dot_general(a, b, NT, preferred_element_type=F32)


def dot_tn(a, b):
    return lax.dot_general(a, b, TN, preferred_element_type=F32)


def norm_parts(x):
    center = x - jnp.mean(x, axis=-1, keepdims=True)
    inv = lax.rsqrt(jnp.mean(center * center, axis=-1, keepdims=True) + 1e-06)
    return center * inv, inv


def swap_halves(a):
    lane = lax.broadcasted_iota(I32, (1, 128), 1)
    first = (lane % HEAD_DIM) < HEAD_DIM // 2
    out = []
    for i in range(a.shape[1] // 128):
        s = a[:, 128 * i : 128 * (i + 1)]
        out.append(jnp.where(first, pltpu.roll(s, 96, 1), pltpu.roll(s, 32, 1)))
    return jnp.concatenate(out, axis=1) if len(out) > 1 else out[0]


def lanes(start, size):
    if isinstance(start, int):
        return slice(start, start + size)
    return pl.ds(pl.multiple_of(start, 128), size)


def rows_at(start, size):
    if isinstance(start, int):
        return slice(start, start + size)
    return pl.ds(pl.multiple_of(start, size), size)


def cols(start, size):
    return (slice(None), pl.ds(start, size))


def pick(flag, want, own, oth, src, dst, sem):
    @pl.when(flag == want)
    def _():
        pltpu.make_async_copy(own.at[src], dst, sem).start()

    @pl.when(flag != want)
    def _():
        pltpu.make_async_copy(oth.at[src], dst, sem).start()


def load(src, dst, sem):
    pltpu.make_async_copy(src, dst, sem).start()


def arrived(src, dst, sem):
    pltpu.make_async_copy(src, dst, sem).wait()


def load_attn(core, own, oth, wa, sems, i):
    pick(core, 0, own, oth, cols(D * i, D), wa.at[i], sems.at[i])


def wait_attn(own, wa, sems, i):
    arrived(own.at[cols(D * i, D)], wa.at[i], sems.at[i])


def hidden_start(core, j):
    return pl.multiple_of(FF // 2 * ((core + j // 2) % 2) + D * (j % 2), 128)


def load_mlp(core, own, oth, w1, wd, sems, j):
    pick(core, 1, own, oth, (slice(None), pl.ds(hidden_start(core, j), D)), w1.at[j], sems.at[j])
    load((own if j < 2 else oth).at[cols(FF + D * (j % 2), D)], wd.at[j], sems.at[4 + j])


class Forward:
    def __init__(self, on_the_way, core, own, oth, wa, w1, wd, sems):
        self.attn = core, own, oth, wa, sems
        self.mlp = core, own, oth, w1, wd, sems.at[pl.ds(4, 8)]
        self.own, self.wa, self.sems, self.on_the_way = own, wa, sems, on_the_way

        @pl.when(on_the_way)
        def _():
            load_attn(*self.attn, 0)
            load_attn(*self.attn, 1)

        @pl.when(jnp.logical_not(on_the_way))
        def _():
            for i in range(4):
                load_attn(*self.attn, i)
                load_mlp(*self.mlp, i)
                wait_attn(own, wa, sems, i)
                wait_mlp(own, w1, wd, self.mlp[-1], i)

    def wait(self, i):
        @pl.when(self.on_the_way)
        def _():
            wait_attn(self.own, self.wa, self.sems, i)
            if i < 2:
                load_attn(*self.attn, i + 2)
            elif i == 2:
                for j in range(4):
                    load_mlp(*self.mlp, j)

    def wait_mlp(self):
        core, own, oth, w1, wd, sems = self.mlp

        @pl.when(self.on_the_way)
        def _():
            for j in range(4):
                wait_mlp(own, w1, wd, sems, j)


def wait_mlp(own, w1, wd, sems, j):
    if w1 is not None:
        arrived(own.at[cols(0, D)], w1.at[j], sems.at[j])
    arrived(own.at[cols(0, D)], wd.at[j], sems.at[4 + j])


def vectors(core, own, oth):
    a, b = own[...], oth[...]
    return jnp.where(core == 0, a, b), jnp.where(core == 0, b, a)


def attention(x, vec, wa, wait, cosf, sinf, segc, segr, qkv, pt, rec, ml, mlt, vt, n_ref):
    xh, inv = norm_parts(x)
    n = (xh * vec[:, GAIN] + vec[:, SHIFT]).astype(BF)
    n_ref[...] = n
    for i in range(3):
        wait(i)
        part = dot(n, wa[i]) + vec[:, FIRST + D * i : FIRST + D * (i + 1)]
        if i < 2:
            part = part * cosf[...] + swap_halves(part) * sinf[...]
        if i == 0:
            part = part * (HEAD_DIM**-0.5 / LN2)
        qkv[:, D * i : D * (i + 1)] = part.astype(BF)
    vt[...] = qkv[:, 2 * D : 3 * D].T
    same = segc == segr
    lane = lax.broadcasted_iota(I32, (1, 128), 1)

    def score(h):
        p = 128 * (h // 2)
        keys = jnp.where((lane // HEAD_DIM) == h % 2, qkv[:, D + p : D + p + 128], BF(0))
        return dot_nt(keys, qkv[:, p : p + 128])

    ahead = score(0)
    for h in range(HEADS):
        st = ahead
        if h + 1 < HEADS:
            ahead = score(h + 1)
        st = jnp.where(same, st, -1e30)
        e = jnp.exp2(st - jnp.max(st, axis=0, keepdims=True))
        r = 1.0 / jnp.sum(e, axis=0, keepdims=True)
        rec[h : h + 1, :] = r
        e = e.astype(BF)
        pt[h] = e
        here = slice(HEAD_DIM * h, HEAD_DIM * (h + 1))
        mlt[here, :] = (dot(vt[here, :], e) * r).astype(BF)
    ml[...] = mlt[...].T
    wait(3)
    out = x + dot(ml[...], wa[3]) + vec[:, SECOND : SECOND + D]
    return out.astype(BF), xh, inv


C0 = 0.7978845608028654
C1 = 0.044715


def gelu(h):
    h2 = h * h
    t = jnp.tanh(C0 * (h + C1 * h * h2))
    half = 0.5 * (1.0 + t)
    return h * half, half + (0.5 * C0) * h * (1.0 - t * t) * (1.0 + (3.0 * C1) * h2)


def norm_back(gn, xh, inv, gain, c):
    u = gn * gain
    gx = inv * (
        u - jnp.mean(u, axis=-1, keepdims=True) - xh * jnp.mean(u * xh, axis=-1, keepdims=True)
    )
    return (c.astype(F32) + gx).astype(BF)


def head_select():
    head = lax.broadcasted_iota(I32, (16, D), 0)
    lane = lax.broadcasted_iota(I32, (16, D), 1)
    return jnp.where(lane // HEAD_DIM == head, 1.0, 0.0).astype(BF)


def split_two(a):
    hi = a.astype(BF)
    return hi, (a - hi.astype(F32)).astype(BF)


def attention_back(c, wo, cosf, sinf, qkv, pt, rec, ml, kt, gm, gqt, dsum, pair_of, emit):
    kt[...] = qkv[:, D : 2 * D].T
    gm_wide = dot_nt(c, wo[...])
    sel = head_select()
    hi, lo = split_two(gm_wide * ml[...].astype(F32))
    row = lax.broadcasted_iota(I32, (16, L), 0)
    recs = jnp.where(row < HEADS, rec[...], 0.0)
    dsum[...] = (dot_nt(sel, hi) + dot_nt(sel, lo)) * recs
    hi, lo = split_two(recs)
    gm[...] = (gm_wide * (dot_tn(hi, sel) + dot_tn(lo, sel))).astype(BF)
    lane = lax.broadcasted_iota(I32, (1, 128), 1)

    def spot(h):
        return lanes(128 * pair_of(h // 2), 128), (lane // HEAD_DIM) == h % 2

    def from_values(h):
        sl, here = spot(h)
        values = qkv[:, lanes(2 * D + 128 * pair_of(h // 2), 128)]
        return dot_nt(jnp.where(here, values, BF(0)), gm[:, sl])

    ahead = from_values(0)
    for h in range(HEADS):
        gpt = ahead
        if h + 1 < HEADS:
            ahead = from_values(h + 1)
        sl, here = spot(h)
        head = 2 * pair_of(h // 2) + h % 2
        e = pt[head]
        gvh = dot(e, jnp.where(here, gm[:, sl], BF(0)))
        gst = (e.astype(F32) * (gpt - dsum[rows_at(head, 1), :])).astype(BF)
        gkh = dot(gst, jnp.where(here, qkv[:, sl], BF(0)))
        kth = kt[rows_at(HEAD_DIM * head, HEAD_DIM), :]
        gqt[h // 2 % 2, HEAD_DIM * (h % 2) : HEAD_DIM * (h % 2 + 1), :] = dot(kth, gst)
        gv = gvh if h % 2 == 0 else gv + gvh
        gk = gkh if h % 2 == 0 else gk + gkh
        if h % 2 == 1:
            gq = gqt[h // 2 % 2].T * (HEAD_DIM**-0.5)
            gk = gk * LN2
            cs, sn = cosf[:, sl], sinf[:, sl]
            sq, sk = swap_halves(gq), swap_halves(gk)
            emit(
                h // 2, sl, sq, sk,
                ((gq * cs - sq * sn).astype(BF), (gk * cs - sk * sn).astype(BF), gv.astype(BF)),
            )


def positions_kernel(flags, grid, vown, voth, cosf, sinf, pos, segr):
    core = flags[0]
    vec = vectors(core, vown, voth)[0]
    h0, w0, h1, w1 = (grid[core, k // 2, k % 2] for k in range(4))
    e1 = h0 * w0
    e2 = e1 + h1 * w1

    def place(t):
        segment = (t >= e1).astype(I32) + (t >= e2).astype(I32)
        width = jnp.where(segment == 0, w0, w1).astype(F32)
        inside = (t - jnp.where(segment == 0, 0, e1)).astype(F32)
        row = jnp.floor((inside + 0.5) / width)
        column = inside - row * width
        return segment, jnp.where(segment < 2, row, 0.0), jnp.where(segment < 2, column, 0.0)

    segment, row, column = place(lax.broadcasted_iota(I32, (L, 128), 0))
    lane = lax.broadcasted_iota(I32, (L, 128), 1)
    pos[...] = jnp.where(lane == 0, column, jnp.where(lane == 1, row, segment.astype(F32)))
    t = lax.broadcasted_iota(I32, (8, L), 1)
    segr[...] = (t >= e1).astype(F32) + (t >= e2).astype(F32)

    def by_lane(start):
        parts = []
        for h in range(HEADS):
            f = vec[:, start + 32 * h : start + 32 * (h + 1)]
            parts += [f, f]
        return jnp.concatenate(parts, axis=1)

    number = lax.broadcasted_iota(I32, (16, D), 0).astype(F32)

    def look_up(which, table):
        hi, rest = split_two(table)
        mid, low = split_two(table - hi.astype(F32))
        tables = jnp.concatenate([hi, mid, low], axis=0)
        hit = (lax.broadcasted_iota(I32, (L, 48), 1) % 16).astype(F32) == which[:, :48]
        return dot(jnp.where(hit, 1.0, 0.0).astype(BF), tables)

    ax = number * by_lane(FIRST + 3 * D)
    ay = number * by_lane(FIRST + 3 * D + HALF)
    cx, sx = look_up(column, jnp.cos(ax)), look_up(column, jnp.sin(ax))
    cy, sy = look_up(row, jnp.cos(ay)), look_up(row, jnp.sin(ay))
    cosf[...] = cx * cy - sx * sy
    lane = lax.broadcasted_iota(I32, (1, D), 1)
    sign = jnp.where(lane % HEAD_DIM < HEAD_DIM // 2, -1.0, 1.0)
    sinf[...] = (sx * cy + cx * sy) * sign


def prepare_kernel(
    flags, x, cot, gain, shift, first, second, keep, send, away, across, vec, table, n
):
    core, layer, where = flags[0], flags[1], flags[2]
    for t in range(table.shape[0]):
        for way, d in ((0, 1), (1, -1)):
            at = lax.rem(where - d * (t % n) + 2 * n, n)
            table[t, way] = at * (D // (2 * n)) + way * HALF
            table[t, 2 + way] = jnp.where(2 * at < n, 2 * at, 2 * (n - at) - 1)
    for at, (mine, other) in enumerate(((x, cot), (cot, x))):

        @pl.when(layer == at)
        def _(mine=mine, other=other):
            keep[...] = mine[:, lanes(L * core, L)]
            send[...] = mine[:, lanes(L * (1 - core), L)]
            away[...] = other[:, lanes(L * core, L)]
            across[...] = other[:, lanes(L * (1 - core), L)]

    vec[:, GAIN] = gain[...]
    vec[:, SHIFT] = shift[...]
    vec[:, FIRST:SECOND] = first[...]
    vec[:, SECOND:] = second[...]


HELD = 5


def first_kernel(
    flags, keep, got, away, across, vown, voth, pos, segr, own, oth, cos_in, sin_in,
    out, field_out, cosf, sinf, wa, w1, wd, field, turned, qkv, pt, rec, ml, mlt, vt, n_ref, sems,
):
    core, layer = flags[0], flags[1]
    loads = Forward((core == 0) & (layer == 0), core, own, oth, wa, w1, wd, sems)
    w = keep.shape[0]
    for k in range(2):
        for at in range(2):

            @pl.when((core == k) & (layer == at))
            def _(k=k, at=at):
                parts = {(at, k): keep, (at, 1 - k): got, (1 - at, k): away, (1 - at, 1 - k): across}
                for s in range(4):
                    turned[w * s : w * (s + 1), :] = parts[s // 2, s % 2][...]

    field[...] = turned[...].T
    keeping = pltpu.make_async_copy(field, field_out, sems.at[12])
    keeping.start()
    @pl.when(layer == 0)
    def _():
        va, vm = vectors(core, vown, voth)
        x_mid, _, _ = attention(
            field[...].astype(F32), va, wa, loads.wait, cosf, sinf, pos[:, 2:3], segr[0:1, :],
            qkv, pt, rec, ml, mlt, vt, n_ref,
        )
        x = x_mid.astype(F32)
        xh, _ = norm_parts(x)
        n = (xh * vm[:, GAIN] + vm[:, SHIFT]).astype(BF)
        loads.wait_mlp()
        acc = x + vm[:, SECOND : SECOND + D]
        first = hidden_bias(core, vm)
        ahead = dot(n, w1[0])
        for j in range(4):
            h = ahead + first[:, D * j : D * (j + 1)]
            if j < 3:
                ahead = dot(n, w1[j + 1])
            acc = acc + dot_nt(gelu(h)[0].astype(BF), wd[j])
        out[...] = acc.astype(BF)

    keeping.wait()


def hidden_bias(core, vm):
    a, b = vm[:, FIRST : FIRST + FF // 2], vm[:, FIRST + FF // 2 : SECOND]
    return jnp.concatenate([jnp.where(core == 0, a, b), jnp.where(core == 0, b, a)], axis=1)


def second_kernel(
    flags, field, got, got_late, vown, voth, pos, segr, *refs,
):
    (
        cosf, sinf, wa, w1, wd, xi, xm, rec, ml, dg, actm, acts, cx, act_out, main_out, tail_out, bundle,
        qkv_out, pt_out, qkv, pt, na, nm, mlt, vt, xha, xhm, kt, gm, gqt, dsum, gp, outs,
    ) = refs[HELD:]
    core, layer = flags[0], flags[1]
    va, vm = vectors(core, vown, voth)
    x = jnp.where(core == 0, got[...].astype(F32), got_late[...].astype(F32))
    x = jnp.where(layer == 0, field[...].astype(F32), x)
    xi[...] = x.astype(BF)
    x_mid, xh, inv_a = attention(
        x, va, wa, lambda what: None, cosf, sinf, pos[:, 2:3], segr[0:1, :], qkv, pt, rec, ml, mlt, vt, na
    )
    xha[...] = xh
    xm[...] = x_mid
    load(qkv, qkv_out, outs.at[7])
    load(pt, pt_out, outs.at[8])
    xh, inv_m = norm_parts(x_mid.astype(F32))
    xhm[...] = xh
    n = (xh * vm[:, GAIN] + vm[:, SHIFT]).astype(BF)
    nm[...] = n
    sides = (
        main_out, tail_out, bundle.at[:, pl.ds(2 * D, D)], bundle.at[:, pl.ds(3 * D, D)],
    )
    load(field, bundle.at[:, pl.ds(4 * D, D)], outs.at[4])
    for when, sources in ((core == 0, (na, ml, nm, nm)), (core != 0, (nm, nm, na, ml))):

        @pl.when(when)
        def _(sources=sources):
            for k, (src, dst) in enumerate(zip(sources, sides)):
                load(src, dst, outs.at[k])

    first = hidden_bias(core, vm)
    c = field[...]

    def forward(j):
        return dot(n, w1[j])

    def chunk(j, h):
        act, slope = gelu(h + first[:, D * j : D * (j + 1)])
        (actm, acts)[j // 2][:, D * (j % 2) : D * (j % 2 + 1)] = act.astype(BF)
        slope = slope.astype(BF)
        dg[:, D * j : D * (j + 1)] = slope
        return slope

    def leave():
        load(acts, bundle.at[:, pl.ds(0, 2 * D)], outs.at[5])
        load(actm, act_out, outs.at[6])

    @pl.when(layer >= 0)
    def _():
        ahead = forward(0), dot(c, wd[0])
        gn = None
        for j in range(4):
            h, ga = ahead
            if j < 3:
                ahead = forward(j + 1), dot(c, wd[j + 1])
            slope = chunk(j, h)
            part = dot_nt((ga * slope.astype(F32)).astype(BF), w1[j])
            gn = part if gn is None else gn + part
        leave()
        c_mid = norm_back(gn, xhm[...], inv_m, vm[:, GAIN], c)

        def emit(p, sl, sq, sk, grads):
            for i in range(3):
                gp[:, D * i + 128 * p : D * i + 128 * (p + 1)] = grads[i]

        attention_back(
            c_mid, wa.at[3], cosf, sinf, qkv, pt, rec, ml, kt, gm, gqt, dsum, lambda p: p, emit
        )
        gn = None
        for i in range(3):
            part = dot_nt(gp[:, D * i : D * (i + 1)], wa[i])
            gn = part if gn is None else gn + part
        cx[...] = norm_back(gn, xha[...], inv_a, va[:, GAIN], c_mid)

    for k, (src, dst) in enumerate(
        tuple((nm, side) for side in sides)
        + ((field, sides[2]), (acts, bundle.at[:, pl.ds(0, 2 * D)]), (actm, act_out), (qkv, qkv_out), (pt, pt_out))
    ):
        arrived(src, dst, outs.at[k])


def late_kernel(flags, x_two, vown, voth, actm, acts, *refs):
    xm, wd = refs[HELD + 1], refs[HELD - 1]
    keep, send = refs[-2:]
    core, layer = flags[0], flags[1]
    vm = vectors(core, vown, voth)[1]
    mid = xm[...].astype(F32)
    acc = mid + vm[:, SECOND : SECOND + D]
    for j in range(4):
        acc = acc + dot_nt((actm, acts)[j // 2][:, D * (j % 2) : D * (j % 2 + 1)], wd[j])
    acc = jnp.where(layer == 0, x_two[...].astype(F32), acc)
    keep[...] = jnp.where(core == 0, mid, acc).astype(BF)
    send[...] = jnp.where(core == 0, acc, mid).astype(BF)


def both_rows(core, keep, got, out, sems):
    return [
        pltpu.make_async_copy(src, out.at[rows_at(L * at, L), :], sems.at[k])
        for k, (src, at) in enumerate(((keep, core), (got, 1 - core)))
    ]


def norm_stats(gn, x, vec):
    xh, inv = norm_parts(x)
    vec[:, GAIN] = jnp.sum(gn * xh, axis=0, keepdims=True)
    vec[:, SHIFT] = jnp.sum(gn, axis=0, keepdims=True)
    return xh, inv


def back_kernel(
    flags, field, got, vown, voth, pos, qkv_in, pt_in, cosf, sinf, wa, w1, wd, xi, xm, rec, ml, dg,
    row_keep, row_send, c_out, vec_keep, keep_out, send_out,
    qkv, pt, gh, gp, va_grad, vm_grad, folded, vec_send, kt, gm, gqt, dsum, outs,
):
    core, layer = flags[0], flags[1]
    load(qkv_in, qkv, outs.at[3])
    load(pt_in, pt, outs.at[4])
    va, vm = vectors(core, vown, voth)
    wide = jnp.where(layer == 0, got[...].astype(F32), field[...].astype(F32))
    c = wide.astype(BF)
    c_out[...] = c
    vm_grad[:, SECOND:] = jnp.sum(wide, axis=0, keepdims=True)

    def from_output(j):
        return dot(c, wd[j])

    ahead = from_output(0)
    gn = None
    for j in range(4):
        ga = ahead
        if j < 3:
            ahead = from_output(j + 1)
        part = (ga * dg[:, D * j : D * (j + 1)].astype(F32)).astype(BF)
        start = hidden_start(core, j)
        gh[:, pl.ds(start, D)] = part
        vm_grad[:, pl.ds(pl.multiple_of(FIRST + start, 128), D)] = jnp.sum(
            part.astype(F32), axis=0, keepdims=True
        )
        part = dot_nt(part, w1[j])
        gn = part if gn is None else gn + part
    for when, dst in ((core == 0, send_out.at[pl.ds(0, L), :]), (core != 0, keep_out)):

        @pl.when(when)
        def _(dst=dst):
            load(gh, dst, outs.at[1])

    xh, inv = norm_stats(gn, xm[...].astype(F32), vm_grad)
    c = norm_back(gn, xh, inv, vm[:, GAIN], c)
    gp[:, 3 * D :] = c
    va_grad[:, FIRST + 5 * D :] = jnp.sum(c.astype(F32), axis=0, keepdims=True)
    colp, rowp = pos[:, 0:1], pos[:, 1:2]

    def emit(p, sl, sq, sk, grads):
        qr = qkv[:, sl].astype(F32) * (LN2 * HEAD_DIM**0.5)
        th = sq * qr + sk * qkv[:, D + 128 * p : D + 128 * (p + 1)].astype(F32)
        at = FIRST + 3 * D + 128 * p
        va_grad[:, at : at + 128] = jnp.sum(th * colp, axis=0, keepdims=True)
        va_grad[:, at + D : at + D + 128] = jnp.sum(th * rowp, axis=0, keepdims=True)
        for i, g in enumerate(grads):
            gp[:, D * i + 128 * p : D * i + 128 * (p + 1)] = g
            va_grad[:, FIRST + D * i + 128 * p : FIRST + D * i + 128 * (p + 1)] = jnp.sum(
                g.astype(F32), axis=0, keepdims=True
            )

    arrived(qkv_in, qkv, outs.at[3])
    arrived(pt_in, pt, outs.at[4])
    attention_back(
        c, wa.at[3], cosf, sinf, qkv, pt, rec, ml, kt, gm, gqt, dsum, lambda p: p, emit
    )
    for when, dst in ((core == 0, keep_out), (core != 0, send_out.at[pl.ds(0, L), :])):

        @pl.when(when)
        def _(dst=dst):
            load(gp, dst, outs.at[2])

    gn = None
    for i in range(3):
        part = dot_nt(gp[:, D * i : D * (i + 1)], wa[i])
        gn = part if gn is None else gn + part
    xh, inv = norm_stats(gn, xi[...].astype(F32), va_grad)
    cx = norm_back(gn, xh, inv, va[:, GAIN], c).astype(F32)
    wide = c.astype(F32)
    row_keep[...] = jnp.where(core == 0, cx, wide).astype(BF)
    row_send[...] = jnp.where(core == 0, wide, cx).astype(BF)
    fold_vector(va_grad, folded)
    a, m = packed_vector(folded), packed_vector(vm_grad)
    vec_keep[...] = jnp.where(core == 0, a, m)
    for k, part in enumerate(split_two(jnp.where(core == 0, m, a))):
        for b in range(3):
            vec_send[:, 128 * (3 * k + b) : 128 * (3 * k + b + 1)] = part[16 * b : 16 * (b + 1), :]
    vec_out = send_out.at[pl.ds(L, 16), pl.ds(0, D)]
    load(vec_send, vec_out, outs.at[0])
    main_rows = pl.ds(0, L)
    arrived(gh, send_out.at[main_rows, :], outs.at[1])
    arrived(gp, keep_out, outs.at[2])
    arrived(vec_send, vec_out, outs.at[0])


def put(stage, value, out, first, sem):
    stage[...] = value.astype(BF)
    copy = pltpu.make_async_copy(stage, out.at[:, pl.ds(first, stage.shape[1])], sem)
    copy.start()
    return copy


def gram_down_kernel(
    flags, c, c_oth, x_keep, x_oth, c_keep, c_send, act, bundle, main0, tail0, right0,
    down, left_main, left_tail, right_out, activations, c_kept, c_sent,
    c1, sides, left, right, sems, row_sems,
):
    leaving = both_rows(flags[0], x_keep, x_oth, activations, row_sems) + [
        pltpu.make_async_copy(src, dst, row_sems.at[2 + k])
        for k, (src, dst) in enumerate(((c_keep, c_kept), (c_send, c_sent)))
    ]
    for copy in leaving:
        copy.start()
    loads = (
        (bundle.at[:, pl.ds(4 * D, D)], c1), (act, right.at[pl.ds(0, L), :]),
        (bundle.at[:, pl.ds(0, 2 * D)], right.at[pl.ds(L, L), :]),
        (tail0, sides.at[0]), (bundle.at[:, pl.ds(3 * D, D)], sides.at[1]),
        (main0, sides.at[2]), (bundle.at[:, pl.ds(2 * D, D)], sides.at[3]),
        (right0, right_out.at[pl.ds(0, L), :]),
    )
    for k, (src, dst) in enumerate(loads):
        load(src, dst, sems.at[k])
    left[:, :L] = c[...].T
    arrived(*loads[0], sems.at[0])

    @pl.when(flags[1] == 0)
    def _():
        left[:, L:] = c_oth[...].T

    @pl.when(flags[1] != 0)
    def _():
        left[:, L:] = c1[...].T

    for k in range(1, 3):
        arrived(*loads[k], sems.at[k])
    down[...] = dot(left[...], right[...]).astype(BF)
    for k in range(4):
        arrived(*loads[3 + k], sems.at[3 + k])
        (left_tail, left_main)[k // 2][:, L * (k % 2) : L * (k % 2 + 1)] = sides[k].T
    arrived(*loads[7], sems.at[7])
    for copy in leaving:
        copy.wait()


def gram_head_kernel(rows, right1, down, left, vec, right0, head, tail_up, tail_down, vec_out, right):
    right[:L, :] = right0[:L, 3 * D :]
    right[L:, :] = right1[:L, 3 * D :]
    head[...] = dot(left[...], right[...]).astype(BF)
    other = [
        jnp.concatenate(
            [right1[L : L + 16, 128 * (3 * k + b) : 128 * (3 * k + b + 1)].astype(F32) for b in range(3)], axis=0
        )
        for k in range(2)
    ]
    total = (vec[...] + (other[0] + other[1])).astype(BF)
    vec_out[...] = total.astype(F32)
    for k, t in enumerate((tail_up, tail_down)):
        here = own_rows(rows, 0, k, t.shape[0])
        t[:, :D] = head[here, :]
        t[:, D : 3 * D] = down[here, :]
        t[:, 3 * D :] = total


def gram_main_kernel(rows, right1, left, right_in, right, main, main_up, main_down):
    right[L:, :] = right1[:L, :]
    main[...] = dot(left[...], right[:, : 3 * D]).astype(BF)
    for k, m in enumerate((main_up, main_down)):
        m[...] = main[own_rows(rows, 0, k, m.shape[0]), :]


def own_rows(rows, t, way, r):
    return pl.ds(pl.multiple_of(rows[t, way], 16), r)


def add_kernel(t, way, rows, got, *refs, count, vector):
    parts, out = refs[:count], refs[count]
    here = own_rows(rows, t, way, got.shape[0])
    at = 0
    for part in parts:
        sl = slice(at, at + part.shape[1])
        out[:, sl] = (got[:, sl].astype(F32) + part[here, :].astype(F32)).astype(BF)
        at += part.shape[1]
    if out.shape[1] > at:
        out[:, at:] = got[:, at:]
    if vector:
        refs[count + 1][...] = got[:, at : at + 128].astype(F32)


def fold_vector(va, out):
    def fold(start):
        v = va[:, start : start + D]
        w = HEAD_DIM // 2
        return jnp.concatenate(
            [v[:, 2 * w * h : 2 * w * h + w] - v[:, 2 * w * h + w : 2 * w * (h + 1)] for h in range(HEADS)],
            axis=1,
        )

    at = FIRST + 3 * D
    out[:, :at] = va[:, :at]
    out[:, at : at + HALF] = fold(at)
    out[:, at + HALF : SECOND] = fold(at + D)
    out[:, SECOND:] = va[:, at + 2 * D :]


def packed_vector(ref):
    rows = [ref[:, 128 * k : 128 * (k + 1)] for k in range(VECTOR // 128)]
    rows += [jnp.zeros((1, 128), F32)] * (PACKED[0] - len(rows))
    return jnp.concatenate(rows, axis=0)


def sum_vectors(table, vectors, slots, outs):
    n = len(vectors)
    if table is None:
        total = vectors[0][...]
    else:
        slots[table[0, 2]] = vectors[0][...]
        for k in range(1, n):
            t, way = (k + 1) // 2, (k + 1) % 2
            slots[table[t, 2 + way]] = vectors[k][...]
        total = slots[0]
        for k in range(1, n):
            total = total + slots[k]
    at = 0
    for out in outs:
        for k in range(out.shape[1] // 128):
            out[:, 128 * k : 128 * (k + 1)] = total[at + k : at + k + 1, :]
        at += out.shape[1] // 128


def place_kernel(spots, whole, flags, rows, *refs):
    count, pair, vectors, into = whole
    ins, refs = refs[: count + pair + vectors], refs[count + pair + vectors + into :]
    out, buf, sems = refs[0], refs[-3], refs[-2]
    copies = []
    if pair:
        copies += both_rows(flags[0], ins[count], ins[count + 1], refs[1], refs[-1])
        copies[0].start()
        copies[1].start()
    r, w = ins[0].shape
    for k, (t, way, column) in enumerate(spots):
        buf[k] = ins[k][...].astype(F32)
        copy = pltpu.make_async_copy(
            buf.at[k], out.at[own_rows(rows, t, way, r), pl.ds(column, w)], sems.at[k]
        )
        copy.start()
        copies.append(copy)
    if vectors:
        outs = refs[1 + pair // 2 : 5 + pair // 2]
        sum_vectors(rows if vectors > 1 else None, ins[count + pair :], refs[-4], outs)
    for copy in copies:
        copy.wait()


SMEM = pl.BlockSpec(memory_space=pltpu.SMEM)
VS = pl.BlockSpec(memory_space=pltpu.VMEM)
HBM = pl.BlockSpec(memory_space=pltpu.HBM)
ANY = pl.BlockSpec(memory_space=pl.ANY)


def sds(shape, dtype=BF):
    return jax.ShapeDtypeStruct(shape, dtype)


def call(kernel, name, in_specs, outs, scratch, flops, nbytes, limit=58, out_specs=None, aliases=None):
    return pl.pallas_call(
        kernel,
        name=name,
        in_specs=in_specs,
        out_specs=[VS] * len(outs) if out_specs is None else out_specs,
        out_shape=outs,
        scratch_shapes=scratch,
        input_output_aliases={} if aliases is None else aliases,
        compiler_params=pltpu.CompilerParams(vmem_limit_bytes=limit * MIB),
        cost_estimate=pl.CostEstimate(flops=flops, bytes_accessed=nbytes, transcendentals=0),
    )


ATTN_W = [VM((4, D, D), BF)]
ANGLES = [VM((L, D), F32), VM((L, D), F32)]
MLP_W = [VM((4, D, D), BF), VM((4, D, D), BF)]
BACK_S = [VM((D, L), BF), VM((L, D), BF), VM((2, 128, L), F32), VM((16, L), F32)]


def in_vmem(a):
    return pltpu.with_memory_space_constraint(a, pltpu.VMEM)


def in_hbm(a):
    return pltpu.with_memory_space_constraint(a, pltpu.HBM)


def row(width=D):
    return VM((L, width), BF)


def row_out(width=D):
    return pltpu.HBM((L, width), BF)


def prepare(flags, n, x, cot, *vecs):
    out = VM((x.shape[0], L), BF)

    def kernel(*refs):
        prepare_kernel(*refs, n)

    table = pltpu.HBM((2 * n if n <= 16 else 1, 4), I32)
    return call(
        kernel, "prepare", [SMEM] + [VS] * 6, [out] * 4 + [pltpu.HBM((1, VECTOR), F32), table], [], 1000,
        int(1e6), 8, out_specs=[VS] * 5 + [SMEM],
    )(flags, *(in_hbm(a) for a in (x, cot) + vecs))


def positions(flags, grid, own, oth):
    hbm = pltpu.HBM
    return call(
        positions_kernel, "positions", [SMEM, SMEM, VS, VS],
        [VM((L, D), F32), VM((L, D), F32), hbm((L, 128), F32), hbm((8, L), F32)],
        [], int(1e8), int(3e6), 56,
    )(flags, grid, own, oth)


def first_pass(*a):
    results = call(
        first_kernel, "first_pass", [SMEM] + [VS] * 8 + [HBM] * 2 + [VS] * 2,
        [row(), row_out()] + ANGLES + ATTN_W + MLP_W,
        [row(), VM((D, L), BF), row(3 * D), VM((HEADS, L, L), BF), VM((16, L), F32), row(), VM((D, L), BF),
         VM((D, L), BF), row(), DMA((13,))],
        int(8e9), int(20e6), 24, out_specs=[VS, HBM] + [VS] * HELD,
        aliases={len(a) - 2: 2, len(a) - 1: 3},
    )(*a)
    return results[0], results[1], results[2:]


SAVED = [VM((L, D), BF), VM((L, D), BF), VM((16, L), F32), VM((L, D), BF), VM((L, FF), BF)]
HEAD_S = [VM((L, 3 * D), BF), VM((HEADS, L, L), BF)]


def second_pass(held, *a):
    outs = [
        row_out(FF // 2), row_out(), row_out(), row_out(5 * D), row_out(3 * D), pltpu.HBM((HEADS, L, L), BF)
    ]
    resident = ANGLES + ATTN_W + MLP_W + SAVED
    results = call(
        second_kernel, "second_pass", [SMEM] + [VS] * (7 + HELD),
        resident + [row(FF // 2), row(FF // 2), row()] + outs,
        HEAD_S + [row(), row(), VM((D, L), BF), VM((D, L), BF), VM((L, D), F32), VM((L, D), F32)]
        + BACK_S + [row(3 * D), DMA((9,))],
        int(18e9), int(20e6), 24, out_specs=[VS] * (len(resident) + 3) + [HBM] * len(outs),
        aliases={len(a) + k: k for k in range(HELD)},
    )(*a, *(in_vmem(x) for x in held))
    n = len(resident)
    return results[:n], results[n : n + 2], results[n + 2], results[n + 3 :]


def late_pass(held, *a):
    results = call(
        late_kernel, "late_pass", [SMEM] + [VS] * (len(a) - 1 + len(held)),
        ANGLES + ATTN_W + MLP_W + SAVED + [sds((L, D))] * 2, [], int(2e9), int(5e6), 24,
        aliases={len(a) + k: k for k in range(len(held))},
    )(*a, *(in_vmem(x) for x in held))
    return results[: len(held)], results[len(held) :]


def back_pass(held, *a):
    return call(
        back_kernel, "back_pass", [SMEM] + [VS] * 5 + [HBM] * 2 + [VS] * len(held),
        [row(), row(), row(), VM(PACKED, F32), row_out(FF), pltpu.HBM((L + 16, FF), BF)],
        HEAD_S
        + [row(FF), row(FF), VM((1, FIRST + 6 * D), F32), VM((1, VECTOR), F32), VM((1, VECTOR), F32),
           VM((16, D), BF)]
        + BACK_S + [DMA((5,))],
        int(10e9), int(15e6), 24, out_specs=[VS] * 4 + [HBM] * 2,
    )(*a, *(in_vmem(x) for x in held))


def gram_down(*a):
    square = VM((D, 2 * L), BF)
    return call(
        gram_down_kernel, "gram_down", [SMEM] + [VS] * 6 + [HBM, ANY] + [HBM] * 3,
        [VM((D, 2 * D), BF), square, square, VM((2 * L, FF), BF), pltpu.HBM((2 * L, D), BF), row_out(), row_out()],
        [row(), VM((4, L, D), BF), square, VM((2 * L, 2 * D), BF), DMA((8,)), DMA((4,))], int(2e9), int(8e6), 20,
        out_specs=[VS] * 4 + [HBM] * 3,
    )(*a)


def gram_head(rows, r, *a):
    wide = VM((r, 3 * D + 128), BF)
    return call(
        gram_head_kernel, "gram_head", [SMEM] + [VS] * 5, [VM((D, D), BF), wide, wide, VM(PACKED, F32)],
        [VM((2 * L, D), BF)], int(1e9), int(5e6), 12,
    )(rows, *a)


def gram_main(rows, r, *a):
    shard = VM((r, 3 * D), BF)
    return call(
        gram_main_kernel, "gram_main", [SMEM] + [VS] * 3,
        [VM((2 * L, FF), BF), VM((D, 3 * D), BF), shard, shard], [], int(6e9), int(12e6), 20, aliases={3: 0},
    )(rows, *a)[1:]


def add(t, way, rows, got, parts, vector, wide):
    count = len(parts)

    def kernel(*refs):
        add_kernel(t, way, *refs, count=count, vector=vector)

    width = sum(p.shape[1] for p in parts)
    out = VM((got.shape[0], width + (128 if wide else 0)), BF)
    results = call(
        kernel, "add", [SMEM] + [VS] * (1 + count), [out] + [VM(PACKED, F32)] * vector, [], 1000, int(2e7), 4
    )(rows, in_vmem(got), *(in_vmem(p) for p in parts))
    return results[0], results[1:]


def place(flags, spots, rows, shards, total, pair=(), vectors=()):
    count = len(shards)
    into = [] if total is None else [total]
    whole = count, len(pair), len(vectors), len(into)

    def kernel(*refs):
        place_kernel(spots, whole, *refs)

    outs = [pltpu.HBM((D, 6 * D), F32)]
    outs += [pltpu.HBM((2 * L, D), BF)] if pair else []
    outs += [sds((1, w), F32) for w in (D, D, FF, D)] if vectors else []
    given = len(shards) + len(pair) + len(vectors)
    return call(
        kernel, "place", [SMEM, SMEM] + [VS] * given + [HBM] * len(into), outs,
        [VM((max(len(vectors), 1),) + PACKED, F32), VM((count,) + shards[0].shape, F32), DMA((count,)), DMA((2,))],
        1000,
        int(2e7), 24, out_specs=[HBM] * (2 if pair else 1) + ([VS] * 4 if vectors else []),
        aliases={given + 2: 0} if into else {},
    )(flags, rows, *shards, *pair, *vectors, *into)


def core_swap(a):
    return lax.ppermute(a, "section", [(0, 1), (1, 0), (2, 3), (3, 2)])


def after(value, first):
    return lax.optimization_barrier((value, first))[0]


class Cycle:
    def __init__(self, rows):
        self.n = n = lax.axis_size("dp")
        self.r = D // (2 * n)
        order = list(range(0, n, 2)) + list(range(n - 1, 0, -2))
        self.pairs = [[(order[k], order[(k + d) % n]) for k in range(n)] for d in (1, -1)]
        self.rows = rows

    def placed(self, k):
        return 2 * self.n - 1 if k == 0 else self.n + k - 1


class Chain:
    def __init__(self, cycle, parts, cur, carries=False):
        self.cycle, self.parts, self.cur, self.carries = cycle, parts, cur, carries
        self.t = 0
        self.shards = []
        self.vectors = []

    def step(self, token):
        c = self.cycle
        got = [lax.ppermute(a, "dp", p) for a, p in zip(self.cur, c.pairs)]
        self.t += 1
        t = self.t
        if t < c.n:
            self.cur = []
            for way in range(2):
                vector = self.carries and t <= (c.n - way) // 2
                out, came = add(
                    t, way, c.rows, after(got[way], token), self.parts, vector, self.carries and t < c.n // 2
                )
                self.cur.append(out)
                self.vectors += came
                token = out
        else:
            first = after(got[0], token)
            self.cur = [first, after(got[1], first)]
        if self.t >= c.n - 1:
            self.shards.append(self.cur)
        return self.cur


def small_ring():
    return lax.axis_size("dp") <= 16


def summed(flags, rows, main, tail, token, pair, vector):
    if not small_ring():
        chains, vector = lax.psum([main, tail], "dp"), lax.psum(vector, "dp")
        return place(flags, [(0, 0, 0), (0, 0, 3 * D)], rows, chains, None, pair, [vector])
    cycle = main.cycle
    n = cycle.n
    total = None
    waiting, results = [], {}
    while main.t < 2 * n - 2:
        for chain, column in ((tail, 3 * D), (main, 0)):
            if total is not None:
                token = (token, total)
            token = chain.step(token)
            whole = len(chain.shards)
            if whole:
                t = cycle.placed(whole - 1)
                waiting += [((t, way, column), chain.shards[-1][way]) for way in range(2)]
            if whole == n or chain is main and whole and whole % 2 == 0:
                now, then = "rows" not in results, "vectors" not in results and whole >= min(4, n)
                total, *more = place(
                    flags, [a for a, _ in waiting], cycle.rows, [b for _, b in waiting], total,
                    pair if now else (), [vector] + tail.vectors if then else (),
                )
                if now:
                    results["rows"] = more.pop(0)
                if then:
                    results["vectors"] = more
                waiting = []
    return total, results["rows"], *results["vectors"]


def body(
    block_input, cotangent, grid_sizes, section_weight, norm_gain, norm_bias, first_vector, second_vector
):
    section = lax.axis_index("section")
    core = section % 2
    n = lax.axis_size("dp")
    i = lax.axis_index("dp")
    where = jnp.where(i % 2 == 0, i // 2, n - 1 - i // 2)
    flags = in_hbm(jnp.stack([core, section // 2, where]).astype(I32))
    first_layer = section < 2

    keep, send, away, across, vown, rows = prepare(
        flags, n, block_input.T, cotangent.T, norm_gain, norm_bias, first_vector, second_vector
    )
    if n % 2 == 0:
        voth = lax.ppermute(
            vown, ("section", "dp"), [(n * s + d, n * (s ^ 1) + (d ^ 1)) for s in range(4) for d in range(n)]
        )
    else:
        voth = core_swap(vown)
    r = D // (2 * n) if small_ring() else PACKED[0]
    cosf, sinf, pos, segr = positions(flags, grid_sizes, in_hbm(vown), voth)
    vown, voth, rows, pos, segr = (in_hbm(a) for a in (vown, voth, rows, pos, segr))
    got = core_swap(send)
    away = lax.ppermute(away, "section", [(0, 2), (1, 3), (2, 0), (3, 1)])
    across = lax.ppermute(across, "section", [(0, 3), (1, 2), (2, 1), (3, 0)])
    own = in_hbm(section_weight[0])
    oth = in_hbm(core_swap(section_weight[0]))

    x_two, field, held = first_pass(
        flags, keep, got, away, across, vown, voth, pos, segr, own, oth, in_vmem(cosf), in_vmem(sinf)
    )
    field = in_hbm(field)
    x_got, x_late = (lax.ppermute(x_two, "section", [pair]) for pair in ((0, 2), (1, 3)))
    held, active, c_two, (act_mine, main_left, tail_left, bundle, qkv, pt) = second_pass(
        held, flags, field, x_got, x_late, vown, voth, pos, segr
    )
    act_mine, main_left, tail_left = (in_hbm(a) for a in (act_mine, main_left, tail_left))
    c_got = lax.ppermute(c_two, "section", [(2, 0), (3, 1)])
    held, (x_keep, x_send) = late_pass(held, flags, x_two, vown, voth, *(in_vmem(a) for a in active))
    c_got = after(c_got, x_keep)
    bundle = core_swap(after(bundle, c_got))
    x_oth = core_swap(after(x_send, c_got))

    c_keep, c_send, c_out, vec, right, right_send = back_pass(
        held, flags, field, c_got, vown, voth, pos, in_hbm(qkv), in_hbm(pt)
    )
    c_oth = core_swap(c_got)
    right_oth = core_swap(after(right_send, (c_oth, bundle, x_oth)))
    down, left_main, left_tail, right, activations, c_keep, c_send = gram_down(
        flags, c_out, c_oth, x_keep, x_oth, in_vmem(c_keep), in_vmem(c_send), act_mine, bundle, main_left, tail_left, in_hbm(right)
    )
    head, *tail_first, vec = gram_head(rows, r, right_oth, down, left_tail, vec, right)
    if small_ring():
        cycle = Cycle(rows)
        tail = Chain(cycle, [head, down], tail_first, True)
    else:
        tail = jnp.concatenate([head, down], axis=1)
    main, *main_first = gram_main(rows, r, right_oth, left_main, right)
    if small_ring():
        main = Chain(cycle, [main], main_first)
        token = main.cur
    else:
        token = main
    weight_grad, input_grads, *vectors = summed(
        flags, rows, main, tail, token, (c_keep, core_swap(after(c_send, token))), vec
    )
    return (
        activations[None],
        input_grads[None],
        weight_grad[None],
        *vectors,
    )


def solution(mesh):
    in_specs = (
        P("dp", "section"),
        P("dp", "section"),
        P("dp", None, None),
        P("section", None, None),
        P("section", None),
        P("section", None),
        P("section", None),
        P("section", None),
    )
    out_specs = (
        P("section", "dp", None),
        P("section", "dp", None),
        P("section", None, None),
        P("section", None),
        P("section", None),
        P("section", None),
        P("section", None),
    )
    return jax.shard_map(body, mesh=mesh, in_specs=in_specs, out_specs=out_specs, check_vma=False)
```

```python
import jax
import jax.numpy as jnp
from jax import lax
from jax.experimental import pallas as pl
from jax.experimental.pallas import tpu as pltpu
from jax.sharding import PartitionSpec as P

D = 768
HEADS = 12
HEAD_DIM = 64
FF = 3072
L = 384
HALF = D // 2
F32 = jnp.float32
BF = jnp.bfloat16
I32 = jnp.int32
NT = (((1,), (1,)), ((), ()))
TN = (((0,), (0,)), ((), ()))
VM = pltpu.VMEM
DMA = pltpu.SemaphoreType.DMA
MIB = 1024 * 1024
LN2 = 0.6931471805599453
GAIN, SHIFT = slice(0, D), slice(D, 2 * D)
FIRST, SECOND = 2 * D, 2 * D + FF
VECTOR = 3 * D + FF
LONGEST = 16
PACKED = (48, 128)


def dot(a, b):
    return jnp.dot(a, b, preferred_element_type=F32)


def dot_nt(a, b):
    return lax.dot_general(a, b, NT, preferred_element_type=F32)


def dot_tn(a, b):
    return lax.dot_general(a, b, TN, preferred_element_type=F32)


def norm_parts(x):
    center = x - jnp.mean(x, axis=-1, keepdims=True)
    inv = lax.rsqrt(jnp.mean(center * center, axis=-1, keepdims=True) + 1e-06)
    return center * inv, inv


def swap_halves(a):
    lane = lax.broadcasted_iota(I32, (1, 128), 1)
    first = (lane % HEAD_DIM) < HEAD_DIM // 2
    out = []
    for i in range(a.shape[1] // 128):
        s = a[:, 128 * i : 128 * (i + 1)]
        out.append(jnp.where(first, pltpu.roll(s, 96, 1), pltpu.roll(s, 32, 1)))
    return jnp.concatenate(out, axis=1) if len(out) > 1 else out[0]


def lanes(start, size):
    if isinstance(start, int):
        return slice(start, start + size)
    return pl.ds(pl.multiple_of(start, 128), size)


def rows_at(start, size):
    if isinstance(start, int):
        return slice(start, start + size)
    return pl.ds(pl.multiple_of(start, size), size)


def cols(start, size):
    return (slice(None), pl.ds(start, size))


def pick(flag, want, own, oth, src, dst, sem):
    @pl.when(flag == want)
    def _():
        pltpu.make_async_copy(own.at[src], dst, sem).start()

    @pl.when(flag != want)
    def _():
        pltpu.make_async_copy(oth.at[src], dst, sem).start()


def load(src, dst, sem):
    pltpu.make_async_copy(src, dst, sem).start()


def arrived(src, dst, sem):
    pltpu.make_async_copy(src, dst, sem).wait()


def load_attn(core, own, oth, wa, sems, i):
    pick(core, 0, own, oth, cols(D * i, D), wa.at[i], sems.at[i])


def wait_attn(own, wa, sems, i):
    arrived(own.at[cols(D * i, D)], wa.at[i], sems.at[i])


def hidden_start(core, j):
    return pl.multiple_of(FF // 2 * ((core + j // 2) % 2) + D * (j % 2), 128)


def load_mlp(core, own, oth, w1, wd, sems, j):
    pick(core, 1, own, oth, (slice(None), pl.ds(hidden_start(core, j), D)), w1.at[j], sems.at[j])
    load((own if j < 2 else oth).at[cols(FF + D * (j % 2), D)], wd.at[j], sems.at[4 + j])


class Forward:
    def __init__(self, on_the_way, core, own, oth, wa, w1, wd, sems):
        self.attn = core, own, oth, wa, sems
        self.mlp = core, own, oth, w1, wd, sems.at[pl.ds(4, 8)]
        self.own, self.wa, self.sems, self.on_the_way = own, wa, sems, on_the_way

        @pl.when(on_the_way)
        def _():
            load_attn(*self.attn, 0)
            load_attn(*self.attn, 1)

        @pl.when(jnp.logical_not(on_the_way))
        def _():
            for i in range(4):
                load_attn(*self.attn, i)
                load_mlp(*self.mlp, i)
                wait_attn(own, wa, sems, i)
                wait_mlp(own, w1, wd, self.mlp[-1], i)

    def wait(self, i):
        @pl.when(self.on_the_way)
        def _():
            wait_attn(self.own, self.wa, self.sems, i)
            if i < 2:
                load_attn(*self.attn, i + 2)
            elif i == 2:
                for j in range(4):
                    load_mlp(*self.mlp, j)

    def wait_mlp(self):
        core, own, oth, w1, wd, sems = self.mlp

        @pl.when(self.on_the_way)
        def _():
            for j in range(4):
                wait_mlp(own, w1, wd, sems, j)


def wait_mlp(own, w1, wd, sems, j):
    if w1 is not None:
        arrived(own.at[cols(0, D)], w1.at[j], sems.at[j])
    arrived(own.at[cols(0, D)], wd.at[j], sems.at[4 + j])


def vectors(core, own, oth):
    a, b = own[...], oth[...]
    return jnp.where(core == 0, a, b), jnp.where(core == 0, b, a)


def attention(x, vec, wa, wait, cosf, sinf, segc, segr, qkv, pt, rec, ml, mlt, vt, n_ref):
    xh, inv = norm_parts(x)
    n = (xh * vec[:, GAIN] + vec[:, SHIFT]).astype(BF)
    n_ref[...] = n
    for i in range(3):
        wait(i)
        part = dot(n, wa[i]) + vec[:, FIRST + D * i : FIRST + D * (i + 1)]
        if i < 2:
            part = part * cosf[...] + swap_halves(part) * sinf[...]
        if i == 0:
            part = part * (HEAD_DIM**-0.5 / LN2)
        qkv[:, D * i : D * (i + 1)] = part.astype(BF)
    vt[...] = qkv[:, 2 * D : 3 * D].T
    same = segc == segr
    lane = lax.broadcasted_iota(I32, (1, 128), 1)

    def score(h):
        p = 128 * (h // 2)
        keys = jnp.where((lane // HEAD_DIM) == h % 2, qkv[:, D + p : D + p + 128], BF(0))
        return dot_nt(keys, qkv[:, p : p + 128])

    ahead = score(0)
    for h in range(HEADS):
        st = ahead
        if h + 1 < HEADS:
            ahead = score(h + 1)
        st = jnp.where(same, st, -1e30)
        e = jnp.exp2(st - jnp.max(st, axis=0, keepdims=True))
        r = 1.0 / jnp.sum(e, axis=0, keepdims=True)
        rec[h : h + 1, :] = r
        e = e.astype(BF)
        pt[h] = e
        here = slice(HEAD_DIM * h, HEAD_DIM * (h + 1))
        mlt[here, :] = (dot(vt[here, :], e) * r).astype(BF)
    ml[...] = mlt[...].T
    wait(3)
    out = x + dot(ml[...], wa[3]) + vec[:, SECOND : SECOND + D]
    return out.astype(BF), xh, inv


C0 = 0.7978845608028654
C1 = 0.044715


def gelu(h):
    h2 = h * h
    t = jnp.tanh(C0 * (h + C1 * h * h2))
    half = 0.5 * (1.0 + t)
    return h * half, half + (0.5 * C0) * h * (1.0 - t * t) * (1.0 + (3.0 * C1) * h2)


def norm_back(gn, xh, inv, gain, c):
    u = gn * gain
    gx = inv * (
        u - jnp.mean(u, axis=-1, keepdims=True) - xh * jnp.mean(u * xh, axis=-1, keepdims=True)
    )
    return (c.astype(F32) + gx).astype(BF)


def head_select():
    head = lax.broadcasted_iota(I32, (16, D), 0)
    lane = lax.broadcasted_iota(I32, (16, D), 1)
    return jnp.where(lane // HEAD_DIM == head, 1.0, 0.0).astype(BF)


def split_two(a):
    hi = a.astype(BF)
    return hi, (a - hi.astype(F32)).astype(BF)


def attention_back(c, wo, cosf, sinf, qkv, pt, rec, ml, kt, gm, gqt, dsum, pair_of, emit):
    kt[...] = qkv[:, D : 2 * D].T
    gm_wide = dot_nt(c, wo[...])
    sel = head_select()
    hi, lo = split_two(gm_wide * ml[...].astype(F32))
    row = lax.broadcasted_iota(I32, (16, L), 0)
    recs = jnp.where(row < HEADS, rec[...], 0.0)
    dsum[...] = (dot_nt(sel, hi) + dot_nt(sel, lo)) * recs
    hi, lo = split_two(recs)
    gm[...] = (gm_wide * (dot_tn(hi, sel) + dot_tn(lo, sel))).astype(BF)
    lane = lax.broadcasted_iota(I32, (1, 128), 1)

    def spot(h):
        return lanes(128 * pair_of(h // 2), 128), (lane // HEAD_DIM) == h % 2

    def from_values(h):
        sl, here = spot(h)
        values = qkv[:, lanes(2 * D + 128 * pair_of(h // 2), 128)]
        return dot_nt(jnp.where(here, values, BF(0)), gm[:, sl])

    ahead = from_values(0)
    for h in range(HEADS):
        gpt = ahead
        if h + 1 < HEADS:
            ahead = from_values(h + 1)
        sl, here = spot(h)
        head = 2 * pair_of(h // 2) + h % 2
        e = pt[head]
        gvh = dot(e, jnp.where(here, gm[:, sl], BF(0)))
        gst = (e.astype(F32) * (gpt - dsum[rows_at(head, 1), :])).astype(BF)
        gkh = dot(gst, jnp.where(here, qkv[:, sl], BF(0)))
        kth = kt[rows_at(HEAD_DIM * head, HEAD_DIM), :]
        gqt[h // 2 % 2, HEAD_DIM * (h % 2) : HEAD_DIM * (h % 2 + 1), :] = dot(kth, gst)
        gv = gvh if h % 2 == 0 else gv + gvh
        gk = gkh if h % 2 == 0 else gk + gkh
        if h % 2 == 1:
            gq = gqt[h // 2 % 2].T * (HEAD_DIM**-0.5)
            gk = gk * LN2
            cs, sn = cosf[:, sl], sinf[:, sl]
            sq, sk = swap_halves(gq), swap_halves(gk)
            emit(
                h // 2, sl, sq, sk,
                ((gq * cs - sq * sn).astype(BF), (gk * cs - sk * sn).astype(BF), gv.astype(BF)),
            )


def positions_kernel(flags, grid, vown, voth, cosf, sinf, pos, segr):
    core = flags[0]
    vec = vectors(core, vown, voth)[0]
    h0, w0, h1, w1 = (grid[core, k // 2, k % 2] for k in range(4))
    e1 = h0 * w0
    e2 = e1 + h1 * w1

    def place(t):
        segment = (t >= e1).astype(I32) + (t >= e2).astype(I32)
        width = jnp.where(segment == 0, w0, w1).astype(F32)
        inside = (t - jnp.where(segment == 0, 0, e1)).astype(F32)
        row = jnp.floor((inside + 0.5) / width)
        column = inside - row * width
        return segment, jnp.where(segment < 2, row, 0.0), jnp.where(segment < 2, column, 0.0)

    segment, row, column = place(lax.broadcasted_iota(I32, (L, 128), 0))
    lane = lax.broadcasted_iota(I32, (L, 128), 1)
    pos[...] = jnp.where(lane == 0, column, jnp.where(lane == 1, row, segment.astype(F32)))
    t = lax.broadcasted_iota(I32, (8, L), 1)
    segr[...] = (t >= e1).astype(F32) + (t >= e2).astype(F32)

    def by_lane(start):
        parts = []
        for h in range(HEADS):
            f = vec[:, start + 32 * h : start + 32 * (h + 1)]
            parts += [f, f]
        return jnp.concatenate(parts, axis=1)

    number = lax.broadcasted_iota(I32, (16, D), 0).astype(F32)

    def look_up(which, table):
        hi, rest = split_two(table)
        mid, low = split_two(table - hi.astype(F32))
        tables = jnp.concatenate([hi, mid, low], axis=0)
        hit = (lax.broadcasted_iota(I32, (L, 48), 1) % 16).astype(F32) == which[:, :48]
        return dot(jnp.where(hit, 1.0, 0.0).astype(BF), tables)

    ax = number * by_lane(FIRST + 3 * D)
    ay = number * by_lane(FIRST + 3 * D + HALF)
    cx, sx = look_up(column, jnp.cos(ax)), look_up(column, jnp.sin(ax))
    cy, sy = look_up(row, jnp.cos(ay)), look_up(row, jnp.sin(ay))
    cosf[...] = cx * cy - sx * sy
    lane = lax.broadcasted_iota(I32, (1, D), 1)
    sign = jnp.where(lane % HEAD_DIM < HEAD_DIM // 2, -1.0, 1.0)
    sinf[...] = (sx * cy + cx * sy) * sign


def prepare_kernel(
    flags, x, cot, gain, shift, first, second, keep, send, away, across, vec, table, n
):
    core, layer, where = flags[0], flags[1], flags[2]
    for t in range(table.shape[0]):
        for way, d in ((0, 1), (1, -1)):
            if n > LONGEST:
                table[t, way], table[t, 2 + way] = 0, 0
                continue
            at = lax.rem(where - d * (t % n) + 2 * n, n)
            table[t, way] = at * (D // (2 * n)) + way * HALF
            table[t, 2 + way] = jnp.where(2 * at < n, 2 * at, 2 * (n - at) - 1)
    for at, (mine, other) in enumerate(((x, cot), (cot, x))):

        @pl.when(layer == at)
        def _(mine=mine, other=other):
            keep[...] = mine[:, lanes(L * core, L)]
            send[...] = mine[:, lanes(L * (1 - core), L)]
            away[...] = other[:, lanes(L * core, L)]
            across[...] = other[:, lanes(L * (1 - core), L)]

    vec[:, GAIN] = gain[...]
    vec[:, SHIFT] = shift[...]
    vec[:, FIRST:SECOND] = first[...]
    vec[:, SECOND:] = second[...]


HELD = 5


def first_kernel(
    flags, keep, got, away, across, vown, voth, pos, segr, own, oth, cos_in, sin_in,
    out, field_out, cosf, sinf, wa, w1, wd, field, turned, qkv, pt, rec, ml, mlt, vt, n_ref, sems,
):
    core, layer = flags[0], flags[1]
    loads = Forward((core == 0) & (layer == 0), core, own, oth, wa, w1, wd, sems)
    w = keep.shape[0]
    for k in range(2):
        for at in range(2):

            @pl.when((core == k) & (layer == at))
            def _(k=k, at=at):
                parts = {(at, k): keep, (at, 1 - k): got, (1 - at, k): away, (1 - at, 1 - k): across}
                for s in range(4):
                    turned[w * s : w * (s + 1), :] = parts[s // 2, s % 2][...]

    field[...] = turned[...].T
    keeping = pltpu.make_async_copy(field, field_out, sems.at[12])
    keeping.start()
    @pl.when(layer == 0)
    def _():
        va, vm = vectors(core, vown, voth)
        x_mid, _, _ = attention(
            field[...].astype(F32), va, wa, loads.wait, cosf, sinf, pos[:, 2:3], segr[0:1, :],
            qkv, pt, rec, ml, mlt, vt, n_ref,
        )
        x = x_mid.astype(F32)
        xh, _ = norm_parts(x)
        n = (xh * vm[:, GAIN] + vm[:, SHIFT]).astype(BF)
        loads.wait_mlp()
        acc = x + vm[:, SECOND : SECOND + D]
        first = hidden_bias(core, vm)
        ahead = dot(n, w1[0])
        for j in range(4):
            h = ahead + first[:, D * j : D * (j + 1)]
            if j < 3:
                ahead = dot(n, w1[j + 1])
            acc = acc + dot_nt(gelu(h)[0].astype(BF), wd[j])
        out[...] = acc.astype(BF)

    keeping.wait()


def hidden_bias(core, vm):
    a, b = vm[:, FIRST : FIRST + FF // 2], vm[:, FIRST + FF // 2 : SECOND]
    return jnp.concatenate([jnp.where(core == 0, a, b), jnp.where(core == 0, b, a)], axis=1)


def second_kernel(
    flags, field, got, got_late, vown, voth, pos, segr, *refs,
):
    (
        cosf, sinf, wa, w1, wd, xi, xm, rec, ml, dg, actm, acts, cx, act_out, main_out, tail_out, bundle,
        qkv_out, pt_out, qkv, pt, na, nm, mlt, vt, xha, xhm, kt, gm, gqt, dsum, gp, outs,
    ) = refs[HELD:]
    core, layer = flags[0], flags[1]
    va, vm = vectors(core, vown, voth)
    x = jnp.where(core == 0, got[...].astype(F32), got_late[...].astype(F32))
    x = jnp.where(layer == 0, field[...].astype(F32), x)
    xi[...] = x.astype(BF)
    x_mid, xh, inv_a = attention(
        x, va, wa, lambda what: None, cosf, sinf, pos[:, 2:3], segr[0:1, :], qkv, pt, rec, ml, mlt, vt, na
    )
    xha[...] = xh
    xm[...] = x_mid
    load(qkv, qkv_out, outs.at[7])
    load(pt, pt_out, outs.at[8])
    xh, inv_m = norm_parts(x_mid.astype(F32))
    xhm[...] = xh
    n = (xh * vm[:, GAIN] + vm[:, SHIFT]).astype(BF)
    nm[...] = n
    sides = (
        main_out, tail_out, bundle.at[:, pl.ds(2 * D, D)], bundle.at[:, pl.ds(3 * D, D)],
    )
    load(field, bundle.at[:, pl.ds(4 * D, D)], outs.at[4])
    for when, sources in ((core == 0, (na, ml, nm, nm)), (core != 0, (nm, nm, na, ml))):

        @pl.when(when)
        def _(sources=sources):
            for k, (src, dst) in enumerate(zip(sources, sides)):
                load(src, dst, outs.at[k])

    first = hidden_bias(core, vm)
    c = field[...]

    def forward(j):
        return dot(n, w1[j])

    def chunk(j, h):
        act, slope = gelu(h + first[:, D * j : D * (j + 1)])
        (actm, acts)[j // 2][:, D * (j % 2) : D * (j % 2 + 1)] = act.astype(BF)
        slope = slope.astype(BF)
        dg[:, D * j : D * (j + 1)] = slope
        return slope

    def leave():
        load(acts, bundle.at[:, pl.ds(0, 2 * D)], outs.at[5])
        load(actm, act_out, outs.at[6])

    @pl.when(layer >= 0)
    def _():
        ahead = forward(0), dot(c, wd[0])
        gn = None
        for j in range(4):
            h, ga = ahead
            if j < 3:
                ahead = forward(j + 1), dot(c, wd[j + 1])
            slope = chunk(j, h)
            part = dot_nt((ga * slope.astype(F32)).astype(BF), w1[j])
            gn = part if gn is None else gn + part
        leave()
        c_mid = norm_back(gn, xhm[...], inv_m, vm[:, GAIN], c)

        def emit(p, sl, sq, sk, grads):
            for i in range(3):
                gp[:, D * i + 128 * p : D * i + 128 * (p + 1)] = grads[i]

        attention_back(
            c_mid, wa.at[3], cosf, sinf, qkv, pt, rec, ml, kt, gm, gqt, dsum, lambda p: p, emit
        )
        gn = None
        for i in range(3):
            part = dot_nt(gp[:, D * i : D * (i + 1)], wa[i])
            gn = part if gn is None else gn + part
        cx[...] = norm_back(gn, xha[...], inv_a, va[:, GAIN], c_mid)

    for k, (src, dst) in enumerate(
        tuple((nm, side) for side in sides)
        + ((field, sides[2]), (acts, bundle.at[:, pl.ds(0, 2 * D)]), (actm, act_out), (qkv, qkv_out), (pt, pt_out))
    ):
        arrived(src, dst, outs.at[k])


def late_kernel(flags, x_two, vown, voth, actm, acts, *refs):
    xm, wd = refs[HELD + 1], refs[HELD - 1]
    keep, send = refs[-2:]
    core, layer = flags[0], flags[1]
    vm = vectors(core, vown, voth)[1]
    mid = xm[...].astype(F32)
    acc = mid + vm[:, SECOND : SECOND + D]
    for j in range(4):
        acc = acc + dot_nt((actm, acts)[j // 2][:, D * (j % 2) : D * (j % 2 + 1)], wd[j])
    acc = jnp.where(layer == 0, x_two[...].astype(F32), acc)
    keep[...] = jnp.where(core == 0, mid, acc).astype(BF)
    send[...] = jnp.where(core == 0, acc, mid).astype(BF)


def both_rows(core, keep, got, out, sems):
    return [
        pltpu.make_async_copy(src, out.at[rows_at(L * at, L), :], sems.at[k])
        for k, (src, at) in enumerate(((keep, core), (got, 1 - core)))
    ]


def norm_stats(gn, x, vec):
    xh, inv = norm_parts(x)
    vec[:, GAIN] = jnp.sum(gn * xh, axis=0, keepdims=True)
    vec[:, SHIFT] = jnp.sum(gn, axis=0, keepdims=True)
    return xh, inv


def back_kernel(
    flags, field, got, vown, voth, pos, qkv_in, pt_in, cosf, sinf, wa, w1, wd, xi, xm, rec, ml, dg,
    row_keep, row_send, c_out, vec_keep, keep_out, send_out,
    qkv, pt, gh, gp, va_grad, vm_grad, folded, vec_send, kt, gm, gqt, dsum, outs,
):
    core, layer = flags[0], flags[1]
    load(qkv_in, qkv, outs.at[3])
    load(pt_in, pt, outs.at[4])
    va, vm = vectors(core, vown, voth)
    wide = jnp.where(layer == 0, got[...].astype(F32), field[...].astype(F32))
    c = wide.astype(BF)
    c_out[...] = c
    vm_grad[:, SECOND:] = jnp.sum(wide, axis=0, keepdims=True)

    def from_output(j):
        return dot(c, wd[j])

    ahead = from_output(0)
    gn = None
    for j in range(4):
        ga = ahead
        if j < 3:
            ahead = from_output(j + 1)
        part = (ga * dg[:, D * j : D * (j + 1)].astype(F32)).astype(BF)
        start = hidden_start(core, j)
        gh[:, pl.ds(start, D)] = part
        vm_grad[:, pl.ds(pl.multiple_of(FIRST + start, 128), D)] = jnp.sum(
            part.astype(F32), axis=0, keepdims=True
        )
        part = dot_nt(part, w1[j])
        gn = part if gn is None else gn + part
    for when, dst in ((core == 0, send_out.at[pl.ds(0, L), :]), (core != 0, keep_out)):

        @pl.when(when)
        def _(dst=dst):
            load(gh, dst, outs.at[1])

    xh, inv = norm_stats(gn, xm[...].astype(F32), vm_grad)
    c = norm_back(gn, xh, inv, vm[:, GAIN], c)
    gp[:, 3 * D :] = c
    va_grad[:, FIRST + 5 * D :] = jnp.sum(c.astype(F32), axis=0, keepdims=True)
    colp, rowp = pos[:, 0:1], pos[:, 1:2]

    def emit(p, sl, sq, sk, grads):
        qr = qkv[:, sl].astype(F32) * (LN2 * HEAD_DIM**0.5)
        th = sq * qr + sk * qkv[:, D + 128 * p : D + 128 * (p + 1)].astype(F32)
        at = FIRST + 3 * D + 128 * p
        va_grad[:, at : at + 128] = jnp.sum(th * colp, axis=0, keepdims=True)
        va_grad[:, at + D : at + D + 128] = jnp.sum(th * rowp, axis=0, keepdims=True)
        for i, g in enumerate(grads):
            gp[:, D * i + 128 * p : D * i + 128 * (p + 1)] = g
            va_grad[:, FIRST + D * i + 128 * p : FIRST + D * i + 128 * (p + 1)] = jnp.sum(
                g.astype(F32), axis=0, keepdims=True
            )

    arrived(qkv_in, qkv, outs.at[3])
    arrived(pt_in, pt, outs.at[4])
    attention_back(
        c, wa.at[3], cosf, sinf, qkv, pt, rec, ml, kt, gm, gqt, dsum, lambda p: p, emit
    )
    for when, dst in ((core == 0, keep_out), (core != 0, send_out.at[pl.ds(0, L), :])):

        @pl.when(when)
        def _(dst=dst):
            load(gp, dst, outs.at[2])

    gn = None
    for i in range(3):
        part = dot_nt(gp[:, D * i : D * (i + 1)], wa[i])
        gn = part if gn is None else gn + part
    xh, inv = norm_stats(gn, xi[...].astype(F32), va_grad)
    cx = norm_back(gn, xh, inv, va[:, GAIN], c).astype(F32)
    wide = c.astype(F32)
    row_keep[...] = jnp.where(core == 0, cx, wide).astype(BF)
    row_send[...] = jnp.where(core == 0, wide, cx).astype(BF)
    fold_vector(va_grad, folded)
    a, m = packed_vector(folded), packed_vector(vm_grad)
    vec_keep[...] = jnp.where(core == 0, a, m)
    for k, part in enumerate(split_two(jnp.where(core == 0, m, a))):
        for b in range(3):
            vec_send[:, 128 * (3 * k + b) : 128 * (3 * k + b + 1)] = part[16 * b : 16 * (b + 1), :]
    vec_out = send_out.at[pl.ds(L, 16), pl.ds(0, D)]
    load(vec_send, vec_out, outs.at[0])
    main_rows = pl.ds(0, L)
    arrived(gh, send_out.at[main_rows, :], outs.at[1])
    arrived(gp, keep_out, outs.at[2])
    arrived(vec_send, vec_out, outs.at[0])


def put(stage, value, out, first, sem):
    stage[...] = value.astype(BF)
    copy = pltpu.make_async_copy(stage, out.at[:, pl.ds(first, stage.shape[1])], sem)
    copy.start()
    return copy


def gram_down_kernel(
    flags, c, c_oth, x_keep, x_oth, c_keep, c_send, act, bundle, main0, tail0, right0,
    down, left_main, left_tail, right_out, activations, c_kept, c_sent,
    c1, sides, left, right, sems, row_sems,
):
    leaving = both_rows(flags[0], x_keep, x_oth, activations, row_sems) + [
        pltpu.make_async_copy(src, dst, row_sems.at[2 + k])
        for k, (src, dst) in enumerate(((c_keep, c_kept), (c_send, c_sent)))
    ]
    for copy in leaving:
        copy.start()
    loads = (
        (bundle.at[:, pl.ds(4 * D, D)], c1), (act, right.at[pl.ds(0, L), :]),
        (bundle.at[:, pl.ds(0, 2 * D)], right.at[pl.ds(L, L), :]),
        (tail0, sides.at[0]), (bundle.at[:, pl.ds(3 * D, D)], sides.at[1]),
        (main0, sides.at[2]), (bundle.at[:, pl.ds(2 * D, D)], sides.at[3]),
        (right0, right_out.at[pl.ds(0, L), :]),
    )
    for k, (src, dst) in enumerate(loads):
        load(src, dst, sems.at[k])
    left[:, :L] = c[...].T
    arrived(*loads[0], sems.at[0])

    @pl.when(flags[1] == 0)
    def _():
        left[:, L:] = c_oth[...].T

    @pl.when(flags[1] != 0)
    def _():
        left[:, L:] = c1[...].T

    for k in range(1, 3):
        arrived(*loads[k], sems.at[k])
    down[...] = dot(left[...], right[...]).astype(BF)
    for k in range(4):
        arrived(*loads[3 + k], sems.at[3 + k])
        (left_tail, left_main)[k // 2][:, L * (k % 2) : L * (k % 2 + 1)] = sides[k].T
    arrived(*loads[7], sems.at[7])
    for copy in leaving:
        copy.wait()


def gram_head_kernel(rows, right1, down, left, vec, right0, head, tail_up, tail_down, vec_out, right):
    right[:L, :] = right0[:L, 3 * D :]
    right[L:, :] = right1[:L, 3 * D :]
    head[...] = dot(left[...], right[...]).astype(BF)
    other = [
        jnp.concatenate(
            [right1[L : L + 16, 128 * (3 * k + b) : 128 * (3 * k + b + 1)].astype(F32) for b in range(3)], axis=0
        )
        for k in range(2)
    ]
    total = (vec[...] + (other[0] + other[1])).astype(BF)
    vec_out[...] = total.astype(F32)
    for k, t in enumerate((tail_up, tail_down)):
        here = own_rows(rows, 0, k, t.shape[0])
        t[:, :D] = head[here, :]
        t[:, D : 3 * D] = down[here, :]
        t[:, 3 * D :] = total


def gram_main_kernel(rows, right1, left, right_in, right, main, main_up, main_down):
    right[L:, :] = right1[:L, :]
    main[...] = dot(left[...], right[:, : 3 * D]).astype(BF)
    for k, m in enumerate((main_up, main_down)):
        m[...] = main[own_rows(rows, 0, k, m.shape[0]), :]


def own_rows(rows, t, way, r):
    return pl.ds(pl.multiple_of(rows[t, way], 16), r)


def add_kernel(t, way, rows, got, *refs, count, vector):
    parts, out = refs[:count], refs[count]
    here = own_rows(rows, t, way, got.shape[0])
    at = 0
    for part in parts:
        sl = slice(at, at + part.shape[1])
        out[:, sl] = (got[:, sl].astype(F32) + part[here, :].astype(F32)).astype(BF)
        at += part.shape[1]
    if out.shape[1] > at:
        out[:, at:] = got[:, at:]
    if vector:
        refs[count + 1][...] = got[:, at : at + 128].astype(F32)


def fold_vector(va, out):
    def fold(start):
        v = va[:, start : start + D]
        w = HEAD_DIM // 2
        return jnp.concatenate(
            [v[:, 2 * w * h : 2 * w * h + w] - v[:, 2 * w * h + w : 2 * w * (h + 1)] for h in range(HEADS)],
            axis=1,
        )

    at = FIRST + 3 * D
    out[:, :at] = va[:, :at]
    out[:, at : at + HALF] = fold(at)
    out[:, at + HALF : SECOND] = fold(at + D)
    out[:, SECOND:] = va[:, at + 2 * D :]


def packed_vector(ref):
    rows = [ref[:, 128 * k : 128 * (k + 1)] for k in range(VECTOR // 128)]
    rows += [jnp.zeros((1, 128), F32)] * (PACKED[0] - len(rows))
    return jnp.concatenate(rows, axis=0)


def sum_vectors(table, vectors, slots, outs):
    n = len(vectors)
    if table is None:
        total = vectors[0][...]
    else:
        slots[table[0, 2]] = vectors[0][...]
        for k in range(1, n):
            t, way = (k + 1) // 2, (k + 1) % 2
            slots[table[t, 2 + way]] = vectors[k][...]
        total = slots[0]
        for k in range(1, n):
            total = total + slots[k]
    at = 0
    for out in outs:
        for k in range(out.shape[1] // 128):
            out[:, 128 * k : 128 * (k + 1)] = total[at + k : at + k + 1, :]
        at += out.shape[1] // 128


def place_kernel(spots, whole, flags, rows, *refs):
    count, pair, vectors, into = whole
    ins, refs = refs[: count + pair + vectors], refs[count + pair + vectors + into :]
    out, buf, sems = refs[0], refs[-3], refs[-2]
    copies = []
    if pair:
        copies += both_rows(flags[0], ins[count], ins[count + 1], refs[1], refs[-1])
        copies[0].start()
        copies[1].start()
    r, w = ins[0].shape
    for k, (t, way, column) in enumerate(spots):
        buf[k] = ins[k][...].astype(F32)
        copy = pltpu.make_async_copy(
            buf.at[k], out.at[own_rows(rows, t, way, r), pl.ds(column, w)], sems.at[k]
        )
        copy.start()
        copies.append(copy)
    if vectors:
        outs = refs[1 + pair // 2 : 5 + pair // 2]
        sum_vectors(rows if vectors > 1 else None, ins[count + pair :], refs[-4], outs)
    for copy in copies:
        copy.wait()


SMEM = pl.BlockSpec(memory_space=pltpu.SMEM)
VS = pl.BlockSpec(memory_space=pltpu.VMEM)
HBM = pl.BlockSpec(memory_space=pltpu.HBM)
ANY = pl.BlockSpec(memory_space=pl.ANY)


def sds(shape, dtype=BF):
    return jax.ShapeDtypeStruct(shape, dtype)


def call(kernel, name, in_specs, outs, scratch, flops, nbytes, limit=58, out_specs=None, aliases=None):
    return pl.pallas_call(
        kernel,
        name=name,
        in_specs=in_specs,
        out_specs=[VS] * len(outs) if out_specs is None else out_specs,
        out_shape=outs,
        scratch_shapes=scratch,
        input_output_aliases={} if aliases is None else aliases,
        compiler_params=pltpu.CompilerParams(vmem_limit_bytes=limit * MIB),
        cost_estimate=pl.CostEstimate(flops=flops, bytes_accessed=nbytes, transcendentals=0),
    )


ATTN_W = [VM((4, D, D), BF)]
ANGLES = [VM((L, D), F32), VM((L, D), F32)]
MLP_W = [VM((4, D, D), BF), VM((4, D, D), BF)]
BACK_S = [VM((D, L), BF), VM((L, D), BF), VM((2, 128, L), F32), VM((16, L), F32)]


def in_vmem(a):
    return pltpu.with_memory_space_constraint(a, pltpu.VMEM)


def in_hbm(a):
    return pltpu.with_memory_space_constraint(a, pltpu.HBM)


def row(width=D):
    return VM((L, width), BF)


def row_out(width=D):
    return pltpu.HBM((L, width), BF)


def prepare(flags, n, x, cot, *vecs):
    out = VM((x.shape[0], L), BF)

    def kernel(*refs):
        prepare_kernel(*refs, n)

    table = pltpu.HBM((2 * n if n <= LONGEST else 1, 4), I32)
    return call(
        kernel, "prepare", [SMEM] + [VS] * 6, [out] * 4 + [pltpu.HBM((1, VECTOR), F32), table], [], 1000,
        int(1e6), 8, out_specs=[VS] * 5 + [SMEM],
    )(flags, *(in_hbm(a) for a in (x, cot) + vecs))


def positions(flags, grid, own, oth):
    hbm = pltpu.HBM
    return call(
        positions_kernel, "positions", [SMEM, SMEM, VS, VS],
        [VM((L, D), F32), VM((L, D), F32), hbm((L, 128), F32), hbm((8, L), F32)],
        [], int(1e8), int(3e6), 56,
    )(flags, grid, own, oth)


def first_pass(*a):
    results = call(
        first_kernel, "first_pass", [SMEM] + [VS] * 8 + [HBM] * 2 + [VS] * 2,
        [row(), row_out()] + ANGLES + ATTN_W + MLP_W,
        [row(), VM((D, L), BF), row(3 * D), VM((HEADS, L, L), BF), VM((16, L), F32), row(), VM((D, L), BF),
         VM((D, L), BF), row(), DMA((13,))],
        int(8e9), int(20e6), 24, out_specs=[VS, HBM] + [VS] * HELD,
        aliases={len(a) - 2: 2, len(a) - 1: 3},
    )(*a)
    return results[0], results[1], results[2:]


SAVED = [VM((L, D), BF), VM((L, D), BF), VM((16, L), F32), VM((L, D), BF), VM((L, FF), BF)]
HEAD_S = [VM((L, 3 * D), BF), VM((HEADS, L, L), BF)]


def second_pass(held, *a):
    outs = [
        row_out(FF // 2), row_out(), row_out(), row_out(5 * D), row_out(3 * D), pltpu.HBM((HEADS, L, L), BF)
    ]
    resident = ANGLES + ATTN_W + MLP_W + SAVED
    results = call(
        second_kernel, "second_pass", [SMEM] + [VS] * (7 + HELD),
        resident + [row(FF // 2), row(FF // 2), row()] + outs,
        HEAD_S + [row(), row(), VM((D, L), BF), VM((D, L), BF), VM((L, D), F32), VM((L, D), F32)]
        + BACK_S + [row(3 * D), DMA((9,))],
        int(18e9), int(20e6), 24, out_specs=[VS] * (len(resident) + 3) + [HBM] * len(outs),
        aliases={len(a) + k: k for k in range(HELD)},
    )(*a, *(in_vmem(x) for x in held))
    n = len(resident)
    return results[:n], results[n : n + 2], results[n + 2], results[n + 3 :]


def late_pass(held, *a):
    results = call(
        late_kernel, "late_pass", [SMEM] + [VS] * (len(a) - 1 + len(held)),
        ANGLES + ATTN_W + MLP_W + SAVED + [sds((L, D))] * 2, [], int(2e9), int(5e6), 24,
        aliases={len(a) + k: k for k in range(len(held))},
    )(*a, *(in_vmem(x) for x in held))
    return results[: len(held)], results[len(held) :]


def back_pass(held, *a):
    return call(
        back_kernel, "back_pass", [SMEM] + [VS] * 5 + [HBM] * 2 + [VS] * len(held),
        [row(), row(), row(), VM(PACKED, F32), row_out(FF), pltpu.HBM((L + 16, FF), BF)],
        HEAD_S
        + [row(FF), row(FF), VM((1, FIRST + 6 * D), F32), VM((1, VECTOR), F32), VM((1, VECTOR), F32),
           VM((16, D), BF)]
        + BACK_S + [DMA((5,))],
        int(10e9), int(15e6), 24, out_specs=[VS] * 4 + [HBM] * 2,
    )(*a, *(in_vmem(x) for x in held))


def gram_down(*a):
    square = VM((D, 2 * L), BF)
    return call(
        gram_down_kernel, "gram_down", [SMEM] + [VS] * 6 + [HBM, ANY] + [HBM] * 3,
        [VM((D, 2 * D), BF), square, square, VM((2 * L, FF), BF), pltpu.HBM((2 * L, D), BF), row_out(), row_out()],
        [row(), VM((4, L, D), BF), square, VM((2 * L, 2 * D), BF), DMA((8,)), DMA((4,))], int(2e9), int(8e6), 20,
        out_specs=[VS] * 4 + [HBM] * 3,
    )(*a)


def gram_head(rows, r, *a):
    wide = VM((r, 3 * D + 128), BF)
    return call(
        gram_head_kernel, "gram_head", [SMEM] + [VS] * 5, [VM((D, D), BF), wide, wide, VM(PACKED, F32)],
        [VM((2 * L, D), BF)], int(1e9), int(5e6), 12,
    )(rows, *a)


def gram_main(rows, r, *a):
    shard = VM((r, 3 * D), BF)
    return call(
        gram_main_kernel, "gram_main", [SMEM] + [VS] * 3,
        [VM((2 * L, FF), BF), VM((D, 3 * D), BF), shard, shard], [], int(6e9), int(12e6), 20, aliases={3: 0},
    )(rows, *a)[1:]


def add(t, way, rows, got, parts, vector, wide):
    count = len(parts)

    def kernel(*refs):
        add_kernel(t, way, *refs, count=count, vector=vector)

    width = sum(p.shape[1] for p in parts)
    out = VM((got.shape[0], width + (128 if wide else 0)), BF)
    results = call(
        kernel, "add", [SMEM] + [VS] * (1 + count), [out] + [VM(PACKED, F32)] * vector, [], 1000, int(2e7), 4
    )(rows, in_vmem(got), *(in_vmem(p) for p in parts))
    return results[0], results[1:]


def place(flags, spots, rows, shards, total, pair=(), vectors=()):
    count = len(shards)
    into = [] if total is None else [total]
    whole = count, len(pair), len(vectors), len(into)

    def kernel(*refs):
        place_kernel(spots, whole, *refs)

    outs = [pltpu.HBM((D, 6 * D), F32)]
    outs += [pltpu.HBM((2 * L, D), BF)] if pair else []
    outs += [sds((1, w), F32) for w in (D, D, FF, D)] if vectors else []
    given = len(shards) + len(pair) + len(vectors)
    return call(
        kernel, "place", [SMEM, SMEM] + [VS] * given + [HBM] * len(into), outs,
        [VM((max(len(vectors), 1),) + PACKED, F32), VM((count,) + shards[0].shape, F32), DMA((count,)), DMA((2,))],
        1000,
        int(2e7), 24, out_specs=[HBM] * (2 if pair else 1) + ([VS] * 4 if vectors else []),
        aliases={given + 2: 0} if into else {},
    )(flags, rows, *shards, *pair, *vectors, *into)


def core_swap(a):
    return lax.ppermute(a, "section", [(0, 1), (1, 0), (2, 3), (3, 2)])


def after(value, first):
    return lax.optimization_barrier((value, first))[0]


class Cycle:
    def __init__(self, rows):
        self.n = n = lax.axis_size("dp")
        self.r = D // (2 * n)
        order = list(range(0, n, 2)) + list(range(n - 1, 0, -2))
        self.pairs = [[(order[k], order[(k + d) % n]) for k in range(n)] for d in (1, -1)]
        self.rows = rows

    def placed(self, k):
        return 2 * self.n - 1 if k == 0 else self.n + k - 1


class Chain:
    def __init__(self, cycle, parts, cur, carries=False):
        self.cycle, self.parts, self.cur, self.carries = cycle, parts, cur, carries
        self.t = 0
        self.shards = []
        self.vectors = []

    def step(self, token):
        c = self.cycle
        got = [lax.ppermute(a, "dp", p) for a, p in zip(self.cur, c.pairs)]
        self.t += 1
        t = self.t
        if t < c.n:
            self.cur = []
            for way in range(2):
                vector = self.carries and t <= (c.n - way) // 2
                out, came = add(
                    t, way, c.rows, after(got[way], token), self.parts, vector, self.carries and t < c.n // 2
                )
                self.cur.append(out)
                self.vectors += came
                token = out
        else:
            first = after(got[0], token)
            self.cur = [first, after(got[1], first)]
        if self.t >= c.n - 1:
            self.shards.append(self.cur)
        return self.cur


def small_ring():
    return lax.axis_size("dp") <= LONGEST


def summed(flags, rows, main, tail, token, pair, vector):
    if not small_ring():
        chains, vector = lax.psum([main, tail], "dp"), lax.psum(vector, "dp")
        return place(flags, [(0, 0, 0), (0, 0, 3 * D)], rows, chains, None, pair, [vector])
    cycle = main.cycle
    n = cycle.n
    total = None
    waiting, results = [], {}
    while main.t < 2 * n - 2:
        for chain, column in ((tail, 3 * D), (main, 0)):
            if total is not None:
                token = (token, total)
            token = chain.step(token)
            whole = len(chain.shards)
            if whole:
                t = cycle.placed(whole - 1)
                waiting += [((t, way, column), chain.shards[-1][way]) for way in range(2)]
            if whole == n or chain is main and whole and whole % 2 == 0:
                now, then = "rows" not in results, "vectors" not in results and whole >= min(4, n)
                total, *more = place(
                    flags, [a for a, _ in waiting], cycle.rows, [b for _, b in waiting], total,
                    pair if now else (), [vector] + tail.vectors if then else (),
                )
                if now:
                    results["rows"] = more.pop(0)
                if then:
                    results["vectors"] = more
                waiting = []
    return total, results["rows"], *results["vectors"]


def body(
    block_input, cotangent, grid_sizes, section_weight, norm_gain, norm_bias, first_vector, second_vector
):
    section = lax.axis_index("section")
    core = section % 2
    n = lax.axis_size("dp")
    i = lax.axis_index("dp")
    where = jnp.where(i % 2 == 0, i // 2, n - 1 - i // 2)
    flags = in_hbm(jnp.stack([core, section // 2, where]).astype(I32))
    first_layer = section < 2

    keep, send, away, across, vown, rows = prepare(
        flags, n, block_input.T, cotangent.T, norm_gain, norm_bias, first_vector, second_vector
    )
    if n % 2 == 0:
        voth = lax.ppermute(
            vown, ("section", "dp"), [(n * s + d, n * (s ^ 1) + (d ^ 1)) for s in range(4) for d in range(n)]
        )
    else:
        voth = core_swap(vown)
    r = D // (2 * n) if small_ring() else PACKED[0]
    cosf, sinf, pos, segr = positions(flags, grid_sizes, in_hbm(vown), voth)
    vown, voth, rows, pos, segr = (in_hbm(a) for a in (vown, voth, rows, pos, segr))
    got = core_swap(send)
    away = lax.ppermute(away, "section", [(0, 2), (1, 3), (2, 0), (3, 1)])
    across = lax.ppermute(across, "section", [(0, 3), (1, 2), (2, 1), (3, 0)])
    own = in_hbm(section_weight[0])
    oth = in_hbm(core_swap(section_weight[0]))

    x_two, field, held = first_pass(
        flags, keep, got, away, across, vown, voth, pos, segr, own, oth, in_vmem(cosf), in_vmem(sinf)
    )
    field = in_hbm(field)
    x_got, x_late = (lax.ppermute(x_two, "section", [pair]) for pair in ((0, 2), (1, 3)))
    held, active, c_two, (act_mine, main_left, tail_left, bundle, qkv, pt) = second_pass(
        held, flags, field, x_got, x_late, vown, voth, pos, segr
    )
    act_mine, main_left, tail_left = (in_hbm(a) for a in (act_mine, main_left, tail_left))
    c_got = lax.ppermute(c_two, "section", [(2, 0), (3, 1)])
    held, (x_keep, x_send) = late_pass(held, flags, x_two, vown, voth, *(in_vmem(a) for a in active))
    c_got = after(c_got, x_keep)
    bundle = core_swap(after(bundle, c_got))
    x_oth = core_swap(after(x_send, c_got))

    c_keep, c_send, c_out, vec, right, right_send = back_pass(
        held, flags, field, c_got, vown, voth, pos, in_hbm(qkv), in_hbm(pt)
    )
    c_oth = core_swap(c_got)
    right_oth = core_swap(after(right_send, (c_oth, bundle, x_oth)))
    down, left_main, left_tail, right, activations, c_keep, c_send = gram_down(
        flags, c_out, c_oth, x_keep, x_oth, in_vmem(c_keep), in_vmem(c_send), act_mine, bundle, main_left, tail_left, in_hbm(right)
    )
    head, *tail_first, vec = gram_head(rows, r, right_oth, down, left_tail, vec, right)
    if small_ring():
        cycle = Cycle(rows)
        tail = Chain(cycle, [head, down], tail_first, True)
    else:
        tail = jnp.concatenate([head, down], axis=1)
    main, *main_first = gram_main(rows, r, right_oth, left_main, right)
    if small_ring():
        main = Chain(cycle, [main], main_first)
        token = main.cur
    else:
        token = main
    weight_grad, input_grads, *vectors = summed(
        flags, rows, main, tail, token, (c_keep, core_swap(after(c_send, token))), vec
    )
    return (
        activations[None],
        input_grads[None],
        weight_grad[None],
        *vectors,
    )


def solution(mesh):
    in_specs = (
        P("dp", "section"),
        P("dp", "section"),
        P("dp", None, None),
        P("section", None, None),
        P("section", None),
        P("section", None),
        P("section", None),
        P("section", None),
    )
    out_specs = (
        P("section", "dp", None),
        P("section", "dp", None),
        P("section", None, None),
        P("section", None),
        P("section", None),
        P("section", None),
        P("section", None),
    )
    return jax.shard_map(body, mesh=mesh, in_specs=in_specs, out_specs=out_specs, check_vma=False)
```

```python
import jax
import jax.numpy as jnp
from jax import lax
from jax.experimental import pallas as pl
from jax.experimental.pallas import tpu as pltpu
from jax.sharding import PartitionSpec as P

D = 768
HEADS = 12
HEAD_DIM = 64
FF = 3072
L = 384
HALF = D // 2
F32 = jnp.float32
BF = jnp.bfloat16
I32 = jnp.int32
NT = (((1,), (1,)), ((), ()))
TN = (((0,), (0,)), ((), ()))
VM = pltpu.VMEM
DMA = pltpu.SemaphoreType.DMA
MIB = 1024 * 1024
LN2 = 0.6931471805599453
GAIN, SHIFT = slice(0, D), slice(D, 2 * D)
FIRST, SECOND = 2 * D, 2 * D + FF
VECTOR = 3 * D + FF
LONGEST = 16
PACKED = (48, 128)


def dot(a, b):
    return jnp.dot(a, b, preferred_element_type=F32)


def dot_nt(a, b):
    return lax.dot_general(a, b, NT, preferred_element_type=F32)


def dot_tn(a, b):
    return lax.dot_general(a, b, TN, preferred_element_type=F32)


def norm_parts(x):
    center = x - jnp.mean(x, axis=-1, keepdims=True)
    inv = lax.rsqrt(jnp.mean(center * center, axis=-1, keepdims=True) + 1e-06)
    return center * inv, inv


def swap_halves(a):
    lane = lax.broadcasted_iota(I32, (1, 128), 1)
    first = (lane % HEAD_DIM) < HEAD_DIM // 2
    out = []
    for i in range(a.shape[1] // 128):
        s = a[:, 128 * i : 128 * (i + 1)]
        out.append(jnp.where(first, pltpu.roll(s, 96, 1), pltpu.roll(s, 32, 1)))
    return jnp.concatenate(out, axis=1) if len(out) > 1 else out[0]


def lanes(start, size):
    if isinstance(start, int):
        return slice(start, start + size)
    return pl.ds(pl.multiple_of(start, 128), size)


def rows_at(start, size):
    if isinstance(start, int):
        return slice(start, start + size)
    return pl.ds(pl.multiple_of(start, size), size)


def cols(start, size):
    return (slice(None), pl.ds(start, size))


def pick(flag, want, own, oth, src, dst, sem):
    @pl.when(flag == want)
    def _():
        pltpu.make_async_copy(own.at[src], dst, sem).start()

    @pl.when(flag != want)
    def _():
        pltpu.make_async_copy(oth.at[src], dst, sem).start()


def load(src, dst, sem):
    pltpu.make_async_copy(src, dst, sem).start()


def arrived(src, dst, sem):
    pltpu.make_async_copy(src, dst, sem).wait()


def load_attn(core, own, oth, wa, sems, i):
    pick(core, 0, own, oth, cols(D * i, D), wa.at[i], sems.at[i])


def wait_attn(own, wa, sems, i):
    arrived(own.at[cols(D * i, D)], wa.at[i], sems.at[i])


def hidden_start(core, j):
    return pl.multiple_of(FF // 2 * ((core + j // 2) % 2) + D * (j % 2), 128)


def load_mlp(core, own, oth, w1, wd, sems, j):
    pick(core, 1, own, oth, (slice(None), pl.ds(hidden_start(core, j), D)), w1.at[j], sems.at[j])
    load((own if j < 2 else oth).at[cols(FF + D * (j % 2), D)], wd.at[j], sems.at[4 + j])


class Forward:
    def __init__(self, on_the_way, core, own, oth, wa, w1, wd, sems):
        self.attn = core, own, oth, wa, sems
        self.mlp = core, own, oth, w1, wd, sems.at[pl.ds(4, 8)]
        self.own, self.wa, self.sems, self.on_the_way = own, wa, sems, on_the_way

        @pl.when(on_the_way)
        def _():
            load_attn(*self.attn, 0)
            load_attn(*self.attn, 1)

        @pl.when(jnp.logical_not(on_the_way))
        def _():
            for i in range(4):
                load_attn(*self.attn, i)
                load_mlp(*self.mlp, i)
                wait_attn(own, wa, sems, i)
                wait_mlp(own, w1, wd, self.mlp[-1], i)

    def wait(self, i):
        @pl.when(self.on_the_way)
        def _():
            wait_attn(self.own, self.wa, self.sems, i)
            if i < 2:
                load_attn(*self.attn, i + 2)
            elif i == 2:
                for j in range(4):
                    load_mlp(*self.mlp, j)

    def wait_mlp(self):
        core, own, oth, w1, wd, sems = self.mlp

        @pl.when(self.on_the_way)
        def _():
            for j in range(4):
                wait_mlp(own, w1, wd, sems, j)


def wait_mlp(own, w1, wd, sems, j):
    if w1 is not None:
        arrived(own.at[cols(0, D)], w1.at[j], sems.at[j])
    arrived(own.at[cols(0, D)], wd.at[j], sems.at[4 + j])


def vectors(core, own, oth):
    a, b = own[...], oth[...]
    return jnp.where(core == 0, a, b), jnp.where(core == 0, b, a)


def attention(x, vec, wa, wait, cosf, sinf, segc, segr, qkv, pt, rec, ml, mlt, vt, n_ref):
    xh, inv = norm_parts(x)
    n = (xh * vec[:, GAIN] + vec[:, SHIFT]).astype(BF)
    n_ref[...] = n
    for i in range(3):
        wait(i)
        part = dot(n, wa[i]) + vec[:, FIRST + D * i : FIRST + D * (i + 1)]
        if i < 2:
            part = part * cosf[...] + swap_halves(part) * sinf[...]
        if i == 0:
            part = part * (HEAD_DIM**-0.5 / LN2)
        qkv[:, D * i : D * (i + 1)] = part.astype(BF)
    vt[...] = qkv[:, 2 * D : 3 * D].T
    same = segc == segr
    lane = lax.broadcasted_iota(I32, (1, 128), 1)

    def score(h):
        p = 128 * (h // 2)
        keys = jnp.where((lane // HEAD_DIM) == h % 2, qkv[:, D + p : D + p + 128], BF(0))
        return dot_nt(keys, qkv[:, p : p + 128])

    ahead = score(0)
    for h in range(HEADS):
        st = ahead
        if h + 1 < HEADS:
            ahead = score(h + 1)
        st = jnp.where(same, st, -1e30)
        e = jnp.exp2(st - jnp.max(st, axis=0, keepdims=True))
        r = 1.0 / jnp.sum(e, axis=0, keepdims=True)
        rec[h : h + 1, :] = r
        e = e.astype(BF)
        pt[h] = e
        here = slice(HEAD_DIM * h, HEAD_DIM * (h + 1))
        mlt[here, :] = (dot(vt[here, :], e) * r).astype(BF)
    ml[...] = mlt[...].T
    wait(3)
    out = x + dot(ml[...], wa[3]) + vec[:, SECOND : SECOND + D]
    return out.astype(BF), xh, inv


C0 = 0.7978845608028654
C1 = 0.044715


def gelu(h):
    h2 = h * h
    t = jnp.tanh(C0 * (h + C1 * h * h2))
    half = 0.5 * (1.0 + t)
    return h * half, half + (0.5 * C0) * h * (1.0 - t * t) * (1.0 + (3.0 * C1) * h2)


def norm_back(gn, xh, inv, gain, c):
    u = gn * gain
    gx = inv * (
        u - jnp.mean(u, axis=-1, keepdims=True) - xh * jnp.mean(u * xh, axis=-1, keepdims=True)
    )
    return (c.astype(F32) + gx).astype(BF)


def head_select():
    head = lax.broadcasted_iota(I32, (16, D), 0)
    lane = lax.broadcasted_iota(I32, (16, D), 1)
    return jnp.where(lane // HEAD_DIM == head, 1.0, 0.0).astype(BF)


def split_two(a):
    hi = a.astype(BF)
    return hi, (a - hi.astype(F32)).astype(BF)


def attention_back(c, wo, cosf, sinf, qkv, pt, rec, ml, kt, gm, gqt, dsum, pair_of, emit):
    kt[...] = qkv[:, D : 2 * D].T
    gm_wide = dot_nt(c, wo[...])
    sel = head_select()
    hi, lo = split_two(gm_wide * ml[...].astype(F32))
    row = lax.broadcasted_iota(I32, (16, L), 0)
    recs = jnp.where(row < HEADS, rec[...], 0.0)
    dsum[...] = (dot_nt(sel, hi) + dot_nt(sel, lo)) * recs
    hi, lo = split_two(recs)
    gm[...] = (gm_wide * (dot_tn(hi, sel) + dot_tn(lo, sel))).astype(BF)
    lane = lax.broadcasted_iota(I32, (1, 128), 1)

    def spot(h):
        return lanes(128 * pair_of(h // 2), 128), (lane // HEAD_DIM) == h % 2

    def from_values(h):
        sl, here = spot(h)
        values = qkv[:, lanes(2 * D + 128 * pair_of(h // 2), 128)]
        return dot_nt(jnp.where(here, values, BF(0)), gm[:, sl])

    ahead = from_values(0)
    for h in range(HEADS):
        gpt = ahead
        if h + 1 < HEADS:
            ahead = from_values(h + 1)
        sl, here = spot(h)
        head = 2 * pair_of(h // 2) + h % 2
        e = pt[head]
        gvh = dot(e, jnp.where(here, gm[:, sl], BF(0)))
        gst = (e.astype(F32) * (gpt - dsum[rows_at(head, 1), :])).astype(BF)
        gkh = dot(gst, jnp.where(here, qkv[:, sl], BF(0)))
        kth = kt[rows_at(HEAD_DIM * head, HEAD_DIM), :]
        gqt[h // 2 % 2, HEAD_DIM * (h % 2) : HEAD_DIM * (h % 2 + 1), :] = dot(kth, gst)
        gv = gvh if h % 2 == 0 else gv + gvh
        gk = gkh if h % 2 == 0 else gk + gkh
        if h % 2 == 1:
            gq = gqt[h // 2 % 2].T * (HEAD_DIM**-0.5)
            gk = gk * LN2
            cs, sn = cosf[:, sl], sinf[:, sl]
            sq, sk = swap_halves(gq), swap_halves(gk)
            emit(
                h // 2, sl, sq, sk,
                ((gq * cs - sq * sn).astype(BF), (gk * cs - sk * sn).astype(BF), gv.astype(BF)),
            )


def positions_kernel(flags, grid, vown, voth, cosf, sinf, pos, segr, kept):
    core = flags[0]
    vec = vectors(core, vown, voth)[0]
    kept[...] = voth[...]
    h0, w0, h1, w1 = (grid[core, k // 2, k % 2] for k in range(4))
    e1 = h0 * w0
    e2 = e1 + h1 * w1

    def place(t):
        segment = (t >= e1).astype(I32) + (t >= e2).astype(I32)
        width = jnp.where(segment == 0, w0, w1).astype(F32)
        inside = (t - jnp.where(segment == 0, 0, e1)).astype(F32)
        row = jnp.floor((inside + 0.5) / width)
        column = inside - row * width
        return segment, jnp.where(segment < 2, row, 0.0), jnp.where(segment < 2, column, 0.0)

    segment, row, column = place(lax.broadcasted_iota(I32, (L, 128), 0))
    lane = lax.broadcasted_iota(I32, (L, 128), 1)
    pos[...] = jnp.where(lane == 0, column, jnp.where(lane == 1, row, segment.astype(F32)))
    t = lax.broadcasted_iota(I32, (8, L), 1)
    segr[...] = (t >= e1).astype(F32) + (t >= e2).astype(F32)

    def by_lane(start):
        parts = []
        for h in range(HEADS):
            f = vec[:, start + 32 * h : start + 32 * (h + 1)]
            parts += [f, f]
        return jnp.concatenate(parts, axis=1)

    number = lax.broadcasted_iota(I32, (16, D), 0).astype(F32)

    def look_up(which, table):
        hi, rest = split_two(table)
        mid, low = split_two(table - hi.astype(F32))
        tables = jnp.concatenate([hi, mid, low], axis=0)
        hit = (lax.broadcasted_iota(I32, (L, 48), 1) % 16).astype(F32) == which[:, :48]
        return dot(jnp.where(hit, 1.0, 0.0).astype(BF), tables)

    ax = number * by_lane(FIRST + 3 * D)
    ay = number * by_lane(FIRST + 3 * D + HALF)
    cx, sx = look_up(column, jnp.cos(ax)), look_up(column, jnp.sin(ax))
    cy, sy = look_up(row, jnp.cos(ay)), look_up(row, jnp.sin(ay))
    cosf[...] = cx * cy - sx * sy
    lane = lax.broadcasted_iota(I32, (1, D), 1)
    sign = jnp.where(lane % HEAD_DIM < HEAD_DIM // 2, -1.0, 1.0)
    sinf[...] = (sx * cy + cx * sy) * sign


def prepare_kernel(
    flags, x, cot, gain, shift, first, second, keep, send, away, across, vec, table, n
):
    core, layer, where = flags[0], flags[1], flags[2]
    for t in range(table.shape[0]):
        for way, d in ((0, 1), (1, -1)):
            if n > LONGEST:
                table[t, way], table[t, 2 + way] = 0, 0
                continue
            at = lax.rem(where - d * (t % n) + 2 * n, n)
            table[t, way] = at * (D // (2 * n)) + way * HALF
            table[t, 2 + way] = jnp.where(2 * at < n, 2 * at, 2 * (n - at) - 1)
    for at, (mine, other) in enumerate(((x, cot), (cot, x))):

        @pl.when(layer == at)
        def _(mine=mine, other=other):
            keep[...] = mine[:, lanes(L * core, L)]
            send[...] = mine[:, lanes(L * (1 - core), L)]
            away[...] = other[:, lanes(L * core, L)]
            across[...] = other[:, lanes(L * (1 - core), L)]

    vec[:, GAIN] = gain[...]
    vec[:, SHIFT] = shift[...]
    vec[:, FIRST:SECOND] = first[...]
    vec[:, SECOND:] = second[...]


HELD = 5


def first_kernel(
    flags, keep, got, away, across, vown, voth, pos, segr, own, oth, cos_in, sin_in,
    out, field_out, cosf, sinf, wa, w1, wd, field, turned, qkv, pt, rec, ml, mlt, vt, n_ref, sems,
):
    core, layer = flags[0], flags[1]
    loads = Forward((core == 0) & (layer == 0), core, own, oth, wa, w1, wd, sems)
    w = keep.shape[0]
    for k in range(2):
        for at in range(2):

            @pl.when((core == k) & (layer == at))
            def _(k=k, at=at):
                parts = {(at, k): keep, (at, 1 - k): got, (1 - at, k): away, (1 - at, 1 - k): across}
                for s in range(4):
                    turned[w * s : w * (s + 1), :] = parts[s // 2, s % 2][...]

    field[...] = turned[...].T
    keeping = pltpu.make_async_copy(field, field_out, sems.at[12])
    keeping.start()
    @pl.when(layer == 0)
    def _():
        va, vm = vectors(core, vown, voth)
        x_mid, _, _ = attention(
            field[...].astype(F32), va, wa, loads.wait, cosf, sinf, pos[:, 2:3], segr[0:1, :],
            qkv, pt, rec, ml, mlt, vt, n_ref,
        )
        x = x_mid.astype(F32)
        xh, _ = norm_parts(x)
        n = (xh * vm[:, GAIN] + vm[:, SHIFT]).astype(BF)
        loads.wait_mlp()
        acc = x + vm[:, SECOND : SECOND + D]
        first = hidden_bias(core, vm)
        ahead = dot(n, w1[0])
        for j in range(4):
            h = ahead + first[:, D * j : D * (j + 1)]
            if j < 3:
                ahead = dot(n, w1[j + 1])
            acc = acc + dot_nt(gelu(h)[0].astype(BF), wd[j])
        out[...] = acc.astype(BF)

    keeping.wait()


def hidden_bias(core, vm):
    a, b = vm[:, FIRST : FIRST + FF // 2], vm[:, FIRST + FF // 2 : SECOND]
    return jnp.concatenate([jnp.where(core == 0, a, b), jnp.where(core == 0, b, a)], axis=1)


def second_kernel(
    flags, field, got, got_late, vown, voth, pos, segr, *refs,
):
    (
        cosf, sinf, wa, w1, wd, xi, xm, rec, ml, dg, actm, acts, cx, act_out, main_out, tail_out, bundle,
        qkv_out, pt_out, qkv, pt, na, nm, mlt, vt, xha, xhm, kt, gm, gqt, dsum, gp, outs,
    ) = refs[HELD:]
    core, layer = flags[0], flags[1]
    va, vm = vectors(core, vown, voth)
    x = jnp.where(core == 0, got[...].astype(F32), got_late[...].astype(F32))
    x = jnp.where(layer == 0, field[...].astype(F32), x)
    xi[...] = x.astype(BF)
    x_mid, xh, inv_a = attention(
        x, va, wa, lambda what: None, cosf, sinf, pos[:, 2:3], segr[0:1, :], qkv, pt, rec, ml, mlt, vt, na
    )
    xha[...] = xh
    xm[...] = x_mid
    load(qkv, qkv_out, outs.at[7])
    load(pt, pt_out, outs.at[8])
    xh, inv_m = norm_parts(x_mid.astype(F32))
    xhm[...] = xh
    n = (xh * vm[:, GAIN] + vm[:, SHIFT]).astype(BF)
    nm[...] = n
    sides = (
        main_out, tail_out, bundle.at[:, pl.ds(2 * D, D)], bundle.at[:, pl.ds(3 * D, D)],
    )
    load(field, bundle.at[:, pl.ds(4 * D, D)], outs.at[4])
    for when, sources in ((core == 0, (na, ml, nm, nm)), (core != 0, (nm, nm, na, ml))):

        @pl.when(when)
        def _(sources=sources):
            for k, (src, dst) in enumerate(zip(sources, sides)):
                load(src, dst, outs.at[k])

    first = hidden_bias(core, vm)
    c = field[...]

    def forward(j):
        return dot(n, w1[j])

    def chunk(j, h):
        act, slope = gelu(h + first[:, D * j : D * (j + 1)])
        (actm, acts)[j // 2][:, D * (j % 2) : D * (j % 2 + 1)] = act.astype(BF)
        slope = slope.astype(BF)
        dg[:, D * j : D * (j + 1)] = slope
        return slope

    def leave():
        load(acts, bundle.at[:, pl.ds(0, 2 * D)], outs.at[5])
        load(actm, act_out, outs.at[6])

    @pl.when(layer >= 0)
    def _():
        ahead = forward(0), dot(c, wd[0])
        gn = None
        for j in range(4):
            h, ga = ahead
            if j < 3:
                ahead = forward(j + 1), dot(c, wd[j + 1])
            slope = chunk(j, h)
            part = dot_nt((ga * slope.astype(F32)).astype(BF), w1[j])
            gn = part if gn is None else gn + part
        leave()
        c_mid = norm_back(gn, xhm[...], inv_m, vm[:, GAIN], c)

        def emit(p, sl, sq, sk, grads):
            for i in range(3):
                gp[:, D * i + 128 * p : D * i + 128 * (p + 1)] = grads[i]

        attention_back(
            c_mid, wa.at[3], cosf, sinf, qkv, pt, rec, ml, kt, gm, gqt, dsum, lambda p: p, emit
        )
        gn = None
        for i in range(3):
            part = dot_nt(gp[:, D * i : D * (i + 1)], wa[i])
            gn = part if gn is None else gn + part
        cx[...] = norm_back(gn, xha[...], inv_a, va[:, GAIN], c_mid)

    for k, (src, dst) in enumerate(
        tuple((nm, side) for side in sides)
        + ((field, sides[2]), (acts, bundle.at[:, pl.ds(0, 2 * D)]), (actm, act_out), (qkv, qkv_out), (pt, pt_out))
    ):
        arrived(src, dst, outs.at[k])


def late_kernel(flags, x_two, vown, voth, actm, acts, *refs):
    xm, wd = refs[HELD + 1], refs[HELD - 1]
    keep, send = refs[-2:]
    core, layer = flags[0], flags[1]
    vm = vectors(core, vown, voth)[1]
    mid = xm[...].astype(F32)
    acc = mid + vm[:, SECOND : SECOND + D]
    for j in range(4):
        acc = acc + dot_nt((actm, acts)[j // 2][:, D * (j % 2) : D * (j % 2 + 1)], wd[j])
    acc = jnp.where(layer == 0, x_two[...].astype(F32), acc)
    keep[...] = jnp.where(core == 0, mid, acc).astype(BF)
    send[...] = jnp.where(core == 0, acc, mid).astype(BF)


def both_rows(core, keep, got, out, sems):
    return [
        pltpu.make_async_copy(src, out.at[rows_at(L * at, L), :], sems.at[k])
        for k, (src, at) in enumerate(((keep, core), (got, 1 - core)))
    ]


def norm_stats(gn, x, vec):
    xh, inv = norm_parts(x)
    vec[:, GAIN] = jnp.sum(gn * xh, axis=0, keepdims=True)
    vec[:, SHIFT] = jnp.sum(gn, axis=0, keepdims=True)
    return xh, inv


def back_kernel(
    flags, field, got, vown, voth, pos, qkv_in, pt_in, cosf, sinf, wa, w1, wd, xi, xm, rec, ml, dg,
    row_keep, row_send, c_out, vec_keep, keep_out, send_out,
    qkv, pt, gh, gp, va_grad, vm_grad, folded, vec_send, kt, gm, gqt, dsum, outs,
):
    core, layer = flags[0], flags[1]
    load(qkv_in, qkv, outs.at[3])
    load(pt_in, pt, outs.at[4])
    va, vm = vectors(core, vown, voth)
    wide = jnp.where(layer == 0, got[...].astype(F32), field[...].astype(F32))
    c = wide.astype(BF)
    c_out[...] = c
    vm_grad[:, SECOND:] = jnp.sum(wide, axis=0, keepdims=True)

    def from_output(j):
        return dot(c, wd[j])

    ahead = from_output(0)
    gn = None
    for j in range(4):
        ga = ahead
        if j < 3:
            ahead = from_output(j + 1)
        part = (ga * dg[:, D * j : D * (j + 1)].astype(F32)).astype(BF)
        start = hidden_start(core, j)
        gh[:, pl.ds(start, D)] = part
        vm_grad[:, pl.ds(pl.multiple_of(FIRST + start, 128), D)] = jnp.sum(
            part.astype(F32), axis=0, keepdims=True
        )
        part = dot_nt(part, w1[j])
        gn = part if gn is None else gn + part
    for when, dst in ((core == 0, send_out.at[pl.ds(0, L), :]), (core != 0, keep_out)):

        @pl.when(when)
        def _(dst=dst):
            load(gh, dst, outs.at[1])

    xh, inv = norm_stats(gn, xm[...].astype(F32), vm_grad)
    c = norm_back(gn, xh, inv, vm[:, GAIN], c)
    gp[:, 3 * D :] = c
    va_grad[:, FIRST + 5 * D :] = jnp.sum(c.astype(F32), axis=0, keepdims=True)
    colp, rowp = pos[:, 0:1], pos[:, 1:2]

    def emit(p, sl, sq, sk, grads):
        qr = qkv[:, sl].astype(F32) * (LN2 * HEAD_DIM**0.5)
        th = sq * qr + sk * qkv[:, D + 128 * p : D + 128 * (p + 1)].astype(F32)
        at = FIRST + 3 * D + 128 * p
        va_grad[:, at : at + 128] = jnp.sum(th * colp, axis=0, keepdims=True)
        va_grad[:, at + D : at + D + 128] = jnp.sum(th * rowp, axis=0, keepdims=True)
        for i, g in enumerate(grads):
            gp[:, D * i + 128 * p : D * i + 128 * (p + 1)] = g
            va_grad[:, FIRST + D * i + 128 * p : FIRST + D * i + 128 * (p + 1)] = jnp.sum(
                g.astype(F32), axis=0, keepdims=True
            )

    arrived(qkv_in, qkv, outs.at[3])
    arrived(pt_in, pt, outs.at[4])
    attention_back(
        c, wa.at[3], cosf, sinf, qkv, pt, rec, ml, kt, gm, gqt, dsum, lambda p: p, emit
    )
    for when, dst in ((core == 0, keep_out), (core != 0, send_out.at[pl.ds(0, L), :])):

        @pl.when(when)
        def _(dst=dst):
            load(gp, dst, outs.at[2])

    gn = None
    for i in range(3):
        part = dot_nt(gp[:, D * i : D * (i + 1)], wa[i])
        gn = part if gn is None else gn + part
    xh, inv = norm_stats(gn, xi[...].astype(F32), va_grad)
    cx = norm_back(gn, xh, inv, va[:, GAIN], c).astype(F32)
    wide = c.astype(F32)
    row_keep[...] = jnp.where(core == 0, cx, wide).astype(BF)
    row_send[...] = jnp.where(core == 0, wide, cx).astype(BF)
    fold_vector(va_grad, folded)
    a, m = packed_vector(folded), packed_vector(vm_grad)
    vec_keep[...] = jnp.where(core == 0, a, m)
    for k, part in enumerate(split_two(jnp.where(core == 0, m, a))):
        for b in range(3):
            vec_send[:, 128 * (3 * k + b) : 128 * (3 * k + b + 1)] = part[16 * b : 16 * (b + 1), :]
    vec_out = send_out.at[pl.ds(L, 16), pl.ds(0, D)]
    load(vec_send, vec_out, outs.at[0])
    main_rows = pl.ds(0, L)
    arrived(gh, send_out.at[main_rows, :], outs.at[1])
    arrived(gp, keep_out, outs.at[2])
    arrived(vec_send, vec_out, outs.at[0])


def put(stage, value, out, first, sem):
    stage[...] = value.astype(BF)
    copy = pltpu.make_async_copy(stage, out.at[:, pl.ds(first, stage.shape[1])], sem)
    copy.start()
    return copy


def gram_down_kernel(
    flags, c, c_oth, x_keep, x_oth, c_keep, c_send, act, bundle, main0, tail0, right0,
    down, left_main, left_tail, right_out, activations, c_kept, c_sent,
    c1, sides, left, right, sems, row_sems,
):
    leaving = both_rows(flags[0], x_keep, x_oth, activations, row_sems) + [
        pltpu.make_async_copy(src, dst, row_sems.at[2 + k])
        for k, (src, dst) in enumerate(((c_keep, c_kept), (c_send, c_sent)))
    ]
    for copy in leaving:
        copy.start()
    loads = (
        (bundle.at[:, pl.ds(4 * D, D)], c1), (act, right.at[pl.ds(0, L), :]),
        (bundle.at[:, pl.ds(0, 2 * D)], right.at[pl.ds(L, L), :]),
        (tail0, sides.at[0]), (bundle.at[:, pl.ds(3 * D, D)], sides.at[1]),
        (main0, sides.at[2]), (bundle.at[:, pl.ds(2 * D, D)], sides.at[3]),
        (right0, right_out.at[pl.ds(0, L), :]),
    )
    for k, (src, dst) in enumerate(loads):
        load(src, dst, sems.at[k])
    left[:, :L] = c[...].T
    arrived(*loads[0], sems.at[0])

    @pl.when(flags[1] == 0)
    def _():
        left[:, L:] = c_oth[...].T

    @pl.when(flags[1] != 0)
    def _():
        left[:, L:] = c1[...].T

    for k in range(1, 3):
        arrived(*loads[k], sems.at[k])
    down[...] = dot(left[...], right[...]).astype(BF)
    for k in range(4):
        arrived(*loads[3 + k], sems.at[3 + k])
        (left_tail, left_main)[k // 2][:, L * (k % 2) : L * (k % 2 + 1)] = sides[k].T
    arrived(*loads[7], sems.at[7])
    for copy in leaving:
        copy.wait()


def gram_head_kernel(rows, right1, down, left, vec, right0, head, tail_up, tail_down, vec_out, right):
    right[:L, :] = right0[:L, 3 * D :]
    right[L:, :] = right1[:L, 3 * D :]
    head[...] = dot(left[...], right[...]).astype(BF)
    other = [
        jnp.concatenate(
            [right1[L : L + 16, 128 * (3 * k + b) : 128 * (3 * k + b + 1)].astype(F32) for b in range(3)], axis=0
        )
        for k in range(2)
    ]
    total = (vec[...] + (other[0] + other[1])).astype(BF)
    vec_out[...] = total.astype(F32)
    for k, t in enumerate((tail_up, tail_down)):
        here = own_rows(rows, 0, k, t.shape[0])
        t[:, :D] = head[here, :]
        t[:, D : 3 * D] = down[here, :]
        t[:, 3 * D :] = total


def gram_main_kernel(rows, right1, left, right_in, right, main, main_up, main_down):
    right[L:, :] = right1[:L, :]
    main[...] = dot(left[...], right[:, : 3 * D]).astype(BF)
    for k, m in enumerate((main_up, main_down)):
        m[...] = main[own_rows(rows, 0, k, m.shape[0]), :]


def own_rows(rows, t, way, r):
    return pl.ds(pl.multiple_of(rows[t, way], 16), r)


def add_kernel(t, way, rows, got, *refs, count, vector):
    parts, out = refs[:count], refs[count]
    here = own_rows(rows, t, way, got.shape[0])
    at = 0
    for part in parts:
        sl = slice(at, at + part.shape[1])
        out[:, sl] = (got[:, sl].astype(F32) + part[here, :].astype(F32)).astype(BF)
        at += part.shape[1]
    if out.shape[1] > at:
        out[:, at:] = got[:, at:]
    if vector:
        refs[count + 1][...] = got[:, at : at + 128].astype(F32)


def fold_vector(va, out):
    def fold(start):
        v = va[:, start : start + D]
        w = HEAD_DIM // 2
        return jnp.concatenate(
            [v[:, 2 * w * h : 2 * w * h + w] - v[:, 2 * w * h + w : 2 * w * (h + 1)] for h in range(HEADS)],
            axis=1,
        )

    at = FIRST + 3 * D
    out[:, :at] = va[:, :at]
    out[:, at : at + HALF] = fold(at)
    out[:, at + HALF : SECOND] = fold(at + D)
    out[:, SECOND:] = va[:, at + 2 * D :]


def packed_vector(ref):
    rows = [ref[:, 128 * k : 128 * (k + 1)] for k in range(VECTOR // 128)]
    rows += [jnp.zeros((1, 128), F32)] * (PACKED[0] - len(rows))
    return jnp.concatenate(rows, axis=0)


def sum_vectors(table, vectors, slots, outs):
    n = len(vectors)
    if table is None:
        total = vectors[0][...]
    else:
        slots[table[0, 2]] = vectors[0][...]
        for k in range(1, n):
            t, way = (k + 1) // 2, (k + 1) % 2
            slots[table[t, 2 + way]] = vectors[k][...]
        total = slots[0]
        for k in range(1, n):
            total = total + slots[k]
    at = 0
    for out in outs:
        for k in range(out.shape[1] // 128):
            out[:, 128 * k : 128 * (k + 1)] = total[at + k : at + k + 1, :]
        at += out.shape[1] // 128


def place_kernel(spots, whole, flags, rows, *refs):
    count, pair, vectors, into = whole
    ins, refs = refs[: count + pair + vectors], refs[count + pair + vectors + into :]
    out, buf, sems = refs[0], refs[-3], refs[-2]
    copies = []
    if pair:
        copies += both_rows(flags[0], ins[count], ins[count + 1], refs[1], refs[-1])
        copies[0].start()
        copies[1].start()
    r, w = ins[0].shape
    for k, (t, way, column) in enumerate(spots):
        buf[k] = ins[k][...].astype(F32)
        copy = pltpu.make_async_copy(
            buf.at[k], out.at[own_rows(rows, t, way, r), pl.ds(column, w)], sems.at[k]
        )
        copy.start()
        copies.append(copy)
    if vectors:
        outs = refs[1 + pair // 2 : 5 + pair // 2]
        sum_vectors(rows if vectors > 1 else None, ins[count + pair :], refs[-4], outs)
    for copy in copies:
        copy.wait()


SMEM = pl.BlockSpec(memory_space=pltpu.SMEM)
VS = pl.BlockSpec(memory_space=pltpu.VMEM)
HBM = pl.BlockSpec(memory_space=pltpu.HBM)
ANY = pl.BlockSpec(memory_space=pl.ANY)


def sds(shape, dtype=BF):
    return jax.ShapeDtypeStruct(shape, dtype)


def call(kernel, name, in_specs, outs, scratch, flops, nbytes, limit=58, out_specs=None, aliases=None):
    return pl.pallas_call(
        kernel,
        name=name,
        in_specs=in_specs,
        out_specs=[VS] * len(outs) if out_specs is None else out_specs,
        out_shape=outs,
        scratch_shapes=scratch,
        input_output_aliases={} if aliases is None else aliases,
        compiler_params=pltpu.CompilerParams(vmem_limit_bytes=limit * MIB),
        cost_estimate=pl.CostEstimate(flops=flops, bytes_accessed=nbytes, transcendentals=0),
    )


ATTN_W = [VM((4, D, D), BF)]
ANGLES = [VM((L, D), F32), VM((L, D), F32)]
MLP_W = [VM((4, D, D), BF), VM((4, D, D), BF)]
BACK_S = [VM((D, L), BF), VM((L, D), BF), VM((2, 128, L), F32), VM((16, L), F32)]


def in_vmem(a):
    return pltpu.with_memory_space_constraint(a, pltpu.VMEM)


def in_hbm(a):
    return pltpu.with_memory_space_constraint(a, pltpu.HBM)


def row(width=D):
    return VM((L, width), BF)


def row_out(width=D):
    return pltpu.HBM((L, width), BF)


def prepare(flags, n, x, cot, *vecs):
    out = VM((x.shape[0], L), BF)

    def kernel(*refs):
        prepare_kernel(*refs, n)

    table = pltpu.HBM((2 * n if n <= LONGEST else 1, 4), I32)
    return call(
        kernel, "prepare", [SMEM] + [VS] * 6, [out] * 4 + [pltpu.HBM((1, VECTOR), F32), table], [], 1000,
        int(1e6), 8, out_specs=[VS] * 5 + [SMEM],
    )(flags, *(in_hbm(a) for a in (x, cot) + vecs))


def positions(flags, grid, own, oth):
    hbm = pltpu.HBM
    return call(
        positions_kernel, "positions", [SMEM, SMEM, VS, VS],
        [VM((L, D), F32), VM((L, D), F32), hbm((L, 128), F32), hbm((8, L), F32),
         hbm((1, VECTOR), F32)],
        [], int(1e8), int(3e6), 56,
    )(flags, grid, own, oth)


def first_pass(*a):
    results = call(
        first_kernel, "first_pass", [SMEM] + [VS] * 8 + [HBM] * 2 + [VS] * 2,
        [row(), row_out()] + ANGLES + ATTN_W + MLP_W,
        [row(), VM((D, L), BF), row(3 * D), VM((HEADS, L, L), BF), VM((16, L), F32), row(), VM((D, L), BF),
         VM((D, L), BF), row(), DMA((13,))],
        int(8e9), int(20e6), 24, out_specs=[VS, HBM] + [VS] * HELD,
        aliases={len(a) - 2: 2, len(a) - 1: 3},
    )(*a)
    return results[0], results[1], results[2:]


SAVED = [VM((L, D), BF), VM((L, D), BF), VM((16, L), F32), VM((L, D), BF), VM((L, FF), BF)]
HEAD_S = [VM((L, 3 * D), BF), VM((HEADS, L, L), BF)]


def second_pass(held, *a):
    outs = [
        row_out(FF // 2), row_out(), row_out(), row_out(5 * D), row_out(3 * D), pltpu.HBM((HEADS, L, L), BF)
    ]
    resident = ANGLES + ATTN_W + MLP_W + SAVED
    results = call(
        second_kernel, "second_pass", [SMEM] + [VS] * (7 + HELD),
        resident + [row(FF // 2), row(FF // 2), row()] + outs,
        HEAD_S + [row(), row(), VM((D, L), BF), VM((D, L), BF), VM((L, D), F32), VM((L, D), F32)]
        + BACK_S + [row(3 * D), DMA((9,))],
        int(18e9), int(20e6), 24, out_specs=[VS] * (len(resident) + 3) + [HBM] * len(outs),
        aliases={len(a) + k: k for k in range(HELD)},
    )(*a, *(in_vmem(x) for x in held))
    n = len(resident)
    return results[:n], results[n : n + 2], results[n + 2], results[n + 3 :]


def late_pass(held, *a):
    results = call(
        late_kernel, "late_pass", [SMEM] + [VS] * (len(a) - 1 + len(held)),
        ANGLES + ATTN_W + MLP_W + SAVED + [sds((L, D))] * 2, [], int(2e9), int(5e6), 24,
        aliases={len(a) + k: k for k in range(len(held))},
    )(*a, *(in_vmem(x) for x in held))
    return results[: len(held)], results[len(held) :]


def back_pass(held, *a):
    return call(
        back_kernel, "back_pass", [SMEM] + [VS] * 5 + [HBM] * 2 + [VS] * len(held),
        [row(), row(), row(), VM(PACKED, F32), row_out(FF), pltpu.HBM((L + 16, FF), BF)],
        HEAD_S
        + [row(FF), row(FF), VM((1, FIRST + 6 * D), F32), VM((1, VECTOR), F32), VM((1, VECTOR), F32),
           VM((16, D), BF)]
        + BACK_S + [DMA((5,))],
        int(10e9), int(15e6), 24, out_specs=[VS] * 4 + [HBM] * 2,
    )(*a, *(in_vmem(x) for x in held))


def gram_down(*a):
    square = VM((D, 2 * L), BF)
    return call(
        gram_down_kernel, "gram_down", [SMEM] + [VS] * 6 + [HBM, ANY] + [HBM] * 3,
        [VM((D, 2 * D), BF), square, square, VM((2 * L, FF), BF), pltpu.HBM((2 * L, D), BF), row_out(), row_out()],
        [row(), VM((4, L, D), BF), square, VM((2 * L, 2 * D), BF), DMA((8,)), DMA((4,))], int(2e9), int(8e6), 20,
        out_specs=[VS] * 4 + [HBM] * 3,
    )(*a)


def gram_head(rows, r, *a):
    wide = VM((r, 3 * D + 128), BF)
    return call(
        gram_head_kernel, "gram_head", [SMEM] + [VS] * 5, [VM((D, D), BF), wide, wide, VM(PACKED, F32)],
        [VM((2 * L, D), BF)], int(1e9), int(5e6), 12,
    )(rows, *a)


def gram_main(rows, r, *a):
    shard = VM((r, 3 * D), BF)
    return call(
        gram_main_kernel, "gram_main", [SMEM] + [VS] * 3,
        [VM((2 * L, FF), BF), VM((D, 3 * D), BF), shard, shard], [], int(6e9), int(12e6), 20, aliases={3: 0},
    )(rows, *a)[1:]


def add(t, way, rows, got, parts, vector, wide):
    count = len(parts)

    def kernel(*refs):
        add_kernel(t, way, *refs, count=count, vector=vector)

    width = sum(p.shape[1] for p in parts)
    out = VM((got.shape[0], width + (128 if wide else 0)), BF)
    results = call(
        kernel, "add", [SMEM] + [VS] * (1 + count), [out] + [VM(PACKED, F32)] * vector, [], 1000, int(2e7), 4
    )(rows, in_vmem(got), *(in_vmem(p) for p in parts))
    return results[0], results[1:]


def place(flags, spots, rows, shards, total, pair=(), vectors=()):
    count = len(shards)
    into = [] if total is None else [total]
    whole = count, len(pair), len(vectors), len(into)

    def kernel(*refs):
        place_kernel(spots, whole, *refs)

    outs = [pltpu.HBM((D, 6 * D), F32)]
    outs += [pltpu.HBM((2 * L, D), BF)] if pair else []
    outs += [sds((1, w), F32) for w in (D, D, FF, D)] if vectors else []
    given = len(shards) + len(pair) + len(vectors)
    return call(
        kernel, "place", [SMEM, SMEM] + [VS] * given + [HBM] * len(into), outs,
        [VM((max(len(vectors), 1),) + PACKED, F32), VM((count,) + shards[0].shape, F32), DMA((count,)), DMA((2,))],
        1000,
        int(2e7), 24, out_specs=[HBM] * (2 if pair else 1) + ([VS] * 4 if vectors else []),
        aliases={given + 2: 0} if into else {},
    )(flags, rows, *shards, *pair, *vectors, *into)


def core_swap(a):
    return lax.ppermute(a, "section", [(0, 1), (1, 0), (2, 3), (3, 2)])


def after(value, first):
    return lax.optimization_barrier((value, first))[0]


class Cycle:
    def __init__(self, rows):
        self.n = n = lax.axis_size("dp")
        self.r = D // (2 * n)
        order = list(range(0, n, 2)) + list(range(n - 1, 0, -2))
        self.pairs = [[(order[k], order[(k + d) % n]) for k in range(n)] for d in (1, -1)]
        self.rows = rows

    def placed(self, k):
        return 2 * self.n - 1 if k == 0 else self.n + k - 1


class Chain:
    def __init__(self, cycle, parts, cur, carries=False):
        self.cycle, self.parts, self.cur, self.carries = cycle, parts, cur, carries
        self.t = 0
        self.shards = []
        self.vectors = []

    def step(self, token):
        c = self.cycle
        got = [lax.ppermute(a, "dp", p) for a, p in zip(self.cur, c.pairs)]
        self.t += 1
        t = self.t
        if t < c.n:
            self.cur = []
            for way in range(2):
                vector = self.carries and t <= (c.n - way) // 2
                out, came = add(
                    t, way, c.rows, after(got[way], token), self.parts, vector, self.carries and t < c.n // 2
                )
                self.cur.append(out)
                self.vectors += came
                token = out
        else:
            first = after(got[0], token)
            self.cur = [first, after(got[1], first)]
        if self.t >= c.n - 1:
            self.shards.append(self.cur)
        return self.cur


def small_ring():
    return lax.axis_size("dp") <= LONGEST


def summed(flags, rows, main, tail, token, pair, vector):
    if not small_ring():
        chains, vector = lax.psum([main, tail], "dp"), lax.psum(vector, "dp")
        return place(flags, [(0, 0, 0), (0, 0, 3 * D)], rows, chains, None, pair, [vector])
    cycle = main.cycle
    n = cycle.n
    total = None
    waiting, results = [], {}
    while main.t < 2 * n - 2:
        for chain, column in ((tail, 3 * D), (main, 0)):
            if total is not None:
                token = (token, total)
            token = chain.step(token)
            whole = len(chain.shards)
            if whole:
                t = cycle.placed(whole - 1)
                waiting += [((t, way, column), chain.shards[-1][way]) for way in range(2)]
            if whole == n or chain is main and whole and whole % 2 == 0:
                now, then = "rows" not in results, "vectors" not in results and whole >= min(4, n)
                total, *more = place(
                    flags, [a for a, _ in waiting], cycle.rows, [b for _, b in waiting], total,
                    pair if now else (), [vector] + tail.vectors if then else (),
                )
                if now:
                    results["rows"] = more.pop(0)
                if then:
                    results["vectors"] = more
                waiting = []
    return total, results["rows"], *results["vectors"]


def body(
    block_input, cotangent, grid_sizes, section_weight, norm_gain, norm_bias, first_vector, second_vector
):
    section = lax.axis_index("section")
    core = section % 2
    n = lax.axis_size("dp")
    i = lax.axis_index("dp")
    where = jnp.where(i % 2 == 0, i // 2, n - 1 - i // 2)
    flags = in_hbm(jnp.stack([core, section // 2, where]).astype(I32))
    first_layer = section < 2

    keep, send, away, across, vown, rows = prepare(
        flags, n, block_input.T, cotangent.T, norm_gain, norm_bias, first_vector, second_vector
    )
    if n % 2 == 0:
        voth = lax.ppermute(
            vown, ("section", "dp"), [(n * s + d, n * (s ^ 1) + (d ^ 1)) for s in range(4) for d in range(n)]
        )
    else:
        voth = core_swap(vown)
    r = D // (2 * n) if small_ring() else PACKED[0]
    cosf, sinf, pos, segr, voth = positions(flags, grid_sizes, in_hbm(vown), in_vmem(voth))
    vown, voth, rows, pos, segr = (in_hbm(a) for a in (vown, voth, rows, pos, segr))
    got = core_swap(send)
    away = lax.ppermute(away, "section", [(0, 2), (1, 3), (2, 0), (3, 1)])
    across = lax.ppermute(across, "section", [(0, 3), (1, 2), (2, 1), (3, 0)])
    own = in_hbm(section_weight[0])
    oth = in_hbm(core_swap(section_weight[0]))

    x_two, field, held = first_pass(
        flags, keep, got, away, across, vown, voth, pos, segr, own, oth, in_vmem(cosf), in_vmem(sinf)
    )
    field = in_hbm(field)
    x_got, x_late = (lax.ppermute(x_two, "section", [pair]) for pair in ((0, 2), (1, 3)))
    held, active, c_two, (act_mine, main_left, tail_left, bundle, qkv, pt) = second_pass(
        held, flags, field, x_got, x_late, vown, voth, pos, segr
    )
    act_mine, main_left, tail_left = (in_hbm(a) for a in (act_mine, main_left, tail_left))
    c_got = lax.ppermute(c_two, "section", [(2, 0), (3, 1)])
    held, (x_keep, x_send) = late_pass(held, flags, x_two, vown, voth, *(in_vmem(a) for a in active))
    c_got = after(c_got, x_keep)
    bundle = core_swap(after(bundle, c_got))
    x_oth = core_swap(after(x_send, c_got))

    c_keep, c_send, c_out, vec, right, right_send = back_pass(
        held, flags, field, c_got, vown, voth, pos, in_hbm(qkv), in_hbm(pt)
    )
    c_oth = core_swap(c_got)
    right_oth = core_swap(after(right_send, (c_oth, bundle, x_oth)))
    down, left_main, left_tail, right, activations, c_keep, c_send = gram_down(
        flags, c_out, c_oth, x_keep, x_oth, in_vmem(c_keep), in_vmem(c_send), act_mine, bundle, main_left, tail_left, in_hbm(right)
    )
    head, *tail_first, vec = gram_head(rows, r, right_oth, down, left_tail, vec, right)
    if small_ring():
        cycle = Cycle(rows)
        tail = Chain(cycle, [head, down], tail_first, True)
    else:
        tail = jnp.concatenate([head, down], axis=1)
    main, *main_first = gram_main(rows, r, right_oth, left_main, right)
    if small_ring():
        main = Chain(cycle, [main], main_first)
        token = main.cur
    else:
        token = main
    weight_grad, input_grads, *vectors = summed(
        flags, rows, main, tail, token, (c_keep, core_swap(after(c_send, token))), vec
    )
    return (
        activations[None],
        input_grads[None],
        weight_grad[None],
        *vectors,
    )


def solution(mesh):
    in_specs = (
        P("dp", "section"),
        P("dp", "section"),
        P("dp", None, None),
        P("section", None, None),
        P("section", None),
        P("section", None),
        P("section", None),
        P("section", None),
    )
    out_specs = (
        P("section", "dp", None),
        P("section", "dp", None),
        P("section", None, None),
        P("section", None),
        P("section", None),
        P("section", None),
        P("section", None),
    )
    return jax.shard_map(body, mesh=mesh, in_specs=in_specs, out_specs=out_specs, check_vma=False)
```
